32 devices in a mesh: dp: 2 (over x), ctx: 16 (over z, y, core).
Axes of the slice: x: 2, y: 2, z: 4, core: 2. Of those that a mesh axis runs over, the one named last changes fastest.
Arguments:
- tokens: bfloat16 [2, 2048, 4096], P('dp', 'ctx'), may hold values from -6 to 6
- proj_weight: bfloat16 [4096, 512], P('dp'), may hold values from -0.09375 to 0.09375
- values: bfloat16 [2, 2048, 2048], P('dp', 'ctx'), may hold values from -60 to 60
- grad_out: bfloat16 [2, 2048, 2048], P('dp', 'ctx'), may hold values from -6 to 6
Outputs:
- attended: bfloat16 [2, 2048, 2048], P('dp', 'ctx')
- grad_tokens: bfloat16 [2, 2048, 4096], P('dp', 'ctx')
- grad_values: bfloat16 [2, 2048, 2048], P('dp', 'ctx')
- grad_proj: float32 [4096, 512], P(('dp', 'ctx'))
The draws below stay inside these ranges and needn't reach their ends.
All inputs are finite; a program needn't handle non-finite values.
Results may differ from the reference program's by a relative error of at most 0.0049.
Values may be sent and summed in bfloat16 or wider, within the bound.
No kernel may reach another device: no remote copies, remote signals or barrier semaphores. Data moves between devices by JAX's collectives and lax.ppermute only.
A program may use at most 192 MiB of HBM per device.

```python
import jax
import jax.numpy as jnp
from jax import lax

D = 4096
H = 16
F = 16
DH = 128
E = 273
TOK_DEV = 128
BATCH = 2
SEQ = 2048


def draw_values(key, part):
    key_random, key_scale = jax.random.split(key, 2)
    scales = jnp.exp(jax.random.uniform(key_scale, (H * DH,), jnp.float32, 0.0, 2.302585))
    random_part = jnp.clip(jax.random.normal(key_random, (BATCH, SEQ, H * DH), jnp.float32), -6.0, 6.0)
    return (random_part * scales).astype(jnp.bfloat16)


def strengthened(entries, own_key, source, target, blocks, factor):
    owner, partner = [(jnp.arange(entries.shape[dim]) // (entries.shape[dim] // blocks)).reshape([-1 if axis == dim else 1 for axis in range(entries.ndim)]) for dim in (source, target)]
    chosen = jax.random.permutation(own_key, blocks)[partner]
    strong = (owner == chosen) | (owner == (partner + blocks // 2) % blocks)
    return jnp.where(strong, factor * entries, entries)


def steps_of(own_key, dims, cuts, smallest, high):
    def one(axis_at, blocks):
        steps = jax.random.uniform(jax.random.fold_in(jax.random.fold_in(own_key, 6), axis_at), (blocks,), jnp.float32, smallest / len(cuts), high / len(cuts))
        return jnp.repeat(jnp.exp(steps), dims[axis_at] // blocks).reshape((-1,) + (1,) * (len(dims) - axis_at - 1))

    loudness = one(*cuts[0])
    for cut in cuts[1:]:
        loudness = loudness * one(*cut)
    return loudness


def centred(rng, extent, width, most, shards=(), kind=jnp.bfloat16):
    gain = steps_of(rng, extent, shards, -0.22, 0.18) if shards else 1.0
    entries = jax.random.normal(rng, extent, jnp.float32) * width * gain
    return jnp.minimum(jnp.maximum(entries, -most), most).astype(kind)


def heavy_noise(rng, extent, scale, reach, shards, heavy, held_as=jnp.bfloat16):
    drawn = scale * jax.random.normal(rng, extent, jnp.float32)
    if shards:
        drawn = drawn * steps_of(rng, extent, shards, -0.22, 0.18)
    return jnp.clip(strengthened(drawn, jax.random.fold_in(rng, 3), *heavy), -reach, reach).astype(held_as)


def setup_inputs(seed: int = 0) -> dict:
    key_list = jax.random.split(jax.random.key(seed), 5)
    tokens = heavy_noise(key_list[0], (BATCH, SEQ, D), 1.0, 6.0, ((0, 2), (1, 16)), (1, 2, 16, 2.0))
    proj_weight = centred(key_list[1], (D, 2 * H * F), D ** -0.5, 0.09375, ((0, 2),))
    values = draw_values(jax.random.fold_in(key_list[4], 71), 0)
    grad_out = centred(key_list[3], (BATCH, SEQ, H * DH), 1.0, 6.0, ((0, 2), (1, 16)))
    return {"tokens": tokens, "proj_weight": proj_weight, "values": values, "grad_out": grad_out}


HIGHEST = lax.Precision.HIGHEST
QUAD_SCALE = 0.17677669529663687
EPSILON = 1e-05

def features(inputs):
    count_heads, count_rows, count_feat = inputs.shape
    linear = jnp.swapaxes(inputs, 1, 2) * 0.5
    square = (inputs[:, :, :, None] * inputs[:, :, None, :]).reshape(count_heads, count_rows, count_feat * count_feat)
    square = jnp.swapaxes(square, 1, 2) * QUAD_SCALE
    constant_row = jnp.ones((count_heads, 1, count_rows), inputs.dtype)
    return jnp.concatenate([constant_row, linear, square], axis=1)

def block_kernel(query_part, key_part):
    count_rows = query_part.shape[1]
    causal = lax.broadcasted_iota(jnp.int32, (count_rows, count_rows), 0) >= lax.broadcasted_iota(jnp.int32, (count_rows, count_rows), 1)
    scores = jnp.einsum('htf,hsf->hts', query_part, key_part, precision=HIGHEST) * 0.25
    kernel = jnp.where(causal, 1.0 + scores + 0.5 * scores * scores, 0.0)
    return (causal, scores, kernel)

def normalize(numerator):
    inv_rms = lax.rsqrt(lax.optimization_barrier(jnp.mean(numerator * numerator, axis=-1, keepdims=True)) + EPSILON)
    return (inv_rms, numerator * inv_rms)

def grad_normalize(inv_rms, normed, upstream):
    return inv_rms * (upstream - normed * lax.optimization_barrier(jnp.mean(normed * upstream, axis=-1, keepdims=True)))

def local_backward(query_part, key_part, value_part, grad_num, causal, scores, kernel, pull_query, pull_key, feat_key, prefix, suffix):
    mixing = jnp.where(causal, jnp.einsum('htd,hsd->hts', grad_num, value_part, precision=HIGHEST), 0.0)
    slope = mixing * (1.0 + scores)
    grad_query = jnp.einsum('hts,hsf->htf', slope, key_part, precision=HIGHEST) * 0.25
    grad_key = jnp.einsum('hts,htf->hsf', slope, query_part, precision=HIGHEST) * 0.25
    grad_query = grad_query + pull_query(jnp.einsum('hed,htd->het', prefix, grad_num, precision=HIGHEST))[0]
    grad_key = grad_key + pull_key(jnp.einsum('hed,htd->het', suffix, value_part, precision=HIGHEST))[0]
    grad_value = jnp.einsum('hts,htd->hsd', kernel, grad_num, precision=HIGHEST)
    grad_value = grad_value + jnp.einsum('het,hed->htd', feat_key, suffix, precision=HIGHEST)
    return (grad_query, grad_key, grad_value)

def split_blocks(matrix, size):
    blocks = matrix.shape[0] // TOK_DEV
    return matrix.reshape(blocks, TOK_DEV, H, size).transpose(0, 2, 1, 3)

def merge_blocks(blocked):
    return blocked.transpose(0, 2, 1, 3).reshape(blocked.shape[0] * blocked.shape[2], -1)

def sequence_pass(tokens_seq, proj_weight, values_seq, grad_seq):
    projected = jnp.dot(tokens_seq, proj_weight, preferred_element_type=jnp.float32)
    query_cols = H * F
    query_all = split_blocks(projected[:, :query_cols], F)
    key_all = split_blocks(projected[:, query_cols:], F)
    value_all = split_blocks(values_seq.astype(jnp.float32), DH)
    upstream_all = split_blocks(grad_seq.astype(jnp.float32), DH)
    zero_state = jnp.zeros((H, E, DH), jnp.float32)

    def forward_step(state, block):
        query_part, key_part, value_part = block
        feat_query = features(query_part)
        feat_key = features(key_part)
        causal, scores, kernel = block_kernel(query_part, key_part)
        numerator = jnp.einsum('hts,hsd->htd', kernel, value_part, precision=HIGHEST)
        numerator = numerator + jnp.einsum('het,hed->htd', feat_query, state, precision=HIGHEST)
        new_state = state + jnp.einsum('het,htd->hed', feat_key, value_part, precision=HIGHEST)
        return (new_state, (numerator, state))
    final_state, (numerators, prefixes) = lax.scan(forward_step, zero_state, (query_all, key_all, value_all))
    inv_rms, normed = normalize(numerators)
    attended = merge_blocks(normed).astype(jnp.bfloat16)
    grad_num_all = grad_normalize(inv_rms, normed, upstream_all)

    def backward_step(suffix, block):
        query_part, key_part, value_part, grad_num, prefix = block
        feat_query, pull_query = jax.vjp(features, query_part)
        feat_key, pull_key = jax.vjp(features, key_part)
        causal, scores, kernel = block_kernel(query_part, key_part)
        grads = local_backward(query_part, key_part, value_part, grad_num, causal, scores, kernel, pull_query, pull_key, feat_key, prefix, suffix)
        new_suffix = suffix + jnp.einsum('het,htd->hed', feat_query, grad_num, precision=HIGHEST)
        return (new_suffix, grads)
    last_suffix, (grad_query, grad_key, grad_value) = lax.scan(backward_step, zero_state, (query_all, key_all, value_all, grad_num_all, prefixes), reverse=True)
    grad_proj_rows = jnp.concatenate([merge_blocks(grad_query), merge_blocks(grad_key)], axis=1).astype(jnp.bfloat16)
    grad_tokens = jnp.dot(grad_proj_rows, proj_weight.T, preferred_element_type=jnp.float32).astype(jnp.bfloat16)
    grad_part = jnp.dot(tokens_seq.T, grad_proj_rows, preferred_element_type=jnp.float32)
    grad_values = merge_blocks(grad_value).astype(jnp.bfloat16)
    return (attended, grad_tokens, grad_values, grad_part)

def reference(tokens, proj_weight, values, grad_out):

    def per_sequence(total, inputs):
        tokens_seq, values_seq, grad_seq = inputs
        attended, grad_tokens, grad_values, grad_part = sequence_pass(tokens_seq, proj_weight, values_seq, grad_seq)
        return (total + grad_part, (attended, grad_tokens, grad_values))
    start_total = jnp.zeros((D, 2 * H * F), jnp.float32)
    grad_proj, (attended, grad_tokens, grad_values) = lax.scan(per_sequence, start_total, (tokens, values, grad_out))
    return (attended, grad_tokens, grad_values, grad_proj)
```

```python
import functools

import jax
import jax.numpy as jnp
from jax import lax
from jax.experimental import pallas as pl
from jax.experimental.pallas import tpu as pltpu
from jax.sharding import PartitionSpec as P

H = 16
F = 16
DH = 128
EPSILON = 1e-05
GROUP = 8
TILE = 256
PSI = 9 * F + 2 * F
PSI_SCALE = (0.5,) + (1.0,) * 7 + (0.5,)

f32 = jnp.float32
bf16 = jnp.bfloat16

NN = (((1,), (0,)), ((), ()))
NT = (((1,), (1,)), ((), ()))


def dot(a, b, dims=NN):
    return lax.dot_general(a, b, dims, preferred_element_type=f32)


def split(x):
    high = x.astype(bf16)
    return high, (x - high.astype(f32)).astype(bf16)


def dot3(a, b, dims=NN):
    a_high, a_low = split(a)
    b_high, b_low = split(b)
    return dot(a_high, b_high, dims) + (dot(a_high, b_low, dims) + dot(a_low, b_high, dims))


def turned(x, r):
    return x if r == 0 else jnp.concatenate([x[r:], x[:r]], axis=0)


def psi(x, weights):
    parts = []
    for r in range(9):
        part = x * turned(x, r)
        parts.append(part * PSI_SCALE[r] if weights and PSI_SCALE[r] != 1.0 else part)
    row = lax.broadcasted_iota(jnp.int32, x.shape, 0)
    return jnp.concatenate(parts + [x, jnp.where(row == 0, 1.0, 0.0)], axis=0)


def pull_psi(x, upstream, weights):
    total = upstream[9 * F : 10 * F]
    for r in range(9):
        part = upstream[r * F : (r + 1) * F]
        if weights and PSI_SCALE[r] != 1.0:
            part = part * PSI_SCALE[r]
        total = total + part * turned(x, r) + turned(part * x, (F - r) % F)
    return total


def feature_major(qk_ref, which, head):
    return jnp.concatenate([qk_ref[src, which, head] for src in range(qk_ref.shape[0])], axis=1)


def rows_of(ref, which, head, start, stop):
    tok = ref.shape[2]
    return jnp.concatenate(
        [
            ref[src, which, :, head * DH : (head + 1) * DH]
            for src in range(start // tok, stop // tok)
        ],
        axis=0,
    )


def score_sides(q, k):
    q_high, q_low = split(q)
    k_high, k_low = split(k)
    left = jnp.concatenate([q_high, q_high, q_low, q_low], axis=0)
    right = jnp.concatenate([k_high, k_low, k_high, k_low], axis=0)
    return left.T, right


def causal_mask(tile, width):
    row = lax.broadcasted_iota(jnp.int32, (tile, width), 0) + (width - tile)
    return row >= lax.broadcasted_iota(jnp.int32, (tile, width), 1)


def state_kernel(qk_ref, vg_ref, state_ref):
    heads = qk_ref.shape[2]
    length = qk_ref.shape[0] * qk_ref.shape[4]
    for head in range(heads):
        high, low = split(psi(feature_major(qk_ref, 1, head), False))
        v = rows_of(vg_ref, 0, head, 0, length)
        state_ref[head] = dot(high, v) + dot(low, v)


def numerator_kernel(qk_ref, vg_ref, num_ref):
    heads = qk_ref.shape[2]
    length = qk_ref.shape[0] * qk_ref.shape[4]
    tile = min(TILE, length)
    for head in range(heads):
        q = feature_major(qk_ref, 0, head) * 0.25
        k = feature_major(qk_ref, 1, head)
        left, right = score_sides(q, k)
        for at in range(0, length, tile):
            width = at + tile
            scores = dot(left[at:width], right[:, :width])
            kernel = jnp.where(
                causal_mask(tile, width), 1.0 + scores * (1.0 + 0.5 * scores), 0.0
            )
            high, low = split(kernel)
            v = rows_of(vg_ref, 0, head, 0, width)
            num_ref[at:width, head * DH : (head + 1) * DH] = dot(high, v) + dot(low, v)


def normalize_kernel(with_state, qk_ref, vg_ref, num_ref, *rest):
    if with_state:
        prefix_ref, attended_ref, grad_ref, carried_ref = rest
    else:
        attended_ref, grad_ref = rest
    heads = qk_ref.shape[2]
    blocks, tok = qk_ref.shape[0], qk_ref.shape[4]
    length = blocks * tok
    for head in range(heads):
        cols = slice(head * DH, (head + 1) * DH)
        numerator = num_ref[:, cols]
        if with_state:
            feat = psi(feature_major(qk_ref, 0, head) * 0.25, True)
            numerator = numerator + dot3(feat.T, prefix_ref[head])
        inv_rms = lax.rsqrt(jnp.mean(numerator * numerator, axis=-1, keepdims=True) + EPSILON)
        normed = numerator * inv_rms
        upstream = rows_of(vg_ref, 1, head, 0, length).astype(f32)
        grad = inv_rms * (
            upstream - normed * jnp.mean(normed * upstream, axis=-1, keepdims=True)
        )
        attended = normed.astype(bf16)
        for src in range(blocks):
            attended_ref[src, :, cols] = attended[src * tok : (src + 1) * tok]
        grad_ref[:, cols] = grad
        if with_state:
            carried_ref[head] = dot3(feat, grad)


def backward_kernel(with_state, qk_ref, vg_ref, grad_ref, *rest):
    if with_state:
        prefix_ref, grad_qk_ref, grad_v_ref = rest
    else:
        grad_qk_ref, grad_v_ref = rest
    heads = qk_ref.shape[2]
    length = qk_ref.shape[0] * qk_ref.shape[4]
    tile = min(TILE, length)
    for head in range(heads):
        cols = slice(head * DH, (head + 1) * DH)
        q = feature_major(qk_ref, 0, head) * 0.25
        k = feature_major(qk_ref, 1, head)
        left, right = score_sides(q, k)
        q_both = jnp.concatenate(split(q), axis=0)
        k_both = jnp.concatenate(split(k), axis=0)
        grad = grad_ref[:, cols]
        grad_t = grad.T
        if with_state:
            grad_q = pull_psi(q, dot3(prefix_ref[head], grad_t), True)
        for at in reversed(range(0, length, tile)):
            width = at + tile
            scores = dot(left[at:width], right[:, :width])
            causal = causal_mask(tile, width)
            v = rows_of(vg_ref, 0, head, 0, width)
            high, low = split(grad[at:width])
            mixing = dot(
                jnp.concatenate([high, low], axis=1), jnp.concatenate([v, v], axis=1), NT
            )
            more = 1.0 + scores
            slope = jnp.where(causal, mixing * more, 0.0).astype(bf16)
            kernel = jnp.where(causal, more + 0.5 * scores * scores, 0.0).astype(bf16)
            both = dot(k_both[:, :width], slope, NT)
            piece = both[:F] + both[F:]
            if with_state:
                piece = piece + grad_q[:, at:width]
            grad_qk_ref[0, head, :, at:width] = piece * 0.25
            both = dot(q_both[:, at:width], slope)
            piece_k = both[:F] + both[F:]
            both = dot(jnp.concatenate(split(grad_t[:, at:width]), axis=0), kernel)
            piece_v = both[:DH] + both[DH:]
            if width == length:
                grad_qk_ref[1, head] = piece_k
                grad_v_ref[head] = piece_v
            else:
                grad_qk_ref[1, head, :, :width] += piece_k
                grad_v_ref[head, :, :width] += piece_v


def finish_kernel(with_state, qk_ref, vg_ref, grad_qk_ref, grad_v_ref, *rest):
    if with_state:
        suffix_ref, rows_ref, out_ref = rest
    else:
        rows_ref, out_ref = rest
    heads = qk_ref.shape[2]
    blocks, tok = qk_ref.shape[0], qk_ref.shape[4]
    length = blocks * tok
    for head in range(heads):
        grad_k = grad_qk_ref[1, head]
        grad_v = grad_v_ref[head]
        if with_state:
            k = feature_major(qk_ref, 1, head)
            v = rows_of(vg_ref, 0, head, 0, length)
            suffix = suffix_ref[head]
            high, low = split(suffix)
            grad_k = grad_k + pull_psi(k, dot(high, v, NT) + dot(low, v, NT), False)
            grad_v = grad_v + dot3(suffix.T, psi(k, False))
        rows_ref[0, head] = grad_qk_ref[0, head].astype(bf16)
        rows_ref[1, head] = grad_k.astype(bf16)
        grad_v = grad_v.T.astype(bf16)
        for src in range(blocks):
            out_ref[src, :, head * DH : (head + 1) * DH] = grad_v[src * tok : (src + 1) * tok]


def call(body, out_shapes, flops, *operands):
    return pl.pallas_call(
        body,
        out_shape=[jax.ShapeDtypeStruct(shape, kind) for shape, kind in out_shapes],
        in_specs=[pl.BlockSpec(memory_space=pltpu.VMEM)] * len(operands),
        out_specs=[pl.BlockSpec(memory_space=pltpu.VMEM)] * len(out_shapes),
        compiler_params=pltpu.CompilerParams(vmem_limit_bytes=48 * 1024 * 1024),
        cost_estimate=pl.CostEstimate(flops=flops, bytes_accessed=4 << 20, transcendentals=0),
    )(*operands)


def local(dp_size, ctx_size, tokens, proj_weight, values, grad_out):
    group = min(GROUP, ctx_size, H)
    runs = ctx_size // group
    heads = H // group
    tok, width = tokens.shape[1:]
    length = group * tok
    cols = proj_weight.shape[1]
    share = width // dp_size
    depth = share // ctx_size
    with_state = runs > 1
    groups = [[run * group + i for i in range(group)] for run in range(runs)]
    dp_at, ctx_at = lax.axis_index("dp"), lax.axis_index("ctx")
    run_at, member = ctx_at // group, ctx_at % group

    def exchange(x):
        return lax.all_to_all(
            x, "ctx", split_axis=0, concat_axis=0, tiled=True, axis_index_groups=groups
        )

    def to_dp(x, shift):
        return lax.ppermute(x, "dp", [(i, (i + shift) % dp_size) for i in range(dp_size)])

    def to_run(x, shift, wrap):
        pairs = [
            (i, (i + shift * group) % ctx_size)
            for i in range(ctx_size)
            if wrap or 0 <= i + shift * group < ctx_size
        ]
        return lax.ppermute(x, "ctx", pairs)

    token_rows = tokens[0]

    def token_part(owner):
        return lax.dynamic_slice_in_dim(token_rows, owner * share, share, axis=1)

    def project(part):
        return lax.dot_general(
            proj_weight, part, (((0,), (1,)), ((), ())), preferred_element_type=f32
        )

    with jax.named_scope("projection"):
        arrived = [
            to_dp(token_part((dp_at + shift) % dp_size), shift) for shift in range(1, dp_size)
        ]
        projected = project(token_part(dp_at))
        for shift in range(1, dp_size):
            projected = projected + to_dp(project(arrived[shift - 1]), -shift)
    with jax.named_scope("to_heads"):
        both = jnp.stack([values[0], grad_out[0]]).reshape(2, tok, group, heads * DH)
        vg = exchange(both.transpose(2, 0, 1, 3))
        qk = exchange(
            projected.reshape(2, group, heads, F, tok).transpose(1, 0, 2, 3, 4)
        )
    with jax.named_scope("weight"):
        pair = 2 if ctx_size % 2 == 0 else 1
        piece = share // pair
        mine = lax.dynamic_slice_in_dim(proj_weight, (ctx_at % pair) * piece, piece, axis=0)
        weights = [proj_weight]
        for shift in range(1, dp_size):
            half = to_dp(mine, shift)
            if pair == 2:
                other = lax.ppermute(half, "ctx", [(i, i ^ 1) for i in range(ctx_size)])
                first = ctx_at % 2 == 0
                half = jnp.concatenate(
                    [jnp.where(first, half, other), jnp.where(first, other, half)], axis=0
                )
            weights.append(half)
    with jax.named_scope("token_columns"):
        token_cols = exchange(
            token_rows.reshape(tok, dp_size * runs, group, depth).transpose(2, 0, 1, 3)
        ).reshape(length, dp_size * runs * depth)

    pairs = heads * length * (length + TILE) // 2
    state_flops = 4 * heads * length * PSI * DH
    state_shape = ((heads, PSI, DH), f32)
    rows_shape = ((length, heads * DH), f32)
    blocks_shape = ((group, tok, heads * DH), bf16)
    prefix, suffix = (), ()
    if with_state:
        (state,) = call(state_kernel, [state_shape], state_flops, qk, vg)
        prefix = (sum(to_run(state, shift, False) for shift in range(1, runs)),)
    (numerator,) = call(numerator_kernel, [rows_shape], pairs * 2 * 512, qk, vg)
    result = call(
        functools.partial(normalize_kernel, with_state),
        [blocks_shape, rows_shape] + [state_shape] * with_state,
        2 * state_flops,
        qk,
        vg,
        numerator,
        *prefix,
    )
    attended, grad_num = result[:2]
    if with_state:
        suffix = (sum(to_run(result[2], -shift, False) for shift in range(1, runs)),)
    grad_qk, grad_v = call(
        functools.partial(backward_kernel, with_state),
        [((2, heads, F, length), f32), ((heads, DH, length), f32)],
        pairs * 2 * 1024,
        qk,
        vg,
        grad_num,
        *prefix,
    )
    rows, grad_v = call(
        functools.partial(finish_kernel, with_state),
        [((2, heads, F, length), bf16), blocks_shape],
        state_flops,
        qk,
        vg,
        grad_qk,
        grad_v,
        *suffix,
    )
    with jax.named_scope("rows"):
        gathered = exchange(jnp.broadcast_to(rows[None], (group,) + rows.shape))
        gathered = gathered.transpose(1, 0, 2, 3, 4).reshape(cols, length)
    with jax.named_scope("from_heads"):
        attended = exchange(attended).transpose(1, 0, 2).reshape(1, tok, H * DH)
        grad_values = exchange(grad_v).transpose(1, 0, 2).reshape(1, tok, H * DH)
    with jax.named_scope("grad_proj"):
        product = lax.dot_general(
            token_cols, gathered, (((0,), (1,)), ((), ())), preferred_element_type=f32
        ).reshape(dp_size, runs, depth, cols)
        total = lax.dynamic_index_in_dim(product, dp_at, 0, keepdims=False)
        for shift in range(1, dp_size):
            part = lax.dynamic_index_in_dim(
                product, (dp_at + shift) % dp_size, 0, keepdims=False
            )
            total = total + to_dp(part.astype(bf16), shift).astype(f32)
        grad_proj = lax.dynamic_index_in_dim(total, run_at, 0, keepdims=False)
        for shift in range(1, runs):
            part = lax.dynamic_index_in_dim(total, (run_at + shift) % runs, 0, keepdims=False)
            grad_proj = grad_proj + to_run(part.astype(bf16), shift, True).astype(f32)
    with jax.named_scope("grad_tokens"):
        own_rows = lax.dynamic_slice_in_dim(gathered, member * tok, tok, axis=1)
        grad_tokens = jnp.zeros((tok, width), bf16)
        for shift in range(dp_size):
            part = lax.dot_general(
                own_rows, weights[shift], (((0,), (1,)), ((), ())), preferred_element_type=f32
            ).astype(bf16)
            grad_tokens = lax.dynamic_update_slice_in_dim(
                grad_tokens, part, ((dp_at - shift) % dp_size) * share, axis=1
            )
    return (attended, grad_tokens[None], grad_values, grad_proj)


def solution(mesh):
    return jax.shard_map(
        functools.partial(local, mesh.shape["dp"], mesh.shape["ctx"]),
        mesh=mesh,
        in_specs=(P("dp", "ctx", None), P("dp", None), P("dp", "ctx", None), P("dp", "ctx", None)),
        out_specs=(
            P("dp", "ctx", None),
            P("dp", "ctx", None),
            P("dp", "ctx", None),
            P(("dp", "ctx"), None),
        ),
        check_vma=False,
    )
```

```python
import functools

import jax
import jax.numpy as jnp
from jax import lax
from jax.experimental import pallas as pl
from jax.experimental.pallas import tpu as pltpu
from jax.sharding import PartitionSpec as P

H = 16
F = 16
DH = 128
EPSILON = 1e-05
GROUP = 8
TILE = 256
PSI = 9 * F + 2 * F
PSI_SCALE = (0.5,) + (1.0,) * 7 + (0.5,)

f32 = jnp.float32
bf16 = jnp.bfloat16

NN = (((1,), (0,)), ((), ()))
NT = (((1,), (1,)), ((), ()))


def dot(a, b, dims=NN):
    return lax.dot_general(a, b, dims, preferred_element_type=f32)


def split(x):
    high = x.astype(bf16)
    return high, (x - high.astype(f32)).astype(bf16)


def dot3(a, b, dims=NN):
    a_high, a_low = split(a)
    b_high, b_low = split(b)
    return dot(a_high, b_high, dims) + (dot(a_high, b_low, dims) + dot(a_low, b_high, dims))


def turned(x, r):
    return x if r == 0 else jnp.concatenate([x[r:], x[:r]], axis=0)


def psi(x, weights):
    parts = []
    for r in range(9):
        part = x * turned(x, r)
        parts.append(part * PSI_SCALE[r] if weights and PSI_SCALE[r] != 1.0 else part)
    row = lax.broadcasted_iota(jnp.int32, x.shape, 0)
    return jnp.concatenate(parts + [x, jnp.where(row == 0, 1.0, 0.0)], axis=0)


def pull_psi(x, upstream, weights):
    total = upstream[9 * F : 10 * F]
    for r in range(9):
        part = upstream[r * F : (r + 1) * F]
        if weights and PSI_SCALE[r] != 1.0:
            part = part * PSI_SCALE[r]
        total = total + part * turned(x, r) + turned(part * x, (F - r) % F)
    return total


def feature_major(qk_ref, which, head):
    return jnp.concatenate([qk_ref[src, which, head] for src in range(qk_ref.shape[0])], axis=1)


def rows_of(ref, which, head, start, stop):
    tok = ref.shape[2]
    return jnp.concatenate(
        [
            ref[src, which, :, head * DH : (head + 1) * DH]
            for src in range(start // tok, stop // tok)
        ],
        axis=0,
    )


def score_sides(q, k):
    q_high, q_low = split(q)
    k_high, k_low = split(k)
    left = jnp.concatenate([q_high, q_high, q_low, q_low], axis=0)
    right = jnp.concatenate([k_high, k_low, k_high, k_low], axis=0)
    return left.T, right


def causal_mask(tile, width):
    row = lax.broadcasted_iota(jnp.int32, (tile, width), 0) + (width - tile)
    return row >= lax.broadcasted_iota(jnp.int32, (tile, width), 1)


def token_parts_kernel(at_ref, tokens_ref, *out_refs):
    count = len(out_refs)
    share = out_refs[0].shape[1]
    for shift, out_ref in enumerate(out_refs):
        owner = lax.rem(at_ref[0] + shift, count)
        out_ref[...] = tokens_ref[0, :, pl.ds(pl.multiple_of(owner * share, share), share)]


def pack_heads_kernel(values_ref, grad_ref, out_ref):
    group, width = out_ref.shape[0], out_ref.shape[3]
    for member in range(group):
        cols = slice(member * width, (member + 1) * width)
        out_ref[member, 0] = values_ref[0, :, cols]
        out_ref[member, 1] = grad_ref[0, :, cols]


def pack_tokens_kernel(depth, tokens_ref, out_ref):
    group, rows = out_ref.shape[:2]
    for member in range(group):
        for part in range(rows // depth):
            first = (part * group + member) * depth
            out_ref[member, part * depth : (part + 1) * depth] = tokens_ref[
                0, :, first : first + depth
            ].T


def projected_blocks(part, weight, out_ref):
    projected = dot(part, weight).T
    group, _, heads, feat, _ = out_ref.shape
    for member in range(group):
        for which in range(2):
            for head in range(heads):
                first = ((which * group + member) * heads + head) * feat
                out_ref[member, which, head] = projected[first : first + feat]


def project_kernel(part_ref, weight_ref, out_ref):
    projected_blocks(part_ref[...], weight_ref[...], out_ref)


def project_rest_kernel(at_ref, own_ref, weight_ref, *rest):
    *part_refs, out_ref = rest
    count = len(part_refs) + 1
    at = at_ref[0]
    out_ref[at] = own_ref[...]
    for shift, part_ref in enumerate(part_refs, 1):
        owner = lax.rem(at + count - shift, count)
        projected_blocks(part_ref[...], weight_ref[...], out_ref.at[owner])


def weight_piece_kernel(at_ref, weight_ref, out_ref):
    size = out_ref.shape[0]
    out_ref[...] = weight_ref[pl.ds(pl.multiple_of(at_ref[0] * size, size), size), :]


def state_kernel(with_state, parts_ref, vg_ref, qk_ref, *state_refs):
    count, blocks, _, heads, _, tok = parts_ref.shape
    for head in range(heads):
        for which in range(2):
            for src in range(blocks):
                total = parts_ref[0, src, which, head]
                for part in range(1, count):
                    total = total + parts_ref[part, src, which, head]
                qk_ref[src, which, head] = total
        if with_state:
            high, low = split(psi(feature_major(qk_ref, 1, head), False))
            v = rows_of(vg_ref, 0, head, 0, blocks * tok)
            state_refs[0][head] = dot(high, v) + dot(low, v)


def numerator_kernel(qk_ref, vg_ref, num_ref):
    heads = qk_ref.shape[2]
    length = qk_ref.shape[0] * qk_ref.shape[4]
    tile = min(TILE, length)
    for head in range(heads):
        q = feature_major(qk_ref, 0, head) * 0.25
        k = feature_major(qk_ref, 1, head)
        left, right = score_sides(q, k)
        for at in range(0, length, tile):
            width = at + tile
            scores = dot(left[at:width], right[:, :width])
            kernel = jnp.where(
                causal_mask(tile, width), 1.0 + scores * (1.0 + 0.5 * scores), 0.0
            )
            high, low = split(kernel)
            v = rows_of(vg_ref, 0, head, 0, width)
            num_ref[at:width, head * DH : (head + 1) * DH] = dot(high, v) + dot(low, v)


def normalize_kernel(with_state, qk_ref, vg_ref, num_ref, *rest):
    if with_state:
        prefix_ref, attended_ref, grad_ref, carried_ref = rest
    else:
        attended_ref, grad_ref = rest
    heads = qk_ref.shape[2]
    blocks, tok = qk_ref.shape[0], qk_ref.shape[4]
    length = blocks * tok
    for head in range(heads):
        cols = slice(head * DH, (head + 1) * DH)
        numerator = num_ref[:, cols]
        if with_state:
            feat = psi(feature_major(qk_ref, 0, head) * 0.25, True)
            numerator = numerator + dot3(feat.T, prefix_ref[head])
        inv_rms = lax.rsqrt(jnp.mean(numerator * numerator, axis=-1, keepdims=True) + EPSILON)
        normed = numerator * inv_rms
        upstream = rows_of(vg_ref, 1, head, 0, length).astype(f32)
        grad = inv_rms * (
            upstream - normed * jnp.mean(normed * upstream, axis=-1, keepdims=True)
        )
        attended = normed.astype(bf16)
        for src in range(blocks):
            attended_ref[src, :, cols] = attended[src * tok : (src + 1) * tok]
        grad_ref[:, cols] = grad
        if with_state:
            carried_ref[head] = dot3(feat, grad)


def backward_kernel(with_state, first, qk_ref, vg_ref, grad_ref, *rest):
    rest = list(rest)
    prefix_ref = rest.pop(0) if with_state else None
    if first == 0:
        attended_in_ref = rest.pop(0)
        attended_ref = rest.pop()
        attended_ref[...] = attended_in_ref[...]
    grad_qk_ref, grad_v_ref = rest[-2:]
    length = qk_ref.shape[0] * qk_ref.shape[4]
    tile = min(TILE, length)
    for at_head in range(grad_v_ref.shape[0]):
        head = first + at_head
        cols = slice(head * DH, (head + 1) * DH)
        q = feature_major(qk_ref, 0, head) * 0.25
        k = feature_major(qk_ref, 1, head)
        left, right = score_sides(q, k)
        q_both = jnp.concatenate(split(q), axis=0)
        k_both = jnp.concatenate(split(k), axis=0)
        grad = grad_ref[:, cols]
        grad_t = grad.T
        if with_state:
            grad_q = pull_psi(q, dot3(prefix_ref[head], grad_t), True)
        for at in reversed(range(0, length, tile)):
            width = at + tile
            scores = dot(left[at:width], right[:, :width])
            causal = causal_mask(tile, width)
            v = rows_of(vg_ref, 0, head, 0, width)
            high, low = split(grad[at:width])
            mixing = dot(
                jnp.concatenate([high, low], axis=1), jnp.concatenate([v, v], axis=1), NT
            )
            more = 1.0 + scores
            slope = jnp.where(causal, mixing * more, 0.0).astype(bf16)
            kernel = jnp.where(causal, more + 0.5 * scores * scores, 0.0).astype(bf16)
            both = dot(k_both[:, :width], slope, NT)
            piece = both[:F] + both[F:]
            if with_state:
                piece = piece + grad_q[:, at:width]
            grad_qk_ref[0, at_head, :, at:width] = piece * 0.25
            both = dot(q_both[:, at:width], slope)
            piece_k = both[:F] + both[F:]
            both = dot(jnp.concatenate(split(grad_t[:, at:width]), axis=0), kernel)
            piece_v = both[:DH] + both[DH:]
            if width == length:
                grad_qk_ref[1, at_head] = piece_k
                grad_v_ref[at_head] = piece_v
            else:
                grad_qk_ref[1, at_head, :, :width] += piece_k
                grad_v_ref[at_head, :, :width] += piece_v


def rows_kernel(with_state, halves, qk_ref, vg_ref, *rest):
    rest = list(rest)
    suffix_ref = rest.pop(0) if with_state else None
    rows_ref = rest[-1]
    blocks, tok = qk_ref.shape[0], qk_ref.shape[4]
    head = 0
    for grad_ref in rest[:halves]:
        for at_head in range(grad_ref.shape[1]):
            grad_k = grad_ref[1, at_head]
            if with_state:
                k = feature_major(qk_ref, 1, head)
                v = rows_of(vg_ref, 0, head, 0, blocks * tok)
                high, low = split(suffix_ref[head])
                grad_k = grad_k + pull_psi(k, dot(high, v, NT) + dot(low, v, NT), False)
            grad_q, grad_k = grad_ref[0, at_head].astype(bf16), grad_k.astype(bf16)
            for member in range(rows_ref.shape[0]):
                rows_ref[member, 0, head] = grad_q
                rows_ref[member, 1, head] = grad_k
            head += 1


def grad_values_kernel(with_state, halves, qk_ref, *rest):
    rest = list(rest)
    suffix_ref = rest.pop(0) if with_state else None
    out_ref = rest[-1]
    blocks, tok = qk_ref.shape[0], qk_ref.shape[4]
    head = 0
    for grad_ref in rest[:halves]:
        for at_head in range(grad_ref.shape[0]):
            grad_v = grad_ref[at_head]
            if with_state:
                feat = psi(feature_major(qk_ref, 1, head), False)
                grad_v = grad_v + dot3(suffix_ref[head].T, feat)
            grad_v = grad_v.T.astype(bf16)
            for src in range(blocks):
                out_ref[src, :, head * DH : (head + 1) * DH] = grad_v[src * tok : (src + 1) * tok]
            head += 1


def unpack_heads_kernel(in_ref, out_ref):
    group, _, width = in_ref.shape
    for member in range(group):
        out_ref[0, :, member * width : (member + 1) * width] = in_ref[member]


def all_rows(rows_ref, cols):
    group, _, heads = rows_ref.shape[:3]
    return jnp.concatenate(
        [
            rows_ref[src, which, head, :, cols]
            for which in range(2)
            for src in range(group)
            for head in range(heads)
        ],
        axis=0,
    )


def product_kernel(at_ref, rows_ref, tokens_ref, *rest):
    *part_refs, total_ref = rest
    tokens = jnp.concatenate([tokens_ref[src] for src in range(tokens_ref.shape[0])], axis=1)
    total_ref[...] = dot(tokens, all_rows(rows_ref, slice(None)), NT)
    count = len(part_refs)
    size = part_refs[0].shape[0]
    for shift, part_ref in enumerate(part_refs):
        owner = lax.rem(at_ref[0] + shift, count)
        part = total_ref[pl.ds(pl.multiple_of(owner * size, size), size), :]
        part_ref[...] = part.astype(part_ref.dtype)


def run_sum_kernel(arrived, at_ref, *rest):
    own_ref, *rest = rest
    total_ref = rest[-1]
    total = own_ref[...]
    for ref in rest[:arrived]:
        total = total + ref[...].astype(f32)
    total_ref[...] = total
    part_refs = rest[arrived:-1]
    size = part_refs[0].shape[0]
    for shift, part_ref in enumerate(part_refs):
        owner = lax.rem(at_ref[0] + shift, len(part_refs))
        part = total_ref[pl.ds(pl.multiple_of(owner * size, size), size), :]
        part_ref[...] = part.astype(part_ref.dtype)


def grad_tokens_kernel(at_ref, rows_ref, *rest):
    *weight_refs, out_ref = rest
    tok = out_ref.shape[1]
    start = pl.multiple_of(at_ref[0] * tok, tok)
    rows = all_rows(rows_ref, pl.ds(start, tok)).T
    for i, weight_ref in enumerate(weight_refs):
        size = weight_ref.shape[0]
        first = pl.multiple_of(at_ref[1 + i], size)
        out_ref[0, :, pl.ds(first, size)] = dot(rows, weight_ref[...], NT).astype(bf16)


VMEM = pl.BlockSpec(memory_space=pltpu.VMEM)
SMEM = pl.BlockSpec(memory_space=pltpu.SMEM)
ANYWHERE = pl.BlockSpec(memory_space=pl.ANY)


def call(body, out_shapes, flops, *operands, scalars=(), after=(), scratch=()):
    at = [jnp.stack([jnp.int32(s) for s in scalars])] if scalars else []
    count = len(at) + len(operands)

    def kernel(*refs):
        body(*refs[:count], *refs[count + len(after) :])

    return pl.pallas_call(
        kernel,
        out_shape=[jax.ShapeDtypeStruct(shape, kind) for shape, kind in out_shapes],
        in_specs=[SMEM] * len(at) + [VMEM] * len(operands) + [ANYWHERE] * len(after),
        out_specs=[VMEM] * len(out_shapes),
        scratch_shapes=scratch,
        compiler_params=pltpu.CompilerParams(vmem_limit_bytes=24 * 1024 * 1024),
        cost_estimate=pl.CostEstimate(flops=flops, bytes_accessed=4 << 20, transcendentals=0),
    )(*at, *operands, *after)


def local(dp_size, ctx_size, tokens, proj_weight, values, grad_out):
    group = min(GROUP, ctx_size, H)
    runs = ctx_size // group
    heads = H // group
    tok, width = tokens.shape[1:]
    length = group * tok
    cols = proj_weight.shape[1]
    share = width // dp_size
    depth = share // ctx_size
    with_state = runs > 1
    groups = [[run * group + i for i in range(group)] for run in range(runs)]
    wide_groups = [
        [dp * ctx_size + i for dp in range(dp_size) for i in members] for members in groups
    ]
    dp_at, ctx_at = lax.axis_index("dp"), lax.axis_index("ctx")
    run_at, member = ctx_at // group, ctx_at % group

    def exchange(x):
        return lax.all_to_all(
            x, "ctx", split_axis=0, concat_axis=0, tiled=True, axis_index_groups=groups
        )

    def to_dp(x, shift):
        return lax.ppermute(x, "dp", [(i, (i + shift) % dp_size) for i in range(dp_size)])

    def to_run(x, shift, wrap):
        pairs = [
            (i, (i + shift * group) % ctx_size)
            for i in range(ctx_size)
            if wrap or 0 <= i + shift * group < ctx_size
        ]
        return lax.ppermute(x, "ctx", pairs)

    qk_shape = ((group, 2, heads, F, tok), f32)
    pairs = length * (length + TILE) // 2
    state_flops = 4 * heads * length * PSI * DH
    state_shape = ((heads, PSI, DH), f32)
    blocks_shape = ((group, tok, heads * DH), bf16)
    project_flops = 2 * tok * share * cols

    own, *parts = call(
        token_parts_kernel, [((tok, share), bf16)] * dp_size, 0, tokens, scalars=(dp_at,)
    )
    arrived = [to_dp(part, shift) for shift, part in enumerate(parts, 1)]
    (vg,) = call(
        pack_heads_kernel,
        [((group, 2, tok, heads * DH), bf16)],
        0,
        values,
        grad_out,
        after=parts[:1],
    )
    vg = exchange(vg)
    (projected,) = call(project_kernel, [qk_shape], project_flops, own, proj_weight)
    (projected,) = call(
        project_rest_kernel,
        [((dp_size,) + qk_shape[0], f32)],
        project_flops,
        projected,
        proj_weight,
        *arrived,
        scalars=(dp_at,),
        after=(vg,),
    )
    qk_parts = lax.all_to_all(
        projected.reshape((dp_size * group,) + qk_shape[0][1:]),
        ("dp", "ctx"),
        split_axis=0,
        concat_axis=0,
        tiled=True,
        axis_index_groups=wide_groups,
    ).reshape(projected.shape)

    pair = 2 if ctx_size % 2 == 0 else 1
    parity = ctx_at % pair
    piece = share // pair
    (mine,) = call(
        weight_piece_kernel,
        [((piece, cols), bf16)],
        0,
        proj_weight,
        scalars=(parity,),
        after=(projected,),
    )
    fetched = [to_dp(mine, shift) for shift in range(1, dp_size)]
    weights, firsts = [proj_weight], [dp_at * share]
    for shift, half in enumerate(fetched, 1):
        base = (dp_at + dp_size - shift) % dp_size * share
        weights.append(half)
        firsts.append(base + parity * piece)
        if pair == 2:
            weights.append(lax.ppermute(half, "ctx", [(i, i ^ 1) for i in range(ctx_size)]))
            firsts.append(base + (1 - parity) * piece)

    qk, *state = call(
        functools.partial(state_kernel, with_state),
        [qk_shape] + [state_shape] * with_state,
        state_flops,
        qk_parts,
        vg,
    )
    if depth % 128 == 0:
        (token_cols,) = call(
            functools.partial(pack_tokens_kernel, depth),
            [((group, dp_size * runs * depth, tok), bf16)],
            0,
            tokens,
            after=(qk,),
        )
    else:
        token_cols = (
            tokens[0]
            .reshape(tok, dp_size * runs, group, depth)
            .transpose(2, 1, 3, 0)
            .reshape(group, dp_size * runs * depth, tok)
        )
    token_cols = exchange(token_cols)

    prefix, suffix = (), ()
    if with_state:
        prefix = (sum(to_run(state[0], shift, False) for shift in range(1, runs)),)
    (numerator,) = call(
        numerator_kernel, [((length, heads * DH), f32)], heads * pairs * 2 * 512, qk, vg
    )
    attended, grad_num, *carried = call(
        functools.partial(normalize_kernel, with_state),
        [blocks_shape, ((length, heads * DH), f32)] + [state_shape] * with_state,
        2 * state_flops,
        qk,
        vg,
        numerator,
        *prefix,
    )
    if with_state:
        suffix = (sum(to_run(carried[0], -shift, False) for shift in range(1, runs)),)
    grad_qks, grad_vs = [], []
    for first in range(0, heads, max(1, heads // 2)):
        count = max(1, heads // 2)
        result = call(
            functools.partial(backward_kernel, with_state, first),
            [((2, count, F, length), f32), ((count, DH, length), f32)]
            + [blocks_shape] * (first == 0),
            count * pairs * 2 * 1024,
            qk,
            vg,
            grad_num,
            *prefix,
            *([attended] if first == 0 else []),
            after=[] if first == 0 else [grad_qks[0], *fetched],
        )
        grad_qks.append(result[0])
        grad_vs.append(result[1])
        if first == 0:
            attended = exchange(result[2])
    (rows,) = call(
        functools.partial(rows_kernel, with_state, len(grad_qks)),
        [((group, 2, heads, F, length), bf16)],
        state_flops,
        qk,
        vg,
        *suffix,
        *grad_qks,
    )
    rows = exchange(rows)

    own, *parts = call(
        product_kernel,
        [((runs * depth, cols), f32)] + [((runs * depth, cols), bf16)] * (dp_size - 1),
        2 * dp_size * runs * depth * length * cols,
        rows,
        token_cols,
        scalars=(dp_at,),
        after=weights[1:] + [attended],
        scratch=[pltpu.VMEM((dp_size * runs * depth, cols), f32)],
    )
    parts = [to_dp(part, shift) for shift, part in enumerate(parts, 1)]
    (grad_values,) = call(
        functools.partial(grad_values_kernel, with_state, len(grad_vs)),
        [blocks_shape],
        state_flops,
        qk,
        *suffix,
        *grad_vs,
        after=(own,),
    )
    grad_values = exchange(grad_values)
    (grad_tokens,) = call(
        grad_tokens_kernel,
        [((1, tok, width), bf16)],
        2 * tok * width * cols,
        rows,
        *weights,
        scalars=(member, *firsts),
        after=(own,),
    )
    grad_proj, *parts = call(
        functools.partial(run_sum_kernel, len(parts)),
        [((depth, cols), f32)] + [((depth, cols), bf16)] * (runs - 1),
        0,
        own,
        *parts,
        scalars=(run_at,),
        scratch=[pltpu.VMEM((runs * depth, cols), f32)],
    )
    for shift, part in enumerate(parts, 1):
        grad_proj = grad_proj + to_run(part, shift, True).astype(f32)
    attended, grad_values = [
        call(unpack_heads_kernel, [((1, tok, H * DH), bf16)], 0, blocks)[0]
        for blocks in (attended, grad_values)
    ]
    return (attended, grad_tokens, grad_values, grad_proj)


def solution(mesh):
    return jax.shard_map(
        functools.partial(local, mesh.shape["dp"], mesh.shape["ctx"]),
        mesh=mesh,
        in_specs=(P("dp", "ctx", None), P("dp", None), P("dp", "ctx", None), P("dp", "ctx", None)),
        out_specs=(
            P("dp", "ctx", None),
            P("dp", "ctx", None),
            P("dp", "ctx", None),
            P(("dp", "ctx"), None),
        ),
        check_vma=False,
    )
```

```python
import functools

import jax
import jax.numpy as jnp
from jax import lax
from jax.experimental import pallas as pl
from jax.experimental.pallas import tpu as pltpu
from jax.sharding import PartitionSpec as P

H = 16
F = 16
DH = 128
EPSILON = 1e-05
GROUP = 8
TILE = 256
VMEM_LIMIT = 16 * 1024 * 1024
PSI = 9 * F + 2 * F
PSI_SCALE = (0.5,) + (1.0,) * 7 + (0.5,)

f32 = jnp.float32
bf16 = jnp.bfloat16

NN = (((1,), (0,)), ((), ()))
NT = (((1,), (1,)), ((), ()))


def dot(a, b, dims=NN):
    return lax.dot_general(a, b, dims, preferred_element_type=f32)


def split(x):
    high = x.astype(bf16)
    return high, (x - high.astype(f32)).astype(bf16)


def dot3(a, b, dims=NN):
    a_high, a_low = split(a)
    b_high, b_low = split(b)
    return dot(a_high, b_high, dims) + (dot(a_high, b_low, dims) + dot(a_low, b_high, dims))


def turned(x, r):
    return x if r == 0 else jnp.concatenate([x[r:], x[:r]], axis=0)


def psi(x, weights):
    parts = []
    for r in range(9):
        part = x * turned(x, r)
        parts.append(part * PSI_SCALE[r] if weights and PSI_SCALE[r] != 1.0 else part)
    row = lax.broadcasted_iota(jnp.int32, x.shape, 0)
    return jnp.concatenate(parts + [x, jnp.where(row == 0, 1.0, 0.0)], axis=0)


def pull_psi(x, upstream, weights):
    total = upstream[9 * F : 10 * F]
    for r in range(9):
        part = upstream[r * F : (r + 1) * F]
        if weights and PSI_SCALE[r] != 1.0:
            part = part * PSI_SCALE[r]
        total = total + part * turned(x, r) + turned(part * x, (F - r) % F)
    return total


def feature_major(qk_ref, which, head):
    return jnp.concatenate([qk_ref[src, which, head] for src in range(qk_ref.shape[0])], axis=1)


def rows_of(ref, which, head, start, stop):
    tok = ref.shape[2]
    return jnp.concatenate(
        [
            ref[src, which, :, head * DH : (head + 1) * DH]
            for src in range(start // tok, stop // tok)
        ],
        axis=0,
    )


def score_sides(q, k):
    q_high, q_low = split(q)
    k_high, k_low = split(k)
    left = jnp.concatenate([q_high, q_high, q_low, q_low], axis=0)
    right = jnp.concatenate([k_high, k_low, k_high, k_low], axis=0)
    return left.T, right


def causal_mask(tile, width):
    row = lax.broadcasted_iota(jnp.int32, (tile, width), 0) + (width - tile)
    return row >= lax.broadcasted_iota(jnp.int32, (tile, width), 1)


def run_copies(sems, pairs):
    copies = [
        pltpu.make_async_copy(source, target, sems.at[i])
        for i, (source, target) in enumerate(pairs)
    ]
    for copy in copies:
        copy.start()
    for copy in copies:
        copy.wait()


def aligned(at, size):
    return pl.ds(pl.multiple_of(at * size, size), size)


def token_parts_kernel(at_ref, tokens_ref, *rest):
    *out_refs, sems = rest
    count, share = len(out_refs) + 1, out_refs[0].shape[1]
    run_copies(
        sems,
        [
            (tokens_ref.at[0, :, aligned(lax.rem(at_ref[0] + shift, count), share)], out_ref)
            for shift, out_ref in enumerate(out_refs, 1)
        ],
    )


def pack_heads_kernel(at_ref, values_ref, grad_ref, *rest):
    *out_refs, sems = rest
    width = out_refs[0].shape[2]
    pairs = []
    for shift, out_ref in enumerate(out_refs):
        cols = aligned(lax.rem(at_ref[0] + shift, len(out_refs)), width)
        pairs.append((values_ref.at[0, :, cols], out_ref.at[0]))
        pairs.append((grad_ref.at[0, :, cols], out_ref.at[1]))
    run_copies(sems, pairs)


def collect_heads_kernel(at_ref, *rest):
    *part_refs, out_ref = rest
    group = len(part_refs)
    for shift, part_ref in enumerate(part_refs):
        out_ref[lax.rem(at_ref[0] + group - shift, group)] = part_ref[...]


def pack_tokens_kernel(depth, at_ref, tokens_ref, *rest):
    *out_refs, sems = rest
    group = len(out_refs)
    pairs = []
    for shift, out_ref in enumerate(out_refs):
        member = lax.rem(at_ref[0] + shift, group)
        for part in range(out_ref.shape[1] // depth):
            pairs.append(
                (
                    tokens_ref.at[0, :, aligned(part * group + member, depth)],
                    out_ref.at[:, part * depth : (part + 1) * depth],
                )
            )
    run_copies(sems, pairs)


def collect_tokens_kernel(at_ref, *rest):
    *part_refs, out_ref = rest
    group, tok = len(part_refs), part_refs[0].shape[0]
    for shift, part_ref in enumerate(part_refs):
        src = lax.rem(at_ref[0] + group - shift, group)
        out_ref[:, aligned(src, tok)] = part_ref[...].T


def projected_blocks(part, weight, out_ref):
    projected = dot(part, weight).T
    group, _, heads, feat, _ = out_ref.shape
    for member in range(group):
        for which in range(2):
            for head in range(heads):
                first = ((which * group + member) * heads + head) * feat
                out_ref[member, which, head] = projected[first : first + feat]


def project_kernel(at_ref, tokens_ref, weight_ref, out_ref, part_ref, sem):
    share = part_ref.shape[1]
    run_copies(sem, [(tokens_ref.at[0, :, aligned(at_ref[0], share)], part_ref)])
    projected_blocks(part_ref[...], weight_ref[...], out_ref)


def project_rest_kernel(at_ref, own_ref, weight_ref, *rest):
    *part_refs, out_ref = rest
    count = len(part_refs) + 1
    at = at_ref[0]
    out_ref[at] = own_ref[...]
    for shift, part_ref in enumerate(part_refs, 1):
        owner = lax.rem(at + count - shift, count)
        projected_blocks(part_ref[...], weight_ref[...], out_ref.at[owner])


def weight_piece_kernel(at_ref, weight_ref, out_ref, sems):
    run_copies(sems, [(weight_ref.at[aligned(at_ref[0], out_ref.shape[0])], out_ref)])


def state_kernel(with_state, parts_ref, vg_ref, qk_ref, *state_refs):
    count, blocks, _, heads, _, tok = parts_ref.shape
    for head in range(heads):
        for which in range(2):
            for src in range(blocks):
                total = parts_ref[0, src, which, head]
                for part in range(1, count):
                    total = total + parts_ref[part, src, which, head]
                qk_ref[src, which, head] = total
        if with_state:
            high, low = split(psi(feature_major(qk_ref, 1, head), False))
            v = rows_of(vg_ref, 0, head, 0, blocks * tok)
            state_refs[0][head] = dot(high, v) + dot(low, v)


def numerator_kernel(qk_ref, vg_ref, num_ref):
    heads = qk_ref.shape[2]
    length = qk_ref.shape[0] * qk_ref.shape[4]
    tile = min(TILE, length)
    for head in range(heads):
        q = feature_major(qk_ref, 0, head) * 0.25
        k = feature_major(qk_ref, 1, head)
        left, right = score_sides(q, k)
        for at in range(0, length, tile):
            width = at + tile
            scores = dot(left[at:width], right[:, :width])
            kernel = jnp.where(
                causal_mask(tile, width), 1.0 + scores * (1.0 + 0.5 * scores), 0.0
            )
            high, low = split(kernel)
            v = rows_of(vg_ref, 0, head, 0, width)
            num_ref[at:width, head * DH : (head + 1) * DH] = dot(high, v) + dot(low, v)


def normalize_kernel(with_state, qk_ref, vg_ref, num_ref, *rest):
    if with_state:
        prefix_ref, attended_ref, grad_ref, carried_ref = rest
    else:
        attended_ref, grad_ref = rest
    heads = qk_ref.shape[2]
    blocks, tok = qk_ref.shape[0], qk_ref.shape[4]
    length = blocks * tok
    for head in range(heads):
        cols = slice(head * DH, (head + 1) * DH)
        numerator = num_ref[:, cols]
        if with_state:
            feat = psi(feature_major(qk_ref, 0, head) * 0.25, True)
            numerator = numerator + dot3(feat.T, prefix_ref[head])
        inv_rms = lax.rsqrt(jnp.mean(numerator * numerator, axis=-1, keepdims=True) + EPSILON)
        normed = numerator * inv_rms
        upstream = rows_of(vg_ref, 1, head, 0, length).astype(f32)
        grad = inv_rms * (
            upstream - normed * jnp.mean(normed * upstream, axis=-1, keepdims=True)
        )
        attended = normed.astype(bf16)
        for src in range(blocks):
            attended_ref[src, :, cols] = attended[src * tok : (src + 1) * tok]
        grad_ref[:, cols] = grad
        if with_state:
            carried_ref[head] = dot3(feat, grad)


def backward_kernel(with_state, first, qk_ref, vg_ref, grad_ref, *rest):
    rest = list(rest)
    prefix_ref = rest.pop(0) if with_state else None
    if first == 0:
        attended_in_ref = rest.pop(0)
        attended_ref = rest.pop()
        attended_ref[...] = attended_in_ref[...]
    grad_qk_ref, grad_v_ref = rest[-2:]
    length = qk_ref.shape[0] * qk_ref.shape[4]
    tile = min(TILE, length)
    for at_head in range(grad_v_ref.shape[0]):
        head = first + at_head
        cols = slice(head * DH, (head + 1) * DH)
        q = feature_major(qk_ref, 0, head) * 0.25
        k = feature_major(qk_ref, 1, head)
        left, right = score_sides(q, k)
        q_both = jnp.concatenate(split(q), axis=0)
        k_both = jnp.concatenate(split(k), axis=0)
        grad = grad_ref[:, cols]
        grad_t = grad.T
        if with_state:
            grad_q = pull_psi(q, dot3(prefix_ref[head], grad_t), True)
        for at in reversed(range(0, length, tile)):
            width = at + tile
            scores = dot(left[at:width], right[:, :width])
            causal = causal_mask(tile, width)
            v = rows_of(vg_ref, 0, head, 0, width)
            high, low = split(grad[at:width])
            mixing = dot(
                jnp.concatenate([high, low], axis=1), jnp.concatenate([v, v], axis=1), NT
            )
            more = 1.0 + scores
            slope = jnp.where(causal, mixing * more, 0.0).astype(bf16)
            kernel = jnp.where(causal, more + 0.5 * scores * scores, 0.0).astype(bf16)
            both = dot(k_both[:, :width], slope, NT)
            piece = both[:F] + both[F:]
            if with_state:
                piece = piece + grad_q[:, at:width]
            grad_qk_ref[0, at_head, :, at:width] = piece * 0.25
            both = dot(q_both[:, at:width], slope)
            piece_k = both[:F] + both[F:]
            both = dot(jnp.concatenate(split(grad_t[:, at:width]), axis=0), kernel)
            piece_v = both[:DH] + both[DH:]
            if width == length:
                grad_qk_ref[1, at_head] = piece_k
                grad_v_ref[at_head] = piece_v
            else:
                grad_qk_ref[1, at_head, :, :width] += piece_k
                grad_v_ref[at_head, :, :width] += piece_v


def rows_kernel(with_state, halves, qk_ref, vg_ref, *rest):
    rest = list(rest)
    suffix_ref = rest.pop(0) if with_state else None
    out_ref = rest[-1]
    blocks, tok = qk_ref.shape[0], qk_ref.shape[4]
    heads = qk_ref.shape[2]
    feats = 2 * heads * F
    fold = blocks * tok // (heads * DH)
    step = tok // fold
    head = 0
    for grad_ref, grad_v_ref in zip(rest[:halves], rest[halves : 2 * halves]):
        for at_head in range(grad_v_ref.shape[0]):
            grad_k = grad_ref[1, at_head]
            grad_v = grad_v_ref[at_head]
            if with_state:
                k = feature_major(qk_ref, 1, head)
                v = rows_of(vg_ref, 0, head, 0, blocks * tok)
                high, low = split(suffix_ref[head])
                grad_k = grad_k + pull_psi(k, dot(high, v, NT) + dot(low, v, NT), False)
                grad_v = grad_v + dot3(suffix_ref[head].T, psi(k, False))
            grad_q, grad_k = grad_ref[0, at_head].astype(bf16), grad_k.astype(bf16)
            grad_v = grad_v.T.astype(bf16)
            for member in range(blocks):
                out_ref[member, head * F : (head + 1) * F] = grad_q
                out_ref[member, (heads + head) * F : (heads + head + 1) * F] = grad_k
                for i in range(fold):
                    first = (i * heads + head) * DH
                    row = member * tok + i * step
                    out_ref[member, feats:, first : first + DH] = grad_v[row : row + step]
            head += 1


def unpack_values_kernel(in_ref, out_ref):
    group, rows, length = in_ref.shape
    width = out_ref.shape[2] // group
    tok = out_ref.shape[1]
    fold = length // width
    step = tok // fold
    for member in range(group):
        for i in range(fold):
            out_ref[0, i * step : (i + 1) * step, member * width : (member + 1) * width] = in_ref[
                member, rows - step :, i * width : (i + 1) * width
            ]


def unpack_heads_kernel(in_ref, out_ref):
    group, _, width = in_ref.shape
    for member in range(group):
        out_ref[0, :, member * width : (member + 1) * width] = in_ref[member]


def all_rows(rows_ref, count, cols):
    half = count // rows_ref.shape[0] // 2
    return jnp.concatenate(
        [
            rows_ref[src, which * half : (which + 1) * half, cols]
            for which in range(2)
            for src in range(rows_ref.shape[0])
        ],
        axis=0,
    )


def product_kernel(at_ref, rows_ref, tokens_ref, *rest):
    *part_refs, total_ref = rest
    count = total_ref.shape[1]
    total_ref[...] = dot(tokens_ref[...], all_rows(rows_ref, count, slice(None)), NT)
    count = len(part_refs)
    size = part_refs[0].shape[0]
    for shift, part_ref in enumerate(part_refs):
        owner = lax.rem(at_ref[0] + shift, count)
        part = total_ref[pl.ds(pl.multiple_of(owner * size, size), size), :]
        part_ref[...] = part.astype(part_ref.dtype)


def run_sum_kernel(arrived, at_ref, *rest):
    own_ref, *rest = rest
    total_ref = rest[-1]
    total = own_ref[...]
    for ref in rest[:arrived]:
        total = total + ref[...].astype(f32)
    total_ref[...] = total
    part_refs = rest[arrived:-1]
    size = part_refs[0].shape[0]
    for shift, part_ref in enumerate(part_refs):
        owner = lax.rem(at_ref[0] + shift, len(part_refs))
        part = total_ref[pl.ds(pl.multiple_of(owner * size, size), size), :]
        part_ref[...] = part.astype(part_ref.dtype)


def grad_tokens_kernel(at_ref, rows_ref, *rest):
    *weight_refs, out_ref = rest
    tok = out_ref.shape[1]
    start = pl.multiple_of(at_ref[0] * tok, tok)
    rows = all_rows(rows_ref, weight_refs[0].shape[1], pl.ds(start, tok)).T
    for i, weight_ref in enumerate(weight_refs):
        size = weight_ref.shape[0]
        first = pl.multiple_of(at_ref[1 + i], size)
        out_ref[0, :, pl.ds(first, size)] = dot(rows, weight_ref[...], NT).astype(bf16)


VMEM = pl.BlockSpec(memory_space=pltpu.VMEM)
SMEM = pl.BlockSpec(memory_space=pltpu.SMEM)
ANYWHERE = pl.BlockSpec(memory_space=pl.ANY)


def call(
    body, outs, *operands, scalars=(), after=(), scratch=(), far_in=0, far_out=False, copies=0
):
    at = [jnp.stack([jnp.int32(s) for s in scalars])] if scalars else []
    count = len(at) + len(operands)

    def kernel(*refs):
        ins, rest = refs[:count], refs[count + len(after) :]
        body(*ins, *rest[: len(outs)], *rest[len(outs) + 1 :])
        rest[len(outs)][...] = jnp.zeros((8, 128), f32)

    *results, token = pl.pallas_call(
        kernel,
        out_shape=[jax.ShapeDtypeStruct(shape, kind) for shape, kind in [*outs, ((8, 128), f32)]],
        in_specs=[SMEM] * len(at)
        + [ANYWHERE] * far_in
        + [VMEM] * (len(operands) - far_in)
        + [ANYWHERE] * len(after),
        out_specs=[ANYWHERE if far_out else VMEM] * len(outs) + [VMEM],
        scratch_shapes=[*scratch] + [pltpu.SemaphoreType.DMA((copies,))] * (copies > 0),
        compiler_params=pltpu.CompilerParams(vmem_limit_bytes=VMEM_LIMIT),
        cost_estimate=pl.CostEstimate(flops=0, bytes_accessed=0, transcendentals=0),
    )(*at, *operands, *after)
    return results, token


def local(dp_size, ctx_size, tokens, proj_weight, values, grad_out):
    group = min(GROUP, ctx_size, H)
    runs = ctx_size // group
    heads = H // group
    tok, width = tokens.shape[1:]
    length = group * tok
    cols = proj_weight.shape[1]
    share = width // dp_size
    depth = share // ctx_size
    with_state = runs > 1
    groups = [[run * group + i for i in range(group)] for run in range(runs)]
    wide_groups = [
        [dp * ctx_size + i for dp in range(dp_size) for i in members] for members in groups
    ]
    dp_at, ctx_at = lax.axis_index("dp"), lax.axis_index("ctx")
    run_at, member = ctx_at // group, ctx_at % group

    def exchange(x):
        return lax.all_to_all(
            x, "ctx", split_axis=0, concat_axis=0, tiled=True, axis_index_groups=groups
        )

    def to_dp(x, shift):
        return lax.ppermute(x, "dp", [(i, (i + shift) % dp_size) for i in range(dp_size)])

    def to_member(x, shift):
        pairs = [(i, i - i % group + (i + shift) % group) for i in range(ctx_size)]
        return lax.ppermute(x, "ctx", pairs)

    def to_run(x, shift, wrap):
        pairs = [
            (i, (i + shift * group) % ctx_size)
            for i in range(ctx_size)
            if wrap or 0 <= i + shift * group < ctx_size
        ]
        return lax.ppermute(x, "ctx", pairs)

    qk_shape = ((group, 2, heads, F, tok), f32)
    state_shape = ((heads, PSI, DH), f32)
    blocks_shape = ((group, tok, heads * DH), bf16)
    rows_shape = ((length, heads * DH), f32)

    parts, token = call(
        token_parts_kernel,
        [((tok, share), bf16)] * (dp_size - 1),
        tokens,
        scalars=(dp_at,),
        far_in=1,
        far_out=True,
        copies=dp_size - 1,
    )
    arrived = [to_dp(part, shift) for shift, part in enumerate(parts, 1)]
    parts, token = call(
        pack_heads_kernel,
        [((2, tok, heads * DH), bf16)] * group,
        values,
        grad_out,
        scalars=(member,),
        after=(token,),
        far_in=2,
        far_out=True,
        copies=2 * group,
    )
    parts = parts[:1] + [to_member(part, shift) for shift, part in enumerate(parts[1:], 1)]
    (vg,), vg_token = call(
        collect_heads_kernel,
        [((group, 2, tok, heads * DH), bf16)],
        *parts,
        scalars=(member,),
    )
    (projected,), token = call(
        project_kernel,
        [qk_shape],
        tokens,
        proj_weight,
        scalars=(dp_at,),
        after=(token,),
        far_in=1,
        copies=1,
        scratch=[pltpu.VMEM((tok, share), bf16)],
    )
    part_shape = (tok, dp_size * runs * depth)
    if depth % 128 == 0:
        parts, token = call(
            functools.partial(pack_tokens_kernel, depth),
            [(part_shape, bf16)] * group,
            tokens,
            scalars=(member,),
            after=(token,),
            far_in=1,
            far_out=True,
            copies=group * dp_size * runs,
        )
    else:
        blocks = tokens[0].reshape(tok, dp_size * runs, group, depth).transpose(2, 0, 1, 3)
        parts = [
            lax.dynamic_index_in_dim(blocks, (member + shift) % group, 0, keepdims=False).reshape(
                part_shape
            )
            for shift in range(group)
        ]
    token_parts = parts[:1] + [to_member(part, shift) for shift, part in enumerate(parts[1:], 1)]

    (projected,), token = call(
        project_rest_kernel,
        [((dp_size,) + qk_shape[0], f32)],
        projected,
        proj_weight,
        *arrived,
        scalars=(dp_at,),
        after=(vg_token,),
    )
    qk_parts = lax.all_to_all(
        projected.reshape((dp_size * group,) + qk_shape[0][1:]),
        ("dp", "ctx"),
        split_axis=0,
        concat_axis=0,
        tiled=True,
        axis_index_groups=wide_groups,
    ).reshape(projected.shape)

    pair = 2 if ctx_size % 2 == 0 else 1
    parity = ctx_at % pair
    piece = share // pair
    (mine,), token = call(
        weight_piece_kernel,
        [((piece, cols), bf16)],
        proj_weight,
        scalars=(parity,),
        after=(token,),
        far_in=1,
        far_out=True,
        copies=1,
    )
    fetched = [to_dp(mine, shift) for shift in range(1, dp_size)]
    weights, firsts = [proj_weight], [dp_at * share]
    for shift, half in enumerate(fetched, 1):
        base = (dp_at + dp_size - shift) % dp_size * share
        weights.append(half)
        firsts.append(base + parity * piece)
        if pair == 2:
            weights.append(lax.ppermute(half, "ctx", [(i, i ^ 1) for i in range(ctx_size)]))
            firsts.append(base + (1 - parity) * piece)

    (qk, *state), token = call(
        functools.partial(state_kernel, with_state),
        [qk_shape] + [state_shape] * with_state,
        qk_parts,
        vg,
    )
    (token_cols,), tokens_token = call(
        collect_tokens_kernel,
        [(part_shape[1:] + (length,), bf16)],
        *token_parts,
        scalars=(member,),
        after=(token,),
    )

    prefix, suffix = (), ()
    if with_state:
        prefix = (sum(to_run(state[0], shift, False) for shift in range(1, runs)),)
    (numerator,), token = call(numerator_kernel, [rows_shape], qk, vg)
    (attended, grad_num, *carried), token = call(
        functools.partial(normalize_kernel, with_state),
        [blocks_shape, rows_shape] + [state_shape] * with_state,
        qk,
        vg,
        numerator,
        *prefix,
        after=(tokens_token,),
    )
    if with_state:
        suffix = (sum(to_run(carried[0], -shift, False) for shift in range(1, runs)),)
    grad_qks, grad_vs = [], []
    for first in range(0, heads, max(1, heads // 2)):
        count = max(1, heads // 2)
        result, token = call(
            functools.partial(backward_kernel, with_state, first),
            [((2, count, F, length), f32), ((count, DH, length), f32)]
            + [blocks_shape] * (first == 0),
            qk,
            vg,
            grad_num,
            *prefix,
            *([attended] if first == 0 else []),
            after=[half[:8, :128] for half in fetched] if first == 0 else [token],
        )
        grad_qks.append(result[0])
        grad_vs.append(result[1])
        if first == 0:
            attended = exchange(result[2])
    (rows,), token = call(
        functools.partial(rows_kernel, with_state, len(grad_qks)),
        [((group, 2 * heads * F + tok * heads * DH // length, length), bf16)],
        qk,
        vg,
        *suffix,
        *grad_qks,
        *grad_vs,
    )
    rows = exchange(rows)
    (attended,), attended_token = call(
        unpack_heads_kernel, [((1, tok, H * DH), bf16)], attended, after=(token,)
    )

    (own, *parts), token = call(
        product_kernel,
        [((runs * depth, cols), f32)] + [((runs * depth, cols), bf16)] * (dp_size - 1),
        rows,
        token_cols,
        scalars=(dp_at,),
        after=(attended_token,),
        scratch=[pltpu.VMEM((dp_size * runs * depth, cols), f32)],
    )
    parts = [to_dp(part, shift) for shift, part in enumerate(parts, 1)]
    (grad_tokens,), tokens_token = call(
        grad_tokens_kernel,
        [((1, tok, width), bf16)],
        rows,
        *weights,
        scalars=(member, *firsts),
        after=(token,),
    )
    (grad_proj, *parts), token = call(
        functools.partial(run_sum_kernel, len(parts)),
        [((depth, cols), f32)] + [((depth, cols), bf16)] * (runs - 1),
        own,
        *parts,
        scalars=(run_at,),
        after=(tokens_token,),
        scratch=[pltpu.VMEM((runs * depth, cols), f32)],
    )
    (grad_values,), token = call(
        unpack_values_kernel, [((1, tok, H * DH), bf16)], rows, after=(token,)
    )
    for shift, part in enumerate(parts, 1):
        grad_proj = grad_proj + to_run(part, shift, True).astype(f32)
    return (attended, grad_tokens, grad_values, grad_proj)


def solution(mesh):
    return jax.shard_map(
        functools.partial(local, mesh.shape["dp"], mesh.shape["ctx"]),
        mesh=mesh,
        in_specs=(P("dp", "ctx", None), P("dp", None), P("dp", "ctx", None), P("dp", "ctx", None)),
        out_specs=(
            P("dp", "ctx", None),
            P("dp", "ctx", None),
            P("dp", "ctx", None),
            P(("dp", "ctx"), None),
        ),
        check_vma=False,
    )
```

```python
import functools

import jax
import jax.numpy as jnp
from jax import lax
from jax.experimental import pallas as pl
from jax.experimental.pallas import tpu as pltpu
from jax.sharding import PartitionSpec as P

H = 16
F = 16
DH = 128
EPSILON = 1e-05
GROUP = 8
TILE = 256
VMEM_LIMIT = 16 * 1024 * 1024
PSI = 9 * F + 2 * F
PSI_SCALE = (0.5,) + (1.0,) * 7 + (0.5,)

f32 = jnp.float32
bf16 = jnp.bfloat16

NN = (((1,), (0,)), ((), ()))
NT = (((1,), (1,)), ((), ()))


def dot(a, b, dims=NN):
    return lax.dot_general(a, b, dims, preferred_element_type=f32)


def split(x):
    high = x.astype(bf16)
    return high, (x - high.astype(f32)).astype(bf16)


def dot3(a, b, dims=NN):
    a_high, a_low = split(a)
    b_high, b_low = split(b)
    return dot(a_high, b_high, dims) + (dot(a_high, b_low, dims) + dot(a_low, b_high, dims))


def turned(x, r):
    return x if r == 0 else jnp.concatenate([x[r:], x[:r]], axis=0)


def psi(x, weights):
    parts = []
    for r in range(9):
        part = x * turned(x, r)
        parts.append(part * PSI_SCALE[r] if weights and PSI_SCALE[r] != 1.0 else part)
    row = lax.broadcasted_iota(jnp.int32, x.shape, 0)
    return jnp.concatenate(parts + [x, jnp.where(row == 0, 1.0, 0.0)], axis=0)


def pull_psi(x, upstream, weights):
    total = upstream[9 * F : 10 * F]
    for r in range(9):
        part = upstream[r * F : (r + 1) * F]
        if weights and PSI_SCALE[r] != 1.0:
            part = part * PSI_SCALE[r]
        total = total + part * turned(x, r) + turned(part * x, (F - r) % F)
    return total


def feature_major(qk_ref, which, head):
    return jnp.concatenate([qk_ref[src, which, head] for src in range(qk_ref.shape[0])], axis=1)


def rows_of(ref, which, head, start, stop):
    tok = ref.shape[2]
    return jnp.concatenate(
        [
            ref[src, which, :, head * DH : (head + 1) * DH]
            for src in range(start // tok, stop // tok)
        ],
        axis=0,
    )


def score_sides(q, k):
    q_high, q_low = split(q)
    k_high, k_low = split(k)
    left = jnp.concatenate([q_high, q_high, q_low, q_low], axis=0)
    right = jnp.concatenate([k_high, k_low, k_high, k_low], axis=0)
    return left.T, right


def causal_mask(tile, width):
    row = lax.broadcasted_iota(jnp.int32, (tile, width), 0) + (width - tile)
    return row >= lax.broadcasted_iota(jnp.int32, (tile, width), 1)


def run_copies(sems, pairs):
    copies = [
        pltpu.make_async_copy(source, target, sems.at[i])
        for i, (source, target) in enumerate(pairs)
    ]
    for copy in copies:
        copy.start()
    for copy in copies:
        copy.wait()


def aligned(at, size):
    return pl.ds(pl.multiple_of(at * size, size), size)


def token_parts_kernel(at_ref, tokens_ref, *rest):
    *out_refs, sems = rest
    count, share = len(out_refs) + 1, out_refs[0].shape[1]
    run_copies(
        sems,
        [
            (tokens_ref.at[0, :, aligned(lax.rem(at_ref[0] + shift, count), share)], out_ref)
            for shift, out_ref in enumerate(out_refs, 1)
        ],
    )


def pack_heads_kernel(at_ref, values_ref, grad_ref, *rest):
    *out_refs, sems = rest
    width = out_refs[0].shape[2]
    pairs = []
    for shift, out_ref in enumerate(out_refs):
        cols = aligned(lax.rem(at_ref[0] + shift, len(out_refs)), width)
        pairs.append((values_ref.at[0, :, cols], out_ref.at[0]))
        pairs.append((grad_ref.at[0, :, cols], out_ref.at[1]))
    run_copies(sems, pairs)


def collect_heads_kernel(at_ref, *rest):
    *part_refs, out_ref = rest
    group = len(part_refs)
    for shift, part_ref in enumerate(part_refs):
        out_ref[lax.rem(at_ref[0] + group - shift, group)] = part_ref[...]


def pack_tokens_kernel(depth, at_ref, tokens_ref, *rest):
    *out_refs, sems = rest
    group = len(out_refs)
    pairs = []
    for shift, out_ref in enumerate(out_refs):
        member = lax.rem(at_ref[0] + shift, group)
        for part in range(out_ref.shape[1] // depth):
            pairs.append(
                (
                    tokens_ref.at[0, :, aligned(part * group + member, depth)],
                    out_ref.at[:, part * depth : (part + 1) * depth],
                )
            )
    run_copies(sems, pairs)


def collect_tokens_kernel(at_ref, *rest):
    *part_refs, out_ref = rest
    group, tok = len(part_refs), part_refs[0].shape[0]
    for shift, part_ref in enumerate(part_refs):
        src = lax.rem(at_ref[0] + group - shift, group)
        out_ref[:, aligned(src, tok)] = part_ref[...].T


def write_blocks(projected, out_ref):
    group, _, heads, feat, _ = out_ref.shape
    for member in range(group):
        for which in range(2):
            for head in range(heads):
                first = ((which * group + member) * heads + head) * feat
                out_ref[member, which, head] = projected[first : first + feat]


def project_kernel(at_ref, tokens_ref, weight_ref, out_ref, part_ref, sem):
    share = part_ref.shape[1]
    run_copies(sem, [(tokens_ref.at[0, :, aligned(at_ref[0], share)], part_ref)])
    write_blocks(dot(part_ref[...], weight_ref[...]).T, out_ref)


def project_rest_kernel(at_ref, own_ref, weight_ref, *rest):
    *part_refs, out_ref, slots_ref, held_ref, sems, out_sems = rest
    count = len(part_refs) + 1
    at = at_ref[0]
    pieces, size = held_ref.shape[:2]
    loads = [
        pltpu.make_async_copy(
            weight_ref.at[i * size : (i + 1) * size], held_ref.at[i], sems.at[i]
        )
        for i in range(pieces)
    ]
    for load in loads:
        load.start()
    copies = [pltpu.make_async_copy(own_ref, out_ref.at[at], out_sems.at[0])]
    copies[0].start()
    for shift, part_ref in enumerate(part_refs, 1):
        total = 0.0
        for i, load in enumerate(loads):
            if shift == 1:
                load.wait()
            total = total + dot(part_ref[:, i * size : (i + 1) * size], held_ref[i])
        write_blocks(total.T, slots_ref.at[shift - 1])
        owner = lax.rem(at + count - shift, count)
        copies.append(
            pltpu.make_async_copy(slots_ref.at[shift - 1], out_ref.at[owner], out_sems.at[shift])
        )
        copies[-1].start()
    for copy in copies:
        copy.wait()


def weight_piece_kernel(at_ref, weight_ref, out_ref, sems):
    run_copies(sems, [(weight_ref.at[aligned(at_ref[0], out_ref.shape[0])], out_ref)])


def state_kernel(with_state, parts_ref, vg_ref, qk_ref, *state_refs):
    count, blocks, _, heads, _, tok = parts_ref.shape
    for head in range(heads):
        for which in range(2):
            for src in range(blocks):
                total = parts_ref[0, src, which, head]
                for part in range(1, count):
                    total = total + parts_ref[part, src, which, head]
                qk_ref[src, which, head] = total
        if with_state:
            high, low = split(psi(feature_major(qk_ref, 1, head), False))
            v = rows_of(vg_ref, 0, head, 0, blocks * tok)
            state_refs[0][head] = dot(high, v) + dot(low, v)


def numerator_kernel(qk_ref, vg_ref, num_ref):
    heads = qk_ref.shape[2]
    length = qk_ref.shape[0] * qk_ref.shape[4]
    tile = min(TILE, length)
    for head in range(heads):
        q = feature_major(qk_ref, 0, head) * 0.25
        k = feature_major(qk_ref, 1, head)
        left, right = score_sides(q, k)
        for at in range(0, length, tile):
            width = at + tile
            scores = dot(left[at:width], right[:, :width])
            kernel = jnp.where(
                causal_mask(tile, width), 1.0 + scores * (1.0 + 0.5 * scores), 0.0
            )
            high, low = split(kernel)
            v = rows_of(vg_ref, 0, head, 0, width)
            num_ref[at:width, head * DH : (head + 1) * DH] = dot(high, v) + dot(low, v)


def normalize_kernel(with_state, qk_ref, vg_ref, num_ref, *rest):
    if with_state:
        prefix_ref, attended_ref, grad_ref, carried_ref = rest
    else:
        attended_ref, grad_ref = rest
    heads = qk_ref.shape[2]
    blocks, tok = qk_ref.shape[0], qk_ref.shape[4]
    length = blocks * tok
    for head in range(heads):
        cols = slice(head * DH, (head + 1) * DH)
        numerator = num_ref[:, cols]
        if with_state:
            feat = psi(feature_major(qk_ref, 0, head) * 0.25, True)
            numerator = numerator + dot3(feat.T, prefix_ref[head])
        inv_rms = lax.rsqrt(jnp.mean(numerator * numerator, axis=-1, keepdims=True) + EPSILON)
        normed = numerator * inv_rms
        upstream = rows_of(vg_ref, 1, head, 0, length).astype(f32)
        grad = inv_rms * (
            upstream - normed * jnp.mean(normed * upstream, axis=-1, keepdims=True)
        )
        attended_ref[:, cols] = normed.astype(bf16)
        grad_ref[:, cols] = grad
        if with_state:
            carried_ref[head] = dot3(feat, grad)


def split_rows_kernel(at_ref, in_ref, *rest):
    *out_refs, sems = rest
    group, tok = len(out_refs), out_refs[0].shape[0]
    run_copies(
        sems,
        [
            (in_ref.at[aligned(lax.rem(at_ref[0] + shift, group), tok)], out_ref)
            for shift, out_ref in enumerate(out_refs)
        ],
    )


def backward_kernel(with_state, qk_ref, vg_ref, grad_ref, *rest):
    if with_state:
        prefix_ref, grad_qk_ref, grad_v_ref = rest
    else:
        grad_qk_ref, grad_v_ref = rest
    length = qk_ref.shape[0] * qk_ref.shape[4]
    tile = min(TILE, length)
    for head in range(grad_v_ref.shape[0]):
        cols = slice(head * DH, (head + 1) * DH)
        q = feature_major(qk_ref, 0, head) * 0.25
        k = feature_major(qk_ref, 1, head)
        left, right = score_sides(q, k)
        q_both = jnp.concatenate(split(q), axis=0)
        k_both = jnp.concatenate(split(k), axis=0)
        grad = grad_ref[:, cols]
        grad_t = grad.T
        if with_state:
            grad_q = pull_psi(q, dot3(prefix_ref[head], grad_t), True)
        for at in reversed(range(0, length, tile)):
            width = at + tile
            scores = dot(left[at:width], right[:, :width])
            causal = causal_mask(tile, width)
            v = rows_of(vg_ref, 0, head, 0, width)
            high, low = split(grad[at:width])
            mixing = dot(
                jnp.concatenate([high, low], axis=1), jnp.concatenate([v, v], axis=1), NT
            )
            more = 1.0 + scores
            slope = jnp.where(causal, mixing * more, 0.0).astype(bf16)
            kernel = jnp.where(causal, more + 0.5 * scores * scores, 0.0).astype(bf16)
            both = dot(k_both[:, :width], slope, NT)
            piece = both[:F] + both[F:]
            if with_state:
                piece = piece + grad_q[:, at:width]
            grad_qk_ref[0, head, :, at:width] = piece * 0.25
            both = dot(q_both[:, at:width], slope)
            piece_k = both[:F] + both[F:]
            both = dot(jnp.concatenate(split(grad_t[:, at:width]), axis=0), kernel)
            piece_v = both[:DH] + both[DH:]
            if width == length:
                grad_qk_ref[1, head] = piece_k
                grad_v_ref[head] = piece_v
            else:
                grad_qk_ref[1, head, :, :width] += piece_k
                grad_v_ref[head, :, :width] += piece_v


def rows_kernel(with_state, qk_ref, vg_ref, grad_qk_ref, *rest):
    *suffix_refs, out_ref, held_ref, sems = rest
    heads = qk_ref.shape[2]
    length = qk_ref.shape[0] * qk_ref.shape[4]
    for head in range(heads):
        grad_k = grad_qk_ref[1, head]
        if with_state:
            k = feature_major(qk_ref, 1, head)
            v = rows_of(vg_ref, 0, head, 0, length)
            high, low = split(suffix_refs[0][head])
            grad_k = grad_k + pull_psi(k, dot(high, v, NT) + dot(low, v, NT), False)
        held_ref[head * F : (head + 1) * F] = grad_qk_ref[0, head].astype(bf16)
        held_ref[(heads + head) * F : (heads + head + 1) * F] = grad_k.astype(bf16)
    run_copies(sems, [(held_ref, out_ref)])


def grad_values_kernel(with_state, at_ref, qk_ref, grad_v_ref, *rest):
    heads = qk_ref.shape[2]
    group, tok = qk_ref.shape[0], qk_ref.shape[4]
    suffix_refs, out_refs = rest[: -group - 2], rest[-group - 2 : -2]
    held_ref, sems = rest[-2:]
    for head in range(heads):
        grad_v = grad_v_ref[head]
        if with_state:
            feat = psi(feature_major(qk_ref, 1, head), False)
            grad_v = grad_v + dot3(suffix_refs[0][head].T, feat)
        held_ref[:, head * DH : (head + 1) * DH] = grad_v.T.astype(bf16)
    split_rows_kernel(at_ref, held_ref, *out_refs, sems)


def unpack_heads_kernel(at_ref, *rest):
    *part_refs, out_ref = rest
    group, width = len(part_refs), part_refs[0].shape[1]
    for shift, part_ref in enumerate(part_refs):
        src = lax.rem(at_ref[0] + group - shift, group)
        out_ref[0, :, aligned(src, width)] = part_ref[...]


def place_rows(at, part_refs, cols, held_ref):
    group, half = len(part_refs), part_refs[0].shape[0] // 2
    for shift, part_ref in enumerate(part_refs):
        src = lax.rem(at + group - shift, group)
        for which in range(2):
            rows = aligned(which * group + src, half)
            held_ref[rows, :] = part_ref[which * half : (which + 1) * half, cols]


def product_kernel(group, at_ref, *rest):
    rows_refs, rest = rest[:group], rest[group:]
    tokens_ref, *part_refs, total_ref, held_ref = rest
    place_rows(at_ref[1], rows_refs, slice(None), held_ref)
    total_ref[...] = dot(tokens_ref[...], held_ref[...], NT)
    count = len(part_refs)
    size = part_refs[0].shape[0]
    for shift, part_ref in enumerate(part_refs):
        owner = lax.rem(at_ref[0] + shift, count)
        part = total_ref[pl.ds(pl.multiple_of(owner * size, size), size), :]
        part_ref[...] = part.astype(part_ref.dtype)


def run_sum_kernel(arrived, at_ref, *rest):
    own_ref, *rest = rest
    total_ref = rest[-1]
    total = own_ref[...]
    for ref in rest[:arrived]:
        total = total + ref[...].astype(f32)
    total_ref[...] = total
    part_refs = rest[arrived:-1]
    size = part_refs[0].shape[0]
    for shift, part_ref in enumerate(part_refs):
        owner = lax.rem(at_ref[0] + shift, len(part_refs))
        part = total_ref[pl.ds(pl.multiple_of(owner * size, size), size), :]
        part_ref[...] = part.astype(part_ref.dtype)


def grad_tokens_kernel(group, at_ref, *rest):
    rows_refs, rest = rest[:group], rest[group:]
    *weight_refs, out_ref, held_ref = rest
    place_rows(at_ref[0], rows_refs, aligned(at_ref[0], out_ref.shape[1]), held_ref)
    rows = held_ref[...].T
    for i, weight_ref in enumerate(weight_refs):
        size = weight_ref.shape[0]
        first = pl.multiple_of(at_ref[1 + i], size)
        out_ref[0, :, pl.ds(first, size)] = dot(rows, weight_ref[...], NT).astype(bf16)


VMEM = pl.BlockSpec(memory_space=pltpu.VMEM)
SMEM = pl.BlockSpec(memory_space=pltpu.SMEM)
FAR = pl.BlockSpec(memory_space=pltpu.HBM)
ANYWHERE = pl.BlockSpec(memory_space=pl.ANY)


def call(
    body,
    outs,
    *operands,
    scalars=(),
    after=(),
    after_far=(),
    scratch=(),
    far_in=(),
    far_out=False,
    copies=(),
):
    at = [jnp.stack([jnp.int32(s) for s in scalars])] if scalars else []
    count = len(at) + len(operands)

    def kernel(*refs):
        ins, rest = refs[:count], refs[count + len(after) + len(after_far) :]
        body(*ins, *rest[: len(outs)], *rest[len(outs) + 1 :])
        rest[len(outs)][...] = jnp.zeros((8, 128), f32)

    *results, token = pl.pallas_call(
        kernel,
        out_shape=[jax.ShapeDtypeStruct(shape, kind) for shape, kind in [*outs, ((8, 128), f32)]],
        in_specs=[SMEM] * len(at)
        + [FAR if i in far_in else VMEM for i in range(len(operands))]
        + [ANYWHERE] * len(after)
        + [FAR] * len(after_far),
        out_specs=[FAR if far_out else VMEM] * len(outs) + [VMEM],
        scratch_shapes=[*scratch] + [pltpu.SemaphoreType.DMA((n,)) for n in copies],
        compiler_params=pltpu.CompilerParams(vmem_limit_bytes=VMEM_LIMIT),
        cost_estimate=pl.CostEstimate(flops=0, bytes_accessed=0, transcendentals=0),
    )(*at, *operands, *after, *after_far)
    return results, token


def local(dp_size, ctx_size, tokens, proj_weight, values, grad_out):
    group = min(GROUP, ctx_size, H)
    runs = ctx_size // group
    heads = H // group
    tok, width = tokens.shape[1:]
    length = group * tok
    cols = proj_weight.shape[1]
    share = width // dp_size
    depth = share // ctx_size
    with_state = runs > 1
    groups = [[run * group + i for i in range(group)] for run in range(runs)]
    wide_groups = [
        [dp * ctx_size + i for dp in range(dp_size) for i in members] for members in groups
    ]
    dp_at, ctx_at = lax.axis_index("dp"), lax.axis_index("ctx")
    run_at, member = ctx_at // group, ctx_at % group

    def exchange(x):
        return lax.all_to_all(
            x, "ctx", split_axis=0, concat_axis=0, tiled=True, axis_index_groups=groups
        )

    def to_dp(x, shift):
        return lax.ppermute(x, "dp", [(i, (i + shift) % dp_size) for i in range(dp_size)])

    def to_member(x, shift):
        pairs = [(i, i - i % group + (i + shift) % group) for i in range(ctx_size)]
        return lax.ppermute(x, "ctx", pairs)

    def to_members(parts):
        return [part if not shift else to_member(part, shift) for shift, part in enumerate(parts)]

    def to_run(x, shift, wrap):
        pairs = [
            (i, (i + shift * group) % ctx_size)
            for i in range(ctx_size)
            if wrap or 0 <= i + shift * group < ctx_size
        ]
        return lax.ppermute(x, "ctx", pairs)

    qk_shape = ((group, 2, heads, F, tok), f32)
    state_shape = ((heads, PSI, DH), f32)
    blocks_shape = ((tok, heads * DH), bf16)
    rows_shape = ((length, heads * DH), f32)

    parts, token = call(
        token_parts_kernel,
        [((tok, share), bf16)] * (dp_size - 1),
        tokens,
        scalars=(dp_at,),
        far_in=(0,),
        far_out=True,
        copies=(dp_size - 1,),
    )
    arrived = [to_dp(part, shift) for shift, part in enumerate(parts, 1)]
    parts, token = call(
        pack_heads_kernel,
        [((2, tok, heads * DH), bf16)] * group,
        values,
        grad_out,
        scalars=(member,),
        after=(token,),
        far_in=(0, 1),
        far_out=True,
        copies=(2 * group,),
    )
    parts = to_members(parts)
    (vg,), vg_token = call(
        collect_heads_kernel,
        [((group, 2, tok, heads * DH), bf16)],
        *parts,
        scalars=(member,),
    )
    (projected,), token = call(
        project_kernel,
        [qk_shape],
        tokens,
        proj_weight,
        scalars=(dp_at,),
        after=(token,),
        far_in=(0,),
        copies=(1,),
        scratch=[pltpu.VMEM((tok, share), bf16)],
    )
    part_shape = (tok, dp_size * runs * depth)
    if depth % 128 == 0:
        parts, token = call(
            functools.partial(pack_tokens_kernel, depth),
            [(part_shape, bf16)] * group,
            tokens,
            scalars=(member,),
            after=(token,),
            far_in=(0,),
            far_out=True,
            copies=(group * dp_size * runs,),
        )
    else:
        blocks = tokens[0].reshape(tok, dp_size * runs, group, depth).transpose(2, 0, 1, 3)
        parts = [
            lax.dynamic_index_in_dim(blocks, (member + shift) % group, 0, keepdims=False).reshape(
                part_shape
            )
            for shift in range(group)
        ]
    token_parts = to_members(parts)

    (projected,), token = call(
        project_rest_kernel,
        [((dp_size,) + qk_shape[0], f32)],
        projected,
        proj_weight,
        *arrived,
        scalars=(dp_at,),
        after=(vg_token,),
        far_in=(1,),
        far_out=True,
        scratch=[
            pltpu.VMEM((dp_size - 1,) + qk_shape[0], f32),
            pltpu.VMEM((4, share // 4, cols), bf16),
        ],
        copies=(4, dp_size),
    )
    qk_parts = lax.all_to_all(
        projected.reshape((dp_size * group,) + qk_shape[0][1:]),
        ("dp", "ctx"),
        split_axis=0,
        concat_axis=0,
        tiled=True,
        axis_index_groups=wide_groups,
    ).reshape(projected.shape)

    pair = 2 if ctx_size % 2 == 0 else 1
    parity = ctx_at % pair
    piece = share // pair
    (mine,), token = call(
        weight_piece_kernel,
        [((piece, cols), bf16)],
        proj_weight,
        scalars=(parity,),
        after=(token,),
        far_in=(0,),
        far_out=True,
        copies=(1,),
    )
    fetched = [to_dp(mine, shift) for shift in range(1, dp_size)]
    weights, firsts = [proj_weight], [dp_at * share]
    for shift, half in enumerate(fetched, 1):
        base = (dp_at + dp_size - shift) % dp_size * share
        weights.append(half)
        firsts.append(base + parity * piece)
        if pair == 2:
            weights.append(lax.ppermute(half, "ctx", [(i, i ^ 1) for i in range(ctx_size)]))
            firsts.append(base + (1 - parity) * piece)

    (qk, *state), token = call(
        functools.partial(state_kernel, with_state),
        [qk_shape] + [state_shape] * with_state,
        qk_parts,
        vg,
    )
    prefix, suffix = (), ()
    if with_state:
        prefix = (sum(to_run(state[0], shift, False) for shift in range(1, runs)),)
    (numerator,), token = call(numerator_kernel, [rows_shape], qk, vg)
    (attended, grad_num, *carried), token = call(
        functools.partial(normalize_kernel, with_state),
        [((length, heads * DH), bf16), rows_shape] + [state_shape] * with_state,
        qk,
        vg,
        numerator,
        *prefix,
        after_far=token_parts[1:],
    )
    if with_state:
        suffix = (sum(to_run(carried[0], -shift, False) for shift in range(1, runs)),)
    (grad_qk, grad_v), token = call(
        functools.partial(backward_kernel, with_state),
        [((2, heads, F, length), f32), ((heads, DH, length), f32)],
        qk,
        vg,
        grad_num,
        *prefix,
        after_far=fetched,
    )
    attended, attended_token = call(
        split_rows_kernel,
        [blocks_shape] * group,
        attended,
        scalars=(member,),
        after=(token,),
        far_out=True,
        copies=(group,),
    )
    (rows,), token = call(
        functools.partial(rows_kernel, with_state),
        [((2 * heads * F, length), bf16)],
        qk,
        vg,
        grad_qk,
        *suffix,
        far_out=True,
        scratch=[pltpu.VMEM((2 * heads * F, length), bf16)],
        copies=(1,),
    )
    rows = [rows] + [to_member(rows, shift) for shift in range(1, group)]
    (token_cols,), tokens_token = call(
        collect_tokens_kernel,
        [(part_shape[1:] + (length,), bf16)],
        *token_parts,
        scalars=(member,),
        after=(token,),
    )
    grad_values, token = call(
        functools.partial(grad_values_kernel, with_state),
        [blocks_shape] * group,
        qk,
        grad_v,
        *suffix,
        scalars=(member,),
        after=(token,),
        far_out=True,
        scratch=[pltpu.VMEM((length, heads * DH), bf16)],
        copies=(group,),
    )
    attended, grad_values = to_members(attended), to_members(grad_values)
    (attended,), attended_token = call(
        unpack_heads_kernel, [((1, tok, H * DH), bf16)], *attended, scalars=(member,)
    )

    held = pltpu.VMEM((cols, length), bf16)
    (own, *parts), token = call(
        functools.partial(product_kernel, group),
        [((runs * depth, cols), f32)] + [((runs * depth, cols), bf16)] * (dp_size - 1),
        *rows,
        token_cols,
        scalars=(dp_at, member),
        after=(attended_token,),
        scratch=[pltpu.VMEM((dp_size * runs * depth, cols), f32), held],
    )
    parts = [to_dp(part, shift) for shift, part in enumerate(parts, 1)]
    (grad_values,), values_token = call(
        unpack_heads_kernel,
        [((1, tok, H * DH), bf16)],
        *grad_values,
        scalars=(member,),
        after=(token,),
    )
    (grad_proj, *parts), token = call(
        functools.partial(run_sum_kernel, len(parts)),
        [((depth, cols), f32)] + [((depth, cols), bf16)] * (runs - 1),
        own,
        *parts,
        scalars=(run_at,),
        after=(values_token,),
        scratch=[pltpu.VMEM((runs * depth, cols), f32)],
    )
    (grad_tokens,), _ = call(
        functools.partial(grad_tokens_kernel, group),
        [((1, tok, width), bf16)],
        *rows,
        *weights,
        scalars=(member, *firsts),
        after=(token,),
        scratch=[pltpu.VMEM((cols, tok), bf16)],
    )
    for shift, part in enumerate(parts, 1):
        grad_proj = grad_proj + to_run(part, shift, True).astype(f32)
    return (attended, grad_tokens, grad_values, grad_proj)


def solution(mesh):
    return jax.shard_map(
        functools.partial(local, mesh.shape["dp"], mesh.shape["ctx"]),
        mesh=mesh,
        in_specs=(P("dp", "ctx", None), P("dp", None), P("dp", "ctx", None), P("dp", "ctx", None)),
        out_specs=(
            P("dp", "ctx", None),
            P("dp", "ctx", None),
            P("dp", "ctx", None),
            P(("dp", "ctx"), None),
        ),
        check_vma=False,
    )
```

```python
import functools

import jax
import jax.numpy as jnp
from jax import lax
from jax.experimental import pallas as pl
from jax.experimental.pallas import tpu as pltpu
from jax.sharding import PartitionSpec as P

H = 16
F = 16
DH = 128
EPSILON = 1e-05
GROUP = 8
TILE = 256
VMEM_LIMIT = 16 * 1024 * 1024
VMEM_MOST = 60 * 1024 * 1024
PSI = 9 * F + 2 * F
PSI_SCALE = (0.5,) + (1.0,) * 7 + (0.5,)

f32 = jnp.float32
bf16 = jnp.bfloat16

NN = (((1,), (0,)), ((), ()))
NT = (((1,), (1,)), ((), ()))


def dot(a, b, dims=NN):
    return lax.dot_general(a, b, dims, preferred_element_type=f32)


def split(x):
    high = x.astype(bf16)
    return high, (x - high.astype(f32)).astype(bf16)


def dot3(a, b, dims=NN):
    a_high, a_low = split(a)
    b_high, b_low = split(b)
    return dot(a_high, b_high, dims) + (dot(a_high, b_low, dims) + dot(a_low, b_high, dims))


def turned(x, r):
    return x if r == 0 else jnp.concatenate([x[r:], x[:r]], axis=0)


def psi(x, weights):
    parts = []
    for r in range(9):
        part = x * turned(x, r)
        parts.append(part * PSI_SCALE[r] if weights and PSI_SCALE[r] != 1.0 else part)
    row = lax.broadcasted_iota(jnp.int32, x.shape, 0)
    return jnp.concatenate(parts + [x, jnp.where(row == 0, 1.0, 0.0)], axis=0)


def pull_psi(x, upstream, weights):
    total = upstream[9 * F : 10 * F]
    for r in range(9):
        part = upstream[r * F : (r + 1) * F]
        if weights and PSI_SCALE[r] != 1.0:
            part = part * PSI_SCALE[r]
        total = total + part * turned(x, r) + turned(part * x, (F - r) % F)
    return total


def feature_major(qk_ref, which, head):
    return jnp.concatenate([qk_ref[src, which, head] for src in range(qk_ref.shape[0])], axis=1)


def rows_of(ref, which, head, start, stop):
    tok = ref.shape[2]
    return jnp.concatenate(
        [
            ref[src, which, :, head * DH : (head + 1) * DH]
            for src in range(start // tok, stop // tok)
        ],
        axis=0,
    )


def score_sides(q, k):
    q_high, q_low = split(q)
    k_high, k_low = split(k)
    left = jnp.concatenate([q_high, q_high, q_low, q_low], axis=0)
    right = jnp.concatenate([k_high, k_low, k_high, k_low], axis=0)
    return left.T, right


def causal_mask(tile, width):
    row = lax.broadcasted_iota(jnp.int32, (tile, width), 0) + (width - tile)
    return row >= lax.broadcasted_iota(jnp.int32, (tile, width), 1)


def run_copies(sems, pairs):
    copies = [
        pltpu.make_async_copy(source, target, sems.at[i])
        for i, (source, target) in enumerate(pairs)
    ]
    for copy in copies:
        copy.start()
    for copy in copies:
        copy.wait()


def aligned(at, size):
    return pl.ds(pl.multiple_of(at * size, size), size)


def token_parts_kernel(at_ref, tokens_ref, *rest):
    *out_refs, sems = rest
    count, share = len(out_refs) + 1, out_refs[0].shape[1]
    run_copies(
        sems,
        [
            (tokens_ref.at[0, :, aligned(lax.rem(at_ref[0] + shift, count), share)], out_ref)
            for shift, out_ref in enumerate(out_refs, 1)
        ],
    )


def pack_heads_kernel(at_ref, values_ref, grad_ref, *rest):
    *out_refs, sems = rest
    width = out_refs[0].shape[2]
    pairs = []
    for shift, out_ref in enumerate(out_refs):
        cols = aligned(lax.rem(at_ref[0] + shift, len(out_refs)), width)
        pairs.append((values_ref.at[0, :, cols], out_ref.at[0]))
        pairs.append((grad_ref.at[0, :, cols], out_ref.at[1]))
    run_copies(sems, pairs)


def collect_heads_kernel(at_ref, *rest):
    *part_refs, out_ref = rest
    group = len(part_refs)
    for shift, part_ref in enumerate(part_refs):
        out_ref[lax.rem(at_ref[0] + group - shift, group)] = part_ref[...]


def pack_tokens_kernel(depth, at_ref, tokens_ref, *rest):
    *out_refs, sems = rest
    group = len(out_refs)
    pairs = []
    for shift, out_ref in enumerate(out_refs):
        member = lax.rem(at_ref[0] + shift, group)
        for part in range(out_ref.shape[1] // depth):
            pairs.append(
                (
                    tokens_ref.at[0, :, aligned(part * group + member, depth)],
                    out_ref.at[:, part * depth : (part + 1) * depth],
                )
            )
    run_copies(sems, pairs)


def collect_tokens_kernel(at_ref, *rest):
    *part_refs, out_ref = rest
    group, tok = len(part_refs), part_refs[0].shape[0]
    for shift, part_ref in enumerate(part_refs):
        src = lax.rem(at_ref[0] + group - shift, group)
        out_ref[:, aligned(src, tok)] = part_ref[...].T


def write_blocks(projected, out_ref):
    group, _, heads, feat, _ = out_ref.shape
    for member in range(group):
        for which in range(2):
            for head in range(heads):
                first = ((which * group + member) * heads + head) * feat
                out_ref[member, which, head] = projected[first : first + feat]


def project_kernel(at_ref, tokens_ref, weight_ref, out_ref, part_ref, sem):
    share = part_ref.shape[1]
    run_copies(sem, [(tokens_ref.at[0, :, aligned(at_ref[0], share)], part_ref)])
    write_blocks(dot(part_ref[...], weight_ref[...]).T, out_ref)


def project_rest_kernel(at_ref, own_ref, weight_ref, *rest):
    *part_refs, out_ref, slots_ref, held_ref, sems, out_sems = rest
    count = len(part_refs) + 1
    at = at_ref[0]
    pieces, size = held_ref.shape[:2]
    loads = [
        pltpu.make_async_copy(
            weight_ref.at[i * size : (i + 1) * size], held_ref.at[i], sems.at[i]
        )
        for i in range(pieces)
    ]
    for load in loads:
        load.start()
    copies = [pltpu.make_async_copy(own_ref, out_ref.at[at], out_sems.at[0])]
    copies[0].start()
    for shift, part_ref in enumerate(part_refs, 1):
        total = 0.0
        for i, load in enumerate(loads):
            if shift == 1:
                load.wait()
            total = total + dot(part_ref[:, i * size : (i + 1) * size], held_ref[i])
        write_blocks(total.T, slots_ref.at[shift - 1])
        owner = lax.rem(at + count - shift, count)
        copies.append(
            pltpu.make_async_copy(slots_ref.at[shift - 1], out_ref.at[owner], out_sems.at[shift])
        )
        copies[-1].start()
    for copy in copies:
        copy.wait()


def weight_piece_kernel(at_ref, weight_ref, out_ref, sems):
    run_copies(sems, [(weight_ref.at[aligned(at_ref[0], out_ref.shape[0])], out_ref)])


def state_kernel(with_state, parts_ref, vg_ref, qk_ref, *state_refs):
    count, blocks, _, heads, _, tok = parts_ref.shape
    for head in range(heads):
        for which in range(2):
            for src in range(blocks):
                total = parts_ref[0, src, which, head]
                for part in range(1, count):
                    total = total + parts_ref[part, src, which, head]
                qk_ref[src, which, head] = total
        if with_state:
            high, low = split(psi(feature_major(qk_ref, 1, head), False))
            v = rows_of(vg_ref, 0, head, 0, blocks * tok)
            state_refs[0][head] = dot(high, v) + dot(low, v)


def numerator_kernel(qk_ref, vg_ref, num_ref):
    heads = qk_ref.shape[2]
    length = qk_ref.shape[0] * qk_ref.shape[4]
    tile = min(TILE, length)
    for head in range(heads):
        q = feature_major(qk_ref, 0, head) * 0.25
        k = feature_major(qk_ref, 1, head)
        left, right = score_sides(q, k)
        for at in range(0, length, tile):
            width = at + tile
            scores = dot(left[at:width], right[:, :width])
            kernel = jnp.where(
                causal_mask(tile, width), 1.0 + scores * (1.0 + 0.5 * scores), 0.0
            )
            high, low = split(kernel)
            v = rows_of(vg_ref, 0, head, 0, width)
            num_ref[at:width, head * DH : (head + 1) * DH] = dot(high, v) + dot(low, v)


def normalize_kernel(with_state, qk_ref, vg_ref, num_ref, *rest):
    if with_state:
        prefix_ref, attended_ref, grad_ref, carried_ref = rest
    else:
        attended_ref, grad_ref = rest
    heads = qk_ref.shape[2]
    blocks, tok = qk_ref.shape[0], qk_ref.shape[4]
    length = blocks * tok
    for head in range(heads):
        cols = slice(head * DH, (head + 1) * DH)
        numerator = num_ref[:, cols]
        if with_state:
            feat = psi(feature_major(qk_ref, 0, head) * 0.25, True)
            numerator = numerator + dot3(feat.T, prefix_ref[head])
        inv_rms = lax.rsqrt(jnp.mean(numerator * numerator, axis=-1, keepdims=True) + EPSILON)
        normed = numerator * inv_rms
        upstream = rows_of(vg_ref, 1, head, 0, length).astype(f32)
        grad = inv_rms * (
            upstream - normed * jnp.mean(normed * upstream, axis=-1, keepdims=True)
        )
        attended_ref[:, cols] = normed.astype(bf16)
        grad_ref[:, cols] = grad
        if with_state:
            carried_ref[head] = dot3(feat, grad)


def leave_kernel(in_ref, out_ref, sems):
    group, tok = out_ref.shape[:2]
    run_copies(
        sems, [(in_ref.at[i * tok : (i + 1) * tok], out_ref.at[i]) for i in range(group)]
    )


def backward_kernel(with_state, qk_ref, vg_ref, grad_ref, *rest):
    if with_state:
        prefix_ref, grad_qk_ref, grad_v_ref = rest
    else:
        grad_qk_ref, grad_v_ref = rest
    length = qk_ref.shape[0] * qk_ref.shape[4]
    tile = min(TILE, length)
    for head in range(grad_v_ref.shape[0]):
        cols = slice(head * DH, (head + 1) * DH)
        q = feature_major(qk_ref, 0, head) * 0.25
        k = feature_major(qk_ref, 1, head)
        left, right = score_sides(q, k)
        q_both = jnp.concatenate(split(q), axis=0)
        k_both = jnp.concatenate(split(k), axis=0)
        grad = grad_ref[:, cols]
        grad_t = grad.T
        if with_state:
            grad_q = pull_psi(q, dot3(prefix_ref[head], grad_t), True)
        for at in reversed(range(0, length, tile)):
            width = at + tile
            scores = dot(left[at:width], right[:, :width])
            causal = causal_mask(tile, width)
            v = rows_of(vg_ref, 0, head, 0, width)
            high, low = split(grad[at:width])
            mixing = dot(
                jnp.concatenate([high, low], axis=1), jnp.concatenate([v, v], axis=1), NT
            )
            more = 1.0 + scores
            slope = jnp.where(causal, mixing * more, 0.0).astype(bf16)
            kernel = jnp.where(causal, more + 0.5 * scores * scores, 0.0).astype(bf16)
            both = dot(k_both[:, :width], slope, NT)
            piece = both[:F] + both[F:]
            if with_state:
                piece = piece + grad_q[:, at:width]
            grad_qk_ref[0, head, :, at:width] = piece * 0.25
            both = dot(q_both[:, at:width], slope)
            piece_k = both[:F] + both[F:]
            both = dot(jnp.concatenate(split(grad_t[:, at:width]), axis=0), kernel)
            piece_v = both[:DH] + both[DH:]
            if width == length:
                grad_qk_ref[1, head] = piece_k
                grad_v_ref[head] = piece_v
            else:
                grad_qk_ref[1, head, :, :width] += piece_k
                grad_v_ref[head, :, :width] += piece_v


def rows_kernel(with_state, qk_ref, vg_ref, grad_qk_ref, *rest):
    *suffix_refs, out_ref, held_ref, sems = rest
    heads = qk_ref.shape[2]
    length = qk_ref.shape[0] * qk_ref.shape[4]
    for head in range(heads):
        grad_k = grad_qk_ref[1, head]
        if with_state:
            k = feature_major(qk_ref, 1, head)
            v = rows_of(vg_ref, 0, head, 0, length)
            high, low = split(suffix_refs[0][head])
            grad_k = grad_k + pull_psi(k, dot(high, v, NT) + dot(low, v, NT), False)
        held_ref[head * F : (head + 1) * F] = grad_qk_ref[0, head].astype(bf16)
        held_ref[(heads + head) * F : (heads + head + 1) * F] = grad_k.astype(bf16)
    run_copies(sems, [(held_ref, out_ref)])


def grad_values_kernel(with_state, qk_ref, grad_v_ref, *rest):
    *suffix_refs, out_ref, held_ref, sems = rest
    heads = qk_ref.shape[2]
    for head in range(heads):
        grad_v = grad_v_ref[head]
        if with_state:
            feat = psi(feature_major(qk_ref, 1, head), False)
            grad_v = grad_v + dot3(suffix_refs[0][head].T, feat)
        held_ref[:, head * DH : (head + 1) * DH] = grad_v.T.astype(bf16)
    leave_kernel(held_ref, out_ref, sems)


def unpack_heads_kernel(in_ref, out_ref):
    group, _, width = in_ref.shape
    for member in range(group):
        out_ref[0, :, member * width : (member + 1) * width] = in_ref[member]


def place_rows(at, part_refs, cols, held_ref):
    group, half = len(part_refs), part_refs[0].shape[0] // 2
    for shift, part_ref in enumerate(part_refs):
        src = lax.rem(at + group - shift, group)
        for which in range(2):
            rows = aligned(which * group + src, half)
            held_ref[rows, :] = part_ref[which * half : (which + 1) * half, cols]


def product_kernel(group, at_ref, *rest):
    rows_refs, rest = rest[:group], rest[group:]
    tokens_ref, *part_refs, total_ref, held_ref = rest
    place_rows(at_ref[1], rows_refs, slice(None), held_ref)
    total_ref[...] = dot(tokens_ref[...], held_ref[...], NT)
    count = len(part_refs)
    size = part_refs[0].shape[0]
    for shift, part_ref in enumerate(part_refs):
        owner = lax.rem(at_ref[0] + shift, count)
        part = total_ref[pl.ds(pl.multiple_of(owner * size, size), size), :]
        part_ref[...] = part.astype(part_ref.dtype)


def run_sum_kernel(arrived, at_ref, *rest):
    own_ref, *rest = rest
    total_ref = rest[-1]
    total = own_ref[...]
    for ref in rest[:arrived]:
        total = total + ref[...].astype(f32)
    total_ref[...] = total
    part_refs = rest[arrived:-1]
    size = part_refs[0].shape[0]
    for shift, part_ref in enumerate(part_refs):
        owner = lax.rem(at_ref[0] + shift, len(part_refs))
        part = total_ref[pl.ds(pl.multiple_of(owner * size, size), size), :]
        part_ref[...] = part.astype(part_ref.dtype)


def grad_tokens_kernel(group, at_ref, *rest):
    rows_refs, rest = rest[:group], rest[group:]
    *weight_refs, out_ref, held_ref = rest
    place_rows(at_ref[0], rows_refs, aligned(at_ref[0], out_ref.shape[1]), held_ref)
    rows = held_ref[...].T
    for i, weight_ref in enumerate(weight_refs):
        size = weight_ref.shape[0]
        first = pl.multiple_of(at_ref[1 + i], size)
        out_ref[0, :, pl.ds(first, size)] = dot(rows, weight_ref[...], NT).astype(bf16)


def final_sum_kernel(own_ref, *rest):
    *part_refs, out_ref = rest
    total = own_ref[...]
    for part_ref in part_refs:
        total = total + part_ref[...].astype(f32)
    out_ref[...] = total


VMEM = pl.BlockSpec(memory_space=pltpu.VMEM)
SMEM = pl.BlockSpec(memory_space=pltpu.SMEM)
FAR = pl.BlockSpec(memory_space=pltpu.HBM)
ANYWHERE = pl.BlockSpec(memory_space=pl.ANY)


def call(
    body,
    outs,
    *operands,
    scalars=(),
    after=(),
    after_far=(),
    scratch=(),
    far_in=(),
    far_out=False,
    copies=(),
    limit=VMEM_LIMIT,
):
    at = [jnp.stack([jnp.int32(s) for s in scalars])] if scalars else []
    count = len(at) + len(operands)

    def kernel(*refs):
        ins, rest = refs[:count], refs[count + len(after) + len(after_far) :]
        body(*ins, *rest[: len(outs)], *rest[len(outs) + 1 :])
        rest[len(outs)][...] = jnp.zeros((8, 128), f32)

    *results, token = pl.pallas_call(
        kernel,
        out_shape=[jax.ShapeDtypeStruct(shape, kind) for shape, kind in [*outs, ((8, 128), f32)]],
        in_specs=[SMEM] * len(at)
        + [FAR if i in far_in else VMEM for i in range(len(operands))]
        + [ANYWHERE] * len(after)
        + [FAR] * len(after_far),
        out_specs=[FAR if far_out else VMEM] * len(outs) + [VMEM],
        scratch_shapes=[*scratch] + [pltpu.SemaphoreType.DMA((n,)) for n in copies],
        compiler_params=pltpu.CompilerParams(vmem_limit_bytes=limit),
        cost_estimate=pl.CostEstimate(flops=0, bytes_accessed=0, transcendentals=0),
    )(*at, *operands, *after, *after_far)
    return results, token


def local(dp_size, ctx_size, tokens, proj_weight, values, grad_out):
    group = min(GROUP, ctx_size, H)
    runs = ctx_size // group
    heads = H // group
    tok, width = tokens.shape[1:]
    length = group * tok
    cols = proj_weight.shape[1]
    share = width // dp_size
    depth = share // ctx_size
    with_state = runs > 1
    groups = [[run * group + i for i in range(group)] for run in range(runs)]
    wide_groups = [
        [dp * ctx_size + i for dp in range(dp_size) for i in members] for members in groups
    ]
    dp_at, ctx_at = lax.axis_index("dp"), lax.axis_index("ctx")
    run_at, member = ctx_at // group, ctx_at % group

    def exchange(x):
        return lax.all_to_all(
            x, "ctx", split_axis=0, concat_axis=0, tiled=True, axis_index_groups=groups
        )

    def to_dp(x, shift):
        return lax.ppermute(x, "dp", [(i, (i + shift) % dp_size) for i in range(dp_size)])

    def to_member(x, shift):
        pairs = [(i, i - i % group + (i + shift) % group) for i in range(ctx_size)]
        return lax.ppermute(x, "ctx", pairs)

    def to_members(parts):
        return [part if not shift else to_member(part, shift) for shift, part in enumerate(parts)]

    def to_run(x, shift, wrap):
        pairs = [
            (i, (i + shift * group) % ctx_size)
            for i in range(ctx_size)
            if wrap or 0 <= i + shift * group < ctx_size
        ]
        return lax.ppermute(x, "ctx", pairs)

    qk_shape = ((group, 2, heads, F, tok), f32)
    state_shape = ((heads, PSI, DH), f32)
    blocks_shape = ((group, tok, heads * DH), bf16)
    rows_shape = ((length, heads * DH), f32)

    parts, token = call(
        token_parts_kernel,
        [((tok, share), bf16)] * (dp_size - 1),
        tokens,
        scalars=(dp_at,),
        far_in=(0,),
        far_out=True,
        copies=(dp_size - 1,),
        limit=VMEM_MOST,
    )
    arrived = [to_dp(part, shift) for shift, part in enumerate(parts, 1)]
    parts, token = call(
        pack_heads_kernel,
        [((2, tok, heads * DH), bf16)] * group,
        values,
        grad_out,
        scalars=(member,),
        after=(token,),
        far_in=(0, 1),
        far_out=True,
        copies=(2 * group,),
        limit=VMEM_MOST,
    )
    parts = to_members(parts)
    (vg,), vg_token = call(
        collect_heads_kernel,
        [((group, 2, tok, heads * DH), bf16)],
        *parts,
        scalars=(member,),
    )
    (projected,), token = call(
        project_kernel,
        [qk_shape],
        tokens,
        proj_weight,
        scalars=(dp_at,),
        after=(token,),
        far_in=(0,),
        copies=(1,),
        scratch=[pltpu.VMEM((tok, share), bf16)],
    )
    part_shape = (tok, dp_size * runs * depth)
    if depth % 128 == 0:
        parts, token = call(
            functools.partial(pack_tokens_kernel, depth),
            [(part_shape, bf16)] * group,
            tokens,
            scalars=(member,),
            after=(token,),
            far_in=(0,),
            far_out=True,
            copies=(group * dp_size * runs,),
            limit=VMEM_MOST,
        )
    else:
        blocks = tokens[0].reshape(tok, dp_size * runs, group, depth).transpose(2, 0, 1, 3)
        parts = [
            lax.dynamic_index_in_dim(blocks, (member + shift) % group, 0, keepdims=False).reshape(
                part_shape
            )
            for shift in range(group)
        ]
    token_parts = to_members(parts)

    (projected,), token = call(
        project_rest_kernel,
        [((dp_size,) + qk_shape[0], f32)],
        projected,
        proj_weight,
        *arrived,
        scalars=(dp_at,),
        after=(vg_token, token),
        far_in=(1,),
        far_out=True,
        scratch=[
            pltpu.VMEM((dp_size - 1,) + qk_shape[0], f32),
            pltpu.VMEM((4, share // 4, cols), bf16),
        ],
        copies=(4, dp_size),
    )
    qk_parts = lax.all_to_all(
        projected.reshape((dp_size * group,) + qk_shape[0][1:]),
        ("dp", "ctx"),
        split_axis=0,
        concat_axis=0,
        tiled=True,
        axis_index_groups=wide_groups,
    ).reshape(projected.shape)

    pair = 2 if ctx_size % 2 == 0 else 1
    parity = ctx_at % pair
    piece = share // pair
    (mine,), token = call(
        weight_piece_kernel,
        [((piece, cols), bf16)],
        proj_weight,
        scalars=(parity,),
        after=(token,),
        far_in=(0,),
        far_out=True,
        copies=(1,),
        limit=VMEM_MOST,
    )
    fetched = [to_dp(mine, shift) for shift in range(1, dp_size)]
    weights, firsts = [proj_weight], [dp_at * share]
    for shift, half in enumerate(fetched, 1):
        base = (dp_at + dp_size - shift) % dp_size * share
        weights.append(half)
        firsts.append(base + parity * piece)
        if pair == 2:
            weights.append(lax.ppermute(half, "ctx", [(i, i ^ 1) for i in range(ctx_size)]))
            firsts.append(base + (1 - parity) * piece)

    (qk, *state), token = call(
        functools.partial(state_kernel, with_state),
        [qk_shape] + [state_shape] * with_state,
        qk_parts,
        vg,
    )
    prefix, suffix = (), ()
    if with_state:
        prefix = (sum(to_run(state[0], shift, False) for shift in range(1, runs)),)
    (numerator,), token = call(numerator_kernel, [rows_shape], qk, vg)
    (attended, grad_num, *carried), token = call(
        functools.partial(normalize_kernel, with_state),
        [((length, heads * DH), bf16), rows_shape] + [state_shape] * with_state,
        qk,
        vg,
        numerator,
        *prefix,
        after_far=token_parts[1:],
    )
    if with_state:
        suffix = (sum(to_run(carried[0], -shift, False) for shift in range(1, runs)),)
    (grad_qk, grad_v), token = call(
        functools.partial(backward_kernel, with_state),
        [((2, heads, F, length), f32), ((heads, DH, length), f32)],
        qk,
        vg,
        grad_num,
        *prefix,
        after_far=fetched,
    )
    (attended,), attended_token = call(
        leave_kernel,
        [blocks_shape],
        attended,
        after=(token,),
        far_out=True,
        copies=(group,),
    )
    attended = exchange(attended)
    (rows,), token = call(
        functools.partial(rows_kernel, with_state),
        [((2 * heads * F, length), bf16)],
        qk,
        vg,
        grad_qk,
        *suffix,
        far_out=True,
        scratch=[pltpu.VMEM((2 * heads * F, length), bf16)],
        copies=(1,),
    )
    rows = [rows] + [to_member(rows, shift) for shift in range(1, group)]
    (token_cols,), tokens_token = call(
        collect_tokens_kernel,
        [(part_shape[1:] + (length,), bf16)],
        *token_parts,
        scalars=(member,),
        after=(token,),
    )
    (grad_values,), token = call(
        functools.partial(grad_values_kernel, with_state),
        [blocks_shape],
        qk,
        grad_v,
        *suffix,
        after=(token,),
        far_out=True,
        scratch=[pltpu.VMEM((length, heads * DH), bf16)],
        copies=(group,),
    )
    grad_values = exchange(grad_values)
    (attended,), attended_token = call(
        unpack_heads_kernel, [((1, tok, H * DH), bf16)], attended
    )

    held = pltpu.VMEM((cols, length), bf16)
    (own, *parts), token = call(
        functools.partial(product_kernel, group),
        [((runs * depth, cols), f32)] + [((runs * depth, cols), bf16)] * (dp_size - 1),
        *rows,
        token_cols,
        scalars=(dp_at, member),
        after=(attended_token, token),
        scratch=[pltpu.VMEM((dp_size * runs * depth, cols), f32), held],
    )
    parts = [to_dp(part, shift) for shift, part in enumerate(parts, 1)]
    (grad_values,), values_token = call(
        unpack_heads_kernel,
        [((1, tok, H * DH), bf16)],
        grad_values,
        after=(token,),
    )
    (grad_proj, *parts), token = call(
        functools.partial(run_sum_kernel, len(parts)),
        [((depth, cols), f32)] + [((depth, cols), bf16)] * (runs - 1),
        own,
        *parts,
        scalars=(run_at,),
        after=(values_token,),
        scratch=[pltpu.VMEM((runs * depth, cols), f32)],
    )
    (grad_tokens,), token = call(
        functools.partial(grad_tokens_kernel, group),
        [((1, tok, width), bf16)],
        *rows,
        *weights,
        scalars=(member, *firsts),
        after=(token,),
        scratch=[pltpu.VMEM((cols, tok), bf16)],
    )
    (grad_proj,), _ = call(
        final_sum_kernel,
        [((depth, cols), f32)],
        grad_proj,
        *[to_run(part, shift, True) for shift, part in enumerate(parts, 1)],
        after=(token,),
    )
    return (attended, grad_tokens, grad_values, grad_proj)


def solution(mesh):
    return jax.shard_map(
        functools.partial(local, mesh.shape["dp"], mesh.shape["ctx"]),
        mesh=mesh,
        in_specs=(P("dp", "ctx", None), P("dp", None), P("dp", "ctx", None), P("dp", "ctx", None)),
        out_specs=(
            P("dp", "ctx", None),
            P("dp", "ctx", None),
            P("dp", "ctx", None),
            P(("dp", "ctx"), None),
        ),
        check_vma=False,
    )
```

```python
import functools

import jax
import jax.numpy as jnp
from jax import lax
from jax.experimental import pallas as pl
from jax.experimental.pallas import tpu as pltpu
from jax.sharding import PartitionSpec as P

H = 16
F = 16
DH = 128
EPSILON = 1e-05
GROUP = 8
TILE = 256
VMEM_LIMIT = 16 * 1024 * 1024
VMEM_MOST = 60 * 1024 * 1024
PSI = 9 * F + 2 * F
PSI_SCALE = (0.5,) + (1.0,) * 7 + (0.5,)

f32 = jnp.float32
bf16 = jnp.bfloat16

NN = (((1,), (0,)), ((), ()))
NT = (((1,), (1,)), ((), ()))


def dot(a, b, dims=NN):
    return lax.dot_general(a, b, dims, preferred_element_type=f32)


def split(x):
    high = x.astype(bf16)
    return high, (x - high.astype(f32)).astype(bf16)


def dot3(a, b, dims=NN):
    a_high, a_low = split(a)
    b_high, b_low = split(b)
    return dot(a_high, b_high, dims) + (dot(a_high, b_low, dims) + dot(a_low, b_high, dims))


def turned(x, r):
    return x if r == 0 else jnp.concatenate([x[r:], x[:r]], axis=0)


def psi(x, weights):
    parts = []
    for r in range(9):
        part = x * turned(x, r)
        parts.append(part * PSI_SCALE[r] if weights and PSI_SCALE[r] != 1.0 else part)
    row = lax.broadcasted_iota(jnp.int32, x.shape, 0)
    return jnp.concatenate(parts + [x, jnp.where(row == 0, 1.0, 0.0)], axis=0)


def pull_psi(x, upstream, weights):
    total = upstream[9 * F : 10 * F]
    for r in range(9):
        part = upstream[r * F : (r + 1) * F]
        if weights and PSI_SCALE[r] != 1.0:
            part = part * PSI_SCALE[r]
        total = total + part * turned(x, r) + turned(part * x, (F - r) % F)
    return total


def feature_major(qk_ref, which, head):
    return jnp.concatenate([qk_ref[src, which, head] for src in range(qk_ref.shape[0])], axis=1)


def rows_of(ref, which, head, start, stop):
    tok = ref.shape[2]
    return jnp.concatenate(
        [
            ref[src, which, :, head * DH : (head + 1) * DH]
            for src in range(start // tok, stop // tok)
        ],
        axis=0,
    )


def score_sides(q, k):
    q_high, q_low = split(q)
    k_high, k_low = split(k)
    left = jnp.concatenate([q_high, q_high, q_low, q_low], axis=0)
    right = jnp.concatenate([k_high, k_low, k_high, k_low], axis=0)
    return left.T, right


def causal_mask(tile, width):
    row = lax.broadcasted_iota(jnp.int32, (tile, width), 0) + (width - tile)
    return row >= lax.broadcasted_iota(jnp.int32, (tile, width), 1)


def run_copies(sems, pairs):
    copies = [
        pltpu.make_async_copy(source, target, sems.at[i])
        for i, (source, target) in enumerate(pairs)
    ]
    for copy in copies:
        copy.start()
    for copy in copies:
        copy.wait()


def relay(held_ref, sems, pairs):
    loads, stores = [], []
    for i, (source, target) in enumerate(pairs):
        held = held_ref.at[i]
        loads.append(pltpu.make_async_copy(source, held, sems.at[2 * i]))
        stores.append(pltpu.make_async_copy(held, target, sems.at[2 * i + 1]))
        loads[-1].start()
    for load, store in zip(loads, stores):
        load.wait()
        store.start()
    for store in stores:
        store.wait()


def aligned(at, size):
    return pl.ds(pl.multiple_of(at * size, size), size)


def token_parts_kernel(at_ref, tokens_ref, *rest):
    *out_refs, held_ref, sems = rest
    count, share = len(out_refs) + 1, out_refs[0].shape[1]
    relay(
        held_ref,
        sems,
        [
            (tokens_ref.at[0, :, aligned(lax.rem(at_ref[0] + shift, count), share)], out_ref)
            for shift, out_ref in enumerate(out_refs, 1)
        ],
    )


def pack_heads_kernel(at_ref, values_ref, grad_ref, *rest):
    *out_refs, held_ref, sems = rest
    width = out_refs[0].shape[2]
    pairs = []
    for shift, out_ref in enumerate(out_refs):
        cols = aligned(lax.rem(at_ref[0] + shift, len(out_refs)), width)
        pairs.append((values_ref.at[0, :, cols], out_ref.at[0]))
        pairs.append((grad_ref.at[0, :, cols], out_ref.at[1]))
    relay(held_ref, sems, pairs)


def collect_heads_kernel(at_ref, *rest):
    *part_refs, out_ref = rest
    group = len(part_refs)
    for shift, part_ref in enumerate(part_refs):
        out_ref[lax.rem(at_ref[0] + group - shift, group)] = part_ref[...]


def pack_tokens_kernel(depth, at_ref, tokens_ref, *rest):
    *out_refs, sems = rest
    group = len(out_refs)
    pairs = []
    for shift, out_ref in enumerate(out_refs):
        member = lax.rem(at_ref[0] + shift, group)
        for part in range(out_ref.shape[1] // depth):
            pairs.append(
                (
                    tokens_ref.at[0, :, aligned(part * group + member, depth)],
                    out_ref.at[:, part * depth : (part + 1) * depth],
                )
            )
    run_copies(sems, pairs)


def collect_tokens_kernel(at_ref, *rest):
    *part_refs, out_ref = rest
    group, tok = len(part_refs), part_refs[0].shape[0]
    for shift, part_ref in enumerate(part_refs):
        src = lax.rem(at_ref[0] + group - shift, group)
        out_ref[:, aligned(src, tok)] = part_ref[...].T


def write_blocks(projected, out_ref):
    group, _, heads, feat, _ = out_ref.shape
    for member in range(group):
        for which in range(2):
            for head in range(heads):
                first = ((which * group + member) * heads + head) * feat
                out_ref[member, which, head] = projected[first : first + feat]


def project_kernel(at_ref, tokens_ref, weight_ref, out_ref, weight_out_ref, part_ref, sem):
    share = part_ref.shape[1]
    run_copies(sem, [(tokens_ref.at[0, :, aligned(at_ref[0], share)], part_ref)])
    weight_out_ref[...] = weight_ref[...]
    write_blocks(dot(part_ref[...], weight_ref[...]).T, out_ref)


def project_rest_kernel(at_ref, own_ref, weight_ref, *rest):
    *part_refs, out_ref = rest
    count = len(part_refs) + 1
    at = at_ref[0]
    out_ref[at] = own_ref[...]
    for shift, part_ref in enumerate(part_refs, 1):
        owner = lax.rem(at + count - shift, count)
        write_blocks(dot(part_ref[...], weight_ref[...]).T, out_ref.at[owner])


def weight_piece_kernel(at_ref, weight_ref, out_ref, sems):
    run_copies(sems, [(weight_ref.at[aligned(at_ref[0], out_ref.shape[0])], out_ref)])


def state_sum(refs, head):
    total = refs[0][head].astype(f32)
    for ref in refs[1:]:
        total = total + ref[head].astype(f32)
    return total


def state_kernel(with_state, parts_ref, vg_ref, qk_ref, *state_refs):
    count, blocks, _, heads, _, tok = parts_ref.shape
    for head in range(heads):
        for which in range(2):
            for src in range(blocks):
                total = parts_ref[0, src, which, head]
                for part in range(1, count):
                    total = total + parts_ref[part, src, which, head]
                qk_ref[src, which, head] = total
        if with_state:
            high, low = split(psi(feature_major(qk_ref, 1, head), False))
            v = rows_of(vg_ref, 0, head, 0, blocks * tok)
            state_refs[0][head] = (dot(high, v) + dot(low, v)).astype(bf16)


def numerator_kernel(qk_ref, vg_ref, num_ref):
    heads = qk_ref.shape[2]
    length = qk_ref.shape[0] * qk_ref.shape[4]
    tile = min(TILE, length)
    for head in range(heads):
        q = feature_major(qk_ref, 0, head) * 0.25
        k = feature_major(qk_ref, 1, head)
        left, right = score_sides(q, k)
        for at in range(0, length, tile):
            width = at + tile
            scores = dot(left[at:width], right[:, :width])
            kernel = jnp.where(
                causal_mask(tile, width), 1.0 + scores * (1.0 + 0.5 * scores), 0.0
            )
            high, low = split(kernel)
            v = rows_of(vg_ref, 0, head, 0, width)
            num_ref[at:width, head * DH : (head + 1) * DH] = dot(high, v) + dot(low, v)


def normalize_kernel(with_state, qk_ref, vg_ref, num_ref, *rest):
    if with_state:
        *prefix_refs, attended_ref, grad_ref, carried_ref = rest
    else:
        attended_ref, grad_ref = rest
    heads = qk_ref.shape[2]
    blocks, tok = qk_ref.shape[0], qk_ref.shape[4]
    length = blocks * tok
    for head in range(heads):
        cols = slice(head * DH, (head + 1) * DH)
        numerator = num_ref[:, cols]
        if with_state:
            feat = psi(feature_major(qk_ref, 0, head) * 0.25, True)
            numerator = numerator + dot3(feat.T, state_sum(prefix_refs, head))
        inv_rms = lax.rsqrt(jnp.mean(numerator * numerator, axis=-1, keepdims=True) + EPSILON)
        normed = numerator * inv_rms
        upstream = rows_of(vg_ref, 1, head, 0, length).astype(f32)
        grad = inv_rms * (
            upstream - normed * jnp.mean(normed * upstream, axis=-1, keepdims=True)
        )
        attended_ref[:, cols] = normed.astype(bf16)
        grad_ref[:, cols] = grad
        if with_state:
            carried_ref[head] = dot3(feat, grad).astype(bf16)


def backward_kernel(with_state, qk_ref, vg_ref, grad_ref, *rest):
    *prefix_refs, grad_qk_ref, grad_v_ref = rest
    length = qk_ref.shape[0] * qk_ref.shape[4]
    tile = min(TILE, length)
    for head in range(grad_v_ref.shape[0]):
        cols = slice(head * DH, (head + 1) * DH)
        q = feature_major(qk_ref, 0, head) * 0.25
        k = feature_major(qk_ref, 1, head)
        left, right = score_sides(q, k)
        q_both = jnp.concatenate(split(q), axis=0)
        k_both = jnp.concatenate(split(k), axis=0)
        grad = grad_ref[:, cols]
        grad_t = grad.T
        if with_state:
            grad_q = pull_psi(q, dot3(state_sum(prefix_refs, head), grad_t), True)
        for at in reversed(range(0, length, tile)):
            width = at + tile
            scores = dot(left[at:width], right[:, :width])
            causal = causal_mask(tile, width)
            v = rows_of(vg_ref, 0, head, 0, width)
            high, low = split(grad[at:width])
            mixing = dot(
                jnp.concatenate([high, low], axis=1), jnp.concatenate([v, v], axis=1), NT
            )
            more = 1.0 + scores
            slopes = split(jnp.where(causal, mixing * more, 0.0))
            kernels = split(jnp.where(causal, more + 0.5 * scores * scores, 0.0))
            both = dot(k_both[:, :width], slopes[0], NT)
            piece = both[:F] + (both[F:] + dot(k_both[:F, :width], slopes[1], NT))
            if with_state:
                piece = piece + grad_q[:, at:width]
            grad_qk_ref[0, head, :, at:width] = piece * 0.25
            both = dot(q_both[:, at:width], slopes[0])
            piece_k = both[:F] + (both[F:] + dot(q_both[:F, at:width], slopes[1]))
            high, low = split(grad_t[:, at:width])
            both = dot(jnp.concatenate([high, low], axis=0), kernels[0])
            piece_v = both[:DH] + (both[DH:] + dot(high, kernels[1]))
            if width == length:
                grad_qk_ref[1, head] = piece_k
                grad_v_ref[head] = piece_v
            else:
                grad_qk_ref[1, head, :, :width] += piece_k
                grad_v_ref[head, :, :width] += piece_v


def rows_kernel(with_state, qk_ref, vg_ref, grad_qk_ref, *rest):
    *suffix_refs, out_ref, held_ref, sems = rest
    heads = qk_ref.shape[2]
    length = qk_ref.shape[0] * qk_ref.shape[4]
    for head in range(heads):
        grad_k = grad_qk_ref[1, head]
        if with_state:
            k = feature_major(qk_ref, 1, head)
            v = rows_of(vg_ref, 0, head, 0, length)
            high, low = split(state_sum(suffix_refs, head))
            grad_k = grad_k + pull_psi(k, dot(high, v, NT) + dot(low, v, NT), False)
        held_ref[head * F : (head + 1) * F] = grad_qk_ref[0, head].astype(bf16)
        held_ref[(heads + head) * F : (heads + head + 1) * F] = grad_k.astype(bf16)
    run_copies(sems, [(held_ref, out_ref)])


def grad_values_kernel(with_state, group, at_ref, qk_ref, attended_ref, grad_v_ref, *rest):
    suffix_refs, out_refs, held_ref = rest[: -group - 1], rest[-group - 1 : -1], rest[-1]
    heads, tok = qk_ref.shape[2], qk_ref.shape[4]
    for head in range(heads):
        grad_v = grad_v_ref[head]
        if with_state:
            feat = psi(feature_major(qk_ref, 1, head), False)
            grad_v = grad_v + dot3(state_sum(suffix_refs, head).T, feat)
        held_ref[:, head * DH : (head + 1) * DH] = grad_v.T.astype(bf16)
    for shift, out_ref in enumerate(out_refs):
        rows = aligned(lax.rem(at_ref[0] + shift, group), tok)
        out_ref[0] = attended_ref[rows, :]
        out_ref[1] = held_ref[rows, :]


def unpack_heads_kernel(at_ref, *rest):
    *part_refs, attended_ref, values_ref = rest
    group, width = len(part_refs), part_refs[0].shape[2]
    for shift, part_ref in enumerate(part_refs):
        cols = aligned(lax.rem(at_ref[0] + group - shift, group), width)
        attended_ref[0, :, cols] = part_ref[0]
        values_ref[0, :, cols] = part_ref[1]


def place_rows(at, part_refs, cols, held_ref):
    group, half = len(part_refs), part_refs[0].shape[0] // 2
    for shift, part_ref in enumerate(part_refs):
        src = lax.rem(at + group - shift, group)
        for which in range(2):
            rows = aligned(which * group + src, half)
            held_ref[rows, :] = part_ref[which * half : (which + 1) * half, cols]


def product_kernel(group, at_ref, *rest):
    rows_refs, rest = rest[:group], rest[group:]
    tokens_ref, *part_refs, total_ref, held_ref = rest
    place_rows(at_ref[1], rows_refs, slice(None), held_ref)
    total_ref[...] = dot(tokens_ref[...], held_ref[...], NT)
    count = len(part_refs)
    size = part_refs[0].shape[0]
    for shift, part_ref in enumerate(part_refs):
        owner = lax.rem(at_ref[0] + shift, count)
        part = total_ref[pl.ds(pl.multiple_of(owner * size, size), size), :]
        part_ref[...] = part.astype(part_ref.dtype)


def run_sum_kernel(arrived, at_ref, *rest):
    own_ref, *rest = rest
    total_ref = rest[-1]
    total = own_ref[...]
    for ref in rest[:arrived]:
        total = total + ref[...].astype(f32)
    total_ref[...] = total
    part_refs = rest[arrived:-1]
    size = part_refs[0].shape[0]
    for shift, part_ref in enumerate(part_refs):
        owner = lax.rem(at_ref[0] + shift, len(part_refs))
        part = total_ref[pl.ds(pl.multiple_of(owner * size, size), size), :]
        part_ref[...] = part.astype(part_ref.dtype)


def grad_tokens_kernel(group, at_ref, *rest):
    rows_refs, rest = rest[:group], rest[group:]
    *weight_refs, out_ref, held_ref = rest
    place_rows(at_ref[0], rows_refs, aligned(at_ref[0], out_ref.shape[1]), held_ref)
    rows = held_ref[...].T
    for i, weight_ref in enumerate(weight_refs):
        size = weight_ref.shape[0]
        first = pl.multiple_of(at_ref[1 + i], size)
        out_ref[0, :, pl.ds(first, size)] = dot(rows, weight_ref[...], NT).astype(bf16)


def final_sum_kernel(own_ref, *rest):
    *part_refs, out_ref = rest
    total = own_ref[...]
    for part_ref in part_refs:
        total = total + part_ref[...].astype(f32)
    out_ref[...] = total


VMEM = pl.BlockSpec(memory_space=pltpu.VMEM)
SMEM = pl.BlockSpec(memory_space=pltpu.SMEM)
FAR = pl.BlockSpec(memory_space=pltpu.HBM)
ANYWHERE = pl.BlockSpec(memory_space=pl.ANY)


def call(
    body,
    outs,
    *operands,
    scalars=(),
    after=(),
    after_far=(),
    scratch=(),
    far_in=(),
    far_out=False,
    copies=(),
    limit=VMEM_LIMIT,
):
    at = [jnp.stack([jnp.int32(s) for s in scalars])] if scalars else []
    count = len(at) + len(operands)

    def kernel(*refs):
        ins, rest = refs[:count], refs[count + len(after) + len(after_far) :]
        body(*ins, *rest[: len(outs)], *rest[len(outs) + 1 :])
        rest[len(outs)][...] = jnp.zeros((8, 128), f32)

    *results, token = pl.pallas_call(
        kernel,
        out_shape=[jax.ShapeDtypeStruct(shape, kind) for shape, kind in [*outs, ((8, 128), f32)]],
        in_specs=[SMEM] * len(at)
        + [FAR if i in far_in else VMEM for i in range(len(operands))]
        + [ANYWHERE] * len(after)
        + [FAR] * len(after_far),
        out_specs=[FAR if far_out else VMEM] * len(outs) + [VMEM],
        scratch_shapes=[*scratch] + [pltpu.SemaphoreType.DMA((n,)) for n in copies],
        compiler_params=pltpu.CompilerParams(vmem_limit_bytes=limit),
        cost_estimate=pl.CostEstimate(flops=0, bytes_accessed=0, transcendentals=0),
    )(*at, *operands, *after, *after_far)
    return results, token


def local(dp_size, ctx_size, tokens, proj_weight, values, grad_out):
    group = min(GROUP, ctx_size, H)
    runs = ctx_size // group
    heads = H // group
    tok, width = tokens.shape[1:]
    length = group * tok
    cols = proj_weight.shape[1]
    share = width // dp_size
    depth = share // ctx_size
    with_state = runs > 1
    groups = [[run * group + i for i in range(group)] for run in range(runs)]
    wide_groups = [
        [dp * ctx_size + i for dp in range(dp_size) for i in members] for members in groups
    ]
    dp_at, ctx_at = lax.axis_index("dp"), lax.axis_index("ctx")
    run_at, member = ctx_at // group, ctx_at % group

    def exchange(x):
        return lax.all_to_all(
            x, "ctx", split_axis=0, concat_axis=0, tiled=True, axis_index_groups=groups
        )

    def to_dp(x, shift):
        return lax.ppermute(x, "dp", [(i, (i + shift) % dp_size) for i in range(dp_size)])

    def to_member(x, shift):
        pairs = [(i, i - i % group + (i + shift) % group) for i in range(ctx_size)]
        return lax.ppermute(x, "ctx", pairs)

    def to_members(parts):
        return [part if not shift else to_member(part, shift) for shift, part in enumerate(parts)]

    def to_run(x, shift, wrap):
        pairs = [
            (i, (i + shift * group) % ctx_size)
            for i in range(ctx_size)
            if wrap or 0 <= i + shift * group < ctx_size
        ]
        return lax.ppermute(x, "ctx", pairs)

    qk_shape = ((group, 2, heads, F, tok), f32)
    state_shape = ((heads, PSI, DH), bf16)
    blocks_shape = ((2, tok, heads * DH), bf16)
    rows_shape = ((length, heads * DH), f32)

    parts, token = call(
        token_parts_kernel,
        [((tok, share), bf16)] * (dp_size - 1),
        tokens,
        scalars=(dp_at,),
        far_in=(0,),
        far_out=True,
        scratch=[pltpu.VMEM((dp_size - 1, tok, share), bf16)],
        copies=(2 * dp_size - 2,),
        limit=VMEM_MOST,
    )
    arrived = [to_dp(part, shift) for shift, part in enumerate(parts, 1)]
    parts, token = call(
        pack_heads_kernel,
        [((2, tok, heads * DH), bf16)] * group,
        values,
        grad_out,
        scalars=(member,),
        after=(token,),
        far_in=(0, 1),
        far_out=True,
        scratch=[pltpu.VMEM((2 * group, tok, heads * DH), bf16)],
        copies=(4 * group,),
        limit=VMEM_MOST,
    )
    parts = to_members(parts)
    (vg,), vg_token = call(
        collect_heads_kernel,
        [((group, 2, tok, heads * DH), bf16)],
        *parts,
        scalars=(member,),
    )
    (projected, weight), token = call(
        project_kernel,
        [qk_shape, (proj_weight.shape, bf16)],
        tokens,
        proj_weight,
        scalars=(dp_at,),
        after=(token,),
        far_in=(0,),
        copies=(1,),
        scratch=[pltpu.VMEM((tok, share), bf16)],
    )
    part_shape = (tok, dp_size * runs * depth)
    if depth % 128 == 0:
        parts, token = call(
            functools.partial(pack_tokens_kernel, depth),
            [(part_shape, bf16)] * group,
            tokens,
            scalars=(member,),
            after=(token,),
            far_in=(0,),
            far_out=True,
            copies=(group * dp_size * runs,),
        )
    else:
        blocks = tokens[0].reshape(tok, dp_size * runs, group, depth).transpose(2, 0, 1, 3)
        parts = [
            lax.dynamic_index_in_dim(blocks, (member + shift) % group, 0, keepdims=False).reshape(
                part_shape
            )
            for shift in range(group)
        ]
    token_parts = to_members(parts)

    (projected,), token = call(
        project_rest_kernel,
        [((dp_size,) + qk_shape[0], f32)],
        projected,
        weight,
        *arrived,
        scalars=(dp_at,),
        after=(vg_token, token),
    )
    qk_parts = lax.all_to_all(
        projected.reshape((dp_size * group,) + qk_shape[0][1:]),
        ("dp", "ctx"),
        split_axis=0,
        concat_axis=0,
        tiled=True,
        axis_index_groups=wide_groups,
    ).reshape(projected.shape)

    pair = 2 if ctx_size % 2 == 0 else 1
    parity = ctx_at % pair
    piece = share // pair
    (mine,), token = call(
        weight_piece_kernel,
        [((piece, cols), bf16)],
        proj_weight,
        scalars=(parity,),
        after=(token,),
        far_in=(0,),
        far_out=True,
        copies=(1,),
    )
    fetched = [to_dp(mine, shift) for shift in range(1, dp_size)]
    weights, firsts = [proj_weight], [dp_at * share]
    for shift, half in enumerate(fetched, 1):
        base = (dp_at + dp_size - shift) % dp_size * share
        weights.append(half)
        firsts.append(base + parity * piece)
        if pair == 2:
            weights.append(lax.ppermute(half, "ctx", [(i, i ^ 1) for i in range(ctx_size)]))
            firsts.append(base + (1 - parity) * piece)

    (qk, *state), token = call(
        functools.partial(state_kernel, with_state),
        [qk_shape] + [state_shape] * with_state,
        qk_parts,
        vg,
    )
    prefix, suffix = (), ()
    if with_state:
        prefix = [to_run(state[0], shift, False) for shift in range(1, runs)]
    (numerator,), token = call(numerator_kernel, [rows_shape], qk, vg)
    (attended, grad_num, *carried), token = call(
        functools.partial(normalize_kernel, with_state),
        [((length, heads * DH), bf16), rows_shape] + [state_shape] * with_state,
        qk,
        vg,
        numerator,
        *prefix,
    )
    if with_state:
        suffix = [to_run(carried[0], -shift, False) for shift in range(1, runs)]
    (grad_qk, grad_v), token = call(
        functools.partial(backward_kernel, with_state),
        [((2, heads, F, length), f32), ((heads, DH, length), f32)],
        qk,
        vg,
        grad_num,
        *prefix,
        after_far=[*fetched, *token_parts[1:]],
    )
    (rows,), token = call(
        functools.partial(rows_kernel, with_state),
        [((2 * heads * F, length), bf16)],
        qk,
        vg,
        grad_qk,
        *suffix,
        far_out=True,
        scratch=[pltpu.VMEM((2 * heads * F, length), bf16)],
        copies=(1,),
    )
    rows = [rows] + [to_member(rows, shift) for shift in range(1, group)]
    (token_cols,), tokens_token = call(
        collect_tokens_kernel,
        [(part_shape[1:] + (length,), bf16)],
        *token_parts,
        scalars=(member,),
        after=(token,),
    )
    results, token = call(
        functools.partial(grad_values_kernel, with_state, group),
        [blocks_shape] * group,
        qk,
        attended,
        grad_v,
        *suffix,
        scalars=(member,),
        after=(token,),
        scratch=[pltpu.VMEM((length, heads * DH), bf16)],
    )
    results = to_members(results)

    held = pltpu.VMEM((cols, length), bf16)
    (own, *parts), token = call(
        functools.partial(product_kernel, group),
        [((runs * depth, cols), f32)] + [((runs * depth, cols), bf16)] * (dp_size - 1),
        *rows,
        token_cols,
        scalars=(dp_at, member),
        after=(token,),
        scratch=[pltpu.VMEM((dp_size * runs * depth, cols), f32), held],
    )
    parts = [to_dp(part, shift) for shift, part in enumerate(parts, 1)]
    (grad_proj, *parts), token = call(
        functools.partial(run_sum_kernel, len(parts)),
        [((depth, cols), f32)] + [((depth, cols), bf16)] * (runs - 1),
        own,
        *parts,
        scalars=(run_at,),
        after_far=results[1 : 1 + group // 2],
        scratch=[pltpu.VMEM((runs * depth, cols), f32)],
    )
    (grad_tokens,), tokens_token = call(
        functools.partial(grad_tokens_kernel, group),
        [((1, tok, width), bf16)],
        *rows,
        *weights,
        scalars=(member, *firsts),
        after=(token,),
        scratch=[pltpu.VMEM((cols, tok), bf16)],
    )
    (attended, grad_values), token = call(
        unpack_heads_kernel,
        [((1, tok, H * DH), bf16)] * 2,
        *results,
        scalars=(member,),
        after=(token,),
    )
    (grad_proj,), _ = call(
        final_sum_kernel,
        [((depth, cols), f32)],
        grad_proj,
        *[to_run(part, shift, True) for shift, part in enumerate(parts, 1)],
        after=(tokens_token, token),
    )
    return (attended, grad_tokens, grad_values, grad_proj)


def solution(mesh):
    return jax.shard_map(
        functools.partial(local, mesh.shape["dp"], mesh.shape["ctx"]),
        mesh=mesh,
        in_specs=(P("dp", "ctx", None), P("dp", None), P("dp", "ctx", None), P("dp", "ctx", None)),
        out_specs=(
            P("dp", "ctx", None),
            P("dp", "ctx", None),
            P("dp", "ctx", None),
            P(("dp", "ctx"), None),
        ),
        check_vma=False,
    )
```

```python
import functools

import jax
import jax.numpy as jnp
from jax import lax
from jax.experimental import pallas as pl
from jax.experimental.pallas import tpu as pltpu
from jax.sharding import PartitionSpec as P

H = 16
F = 16
DH = 128
EPSILON = 1e-05
GROUP = 8
TILE = 256
VMEM_LIMIT = 16 * 1024 * 1024
PSI = 9 * F + 2 * F
PSI_SCALE = (0.5,) + (1.0,) * 7 + (0.5,)

f32 = jnp.float32
bf16 = jnp.bfloat16

NN = (((1,), (0,)), ((), ()))
NT = (((1,), (1,)), ((), ()))


def dot(a, b, dims=NN):
    return lax.dot_general(a, b, dims, preferred_element_type=f32)


def split(x):
    high = x.astype(bf16)
    return high, (x - high.astype(f32)).astype(bf16)


def dot3(a, b, dims=NN):
    a_high, a_low = split(a)
    b_high, b_low = split(b)
    return dot(a_high, b_high, dims) + (dot(a_high, b_low, dims) + dot(a_low, b_high, dims))


def turned(x, r):
    return x if r == 0 else jnp.concatenate([x[r:], x[:r]], axis=0)


def psi(x, weights):
    parts = []
    for r in range(9):
        part = x * turned(x, r)
        parts.append(part * PSI_SCALE[r] if weights and PSI_SCALE[r] != 1.0 else part)
    row = lax.broadcasted_iota(jnp.int32, x.shape, 0)
    return jnp.concatenate(parts + [x, jnp.where(row == 0, 1.0, 0.0)], axis=0)


def pull_psi(x, upstream, weights):
    total = upstream[9 * F : 10 * F]
    for r in range(9):
        part = upstream[r * F : (r + 1) * F]
        if weights and PSI_SCALE[r] != 1.0:
            part = part * PSI_SCALE[r]
        total = total + part * turned(x, r) + turned(part * x, (F - r) % F)
    return total


def feature_major(qk_ref, which, head):
    return jnp.concatenate([qk_ref[src, which, head] for src in range(qk_ref.shape[0])], axis=1)


def rows_of(ref, which, head, start, stop):
    tok = ref.shape[2]
    return jnp.concatenate(
        [
            ref[src, which, :, head * DH : (head + 1) * DH]
            for src in range(start // tok, stop // tok)
        ],
        axis=0,
    )


def score_sides(q, k):
    q_high, q_low = split(q)
    k_high, k_low = split(k)
    left = jnp.concatenate([q_high, q_high, q_low, q_low], axis=0)
    right = jnp.concatenate([k_high, k_low, k_high, k_low], axis=0)
    return left.T, right


def causal_mask(tile, width):
    row = lax.broadcasted_iota(jnp.int32, (tile, width), 0) + (width - tile)
    return row >= lax.broadcasted_iota(jnp.int32, (tile, width), 1)


def run_copies(sems, pairs):
    copies = [
        pltpu.make_async_copy(source, target, sems.at[i])
        for i, (source, target) in enumerate(pairs)
    ]
    for copy in copies:
        copy.start()
    for copy in copies:
        copy.wait()


def aligned(at, size):
    return pl.ds(pl.multiple_of(at * size, size), size)


def token_parts_kernel(at_ref, tokens_ref, *rest):
    *out_refs, sems = rest
    count, share = len(out_refs) + 1, out_refs[0].shape[1]
    run_copies(
        sems,
        [
            (tokens_ref.at[0, :, aligned(lax.rem(at_ref[0] + shift, count), share)], out_ref)
            for shift, out_ref in enumerate(out_refs, 1)
        ],
    )


def pack_heads_kernel(at_ref, values_ref, grad_ref, *out_refs):
    width = out_refs[0].shape[2]
    for shift, out_ref in enumerate(out_refs):
        cols = aligned(lax.rem(at_ref[0] + shift, len(out_refs)), width)
        out_ref[0] = values_ref[0, :, cols]
        out_ref[1] = grad_ref[0, :, cols]


def collect_heads_kernel(at_ref, *rest):
    *part_refs, out_ref = rest
    group = len(part_refs)
    for shift, part_ref in enumerate(part_refs):
        out_ref[lax.rem(at_ref[0] + group - shift, group)] = part_ref[...]


def collect_tokens_kernel(in_ref, out_ref):
    group, tok = in_ref.shape[:2]
    for src in range(group):
        out_ref[:, src * tok : (src + 1) * tok] = in_ref[src].T


def write_blocks(projected, out_ref):
    group, _, heads, feat, _ = out_ref.shape
    for member in range(group):
        for which in range(2):
            for head in range(heads):
                first = ((which * group + member) * heads + head) * feat
                out_ref[member, which, head] = projected[first : first + feat]


def project_kernel(at_ref, tokens_ref, weight_ref, out_ref, part_ref, sem):
    share = part_ref.shape[1]
    run_copies(sem, [(tokens_ref.at[0, :, aligned(at_ref[0], share)], part_ref)])
    write_blocks(dot(part_ref[...], weight_ref[...]).T, out_ref)


def project_rest_kernel(at_ref, own_ref, weight_ref, *rest):
    *part_refs, out_ref = rest
    count = len(part_refs) + 1
    at = at_ref[0]
    out_ref[at] = own_ref[...]
    for shift, part_ref in enumerate(part_refs, 1):
        owner = lax.rem(at + count - shift, count)
        write_blocks(dot(part_ref[...], weight_ref[...]).T, out_ref.at[owner])


def weight_piece_kernel(at_ref, weight_ref, out_ref, sems):
    run_copies(sems, [(weight_ref.at[aligned(at_ref[0], out_ref.shape[0])], out_ref)])


def state_sum(refs, head):
    total = refs[0][head].astype(f32)
    for ref in refs[1:]:
        total = total + ref[head].astype(f32)
    return total


def state_kernel(with_state, parts_ref, vg_ref, qk_ref, *state_refs):
    count, blocks, _, heads, _, tok = parts_ref.shape
    for head in range(heads):
        for which in range(2):
            for src in range(blocks):
                total = parts_ref[0, src, which, head]
                for part in range(1, count):
                    total = total + parts_ref[part, src, which, head]
                qk_ref[src, which, head] = total
        if with_state:
            high, low = split(psi(feature_major(qk_ref, 1, head), False))
            v = rows_of(vg_ref, 0, head, 0, blocks * tok)
            state_refs[0][head] = (dot(high, v) + dot(low, v)).astype(bf16)


def numerator_kernel(depth, qk_ref, vg_ref, *rest):
    if depth:
        tokens_ref, num_ref, out_ref, sems = rest
        group = out_ref.shape[0]
        copies = [
            pltpu.make_async_copy(
                tokens_ref.at[0, :, (part * group + i) * depth : (part * group + i + 1) * depth],
                out_ref.at[i, :, part * depth : (part + 1) * depth],
                sems.at[part * group + i],
            )
            for i in range(group)
            for part in range(out_ref.shape[2] // depth)
        ]
    else:
        (num_ref,), copies = rest, []
    for copy in copies:
        copy.start()
    heads = qk_ref.shape[2]
    length = qk_ref.shape[0] * qk_ref.shape[4]
    tile = min(TILE, length)
    for head in range(heads):
        q = feature_major(qk_ref, 0, head) * 0.25
        k = feature_major(qk_ref, 1, head)
        left, right = score_sides(q, k)
        for at in range(0, length, tile):
            width = at + tile
            scores = dot(left[at:width], right[:, :width])
            kernel = jnp.where(
                causal_mask(tile, width), 1.0 + scores * (1.0 + 0.5 * scores), 0.0
            )
            high, low = split(kernel)
            v = rows_of(vg_ref, 0, head, 0, width)
            num_ref[at:width, head * DH : (head + 1) * DH] = dot(high, v) + dot(low, v)
    for copy in copies:
        copy.wait()


def normalize_kernel(with_state, qk_ref, vg_ref, num_ref, *rest):
    if with_state:
        *prefix_refs, attended_ref, grad_ref, carried_ref = rest
    else:
        attended_ref, grad_ref = rest
    heads = qk_ref.shape[2]
    blocks, tok = qk_ref.shape[0], qk_ref.shape[4]
    length = blocks * tok
    for head in range(heads):
        cols = slice(head * DH, (head + 1) * DH)
        numerator = num_ref[:, cols]
        if with_state:
            feat = psi(feature_major(qk_ref, 0, head) * 0.25, True)
            numerator = numerator + dot3(feat.T, state_sum(prefix_refs, head))
        inv_rms = lax.rsqrt(jnp.mean(numerator * numerator, axis=-1, keepdims=True) + EPSILON)
        normed = numerator * inv_rms
        upstream = rows_of(vg_ref, 1, head, 0, length).astype(f32)
        grad = inv_rms * (
            upstream - normed * jnp.mean(normed * upstream, axis=-1, keepdims=True)
        )
        attended_ref[:, cols] = normed.astype(bf16)
        grad_ref[:, cols] = grad
        if with_state:
            carried_ref[head] = dot3(feat, grad).astype(bf16)


def backward_kernel(with_state, qk_ref, vg_ref, grad_ref, *rest):
    *prefix_refs, grad_qk_ref, grad_v_ref = rest
    length = qk_ref.shape[0] * qk_ref.shape[4]
    tile = min(TILE, length)
    for head in range(grad_v_ref.shape[0]):
        cols = slice(head * DH, (head + 1) * DH)
        q = feature_major(qk_ref, 0, head) * 0.25
        k = feature_major(qk_ref, 1, head)
        left, right = score_sides(q, k)
        q_both = jnp.concatenate(split(q), axis=0)
        k_both = jnp.concatenate(split(k), axis=0)
        grad = grad_ref[:, cols]
        grad_t = grad.T
        if with_state:
            grad_q = pull_psi(q, dot3(state_sum(prefix_refs, head), grad_t), True)
        for at in reversed(range(0, length, tile)):
            width = at + tile
            scores = dot(left[at:width], right[:, :width])
            causal = causal_mask(tile, width)
            v = rows_of(vg_ref, 0, head, 0, width)
            high, low = split(grad[at:width])
            mixing = dot(
                jnp.concatenate([high, low], axis=1), jnp.concatenate([v, v], axis=1), NT
            )
            more = 1.0 + scores
            slopes = split(jnp.where(causal, mixing * more, 0.0))
            kernels = split(jnp.where(causal, more + 0.5 * scores * scores, 0.0))
            both = dot(k_both[:, :width], slopes[0], NT)
            piece = both[:F] + (both[F:] + dot(k_both[:F, :width], slopes[1], NT))
            if with_state:
                piece = piece + grad_q[:, at:width]
            grad_qk_ref[0, head, :, at:width] = piece * 0.25
            both = dot(q_both[:, at:width], slopes[0])
            piece_k = both[:F] + (both[F:] + dot(q_both[:F, at:width], slopes[1]))
            high, low = split(grad_t[:, at:width])
            both = dot(jnp.concatenate([high, low], axis=0), kernels[0])
            piece_v = both[:DH] + (both[DH:] + dot(high, kernels[1]))
            if width == length:
                grad_qk_ref[1, head] = piece_k
                grad_v_ref[head] = piece_v
            else:
                grad_qk_ref[1, head, :, :width] += piece_k
                grad_v_ref[head, :, :width] += piece_v


def rows_kernel(with_state, qk_ref, vg_ref, grad_qk_ref, *rest):
    *suffix_refs, out_ref, held_ref, sems = rest
    heads = qk_ref.shape[2]
    length = qk_ref.shape[0] * qk_ref.shape[4]
    for head in range(heads):
        grad_k = grad_qk_ref[1, head]
        if with_state:
            k = feature_major(qk_ref, 1, head)
            v = rows_of(vg_ref, 0, head, 0, length)
            high, low = split(state_sum(suffix_refs, head))
            grad_k = grad_k + pull_psi(k, dot(high, v, NT) + dot(low, v, NT), False)
        held_ref[head * F : (head + 1) * F] = grad_qk_ref[0, head].astype(bf16)
        held_ref[(heads + head) * F : (heads + head + 1) * F] = grad_k.astype(bf16)
    run_copies(sems, [(held_ref, out_ref)])


def grad_values_kernel(with_state, at_ref, qk_ref, attended_ref, grad_v_ref, *rest):
    *suffix_refs, keep_ref, send_ref, held_ref = rest
    heads, tok = qk_ref.shape[2], qk_ref.shape[4]
    for head in range(heads):
        grad_v = grad_v_ref[head]
        if with_state:
            feat = psi(feature_major(qk_ref, 1, head), False)
            grad_v = grad_v + dot3(state_sum(suffix_refs, head).T, feat)
        held_ref[:, head * DH : (head + 1) * DH] = grad_v.T.astype(bf16)
    chips = keep_ref.shape[0]
    for shift in range(chips):
        chip = lax.rem(at_ref[0] + shift, chips)
        for core, out_ref in ((at_ref[1], keep_ref), (1 - at_ref[1], send_ref)):
            rows = aligned(2 * chip + core, tok)
            out_ref[shift, 0] = attended_ref[rows, :]
            out_ref[shift, 1] = held_ref[rows, :]


def pair_kernel(at_ref, keep_ref, got_ref, *out_refs):
    for shift, out_ref in enumerate(out_refs):
        out_ref[at_ref[1]] = keep_ref[shift]
        out_ref[1 - at_ref[1]] = got_ref[shift]


def unpack_heads_kernel(at_ref, *rest):
    *part_refs, attended_ref, values_ref = rest
    chips, width = len(part_refs), part_refs[0].shape[3]
    for shift, part_ref in enumerate(part_refs):
        chip = lax.rem(at_ref[0] + chips - shift, chips)
        for core in range(2):
            cols = aligned(2 * chip + core, width)
            attended_ref[0, :, cols] = part_ref[core, 0]
            values_ref[0, :, cols] = part_ref[core, 1]


def place_rows(chip_at, core_at, part_refs, cols, held_ref):
    chips, half = len(part_refs) // 2, part_refs[0].shape[0] // 2
    for shift in range(chips):
        chip = lax.rem(chip_at + chips - shift, chips)
        for side, core in ((0, core_at), (1, 1 - core_at)):
            part_ref = part_refs[2 * shift + side]
            for which in range(2):
                rows = aligned(which * 2 * chips + 2 * chip + core, half)
                held_ref[rows, :] = part_ref[which * half : (which + 1) * half, cols]


def product_kernel(group, at_ref, *rest):
    rows_refs, rest = rest[:group], rest[group:]
    tokens_ref, *part_refs, total_ref, held_ref = rest
    place_rows(at_ref[1], at_ref[2], rows_refs, slice(None), held_ref)
    total_ref[...] = dot(tokens_ref[...], held_ref[...], NT)
    count = len(part_refs)
    size = part_refs[0].shape[0]
    for shift, part_ref in enumerate(part_refs):
        owner = lax.rem(at_ref[0] + shift, count)
        part = total_ref[pl.ds(pl.multiple_of(owner * size, size), size), :]
        part_ref[...] = part.astype(part_ref.dtype)


def run_sum_kernel(arrived, at_ref, *rest):
    own_ref, *rest = rest
    total_ref = rest[-1]
    total = own_ref[...]
    for ref in rest[:arrived]:
        total = total + ref[...].astype(f32)
    total_ref[...] = total
    part_refs = rest[arrived:-1]
    size = part_refs[0].shape[0]
    for shift, part_ref in enumerate(part_refs):
        owner = lax.rem(at_ref[0] + shift, len(part_refs))
        part = total_ref[pl.ds(pl.multiple_of(owner * size, size), size), :]
        part_ref[...] = part.astype(part_ref.dtype)


def grad_tokens_kernel(group, at_ref, *rest):
    rows_refs, rest = rest[:group], rest[group:]
    *weight_refs, out_ref, held_ref = rest
    member = 2 * at_ref[0] + at_ref[1]
    place_rows(at_ref[0], at_ref[1], rows_refs, aligned(member, out_ref.shape[1]), held_ref)
    rows = held_ref[...].T
    for i, weight_ref in enumerate(weight_refs):
        size = weight_ref.shape[0]
        first = pl.multiple_of(at_ref[2 + i], size)
        out_ref[0, :, pl.ds(first, size)] = dot(rows, weight_ref[...], NT).astype(bf16)


def final_sum_kernel(own_ref, *rest):
    *part_refs, out_ref = rest
    total = own_ref[...]
    for part_ref in part_refs:
        total = total + part_ref[...].astype(f32)
    out_ref[...] = total


VMEM = pl.BlockSpec(memory_space=pltpu.VMEM)
SMEM = pl.BlockSpec(memory_space=pltpu.SMEM)
FAR = pl.BlockSpec(memory_space=pltpu.HBM)
ANYWHERE = pl.BlockSpec(memory_space=pl.ANY)


def call(
    body,
    outs,
    *operands,
    scalars=(),
    after=(),
    after_far=(),
    scratch=(),
    far_in=(),
    far_out=False,
    copies=(),
):
    at = [jnp.stack([jnp.int32(s) for s in scalars])] if scalars else []
    count = len(at) + len(operands)

    def kernel(*refs):
        ins, rest = refs[:count], refs[count + len(after) + len(after_far) :]
        body(*ins, *rest[: len(outs)], *rest[len(outs) + 1 :])
        rest[len(outs)][...] = jnp.zeros((8, 128), f32)

    *results, token = pl.pallas_call(
        kernel,
        out_shape=[jax.ShapeDtypeStruct(shape, kind) for shape, kind in [*outs, ((8, 128), f32)]],
        in_specs=[SMEM] * len(at)
        + [FAR if i in far_in else VMEM for i in range(len(operands))]
        + [ANYWHERE] * len(after)
        + [FAR] * len(after_far),
        out_specs=[FAR if far_out else VMEM] * len(outs) + [VMEM],
        scratch_shapes=[*scratch] + [pltpu.SemaphoreType.DMA((n,)) for n in copies],
        compiler_params=pltpu.CompilerParams(vmem_limit_bytes=VMEM_LIMIT),
        cost_estimate=pl.CostEstimate(flops=0, bytes_accessed=0, transcendentals=0),
    )(*at, *operands, *after, *after_far)
    return results, token


def local(dp_size, ctx_size, tokens, proj_weight, values, grad_out):
    group = min(GROUP, ctx_size, H)
    runs = ctx_size // group
    heads = H // group
    tok, width = tokens.shape[1:]
    length = group * tok
    cols = proj_weight.shape[1]
    share = width // dp_size
    depth = share // ctx_size
    with_state = runs > 1
    groups = [[run * group + i for i in range(group)] for run in range(runs)]
    wide_groups = [
        [dp * ctx_size + i for dp in range(dp_size) for i in members] for members in groups
    ]
    dp_at, ctx_at = lax.axis_index("dp"), lax.axis_index("ctx")
    run_at, member = ctx_at // group, ctx_at % group

    def exchange(x):
        return lax.all_to_all(
            x, "ctx", split_axis=0, concat_axis=0, tiled=True, axis_index_groups=groups
        )

    def to_dp(x, shift):
        return lax.ppermute(x, "dp", [(i, (i + shift) % dp_size) for i in range(dp_size)])

    def to_member(x, shift):
        pairs = [(i, i - i % group + (i + shift) % group) for i in range(ctx_size)]
        return lax.ppermute(x, "ctx", pairs)

    def to_members(parts):
        return [part if not shift else to_member(part, shift) for shift, part in enumerate(parts)]

    def to_run(x, shift, wrap):
        pairs = [
            (i, (i + shift * group) % ctx_size)
            for i in range(ctx_size)
            if wrap or 0 <= i + shift * group < ctx_size
        ]
        return lax.ppermute(x, "ctx", pairs)

    qk_shape = ((group, 2, heads, F, tok), f32)
    state_shape = ((heads, PSI, DH), bf16)
    blocks_shape = ((2, tok, heads * DH), bf16)
    rows_shape = ((length, heads * DH), f32)

    parts, token = call(
        token_parts_kernel,
        [((tok, share), bf16)] * (dp_size - 1),
        tokens,
        scalars=(dp_at,),
        far_in=(0,),
        far_out=True,
        copies=(dp_size - 1,),
    )
    arrived = [to_dp(part, shift) for shift, part in enumerate(parts, 1)]
    parts, token = call(
        pack_heads_kernel,
        [((2, tok, heads * DH), bf16)] * group,
        values,
        grad_out,
        scalars=(member,),
        after=(token,),
    )
    parts = to_members(parts)
    (vg,), vg_token = call(
        collect_heads_kernel,
        [((group, 2, tok, heads * DH), bf16)],
        *parts,
        scalars=(member,),
    )
    (projected,), token = call(
        project_kernel,
        [qk_shape],
        tokens,
        proj_weight,
        scalars=(dp_at,),
        after=(token,),
        far_in=(0,),
        copies=(1,),
        scratch=[pltpu.VMEM((tok, share), bf16)],
    )
    (projected,), token = call(
        project_rest_kernel,
        [((dp_size,) + qk_shape[0], f32)],
        projected,
        proj_weight,
        *arrived,
        scalars=(dp_at,),
        after=(vg_token, token),
    )
    qk_parts = lax.all_to_all(
        projected.reshape((dp_size * group,) + qk_shape[0][1:]),
        ("dp", "ctx"),
        split_axis=0,
        concat_axis=0,
        tiled=True,
        axis_index_groups=wide_groups,
    ).reshape(projected.shape)

    pair = 2 if ctx_size % 2 == 0 else 1
    parity = ctx_at % pair
    piece = share // pair
    (mine,), token = call(
        weight_piece_kernel,
        [((piece, cols), bf16)],
        proj_weight,
        scalars=(parity,),
        after=(token,),
        far_in=(0,),
        far_out=True,
        copies=(1,),
    )
    fetched = [to_dp(mine, shift) for shift in range(1, dp_size)]
    weights, firsts = [proj_weight], [dp_at * share]
    for shift, half in enumerate(fetched, 1):
        base = (dp_at + dp_size - shift) % dp_size * share
        weights.append(half)
        firsts.append(base + parity * piece)
        if pair == 2:
            weights.append(lax.ppermute(half, "ctx", [(i, i ^ 1) for i in range(ctx_size)]))
            firsts.append(base + (1 - parity) * piece)

    (qk, *state), token = call(
        functools.partial(state_kernel, with_state),
        [qk_shape] + [state_shape] * with_state,
        qk_parts,
        vg,
    )
    prefix, suffix = (), ()
    if with_state:
        prefix = [to_run(state[0], shift, False) for shift in range(1, runs)]
    cols_shape = (group, tok, dp_size * runs * depth)
    if depth % 128 == 0:
        (numerator, token_cols), token = call(
            functools.partial(numerator_kernel, depth),
            [rows_shape, (cols_shape, bf16)],
            qk,
            vg,
            tokens,
            copies=(group * dp_size * runs,),
        )
    else:
        (numerator,), token = call(
            functools.partial(numerator_kernel, 0), [rows_shape], qk, vg
        )
        token_cols = tokens[0].reshape(tok, dp_size * runs, group, depth)
        token_cols = token_cols.transpose(2, 0, 1, 3).reshape(cols_shape)
    token_cols = exchange(token_cols)
    (attended, grad_num, *carried), token = call(
        functools.partial(normalize_kernel, with_state),
        [((length, heads * DH), bf16), rows_shape] + [state_shape] * with_state,
        qk,
        vg,
        numerator,
        *prefix,
    )
    if with_state:
        suffix = [to_run(carried[0], -shift, False) for shift in range(1, runs)]
    (grad_qk, grad_v), token = call(
        functools.partial(backward_kernel, with_state),
        [((2, heads, F, length), f32), ((heads, DH, length), f32)],
        qk,
        vg,
        grad_num,
        *prefix,
        after_far=fetched,
    )
    (rows,), token = call(
        functools.partial(rows_kernel, with_state),
        [((2 * heads * F, length), bf16)],
        qk,
        vg,
        grad_qk,
        *suffix,
        far_out=True,
        scratch=[pltpu.VMEM((2 * heads * F, length), bf16)],
        copies=(1,),
    )
    chips = group // 2
    chip_at = member // 2

    def to_chip(x, shift):
        return x if shift == 0 else to_member(x, 2 * shift)

    def to_other_core(x):
        return lax.ppermute(x, "ctx", [(i, i ^ 1) for i in range(ctx_size)])

    rows = [to_chip(rows, shift) for shift in range(chips)]
    rows = [side for part in rows for side in (part, to_other_core(part))]
    (token_cols,), tokens_token = call(
        collect_tokens_kernel,
        [((cols_shape[2], length), bf16)],
        token_cols,
        after=(token,),
    )
    (keep, send), token = call(
        functools.partial(grad_values_kernel, with_state),
        [((chips, 2, tok, heads * DH), bf16)] * 2,
        qk,
        attended,
        grad_v,
        *suffix,
        scalars=(chip_at, ctx_at % 2),
        after=(token,),
        scratch=[pltpu.VMEM((length, heads * DH), bf16)],
    )
    results, token = call(
        pair_kernel,
        [((2, 2, tok, heads * DH), bf16)] * chips,
        keep,
        to_other_core(send),
        scalars=(chip_at, ctx_at % 2),
    )
    results = [to_chip(part, shift) for shift, part in enumerate(results)]

    held = pltpu.VMEM((cols, length), bf16)
    (own, *parts), token = call(
        functools.partial(product_kernel, 2 * chips),
        [((runs * depth, cols), f32)] + [((runs * depth, cols), bf16)] * (dp_size - 1),
        *rows,
        token_cols,
        scalars=(dp_at, chip_at, ctx_at % 2),
        after=(token,),
        scratch=[pltpu.VMEM((dp_size * runs * depth, cols), f32), held],
    )
    parts = [to_dp(part, shift) for shift, part in enumerate(parts, 1)]
    (grad_tokens,), tokens_token = call(
        functools.partial(grad_tokens_kernel, 2 * chips),
        [((1, tok, width), bf16)],
        *rows,
        *weights,
        scalars=(chip_at, ctx_at % 2, *firsts),
        after=(token,),
        scratch=[pltpu.VMEM((cols, tok), bf16)],
    )
    (grad_proj, *parts), token = call(
        functools.partial(run_sum_kernel, len(parts)),
        [((depth, cols), f32)] + [((depth, cols), bf16)] * (runs - 1),
        own,
        *parts,
        scalars=(run_at,),
        after=(tokens_token,),
        scratch=[pltpu.VMEM((runs * depth, cols), f32)],
    )
    (attended, grad_values), token = call(
        unpack_heads_kernel,
        [((1, tok, H * DH), bf16)] * 2,
        *results,
        scalars=(chip_at,),
        after=(token,),
    )
    (grad_proj,), _ = call(
        final_sum_kernel,
        [((depth, cols), f32)],
        grad_proj,
        *[to_run(part, shift, True) for shift, part in enumerate(parts, 1)],
        after=(token,),
    )
    return (attended, grad_tokens, grad_values, grad_proj)


def solution(mesh):
    return jax.shard_map(
        functools.partial(local, mesh.shape["dp"], mesh.shape["ctx"]),
        mesh=mesh,
        in_specs=(P("dp", "ctx", None), P("dp", None), P("dp", "ctx", None), P("dp", "ctx", None)),
        out_specs=(
            P("dp", "ctx", None),
            P("dp", "ctx", None),
            P("dp", "ctx", None),
            P(("dp", "ctx"), None),
        ),
        check_vma=False,
    )
```

```python
import functools

import jax
import jax.numpy as jnp
from jax import lax
from jax.experimental import pallas as pl
from jax.experimental.pallas import tpu as pltpu
from jax.sharding import PartitionSpec as P

H = 16
F = 16
DH = 128
EPSILON = 1e-05
GROUP = 8
TILE = 256
VMEM_LIMIT = 16 * 1024 * 1024
PSI = 9 * F + 2 * F
PSI_SCALE = (0.5,) + (1.0,) * 7 + (0.5,)

f32 = jnp.float32
bf16 = jnp.bfloat16

NN = (((1,), (0,)), ((), ()))
NT = (((1,), (1,)), ((), ()))


def dot(a, b, dims=NN):
    return lax.dot_general(a, b, dims, preferred_element_type=f32)


def split(x):
    high = x.astype(bf16)
    return high, (x - high.astype(f32)).astype(bf16)


def dot3(a, b, dims=NN):
    a_high, a_low = split(a)
    b_high, b_low = split(b)
    return dot(a_high, b_high, dims) + (dot(a_high, b_low, dims) + dot(a_low, b_high, dims))


def turned(x, r):
    return x if r == 0 else jnp.concatenate([x[r:], x[:r]], axis=0)


def psi(x, weights):
    parts = []
    for r in range(9):
        part = x * turned(x, r)
        parts.append(part * PSI_SCALE[r] if weights and PSI_SCALE[r] != 1.0 else part)
    row = lax.broadcasted_iota(jnp.int32, x.shape, 0)
    return jnp.concatenate(parts + [x, jnp.where(row == 0, 1.0, 0.0)], axis=0)


def pull_psi(x, upstream, weights):
    total = upstream[9 * F : 10 * F]
    for r in range(9):
        part = upstream[r * F : (r + 1) * F]
        if weights and PSI_SCALE[r] != 1.0:
            part = part * PSI_SCALE[r]
        total = total + part * turned(x, r) + turned(part * x, (F - r) % F)
    return total


def feature_major(qk_ref, which, head):
    return jnp.concatenate([qk_ref[src, which, head] for src in range(qk_ref.shape[0])], axis=1)


def rows_of(ref, which, head, start, stop):
    tok = ref.shape[2]
    return jnp.concatenate(
        [
            ref[src, which, :, head * DH : (head + 1) * DH]
            for src in range(start // tok, stop // tok)
        ],
        axis=0,
    )


def score_sides(q, k):
    q_high, q_low = split(q)
    k_high, k_low = split(k)
    left = jnp.concatenate([q_high, q_high, q_low, q_low], axis=0)
    right = jnp.concatenate([k_high, k_low, k_high, k_low], axis=0)
    return left.T, right


def causal_mask(tile, width):
    row = lax.broadcasted_iota(jnp.int32, (tile, width), 0) + (width - tile)
    return row >= lax.broadcasted_iota(jnp.int32, (tile, width), 1)


def run_copies(sems, pairs):
    copies = [
        pltpu.make_async_copy(source, target, sems.at[i])
        for i, (source, target) in enumerate(pairs)
    ]
    for copy in copies:
        copy.start()
    for copy in copies:
        copy.wait()


def aligned(at, size):
    return pl.ds(pl.multiple_of(at * size, size), size)


def token_parts_kernel(at_ref, tokens_ref, *rest):
    *out_refs, sems = rest
    count, share = len(out_refs) + 1, out_refs[0].shape[1]
    run_copies(
        sems,
        [
            (tokens_ref.at[0, :, aligned(lax.rem(at_ref[0] + shift, count), share)], out_ref)
            for shift, out_ref in enumerate(out_refs, 1)
        ],
    )


def pack_heads_kernel(at_ref, values_ref, grad_ref, *out_refs):
    width = out_refs[0].shape[2]
    for shift, out_ref in enumerate(out_refs):
        cols = aligned(lax.rem(at_ref[0] + shift, len(out_refs)), width)
        out_ref[0] = values_ref[0, :, cols]
        out_ref[1] = grad_ref[0, :, cols]


def collect_heads_kernel(at_ref, *rest):
    *part_refs, out_ref = rest
    group = len(part_refs)
    for shift, part_ref in enumerate(part_refs):
        out_ref[lax.rem(at_ref[0] + group - shift, group)] = part_ref[...]


def pack_tokens_kernel(depth, at_ref, tokens_ref, keep_ref, send_ref):
    chips, _, rows = keep_ref.shape
    for shift in range(chips):
        chip = lax.rem(at_ref[0] + shift, chips)
        for core, out_ref in ((at_ref[1], keep_ref), (1 - at_ref[1], send_ref)):
            for part in range(rows // depth):
                cols = aligned(2 * (part * chips + chip) + core, depth)
                out_ref[shift, :, part * depth : (part + 1) * depth] = tokens_ref[0, :, cols]


def collect_tokens_kernel(at_ref, *rest):
    *part_refs, out_ref = rest
    chips, tok = len(part_refs), part_refs[0].shape[1]
    for shift, part_ref in enumerate(part_refs):
        chip = lax.rem(at_ref[0] + chips - shift, chips)
        for core in range(2):
            out_ref[:, aligned(2 * chip + core, tok)] = part_ref[core].T


def write_blocks(projected, out_ref):
    group, _, heads, feat, _ = out_ref.shape
    for member in range(group):
        for which in range(2):
            for head in range(heads):
                first = ((which * group + member) * heads + head) * feat
                out_ref[member, which, head] = projected[first : first + feat]


def project_kernel(at_ref, tokens_ref, weight_ref, out_ref, part_ref, sem):
    share = part_ref.shape[1]
    run_copies(sem, [(tokens_ref.at[0, :, aligned(at_ref[0], share)], part_ref)])
    write_blocks(dot(part_ref[...], weight_ref[...]).T, out_ref)


def project_rest_kernel(at_ref, own_ref, weight_ref, *rest):
    *part_refs, out_ref = rest
    count = len(part_refs) + 1
    at = at_ref[0]
    out_ref[at] = own_ref[...]
    for shift, part_ref in enumerate(part_refs, 1):
        owner = lax.rem(at + count - shift, count)
        write_blocks(dot(part_ref[...], weight_ref[...]).T, out_ref.at[owner])


def weight_piece_kernel(at_ref, weight_ref, out_ref, sems):
    run_copies(sems, [(weight_ref.at[aligned(at_ref[0], out_ref.shape[0])], out_ref)])


def state_sum(refs, head):
    total = refs[0][head].astype(f32)
    for ref in refs[1:]:
        total = total + ref[head].astype(f32)
    return total


def state_kernel(with_state, parts_ref, vg_ref, qk_ref, *state_refs):
    count, blocks, _, heads, _, tok = parts_ref.shape
    for head in range(heads):
        for which in range(2):
            for src in range(blocks):
                total = parts_ref[0, src, which, head]
                for part in range(1, count):
                    total = total + parts_ref[part, src, which, head]
                qk_ref[src, which, head] = total
        if with_state:
            high, low = split(psi(feature_major(qk_ref, 1, head), False))
            v = rows_of(vg_ref, 0, head, 0, blocks * tok)
            state_refs[0][head] = (dot(high, v) + dot(low, v)).astype(bf16)


def numerator_kernel(qk_ref, vg_ref, num_ref):
    heads = qk_ref.shape[2]
    length = qk_ref.shape[0] * qk_ref.shape[4]
    tile = min(TILE, length)
    for head in range(heads):
        q = feature_major(qk_ref, 0, head) * 0.25
        k = feature_major(qk_ref, 1, head)
        left, right = score_sides(q, k)
        for at in range(0, length, tile):
            width = at + tile
            scores = dot(left[at:width], right[:, :width])
            kernel = jnp.where(
                causal_mask(tile, width), 1.0 + scores * (1.0 + 0.5 * scores), 0.0
            )
            high, low = split(kernel)
            v = rows_of(vg_ref, 0, head, 0, width)
            num_ref[at:width, head * DH : (head + 1) * DH] = dot(high, v) + dot(low, v)


def normalize_kernel(with_state, qk_ref, vg_ref, num_ref, *rest):
    if with_state:
        *prefix_refs, attended_ref, grad_ref, carried_ref = rest
    else:
        attended_ref, grad_ref = rest
    heads = qk_ref.shape[2]
    blocks, tok = qk_ref.shape[0], qk_ref.shape[4]
    length = blocks * tok
    for head in range(heads):
        cols = slice(head * DH, (head + 1) * DH)
        numerator = num_ref[:, cols]
        if with_state:
            feat = psi(feature_major(qk_ref, 0, head) * 0.25, True)
            numerator = numerator + dot3(feat.T, state_sum(prefix_refs, head))
        inv_rms = lax.rsqrt(jnp.mean(numerator * numerator, axis=-1, keepdims=True) + EPSILON)
        normed = numerator * inv_rms
        upstream = rows_of(vg_ref, 1, head, 0, length).astype(f32)
        grad = inv_rms * (
            upstream - normed * jnp.mean(normed * upstream, axis=-1, keepdims=True)
        )
        attended_ref[:, cols] = normed.astype(bf16)
        grad_ref[:, cols] = grad
        if with_state:
            carried_ref[head] = dot3(feat, grad).astype(bf16)


def backward_kernel(with_state, qk_ref, vg_ref, grad_ref, *rest):
    *prefix_refs, grad_qk_ref, grad_v_ref = rest
    length = qk_ref.shape[0] * qk_ref.shape[4]
    tile = min(TILE, length)
    for head in range(grad_v_ref.shape[0]):
        cols = slice(head * DH, (head + 1) * DH)
        q = feature_major(qk_ref, 0, head) * 0.25
        k = feature_major(qk_ref, 1, head)
        left, right = score_sides(q, k)
        q_both = jnp.concatenate(split(q), axis=0)
        k_both = jnp.concatenate(split(k), axis=0)
        grad = grad_ref[:, cols]
        grad_t = grad.T
        if with_state:
            grad_q = pull_psi(q, dot3(state_sum(prefix_refs, head), grad_t), True)
        for at in reversed(range(0, length, tile)):
            width = at + tile
            scores = dot(left[at:width], right[:, :width])
            causal = causal_mask(tile, width)
            v = rows_of(vg_ref, 0, head, 0, width)
            high, low = split(grad[at:width])
            mixing = dot(
                jnp.concatenate([high, low], axis=1), jnp.concatenate([v, v], axis=1), NT
            )
            more = 1.0 + scores
            slopes = split(jnp.where(causal, mixing * more, 0.0))
            kernels = split(jnp.where(causal, more + 0.5 * scores * scores, 0.0))
            both = dot(k_both[:, :width], slopes[0], NT)
            piece = both[:F] + (both[F:] + dot(k_both[:F, :width], slopes[1], NT))
            if with_state:
                piece = piece + grad_q[:, at:width]
            grad_qk_ref[0, head, :, at:width] = piece * 0.25
            both = dot(q_both[:, at:width], slopes[0])
            piece_k = both[:F] + (both[F:] + dot(q_both[:F, at:width], slopes[1]))
            high, low = split(grad_t[:, at:width])
            both = dot(jnp.concatenate([high, low], axis=0), kernels[0])
            piece_v = both[:DH] + (both[DH:] + dot(high, kernels[1]))
            if width == length:
                grad_qk_ref[1, head] = piece_k
                grad_v_ref[head] = piece_v
            else:
                grad_qk_ref[1, head, :, :width] += piece_k
                grad_v_ref[head, :, :width] += piece_v


def rows_kernel(with_state, qk_ref, vg_ref, grad_qk_ref, *rest):
    *suffix_refs, out_ref, held_ref, sems = rest
    heads = qk_ref.shape[2]
    length = qk_ref.shape[0] * qk_ref.shape[4]
    for head in range(heads):
        grad_k = grad_qk_ref[1, head]
        if with_state:
            k = feature_major(qk_ref, 1, head)
            v = rows_of(vg_ref, 0, head, 0, length)
            high, low = split(state_sum(suffix_refs, head))
            grad_k = grad_k + pull_psi(k, dot(high, v, NT) + dot(low, v, NT), False)
        held_ref[head * F : (head + 1) * F] = grad_qk_ref[0, head].astype(bf16)
        held_ref[(heads + head) * F : (heads + head + 1) * F] = grad_k.astype(bf16)
    run_copies(sems, [(held_ref, out_ref)])


def grad_values_kernel(with_state, at_ref, qk_ref, attended_ref, grad_v_ref, *rest):
    *suffix_refs, keep_ref, send_ref, held_ref = rest
    heads, tok = qk_ref.shape[2], qk_ref.shape[4]
    for head in range(heads):
        grad_v = grad_v_ref[head]
        if with_state:
            feat = psi(feature_major(qk_ref, 1, head), False)
            grad_v = grad_v + dot3(state_sum(suffix_refs, head).T, feat)
        held_ref[:, head * DH : (head + 1) * DH] = grad_v.T.astype(bf16)
    chips = keep_ref.shape[0]
    for shift in range(chips):
        chip = lax.rem(at_ref[0] + shift, chips)
        for core, out_ref in ((at_ref[1], keep_ref), (1 - at_ref[1], send_ref)):
            rows = aligned(2 * chip + core, tok)
            out_ref[shift, 0] = attended_ref[rows, :]
            out_ref[shift, 1] = held_ref[rows, :]


def pair_kernel(at_ref, keep_ref, got_ref, *out_refs):
    for shift, out_ref in enumerate(out_refs):
        out_ref[at_ref[1]] = keep_ref[shift]
        out_ref[1 - at_ref[1]] = got_ref[shift]


def unpack_heads_kernel(at_ref, *rest):
    *part_refs, attended_ref, values_ref = rest
    chips, width = len(part_refs), part_refs[0].shape[3]
    for shift, part_ref in enumerate(part_refs):
        chip = lax.rem(at_ref[0] + chips - shift, chips)
        for core in range(2):
            cols = aligned(2 * chip + core, width)
            attended_ref[0, :, cols] = part_ref[core, 0]
            values_ref[0, :, cols] = part_ref[core, 1]


def place_rows(chip_at, core_at, part_refs, cols, held_ref):
    chips, half = len(part_refs) // 2, part_refs[0].shape[0] // 2
    for shift in range(chips):
        chip = lax.rem(chip_at + chips - shift, chips)
        for side, core in ((0, core_at), (1, 1 - core_at)):
            part_ref = part_refs[2 * shift + side]
            for which in range(2):
                rows = aligned(which * 2 * chips + 2 * chip + core, half)
                held_ref[rows, :] = part_ref[which * half : (which + 1) * half, cols]


def product_kernel(group, at_ref, *rest):
    rows_refs, rest = rest[:group], rest[group:]
    tokens_ref, *part_refs, total_ref, held_ref = rest
    place_rows(at_ref[1], at_ref[2], rows_refs, slice(None), held_ref)
    total_ref[...] = dot(tokens_ref[...], held_ref[...], NT)
    count = len(part_refs)
    size = part_refs[0].shape[0]
    for shift, part_ref in enumerate(part_refs):
        owner = lax.rem(at_ref[0] + shift, count)
        part = total_ref[pl.ds(pl.multiple_of(owner * size, size), size), :]
        part_ref[...] = part.astype(part_ref.dtype)


def run_sum_kernel(arrived, at_ref, *rest):
    own_ref, *rest = rest
    total_ref = rest[-1]
    total = own_ref[...]
    for ref in rest[:arrived]:
        total = total + ref[...].astype(f32)
    total_ref[...] = total
    part_refs = rest[arrived:-1]
    size = part_refs[0].shape[0]
    for shift, part_ref in enumerate(part_refs):
        owner = lax.rem(at_ref[0] + shift, len(part_refs))
        part = total_ref[pl.ds(pl.multiple_of(owner * size, size), size), :]
        part_ref[...] = part.astype(part_ref.dtype)


def grad_tokens_kernel(group, at_ref, *rest):
    rows_refs, rest = rest[:group], rest[group:]
    *weight_refs, out_ref, held_ref = rest
    member = 2 * at_ref[0] + at_ref[1]
    place_rows(at_ref[0], at_ref[1], rows_refs, aligned(member, out_ref.shape[1]), held_ref)
    rows = held_ref[...].T
    for i, weight_ref in enumerate(weight_refs):
        size = weight_ref.shape[0]
        first = pl.multiple_of(at_ref[2 + i], size)
        out_ref[0, :, pl.ds(first, size)] = dot(rows, weight_ref[...], NT).astype(bf16)


def final_sum_kernel(own_ref, *rest):
    *part_refs, out_ref = rest
    total = own_ref[...]
    for part_ref in part_refs:
        total = total + part_ref[...].astype(f32)
    out_ref[...] = total


VMEM = pl.BlockSpec(memory_space=pltpu.VMEM)
SMEM = pl.BlockSpec(memory_space=pltpu.SMEM)
FAR = pl.BlockSpec(memory_space=pltpu.HBM)
ANYWHERE = pl.BlockSpec(memory_space=pl.ANY)


def call(
    body,
    outs,
    *operands,
    scalars=(),
    after=(),
    after_far=(),
    scratch=(),
    far_in=(),
    far_out=False,
    copies=(),
):
    at = [jnp.stack([jnp.int32(s) for s in scalars])] if scalars else []
    count = len(at) + len(operands)

    def kernel(*refs):
        ins, rest = refs[:count], refs[count + len(after) + len(after_far) :]
        body(*ins, *rest[: len(outs)], *rest[len(outs) + 1 :])
        rest[len(outs)][...] = jnp.zeros((8, 128), f32)

    *results, token = pl.pallas_call(
        kernel,
        out_shape=[jax.ShapeDtypeStruct(shape, kind) for shape, kind in [*outs, ((8, 128), f32)]],
        in_specs=[SMEM] * len(at)
        + [FAR if i in far_in else VMEM for i in range(len(operands))]
        + [ANYWHERE] * len(after)
        + [FAR] * len(after_far),
        out_specs=[FAR if far_out else VMEM] * len(outs) + [VMEM],
        scratch_shapes=[*scratch] + [pltpu.SemaphoreType.DMA((n,)) for n in copies],
        compiler_params=pltpu.CompilerParams(vmem_limit_bytes=VMEM_LIMIT),
        cost_estimate=pl.CostEstimate(flops=0, bytes_accessed=0, transcendentals=0),
    )(*at, *operands, *after, *after_far)
    return results, token


def local(dp_size, ctx_size, tokens, proj_weight, values, grad_out):
    group = min(GROUP, ctx_size, H)
    runs = ctx_size // group
    heads = H // group
    tok, width = tokens.shape[1:]
    length = group * tok
    cols = proj_weight.shape[1]
    share = width // dp_size
    depth = share // ctx_size
    with_state = runs > 1
    groups = [[run * group + i for i in range(group)] for run in range(runs)]
    wide_groups = [
        [dp * ctx_size + i for dp in range(dp_size) for i in members] for members in groups
    ]
    dp_at, ctx_at = lax.axis_index("dp"), lax.axis_index("ctx")
    run_at, member = ctx_at // group, ctx_at % group

    def exchange(x):
        return lax.all_to_all(
            x, "ctx", split_axis=0, concat_axis=0, tiled=True, axis_index_groups=groups
        )

    def to_dp(x, shift):
        return lax.ppermute(x, "dp", [(i, (i + shift) % dp_size) for i in range(dp_size)])

    def to_member(x, shift):
        pairs = [(i, i - i % group + (i + shift) % group) for i in range(ctx_size)]
        return lax.ppermute(x, "ctx", pairs)

    def to_members(parts):
        return [part if not shift else to_member(part, shift) for shift, part in enumerate(parts)]

    chips = group // 2
    chip_at = member // 2

    def to_chip(x, shift):
        return x if shift == 0 else to_member(x, 2 * shift)

    def to_other_core(x):
        return lax.ppermute(x, "ctx", [(i, i ^ 1) for i in range(ctx_size)])

    def to_run(x, shift, wrap):
        pairs = [
            (i, (i + shift * group) % ctx_size)
            for i in range(ctx_size)
            if wrap or 0 <= i + shift * group < ctx_size
        ]
        return lax.ppermute(x, "ctx", pairs)

    qk_shape = ((group, 2, heads, F, tok), f32)
    state_shape = ((heads, PSI, DH), bf16)
    blocks_shape = ((2, tok, heads * DH), bf16)
    rows_shape = ((length, heads * DH), f32)

    parts, token = call(
        token_parts_kernel,
        [((tok, share), bf16)] * (dp_size - 1),
        tokens,
        scalars=(dp_at,),
        far_in=(0,),
        far_out=True,
        copies=(dp_size - 1,),
    )
    arrived = [to_dp(part, shift) for shift, part in enumerate(parts, 1)]
    parts, token = call(
        pack_heads_kernel,
        [((2, tok, heads * DH), bf16)] * group,
        values,
        grad_out,
        scalars=(member,),
        after=(token,),
    )
    parts = to_members(parts)
    (vg,), _ = call(
        collect_heads_kernel,
        [((group, 2, tok, heads * DH), bf16)],
        *parts,
        scalars=(member,),
    )
    (projected,), token = call(
        project_kernel,
        [qk_shape],
        tokens,
        proj_weight,
        scalars=(dp_at,),
        after=(token,),
        far_in=(0,),
        copies=(1,),
        scratch=[pltpu.VMEM((tok, share), bf16)],
    )
    (projected,), token = call(
        project_rest_kernel,
        [((dp_size,) + qk_shape[0], f32)],
        projected,
        proj_weight,
        *arrived,
        scalars=(dp_at,),
        after=(token,),
        after_far=parts[1 : 1 + group // 2],
    )
    part_shape = (tok, dp_size * runs * depth)
    if depth % 128 == 0:
        (keep, send), _ = call(
            functools.partial(pack_tokens_kernel, depth),
            [((chips,) + part_shape, bf16)] * 2,
            tokens,
            scalars=(chip_at, ctx_at % 2),
        )
    else:
        blocks = tokens[0].reshape(tok, dp_size * runs, chips, 2, depth).transpose(2, 3, 0, 1, 4)
        blocks = blocks.reshape(chips, 2, *part_shape)
        blocks = jnp.stack([blocks[(chip_at + shift) % chips] for shift in range(chips)])
        keep, send = blocks[:, ctx_at % 2], blocks[:, 1 - ctx_at % 2]
    token_parts, _ = call(
        pair_kernel,
        [((2,) + part_shape, bf16)] * chips,
        keep,
        to_other_core(send),
        scalars=(chip_at, ctx_at % 2),
        after=(token,),
    )
    token_parts = [to_chip(part, shift) for shift, part in enumerate(token_parts)]
    qk_parts = lax.all_to_all(
        projected.reshape((dp_size * group,) + qk_shape[0][1:]),
        ("dp", "ctx"),
        split_axis=0,
        concat_axis=0,
        tiled=True,
        axis_index_groups=wide_groups,
    ).reshape(projected.shape)

    pair = 2 if ctx_size % 2 == 0 else 1
    parity = ctx_at % pair
    piece = share // pair
    (mine,), token = call(
        weight_piece_kernel,
        [((piece, cols), bf16)],
        proj_weight,
        scalars=(parity,),
        after=(token,),
        far_in=(0,),
        far_out=True,
        copies=(1,),
    )
    fetched = [to_dp(mine, shift) for shift in range(1, dp_size)]
    weights, firsts = [proj_weight], [dp_at * share]
    for shift, half in enumerate(fetched, 1):
        base = (dp_at + dp_size - shift) % dp_size * share
        weights.append(half)
        firsts.append(base + parity * piece)
        if pair == 2:
            weights.append(lax.ppermute(half, "ctx", [(i, i ^ 1) for i in range(ctx_size)]))
            firsts.append(base + (1 - parity) * piece)

    (qk, *state), token = call(
        functools.partial(state_kernel, with_state),
        [qk_shape] + [state_shape] * with_state,
        qk_parts,
        vg,
    )
    prefix, suffix = (), ()
    if with_state:
        prefix = [to_run(state[0], shift, False) for shift in range(1, runs)]
    (numerator,), token = call(
        numerator_kernel, [rows_shape], qk, vg, after_far=token_parts[1:]
    )
    (attended, grad_num, *carried), token = call(
        functools.partial(normalize_kernel, with_state),
        [((length, heads * DH), bf16), rows_shape] + [state_shape] * with_state,
        qk,
        vg,
        numerator,
        *prefix,
    )
    if with_state:
        suffix = [to_run(carried[0], -shift, False) for shift in range(1, runs)]
    (grad_qk, grad_v), token = call(
        functools.partial(backward_kernel, with_state),
        [((2, heads, F, length), f32), ((heads, DH, length), f32)],
        qk,
        vg,
        grad_num,
        *prefix,
        after_far=fetched,
    )
    (token_cols,), token = call(
        collect_tokens_kernel,
        [(part_shape[1:] + (length,), bf16)],
        *token_parts,
        scalars=(chip_at,),
        after=(token,),
    )
    (rows,), token = call(
        functools.partial(rows_kernel, with_state),
        [((2 * heads * F, length), bf16)],
        qk,
        vg,
        grad_qk,
        *suffix,
        after=(token,),
        far_out=True,
        scratch=[pltpu.VMEM((2 * heads * F, length), bf16)],
        copies=(1,),
    )
    rows = [to_chip(rows, shift) for shift in range(chips)]
    rows = [side for part in rows for side in (part, to_other_core(part))]
    (keep, send), token = call(
        functools.partial(grad_values_kernel, with_state),
        [((chips, 2, tok, heads * DH), bf16)] * 2,
        qk,
        attended,
        grad_v,
        *suffix,
        scalars=(chip_at, ctx_at % 2),
        after_far=rows[1:2],
        scratch=[pltpu.VMEM((length, heads * DH), bf16)],
    )
    results, token = call(
        pair_kernel,
        [((2, 2, tok, heads * DH), bf16)] * chips,
        keep,
        to_other_core(send),
        scalars=(chip_at, ctx_at % 2),
    )
    results = [to_chip(part, shift) for shift, part in enumerate(results)]

    held = pltpu.VMEM((cols, length), bf16)
    (own, *parts), token = call(
        functools.partial(product_kernel, 2 * chips),
        [((runs * depth, cols), f32)] + [((runs * depth, cols), bf16)] * (dp_size - 1),
        *rows,
        token_cols,
        scalars=(dp_at, chip_at, ctx_at % 2),
        after=(token,),
        scratch=[pltpu.VMEM((dp_size * runs * depth, cols), f32), held],
    )
    parts = [to_dp(part, shift) for shift, part in enumerate(parts, 1)]
    (grad_tokens,), tokens_token = call(
        functools.partial(grad_tokens_kernel, 2 * chips),
        [((1, tok, width), bf16)],
        *rows,
        *weights,
        scalars=(chip_at, ctx_at % 2, *firsts),
        after=(token,),
        scratch=[pltpu.VMEM((cols, tok), bf16)],
    )
    (grad_proj, *parts), token = call(
        functools.partial(run_sum_kernel, len(parts)),
        [((depth, cols), f32)] + [((depth, cols), bf16)] * (runs - 1),
        own,
        *parts,
        scalars=(run_at,),
        after=(tokens_token,),
        scratch=[pltpu.VMEM((runs * depth, cols), f32)],
    )
    (attended, grad_values), token = call(
        unpack_heads_kernel,
        [((1, tok, H * DH), bf16)] * 2,
        *results,
        scalars=(chip_at,),
        after=(token,),
    )
    (grad_proj,), _ = call(
        final_sum_kernel,
        [((depth, cols), f32)],
        grad_proj,
        *[to_run(part, shift, True) for shift, part in enumerate(parts, 1)],
        after=(token,),
    )
    return (attended, grad_tokens, grad_values, grad_proj)


def solution(mesh):
    return jax.shard_map(
        functools.partial(local, mesh.shape["dp"], mesh.shape["ctx"]),
        mesh=mesh,
        in_specs=(P("dp", "ctx", None), P("dp", None), P("dp", "ctx", None), P("dp", "ctx", None)),
        out_specs=(
            P("dp", "ctx", None),
            P("dp", "ctx", None),
            P("dp", "ctx", None),
            P(("dp", "ctx"), None),
        ),
        check_vma=False,
    )
```

```python
import functools

import jax
import jax.numpy as jnp
from jax import lax
from jax.experimental import pallas as pl
from jax.experimental.pallas import tpu as pltpu
from jax.sharding import PartitionSpec as P

H = 16
F = 16
DH = 128
EPSILON = 1e-05
GROUP = 8
TILE = 256
VMEM_LIMIT = 16 * 1024 * 1024
PSI = 9 * F + 2 * F
PSI_SCALE = (0.5,) + (1.0,) * 7 + (0.5,)

f32 = jnp.float32
bf16 = jnp.bfloat16

NN = (((1,), (0,)), ((), ()))
NT = (((1,), (1,)), ((), ()))


def dot(a, b, dims=NN):
    return lax.dot_general(a, b, dims, preferred_element_type=f32)


def split(x):
    high = x.astype(bf16)
    return high, (x - high.astype(f32)).astype(bf16)


def dot3(a, b, dims=NN):
    a_high, a_low = split(a)
    b_high, b_low = split(b)
    return dot(a_high, b_high, dims) + (dot(a_high, b_low, dims) + dot(a_low, b_high, dims))


def turned(x, r):
    return x if r == 0 else jnp.concatenate([x[r:], x[:r]], axis=0)


def psi(x, weights):
    parts = []
    for r in range(9):
        part = x * turned(x, r)
        parts.append(part * PSI_SCALE[r] if weights and PSI_SCALE[r] != 1.0 else part)
    row = lax.broadcasted_iota(jnp.int32, x.shape, 0)
    return jnp.concatenate(parts + [x, jnp.where(row == 0, 1.0, 0.0)], axis=0)


def pull_psi(x, upstream, weights):
    total = upstream[9 * F : 10 * F]
    for r in range(9):
        part = upstream[r * F : (r + 1) * F]
        if weights and PSI_SCALE[r] != 1.0:
            part = part * PSI_SCALE[r]
        total = total + part * turned(x, r) + turned(part * x, (F - r) % F)
    return total


def feature_major(qk_ref, which, head):
    return jnp.concatenate([qk_ref[src, which, head] for src in range(qk_ref.shape[0])], axis=1)


def rows_of(ref, which, head, start, stop):
    tok = ref.shape[2]
    return jnp.concatenate(
        [
            ref[src, which, :, head * DH : (head + 1) * DH]
            for src in range(start // tok, stop // tok)
        ],
        axis=0,
    )


def score_sides(q, k):
    q_high, q_low = split(q)
    k_high, k_low = split(k)
    left = jnp.concatenate([q_high, q_high, q_low, q_low], axis=0)
    right = jnp.concatenate([k_high, k_low, k_high, k_low], axis=0)
    return left.T, right


def causal_mask(tile, width):
    row = lax.broadcasted_iota(jnp.int32, (tile, width), 0) + (width - tile)
    return row >= lax.broadcasted_iota(jnp.int32, (tile, width), 1)


def run_copies(sems, pairs):
    copies = [
        pltpu.make_async_copy(source, target, sems.at[i])
        for i, (source, target) in enumerate(pairs)
    ]
    for copy in copies:
        copy.start()
    for copy in copies:
        copy.wait()


def aligned(at, size):
    return pl.ds(pl.multiple_of(at * size, size), size)


def token_parts_kernel(at_ref, tokens_ref, *rest):
    *out_refs, sems = rest
    count, share = len(out_refs) + 1, out_refs[0].shape[1]
    run_copies(
        sems,
        [
            (tokens_ref.at[0, :, aligned(lax.rem(at_ref[0] + shift, count), share)], out_ref)
            for shift, out_ref in enumerate(out_refs, 1)
        ],
    )


def pack_heads_kernel(at_ref, values_ref, grad_ref, *out_refs):
    width = out_refs[0].shape[2]
    for shift, out_ref in enumerate(out_refs):
        cols = aligned(lax.rem(at_ref[0] + shift, len(out_refs)), width)
        out_ref[0] = values_ref[0, :, cols]
        out_ref[1] = grad_ref[0, :, cols]


def collect_heads_kernel(at_ref, *rest):
    *part_refs, out_ref = rest
    group = len(part_refs)
    for shift, part_ref in enumerate(part_refs):
        out_ref[lax.rem(at_ref[0] + group - shift, group)] = part_ref[...]


def pack_tokens_kernel(depth, at_ref, tokens_ref, keep_ref, send_ref):
    chips, _, rows = keep_ref.shape
    for shift in range(chips):
        chip = lax.rem(at_ref[0] + shift, chips)
        for core, out_ref in ((at_ref[1], keep_ref), (1 - at_ref[1], send_ref)):
            for part in range(rows // depth):
                cols = aligned(2 * (part * chips + chip) + core, depth)
                out_ref[shift, :, part * depth : (part + 1) * depth] = tokens_ref[0, :, cols]


def collect_tokens_kernel(at_ref, *rest):
    *part_refs, out_ref = rest
    chips, tok = len(part_refs), part_refs[0].shape[1]
    for shift, part_ref in enumerate(part_refs):
        chip = lax.rem(at_ref[0] + chips - shift, chips)
        for core in range(2):
            out_ref[:, aligned(2 * chip + core, tok)] = part_ref[core].T


def write_blocks(projected, out_ref):
    group, _, heads, feat, _ = out_ref.shape
    for member in range(group):
        for which in range(2):
            for head in range(heads):
                first = ((which * group + member) * heads + head) * feat
                out_ref[member, which, head] = projected[first : first + feat]


def project_kernel(at_ref, tokens_ref, weight_ref, out_ref, part_ref, sem):
    share = part_ref.shape[1]
    run_copies(sem, [(tokens_ref.at[0, :, aligned(at_ref[0], share)], part_ref)])
    write_blocks(dot(part_ref[...], weight_ref[...]).T, out_ref)


def project_rest_kernel(at_ref, own_ref, weight_ref, *rest):
    *part_refs, out_ref = rest
    count = len(part_refs) + 1
    at = at_ref[0]
    out_ref[at] = own_ref[...]
    for shift, part_ref in enumerate(part_refs, 1):
        owner = lax.rem(at + count - shift, count)
        write_blocks(dot(part_ref[...], weight_ref[...]).T, out_ref.at[owner])


def weight_piece_kernel(at_ref, weight_ref, out_ref, sems):
    run_copies(sems, [(weight_ref.at[aligned(at_ref[0], out_ref.shape[0])], out_ref)])


def state_sum(refs, head):
    total = refs[0][head].astype(f32)
    for ref in refs[1:]:
        total = total + ref[head].astype(f32)
    return total


def state_kernel(with_state, parts_ref, vg_ref, qk_ref, *state_refs):
    count, blocks, _, heads, _, tok = parts_ref.shape
    for head in range(heads):
        for which in range(2):
            for src in range(blocks):
                total = parts_ref[0, src, which, head]
                for part in range(1, count):
                    total = total + parts_ref[part, src, which, head]
                qk_ref[src, which, head] = total
        if with_state:
            high, low = split(psi(feature_major(qk_ref, 1, head), False))
            v = rows_of(vg_ref, 0, head, 0, blocks * tok)
            state_refs[0][head] = (dot(high, v) + dot(low, v)).astype(bf16)


def numerator_kernel(qk_ref, vg_ref, num_ref):
    heads = qk_ref.shape[2]
    length = qk_ref.shape[0] * qk_ref.shape[4]
    tile = min(TILE, length)
    for head in range(heads):
        q = feature_major(qk_ref, 0, head) * 0.25
        k = feature_major(qk_ref, 1, head)
        left, right = score_sides(q, k)
        for at in range(0, length, tile):
            width = at + tile
            scores = dot(left[at:width], right[:, :width])
            kernel = jnp.where(
                causal_mask(tile, width), 1.0 + scores * (1.0 + 0.5 * scores), 0.0
            )
            high, low = split(kernel)
            v = rows_of(vg_ref, 0, head, 0, width)
            num_ref[at:width, head * DH : (head + 1) * DH] = dot(high, v) + dot(low, v)


def normalize_kernel(with_state, qk_ref, vg_ref, num_ref, *rest):
    if with_state:
        *prefix_refs, attended_ref, grad_ref, carried_ref = rest
    else:
        attended_ref, grad_ref = rest
    heads = qk_ref.shape[2]
    blocks, tok = qk_ref.shape[0], qk_ref.shape[4]
    length = blocks * tok
    for head in range(heads):
        cols = slice(head * DH, (head + 1) * DH)
        numerator = num_ref[:, cols]
        if with_state:
            feat = psi(feature_major(qk_ref, 0, head) * 0.25, True)
            numerator = numerator + dot3(feat.T, state_sum(prefix_refs, head))
        inv_rms = lax.rsqrt(jnp.mean(numerator * numerator, axis=-1, keepdims=True) + EPSILON)
        normed = numerator * inv_rms
        upstream = rows_of(vg_ref, 1, head, 0, length).astype(f32)
        grad = inv_rms * (
            upstream - normed * jnp.mean(normed * upstream, axis=-1, keepdims=True)
        )
        attended_ref[:, cols] = normed.astype(bf16)
        grad_ref[:, cols] = grad
        if with_state:
            carried_ref[head] = dot3(feat, grad).astype(bf16)


def backward_kernel(with_state, qk_ref, vg_ref, grad_ref, *rest):
    *prefix_refs, grad_qk_ref, grad_v_ref = rest
    length = qk_ref.shape[0] * qk_ref.shape[4]
    tile = min(TILE, length)
    for head in range(grad_v_ref.shape[0]):
        cols = slice(head * DH, (head + 1) * DH)
        q = feature_major(qk_ref, 0, head) * 0.25
        k = feature_major(qk_ref, 1, head)
        left, right = score_sides(q, k)
        q_both = jnp.concatenate(split(q), axis=0)
        k_both = jnp.concatenate(split(k), axis=0)
        grad = grad_ref[:, cols]
        grad_t = grad.T
        if with_state:
            grad_q = pull_psi(q, dot3(state_sum(prefix_refs, head), grad_t), True)
        for at in reversed(range(0, length, tile)):
            width = at + tile
            scores = dot(left[at:width], right[:, :width])
            causal = causal_mask(tile, width)
            v = rows_of(vg_ref, 0, head, 0, width)
            high, low = split(grad[at:width])
            mixing = dot(
                jnp.concatenate([high, low], axis=1), jnp.concatenate([v, v], axis=1), NT
            )
            more = 1.0 + scores
            slopes = split(jnp.where(causal, mixing * more, 0.0))
            kernels = split(jnp.where(causal, more + 0.5 * scores * scores, 0.0))
            both = dot(k_both[:, :width], slopes[0], NT)
            piece = both[:F] + (both[F:] + dot(k_both[:F, :width], slopes[1], NT))
            if with_state:
                piece = piece + grad_q[:, at:width]
            grad_qk_ref[0, head, :, at:width] = piece * 0.25
            both = dot(q_both[:, at:width], slopes[0])
            piece_k = both[:F] + (both[F:] + dot(q_both[:F, at:width], slopes[1]))
            high, low = split(grad_t[:, at:width])
            both = dot(jnp.concatenate([high, low], axis=0), kernels[0])
            piece_v = both[:DH] + (both[DH:] + dot(high, kernels[1]))
            if width == length:
                grad_qk_ref[1, head] = piece_k
                grad_v_ref[head] = piece_v
            else:
                grad_qk_ref[1, head, :, :width] += piece_k
                grad_v_ref[head, :, :width] += piece_v


def rows_kernel(with_state, qk_ref, vg_ref, grad_qk_ref, *rest):
    *suffix_refs, out_ref, held_ref, sems = rest
    heads = qk_ref.shape[2]
    length = qk_ref.shape[0] * qk_ref.shape[4]
    for head in range(heads):
        grad_k = grad_qk_ref[1, head]
        if with_state:
            k = feature_major(qk_ref, 1, head)
            v = rows_of(vg_ref, 0, head, 0, length)
            high, low = split(state_sum(suffix_refs, head))
            grad_k = grad_k + pull_psi(k, dot(high, v, NT) + dot(low, v, NT), False)
        held_ref[head * F : (head + 1) * F] = grad_qk_ref[0, head].astype(bf16)
        held_ref[(heads + head) * F : (heads + head + 1) * F] = grad_k.astype(bf16)
    run_copies(sems, [(held_ref, out_ref)])


def grad_values_kernel(with_state, at_ref, qk_ref, attended_ref, grad_v_ref, *rest):
    *suffix_refs, keep_ref, send_ref, held_ref = rest
    heads, tok = qk_ref.shape[2], qk_ref.shape[4]
    for head in range(heads):
        grad_v = grad_v_ref[head]
        if with_state:
            feat = psi(feature_major(qk_ref, 1, head), False)
            grad_v = grad_v + dot3(state_sum(suffix_refs, head).T, feat)
        held_ref[:, head * DH : (head + 1) * DH] = grad_v.T.astype(bf16)
    chips = keep_ref.shape[0]
    for shift in range(chips):
        chip = lax.rem(at_ref[0] + shift, chips)
        for core, out_ref in ((at_ref[1], keep_ref), (1 - at_ref[1], send_ref)):
            rows = aligned(2 * chip + core, tok)
            out_ref[shift, 0] = attended_ref[rows, :]
            out_ref[shift, 1] = held_ref[rows, :]


def pair_kernel(at_ref, keep_ref, got_ref, *out_refs):
    for shift, out_ref in enumerate(out_refs):
        out_ref[at_ref[1]] = keep_ref[shift]
        out_ref[1 - at_ref[1]] = got_ref[shift]


def unpack_heads_kernel(at_ref, *rest):
    *part_refs, attended_ref, values_ref = rest
    chips, width = len(part_refs), part_refs[0].shape[3]
    for shift, part_ref in enumerate(part_refs):
        chip = lax.rem(at_ref[0] + chips - shift, chips)
        for core in range(2):
            cols = aligned(2 * chip + core, width)
            attended_ref[0, :, cols] = part_ref[core, 0]
            values_ref[0, :, cols] = part_ref[core, 1]


def place_rows(chip_at, core_at, part_refs, cols, held_ref):
    chips, half = len(part_refs) // 2, part_refs[0].shape[0] // 2
    for shift in range(chips):
        chip = lax.rem(chip_at + chips - shift, chips)
        for side, core in ((0, core_at), (1, 1 - core_at)):
            part_ref = part_refs[2 * shift + side]
            for which in range(2):
                rows = aligned(which * 2 * chips + 2 * chip + core, half)
                held_ref[rows, :] = part_ref[which * half : (which + 1) * half, cols]


def product_kernel(group, at_ref, *rest):
    rows_refs, rest = rest[:group], rest[group:]
    tokens_ref, *part_refs, total_ref, held_ref = rest
    place_rows(at_ref[1], at_ref[2], rows_refs, slice(None), held_ref)
    total_ref[...] = dot(tokens_ref[...], held_ref[...], NT)
    count = len(part_refs)
    size = part_refs[0].shape[0]
    for shift, part_ref in enumerate(part_refs):
        owner = lax.rem(at_ref[0] + shift, count)
        part = total_ref[pl.ds(pl.multiple_of(owner * size, size), size), :]
        part_ref[...] = part.astype(part_ref.dtype)


def run_sum_kernel(arrived, at_ref, *rest):
    own_ref, *rest = rest
    total_ref = rest[-1]
    total = own_ref[...]
    for ref in rest[:arrived]:
        total = total + ref[...].astype(f32)
    total_ref[...] = total
    part_refs = rest[arrived:-1]
    size = part_refs[0].shape[0]
    for shift, part_ref in enumerate(part_refs):
        owner = lax.rem(at_ref[0] + shift, len(part_refs))
        part = total_ref[pl.ds(pl.multiple_of(owner * size, size), size), :]
        part_ref[...] = part.astype(part_ref.dtype)


def grad_tokens_kernel(group, at_ref, *rest):
    rows_refs, rest = rest[:group], rest[group:]
    *weight_refs, out_ref, held_ref = rest
    member = 2 * at_ref[0] + at_ref[1]
    place_rows(at_ref[0], at_ref[1], rows_refs, aligned(member, out_ref.shape[1]), held_ref)
    rows = held_ref[...].T
    for i, weight_ref in enumerate(weight_refs):
        size = weight_ref.shape[0]
        first = pl.multiple_of(at_ref[2 + i], size)
        out_ref[0, :, pl.ds(first, size)] = dot(rows, weight_ref[...], NT).astype(bf16)


def final_sum_kernel(own_ref, *rest):
    *part_refs, out_ref = rest
    total = own_ref[...]
    for part_ref in part_refs:
        total = total + part_ref[...].astype(f32)
    out_ref[...] = total


VMEM = pl.BlockSpec(memory_space=pltpu.VMEM)
SMEM = pl.BlockSpec(memory_space=pltpu.SMEM)
FAR = pl.BlockSpec(memory_space=pltpu.HBM)
ANYWHERE = pl.BlockSpec(memory_space=pl.ANY)


def call(
    body,
    outs,
    *operands,
    scalars=(),
    after=(),
    after_far=(),
    scratch=(),
    far_in=(),
    far_out=False,
    copies=(),
):
    at = [jnp.stack([jnp.int32(s) for s in scalars])] if scalars else []
    count = len(at) + len(operands)

    def kernel(*refs):
        ins, rest = refs[:count], refs[count + len(after) + len(after_far) :]
        body(*ins, *rest[: len(outs)], *rest[len(outs) + 1 :])
        rest[len(outs)][...] = jnp.zeros((8, 128), f32)

    *results, token = pl.pallas_call(
        kernel,
        out_shape=[jax.ShapeDtypeStruct(shape, kind) for shape, kind in [*outs, ((8, 128), f32)]],
        in_specs=[SMEM] * len(at)
        + [FAR if i in far_in else VMEM for i in range(len(operands))]
        + [ANYWHERE] * len(after)
        + [FAR] * len(after_far),
        out_specs=[FAR if far_out else VMEM] * len(outs) + [VMEM],
        scratch_shapes=[*scratch] + [pltpu.SemaphoreType.DMA((n,)) for n in copies],
        compiler_params=pltpu.CompilerParams(vmem_limit_bytes=VMEM_LIMIT),
        cost_estimate=pl.CostEstimate(flops=0, bytes_accessed=0, transcendentals=0),
    )(*at, *operands, *after, *after_far)
    return results, token


def local(dp_size, ctx_size, tokens, proj_weight, values, grad_out):
    group = min(GROUP, ctx_size, H)
    runs = ctx_size // group
    heads = H // group
    tok, width = tokens.shape[1:]
    length = group * tok
    cols = proj_weight.shape[1]
    share = width // dp_size
    depth = share // ctx_size
    with_state = runs > 1
    groups = [[run * group + i for i in range(group)] for run in range(runs)]
    wide_groups = [
        [dp * ctx_size + i for dp in range(dp_size) for i in members] for members in groups
    ]
    dp_at, ctx_at = lax.axis_index("dp"), lax.axis_index("ctx")
    run_at, member = ctx_at // group, ctx_at % group

    def exchange(x):
        return lax.all_to_all(
            x, "ctx", split_axis=0, concat_axis=0, tiled=True, axis_index_groups=groups
        )

    def to_dp(x, shift):
        return lax.ppermute(x, "dp", [(i, (i + shift) % dp_size) for i in range(dp_size)])

    def to_member(x, shift):
        pairs = [(i, i - i % group + (i + shift) % group) for i in range(ctx_size)]
        return lax.ppermute(x, "ctx", pairs)

    def to_members(parts):
        return [part if not shift else to_member(part, shift) for shift, part in enumerate(parts)]

    chips = group // 2
    chip_at = member // 2

    def to_chip(x, shift):
        return x if shift == 0 else to_member(x, 2 * shift)

    def to_other_core(x):
        return lax.ppermute(x, "ctx", [(i, i ^ 1) for i in range(ctx_size)])

    def to_run(x, shift, wrap):
        pairs = [
            (i, (i + shift * group) % ctx_size)
            for i in range(ctx_size)
            if wrap or 0 <= i + shift * group < ctx_size
        ]
        return lax.ppermute(x, "ctx", pairs)

    qk_shape = ((group, 2, heads, F, tok), f32)
    state_shape = ((heads, PSI, DH), bf16)
    blocks_shape = ((2, tok, heads * DH), bf16)
    rows_shape = ((length, heads * DH), f32)

    parts, token = call(
        token_parts_kernel,
        [((tok, share), bf16)] * (dp_size - 1),
        tokens,
        scalars=(dp_at,),
        far_in=(0,),
        far_out=True,
        copies=(dp_size - 1,),
    )
    arrived = [to_dp(part, shift) for shift, part in enumerate(parts, 1)]
    parts, token = call(
        pack_heads_kernel,
        [((2, tok, heads * DH), bf16)] * group,
        values,
        grad_out,
        scalars=(member,),
        after=(token,),
    )
    parts = to_members(parts)
    (vg,), vg_token = call(
        collect_heads_kernel,
        [((group, 2, tok, heads * DH), bf16)],
        *parts,
        scalars=(member,),
    )
    (projected,), token = call(
        project_kernel,
        [qk_shape],
        tokens,
        proj_weight,
        scalars=(dp_at,),
        after=(token,),
        far_in=(0,),
        copies=(1,),
        scratch=[pltpu.VMEM((tok, share), bf16)],
    )
    (projected,), token = call(
        project_rest_kernel,
        [((dp_size,) + qk_shape[0], f32)],
        projected,
        proj_weight,
        *arrived,
        scalars=(dp_at,),
        after=(vg_token, token),
    )
    part_shape = (tok, dp_size * runs * depth)
    if depth % 128 == 0:
        (keep, send), _ = call(
            functools.partial(pack_tokens_kernel, depth),
            [((chips,) + part_shape, bf16)] * 2,
            tokens,
            scalars=(chip_at, ctx_at % 2),
        )
    else:
        blocks = tokens[0].reshape(tok, dp_size * runs, chips, 2, depth).transpose(2, 3, 0, 1, 4)
        blocks = blocks.reshape(chips, 2, *part_shape)
        blocks = jnp.stack([blocks[(chip_at + shift) % chips] for shift in range(chips)])
        keep, send = blocks[:, ctx_at % 2], blocks[:, 1 - ctx_at % 2]
    token_parts, _ = call(
        pair_kernel,
        [((2,) + part_shape, bf16)] * chips,
        keep,
        to_other_core(send),
        scalars=(chip_at, ctx_at % 2),
        after=(token,),
    )
    token_parts = [to_chip(part, shift) for shift, part in enumerate(token_parts)]
    qk_parts = lax.all_to_all(
        projected.reshape((dp_size * group,) + qk_shape[0][1:]),
        ("dp", "ctx"),
        split_axis=0,
        concat_axis=0,
        tiled=True,
        axis_index_groups=wide_groups,
    ).reshape(projected.shape)

    pair = 2 if ctx_size % 2 == 0 else 1
    parity = ctx_at % pair
    piece = share // pair
    (mine,), token = call(
        weight_piece_kernel,
        [((piece, cols), bf16)],
        proj_weight,
        scalars=(parity,),
        after=(token,),
        far_in=(0,),
        far_out=True,
        copies=(1,),
    )
    fetched = [to_dp(mine, shift) for shift in range(1, dp_size)]
    weights, firsts = [proj_weight], [dp_at * share]
    for shift, half in enumerate(fetched, 1):
        base = (dp_at + dp_size - shift) % dp_size * share
        weights.append(half)
        firsts.append(base + parity * piece)
        if pair == 2:
            weights.append(lax.ppermute(half, "ctx", [(i, i ^ 1) for i in range(ctx_size)]))
            firsts.append(base + (1 - parity) * piece)

    (qk, *state), token = call(
        functools.partial(state_kernel, with_state),
        [qk_shape] + [state_shape] * with_state,
        qk_parts,
        vg,
    )
    prefix, suffix = (), ()
    if with_state:
        prefix = [to_run(state[0], shift, False) for shift in range(1, runs)]
    (numerator,), token = call(numerator_kernel, [rows_shape], qk, vg)
    (attended, grad_num, *carried), token = call(
        functools.partial(normalize_kernel, with_state),
        [((length, heads * DH), bf16), rows_shape] + [state_shape] * with_state,
        qk,
        vg,
        numerator,
        *prefix,
        after_far=token_parts[1:],
    )
    if with_state:
        suffix = [to_run(carried[0], -shift, False) for shift in range(1, runs)]
    (grad_qk, grad_v), token = call(
        functools.partial(backward_kernel, with_state),
        [((2, heads, F, length), f32), ((heads, DH, length), f32)],
        qk,
        vg,
        grad_num,
        *prefix,
        after_far=fetched,
    )
    (token_cols,), token = call(
        collect_tokens_kernel,
        [(part_shape[1:] + (length,), bf16)],
        *token_parts,
        scalars=(chip_at,),
        after=(token,),
    )
    (rows,), token = call(
        functools.partial(rows_kernel, with_state),
        [((2 * heads * F, length), bf16)],
        qk,
        vg,
        grad_qk,
        *suffix,
        after=(token,),
        far_out=True,
        scratch=[pltpu.VMEM((2 * heads * F, length), bf16)],
        copies=(1,),
    )
    rows = [to_chip(rows, shift) for shift in range(chips)]
    rows = [side for part in rows for side in (part, to_other_core(part))]
    (keep, send), token = call(
        functools.partial(grad_values_kernel, with_state),
        [((chips, 2, tok, heads * DH), bf16)] * 2,
        qk,
        attended,
        grad_v,
        *suffix,
        scalars=(chip_at, ctx_at % 2),
        after_far=rows[2::2],
        scratch=[pltpu.VMEM((length, heads * DH), bf16)],
    )
    got = to_other_core(send)
    results, _ = call(
        pair_kernel,
        [((2, 2, tok, heads * DH), bf16)] * chips,
        keep,
        got,
        scalars=(chip_at, ctx_at % 2),
    )
    results = [to_chip(part, shift) for shift, part in enumerate(results)]

    held = pltpu.VMEM((cols, length), bf16)
    (own, *parts), token = call(
        functools.partial(product_kernel, 2 * chips),
        [((runs * depth, cols), f32)] + [((runs * depth, cols), bf16)] * (dp_size - 1),
        *rows,
        token_cols,
        scalars=(dp_at, chip_at, ctx_at % 2),
        after=(token,),
        after_far=(got,),
        scratch=[pltpu.VMEM((dp_size * runs * depth, cols), f32), held],
    )
    parts = [to_dp(part, shift) for shift, part in enumerate(parts, 1)]
    (grad_proj, *parts), token = call(
        functools.partial(run_sum_kernel, len(parts)),
        [((depth, cols), f32)] + [((depth, cols), bf16)] * (runs - 1),
        own,
        *parts,
        scalars=(run_at,),
        scratch=[pltpu.VMEM((runs * depth, cols), f32)],
    )
    (grad_tokens,), tokens_token = call(
        functools.partial(grad_tokens_kernel, 2 * chips),
        [((1, tok, width), bf16)],
        *rows,
        *weights,
        scalars=(chip_at, ctx_at % 2, *firsts),
        after=(token,),
        scratch=[pltpu.VMEM((cols, tok), bf16)],
    )
    (attended, grad_values), token = call(
        unpack_heads_kernel,
        [((1, tok, H * DH), bf16)] * 2,
        *results,
        scalars=(chip_at,),
        after=(token,),
    )
    (grad_proj,), _ = call(
        final_sum_kernel,
        [((depth, cols), f32)],
        grad_proj,
        *[to_run(part, shift, True) for shift, part in enumerate(parts, 1)],
        after=(token, tokens_token),
    )
    return (attended, grad_tokens, grad_values, grad_proj)


def solution(mesh):
    return jax.shard_map(
        functools.partial(local, mesh.shape["dp"], mesh.shape["ctx"]),
        mesh=mesh,
        in_specs=(P("dp", "ctx", None), P("dp", None), P("dp", "ctx", None), P("dp", "ctx", None)),
        out_specs=(
            P("dp", "ctx", None),
            P("dp", "ctx", None),
            P("dp", "ctx", None),
            P(("dp", "ctx"), None),
        ),
        check_vma=False,
    )
```

```python
import functools

import jax
import jax.numpy as jnp
from jax import lax
from jax.experimental import pallas as pl
from jax.experimental.pallas import tpu as pltpu
from jax.sharding import PartitionSpec as P

H = 16
F = 16
DH = 128
EPSILON = 1e-05
GROUP = 8
TILE = 256
VMEM_LIMIT = 16 * 1024 * 1024
PSI = 9 * F + 2 * F
PSI_SCALE = (0.5,) + (1.0,) * 7 + (0.5,)

f32 = jnp.float32
bf16 = jnp.bfloat16

NN = (((1,), (0,)), ((), ()))
NT = (((1,), (1,)), ((), ()))


def dot(a, b, dims=NN):
    return lax.dot_general(a, b, dims, preferred_element_type=f32)


def split(x):
    high = x.astype(bf16)
    return high, (x - high.astype(f32)).astype(bf16)


def dot3(a, b, dims=NN):
    a_high, a_low = split(a)
    b_high, b_low = split(b)
    return dot(a_high, b_high, dims) + (dot(a_high, b_low, dims) + dot(a_low, b_high, dims))


def turned(x, r):
    return x if r == 0 else jnp.concatenate([x[r:], x[:r]], axis=0)


def psi(x, weights):
    parts = []
    for r in range(9):
        part = x * turned(x, r)
        parts.append(part * PSI_SCALE[r] if weights and PSI_SCALE[r] != 1.0 else part)
    row = lax.broadcasted_iota(jnp.int32, x.shape, 0)
    return jnp.concatenate(parts + [x, jnp.where(row == 0, 1.0, 0.0)], axis=0)


def pull_psi(x, upstream, weights):
    total = upstream[9 * F : 10 * F]
    for r in range(9):
        part = upstream[r * F : (r + 1) * F]
        if weights and PSI_SCALE[r] != 1.0:
            part = part * PSI_SCALE[r]
        total = total + part * turned(x, r) + turned(part * x, (F - r) % F)
    return total


def feature_major(qk_ref, which, head):
    return jnp.concatenate([qk_ref[src, which, head] for src in range(qk_ref.shape[0])], axis=1)


def rows_of(ref, which, head, start, stop):
    tok = ref.shape[2]
    return jnp.concatenate(
        [
            ref[src, which, :, head * DH : (head + 1) * DH]
            for src in range(start // tok, stop // tok)
        ],
        axis=0,
    )


def score_sides(q, k):
    q_high, q_low = split(q)
    k_high, k_low = split(k)
    left = jnp.concatenate([q_high, q_high, q_low, q_low], axis=0)
    right = jnp.concatenate([k_high, k_low, k_high, k_low], axis=0)
    return left.T, right


def causal_mask(tile, width):
    row = lax.broadcasted_iota(jnp.int32, (tile, width), 0) + (width - tile)
    return row >= lax.broadcasted_iota(jnp.int32, (tile, width), 1)


def run_copies(sems, pairs):
    copies = [
        pltpu.make_async_copy(source, target, sems.at[i])
        for i, (source, target) in enumerate(pairs)
    ]
    for copy in copies:
        copy.start()
    for copy in copies:
        copy.wait()


def aligned(at, size):
    return pl.ds(pl.multiple_of(at * size, size), size)


def token_parts_kernel(at_ref, tokens_ref, *rest):
    *out_refs, sems = rest
    count, share = len(out_refs) + 1, out_refs[0].shape[1]
    run_copies(
        sems,
        [
            (tokens_ref.at[0, :, aligned(lax.rem(at_ref[0] + shift, count), share)], out_ref)
            for shift, out_ref in enumerate(out_refs, 1)
        ],
    )


def pack_heads_kernel(at_ref, values_ref, grad_ref, keep_ref, send_ref):
    chips, width = keep_ref.shape[0], keep_ref.shape[3]
    for shift in range(chips):
        chip = lax.rem(at_ref[0] + shift, chips)
        for core, out_ref in ((at_ref[1], keep_ref), (1 - at_ref[1], send_ref)):
            cols = aligned(2 * chip + core, width)
            out_ref[shift, 0] = values_ref[0, :, cols]
            out_ref[shift, 1] = grad_ref[0, :, cols]


def collect_heads_kernel(at_ref, *rest):
    *part_refs, out_ref = rest
    chips = len(part_refs)
    for shift, part_ref in enumerate(part_refs):
        chip = lax.rem(at_ref[0] + chips - shift, chips)
        for core in range(2):
            out_ref[2 * chip + core] = part_ref[core]


def pack_tokens_kernel(depth, at_ref, tokens_ref, keep_ref, send_ref):
    chips, _, rows = keep_ref.shape
    for shift in range(chips):
        chip = lax.rem(at_ref[0] + shift, chips)
        for core, out_ref in ((at_ref[1], keep_ref), (1 - at_ref[1], send_ref)):
            for part in range(rows // depth):
                cols = aligned(2 * (part * chips + chip) + core, depth)
                out_ref[shift, :, part * depth : (part + 1) * depth] = tokens_ref[0, :, cols]


def collect_tokens_kernel(at_ref, *rest):
    *part_refs, out_ref = rest
    chips, tok = len(part_refs), part_refs[0].shape[1]
    for shift, part_ref in enumerate(part_refs):
        chip = lax.rem(at_ref[0] + chips - shift, chips)
        for core in range(2):
            out_ref[:, aligned(2 * chip + core, tok)] = part_ref[core].T


def write_blocks(projected, out_ref):
    group, _, heads, feat, _ = out_ref.shape
    for member in range(group):
        for which in range(2):
            for head in range(heads):
                first = ((which * group + member) * heads + head) * feat
                out_ref[member, which, head] = projected[first : first + feat]


def project_kernel(at_ref, tokens_ref, weight_ref, out_ref, part_ref, sem):
    share = part_ref.shape[1]
    run_copies(sem, [(tokens_ref.at[0, :, aligned(at_ref[0], share)], part_ref)])
    write_blocks(dot(part_ref[...], weight_ref[...]).T, out_ref)


def project_rest_kernel(at_ref, own_ref, weight_ref, *rest):
    *part_refs, out_ref = rest
    count = len(part_refs) + 1
    at = at_ref[0]
    out_ref[at] = own_ref[...]
    for shift, part_ref in enumerate(part_refs, 1):
        owner = lax.rem(at + count - shift, count)
        write_blocks(dot(part_ref[...], weight_ref[...]).T, out_ref.at[owner])


def weight_piece_kernel(at_ref, weight_ref, out_ref, sems):
    run_copies(sems, [(weight_ref.at[aligned(at_ref[0], out_ref.shape[0])], out_ref)])


def state_sum(refs, head):
    total = refs[0][head].astype(f32)
    for ref in refs[1:]:
        total = total + ref[head].astype(f32)
    return total


def state_kernel(with_state, parts_ref, vg_ref, qk_ref, *state_refs):
    count, blocks, _, heads, _, tok = parts_ref.shape
    for head in range(heads):
        for which in range(2):
            for src in range(blocks):
                total = parts_ref[0, src, which, head]
                for part in range(1, count):
                    total = total + parts_ref[part, src, which, head]
                qk_ref[src, which, head] = total
        if with_state:
            high, low = split(psi(feature_major(qk_ref, 1, head), False))
            v = rows_of(vg_ref, 0, head, 0, blocks * tok)
            state_refs[0][head] = (dot(high, v) + dot(low, v)).astype(bf16)


def numerator_kernel(qk_ref, vg_ref, num_ref):
    heads = qk_ref.shape[2]
    length = qk_ref.shape[0] * qk_ref.shape[4]
    tile = min(TILE, length)
    for head in range(heads):
        q = feature_major(qk_ref, 0, head) * 0.25
        k = feature_major(qk_ref, 1, head)
        left, right = score_sides(q, k)
        for at in range(0, length, tile):
            width = at + tile
            scores = dot(left[at:width], right[:, :width])
            kernel = jnp.where(
                causal_mask(tile, width), 1.0 + scores * (1.0 + 0.5 * scores), 0.0
            )
            high, low = split(kernel)
            v = rows_of(vg_ref, 0, head, 0, width)
            num_ref[at:width, head * DH : (head + 1) * DH] = dot(high, v) + dot(low, v)


def normalize_kernel(with_state, qk_ref, vg_ref, num_ref, *rest):
    if with_state:
        *prefix_refs, attended_ref, grad_ref, carried_ref = rest
    else:
        attended_ref, grad_ref = rest
    heads = qk_ref.shape[2]
    blocks, tok = qk_ref.shape[0], qk_ref.shape[4]
    length = blocks * tok
    for head in range(heads):
        cols = slice(head * DH, (head + 1) * DH)
        numerator = num_ref[:, cols]
        if with_state:
            feat = psi(feature_major(qk_ref, 0, head) * 0.25, True)
            numerator = numerator + dot3(feat.T, state_sum(prefix_refs, head))
        inv_rms = lax.rsqrt(jnp.mean(numerator * numerator, axis=-1, keepdims=True) + EPSILON)
        normed = numerator * inv_rms
        upstream = rows_of(vg_ref, 1, head, 0, length).astype(f32)
        grad = inv_rms * (
            upstream - normed * jnp.mean(normed * upstream, axis=-1, keepdims=True)
        )
        attended_ref[:, cols] = normed.astype(bf16)
        grad_ref[:, cols] = grad
        if with_state:
            carried_ref[head] = dot3(feat, grad).astype(bf16)


def backward_kernel(with_state, qk_ref, vg_ref, grad_ref, *rest):
    *prefix_refs, grad_qk_ref, grad_v_ref = rest
    length = qk_ref.shape[0] * qk_ref.shape[4]
    tile = min(TILE, length)
    for head in range(grad_v_ref.shape[0]):
        cols = slice(head * DH, (head + 1) * DH)
        q = feature_major(qk_ref, 0, head) * 0.25
        k = feature_major(qk_ref, 1, head)
        left, right = score_sides(q, k)
        q_both = jnp.concatenate(split(q), axis=0)
        k_both = jnp.concatenate(split(k), axis=0)
        grad = grad_ref[:, cols]
        grad_t = grad.T
        if with_state:
            grad_q = pull_psi(q, dot3(state_sum(prefix_refs, head), grad_t), True)
        for at in reversed(range(0, length, tile)):
            width = at + tile
            scores = dot(left[at:width], right[:, :width])
            causal = causal_mask(tile, width)
            v = rows_of(vg_ref, 0, head, 0, width)
            high, low = split(grad[at:width])
            mixing = dot(
                jnp.concatenate([high, low], axis=1), jnp.concatenate([v, v], axis=1), NT
            )
            more = 1.0 + scores
            slopes = split(jnp.where(causal, mixing * more, 0.0))
            kernels = split(jnp.where(causal, more + 0.5 * scores * scores, 0.0))
            both = dot(k_both[:, :width], slopes[0], NT)
            piece = both[:F] + (both[F:] + dot(k_both[:F, :width], slopes[1], NT))
            if with_state:
                piece = piece + grad_q[:, at:width]
            grad_qk_ref[0, head, :, at:width] = piece * 0.25
            both = dot(q_both[:, at:width], slopes[0])
            piece_k = both[:F] + (both[F:] + dot(q_both[:F, at:width], slopes[1]))
            high, low = split(grad_t[:, at:width])
            both = dot(jnp.concatenate([high, low], axis=0), kernels[0])
            piece_v = both[:DH] + (both[DH:] + dot(high, kernels[1]))
            if width == length:
                grad_qk_ref[1, head] = piece_k
                grad_v_ref[head] = piece_v
            else:
                grad_qk_ref[1, head, :, :width] += piece_k
                grad_v_ref[head, :, :width] += piece_v


def rows_kernel(with_state, qk_ref, vg_ref, grad_qk_ref, *rest):
    *suffix_refs, out_ref, held_ref, sems = rest
    heads = qk_ref.shape[2]
    length = qk_ref.shape[0] * qk_ref.shape[4]
    for head in range(heads):
        grad_k = grad_qk_ref[1, head]
        if with_state:
            k = feature_major(qk_ref, 1, head)
            v = rows_of(vg_ref, 0, head, 0, length)
            high, low = split(state_sum(suffix_refs, head))
            grad_k = grad_k + pull_psi(k, dot(high, v, NT) + dot(low, v, NT), False)
        held_ref[head * F : (head + 1) * F] = grad_qk_ref[0, head].astype(bf16)
        held_ref[(heads + head) * F : (heads + head + 1) * F] = grad_k.astype(bf16)
    run_copies(sems, [(held_ref, out_ref)])


def grad_values_kernel(with_state, at_ref, qk_ref, attended_ref, grad_v_ref, *rest):
    *suffix_refs, keep_ref, send_ref, held_ref = rest
    heads, tok = qk_ref.shape[2], qk_ref.shape[4]
    for head in range(heads):
        grad_v = grad_v_ref[head]
        if with_state:
            feat = psi(feature_major(qk_ref, 1, head), False)
            grad_v = grad_v + dot3(state_sum(suffix_refs, head).T, feat)
        held_ref[:, head * DH : (head + 1) * DH] = grad_v.T.astype(bf16)
    chips = keep_ref.shape[0]
    for shift in range(chips):
        chip = lax.rem(at_ref[0] + shift, chips)
        for core, out_ref in ((at_ref[1], keep_ref), (1 - at_ref[1], send_ref)):
            rows = aligned(2 * chip + core, tok)
            out_ref[shift, 0] = attended_ref[rows, :]
            out_ref[shift, 1] = held_ref[rows, :]


def pair_kernel(at_ref, keep_ref, got_ref, *out_refs):
    for shift, out_ref in enumerate(out_refs):
        out_ref[at_ref[1]] = keep_ref[shift]
        out_ref[1 - at_ref[1]] = got_ref[shift]


def unpack_heads_kernel(at_ref, *rest):
    *part_refs, attended_ref, values_ref = rest
    chips, width = len(part_refs), part_refs[0].shape[3]
    for shift, part_ref in enumerate(part_refs):
        chip = lax.rem(at_ref[0] + chips - shift, chips)
        for core in range(2):
            cols = aligned(2 * chip + core, width)
            attended_ref[0, :, cols] = part_ref[core, 0]
            values_ref[0, :, cols] = part_ref[core, 1]


def place_rows(chip_at, core_at, part_refs, cols, held_ref):
    chips, half = len(part_refs) // 2, part_refs[0].shape[0] // 2
    for shift in range(chips):
        chip = lax.rem(chip_at + chips - shift, chips)
        for side, core in ((0, core_at), (1, 1 - core_at)):
            part_ref = part_refs[2 * shift + side]
            for which in range(2):
                rows = aligned(which * 2 * chips + 2 * chip + core, half)
                held_ref[rows, :] = part_ref[which * half : (which + 1) * half, cols]


def product_kernel(group, at_ref, *rest):
    rows_refs, rest = rest[:group], rest[group:]
    tokens_ref, *part_refs, total_ref, held_ref = rest
    place_rows(at_ref[1], at_ref[2], rows_refs, slice(None), held_ref)
    total_ref[...] = dot(tokens_ref[...], held_ref[...], NT)
    count = len(part_refs)
    size = part_refs[0].shape[0]
    for shift, part_ref in enumerate(part_refs):
        owner = lax.rem(at_ref[0] + shift, count)
        part = total_ref[pl.ds(pl.multiple_of(owner * size, size), size), :]
        part_ref[...] = part.astype(part_ref.dtype)


def run_sum_kernel(arrived, at_ref, *rest):
    own_ref, *rest = rest
    total_ref = rest[-1]
    total = own_ref[...]
    for ref in rest[:arrived]:
        total = total + ref[...].astype(f32)
    total_ref[...] = total
    part_refs = rest[arrived:-1]
    size = part_refs[0].shape[0]
    for shift, part_ref in enumerate(part_refs):
        owner = lax.rem(at_ref[0] + shift, len(part_refs))
        part = total_ref[pl.ds(pl.multiple_of(owner * size, size), size), :]
        part_ref[...] = part.astype(part_ref.dtype)


def grad_tokens_kernel(group, at_ref, *rest):
    rows_refs, rest = rest[:group], rest[group:]
    *weight_refs, out_ref, held_ref = rest
    member = 2 * at_ref[0] + at_ref[1]
    place_rows(at_ref[0], at_ref[1], rows_refs, aligned(member, out_ref.shape[1]), held_ref)
    rows = held_ref[...].T
    for i, weight_ref in enumerate(weight_refs):
        size = weight_ref.shape[0]
        first = pl.multiple_of(at_ref[2 + i], size)
        out_ref[0, :, pl.ds(first, size)] = dot(rows, weight_ref[...], NT).astype(bf16)


def final_sum_kernel(own_ref, *rest):
    *part_refs, out_ref = rest
    total = own_ref[...]
    for part_ref in part_refs:
        total = total + part_ref[...].astype(f32)
    out_ref[...] = total


VMEM = pl.BlockSpec(memory_space=pltpu.VMEM)
SMEM = pl.BlockSpec(memory_space=pltpu.SMEM)
FAR = pl.BlockSpec(memory_space=pltpu.HBM)
ANYWHERE = pl.BlockSpec(memory_space=pl.ANY)


def call(
    body,
    outs,
    *operands,
    scalars=(),
    after=(),
    after_far=(),
    scratch=(),
    far_in=(),
    far_out=False,
    copies=(),
):
    at = [jnp.stack([jnp.int32(s) for s in scalars])] if scalars else []
    count = len(at) + len(operands)

    def kernel(*refs):
        ins, rest = refs[:count], refs[count + len(after) + len(after_far) :]
        body(*ins, *rest[: len(outs)], *rest[len(outs) + 1 :])
        rest[len(outs)][...] = jnp.zeros((8, 128), f32)

    *results, token = pl.pallas_call(
        kernel,
        out_shape=[jax.ShapeDtypeStruct(shape, kind) for shape, kind in [*outs, ((8, 128), f32)]],
        in_specs=[SMEM] * len(at)
        + [FAR if i in far_in else VMEM for i in range(len(operands))]
        + [ANYWHERE] * len(after)
        + [FAR] * len(after_far),
        out_specs=[FAR if far_out else VMEM] * len(outs) + [VMEM],
        scratch_shapes=[*scratch] + [pltpu.SemaphoreType.DMA((n,)) for n in copies],
        compiler_params=pltpu.CompilerParams(vmem_limit_bytes=VMEM_LIMIT),
        cost_estimate=pl.CostEstimate(flops=0, bytes_accessed=0, transcendentals=0),
    )(*at, *operands, *after, *after_far)
    return results, token


def local(dp_size, ctx_size, tokens, proj_weight, values, grad_out):
    group = min(GROUP, ctx_size, H)
    runs = ctx_size // group
    heads = H // group
    tok, width = tokens.shape[1:]
    length = group * tok
    cols = proj_weight.shape[1]
    share = width // dp_size
    depth = share // ctx_size
    with_state = runs > 1
    groups = [[run * group + i for i in range(group)] for run in range(runs)]
    wide_groups = [
        [dp * ctx_size + i for dp in range(dp_size) for i in members] for members in groups
    ]
    dp_at, ctx_at = lax.axis_index("dp"), lax.axis_index("ctx")
    run_at, member = ctx_at // group, ctx_at % group

    def exchange(x):
        return lax.all_to_all(
            x, "ctx", split_axis=0, concat_axis=0, tiled=True, axis_index_groups=groups
        )

    def to_dp(x, shift):
        return lax.ppermute(x, "dp", [(i, (i + shift) % dp_size) for i in range(dp_size)])

    def to_member(x, shift):
        pairs = [(i, i - i % group + (i + shift) % group) for i in range(ctx_size)]
        return lax.ppermute(x, "ctx", pairs)

    chips = group // 2
    chip_at = member // 2

    def to_chip(x, shift):
        return x if shift == 0 else to_member(x, 2 * shift)

    def to_other_core(x):
        return lax.ppermute(x, "ctx", [(i, i ^ 1) for i in range(ctx_size)])

    def to_run(x, shift, wrap):
        pairs = [
            (i, (i + shift * group) % ctx_size)
            for i in range(ctx_size)
            if wrap or 0 <= i + shift * group < ctx_size
        ]
        return lax.ppermute(x, "ctx", pairs)

    qk_shape = ((group, 2, heads, F, tok), f32)
    state_shape = ((heads, PSI, DH), bf16)
    blocks_shape = ((2, tok, heads * DH), bf16)
    rows_shape = ((length, heads * DH), f32)

    parts, token = call(
        token_parts_kernel,
        [((tok, share), bf16)] * (dp_size - 1),
        tokens,
        scalars=(dp_at,),
        far_in=(0,),
        far_out=True,
        copies=(dp_size - 1,),
    )
    arrived = [to_dp(part, shift) for shift, part in enumerate(parts, 1)]
    (keep, send), token = call(
        pack_heads_kernel,
        [((chips, 2, tok, heads * DH), bf16)] * 2,
        values,
        grad_out,
        scalars=(chip_at, ctx_at % 2),
        after=(token,),
    )
    parts, heads_token = call(
        pair_kernel,
        [((2, 2, tok, heads * DH), bf16)] * chips,
        keep,
        to_other_core(send),
        scalars=(chip_at, ctx_at % 2),
    )
    (vg,), _ = call(
        collect_heads_kernel,
        [((group, 2, tok, heads * DH), bf16)],
        *[to_chip(part, shift) for shift, part in enumerate(parts)],
        scalars=(chip_at,),
    )
    (projected,), token = call(
        project_kernel,
        [qk_shape],
        tokens,
        proj_weight,
        scalars=(dp_at,),
        after=(token,),
        far_in=(0,),
        copies=(1,),
        scratch=[pltpu.VMEM((tok, share), bf16)],
    )
    (projected,), token = call(
        project_rest_kernel,
        [((dp_size,) + qk_shape[0], f32)],
        projected,
        proj_weight,
        *arrived,
        scalars=(dp_at,),
        after=(heads_token, token),
    )
    part_shape = (tok, dp_size * runs * depth)
    if depth % 128 == 0:
        (keep, send), _ = call(
            functools.partial(pack_tokens_kernel, depth),
            [((chips,) + part_shape, bf16)] * 2,
            tokens,
            scalars=(chip_at, ctx_at % 2),
        )
    else:
        blocks = tokens[0].reshape(tok, dp_size * runs, chips, 2, depth).transpose(2, 3, 0, 1, 4)
        blocks = blocks.reshape(chips, 2, *part_shape)
        blocks = jnp.stack([blocks[(chip_at + shift) % chips] for shift in range(chips)])
        keep, send = blocks[:, ctx_at % 2], blocks[:, 1 - ctx_at % 2]
    token_parts, _ = call(
        pair_kernel,
        [((2,) + part_shape, bf16)] * chips,
        keep,
        to_other_core(send),
        scalars=(chip_at, ctx_at % 2),
        after=(token,),
    )
    token_parts = [to_chip(part, shift) for shift, part in enumerate(token_parts)]
    qk_parts = lax.all_to_all(
        projected.reshape((dp_size * group,) + qk_shape[0][1:]),
        ("dp", "ctx"),
        split_axis=0,
        concat_axis=0,
        tiled=True,
        axis_index_groups=wide_groups,
    ).reshape(projected.shape)

    pair = 2 if ctx_size % 2 == 0 else 1
    parity = ctx_at % pair
    piece = share // pair
    (mine,), token = call(
        weight_piece_kernel,
        [((piece, cols), bf16)],
        proj_weight,
        scalars=(parity,),
        after=(token,),
        far_in=(0,),
        far_out=True,
        copies=(1,),
    )
    fetched = [to_dp(mine, shift) for shift in range(1, dp_size)]
    weights, firsts = [proj_weight], [dp_at * share]
    for shift, half in enumerate(fetched, 1):
        base = (dp_at + dp_size - shift) % dp_size * share
        weights.append(half)
        firsts.append(base + parity * piece)
        if pair == 2:
            weights.append(lax.ppermute(half, "ctx", [(i, i ^ 1) for i in range(ctx_size)]))
            firsts.append(base + (1 - parity) * piece)

    (qk, *state), token = call(
        functools.partial(state_kernel, with_state),
        [qk_shape] + [state_shape] * with_state,
        qk_parts,
        vg,
    )
    prefix, suffix = (), ()
    if with_state:
        prefix = [to_run(state[0], shift, False) for shift in range(1, runs)]
    (numerator,), token = call(numerator_kernel, [rows_shape], qk, vg)
    (attended, grad_num, *carried), token = call(
        functools.partial(normalize_kernel, with_state),
        [((length, heads * DH), bf16), rows_shape] + [state_shape] * with_state,
        qk,
        vg,
        numerator,
        *prefix,
        after_far=token_parts[1:],
    )
    if with_state:
        suffix = [to_run(carried[0], -shift, False) for shift in range(1, runs)]
    (grad_qk, grad_v), token = call(
        functools.partial(backward_kernel, with_state),
        [((2, heads, F, length), f32), ((heads, DH, length), f32)],
        qk,
        vg,
        grad_num,
        *prefix,
        after_far=fetched,
    )
    (token_cols,), token = call(
        collect_tokens_kernel,
        [(part_shape[1:] + (length,), bf16)],
        *token_parts,
        scalars=(chip_at,),
        after=(token,),
    )
    (rows,), token = call(
        functools.partial(rows_kernel, with_state),
        [((2 * heads * F, length), bf16)],
        qk,
        vg,
        grad_qk,
        *suffix,
        after=(token,),
        far_out=True,
        scratch=[pltpu.VMEM((2 * heads * F, length), bf16)],
        copies=(1,),
    )
    rows = [to_chip(rows, shift) for shift in range(chips)]
    rows = [side for part in rows for side in (part, to_other_core(part))]
    (keep, send), token = call(
        functools.partial(grad_values_kernel, with_state),
        [((chips, 2, tok, heads * DH), bf16)] * 2,
        qk,
        attended,
        grad_v,
        *suffix,
        scalars=(chip_at, ctx_at % 2),
        after_far=rows[4::2],
        scratch=[pltpu.VMEM((length, heads * DH), bf16)],
    )
    got = to_other_core(send)
    results, token = call(
        pair_kernel,
        [((2, 2, tok, heads * DH), bf16)] * chips,
        keep,
        got,
        scalars=(chip_at, ctx_at % 2),
    )
    results = [to_chip(part, shift) for shift, part in enumerate(results)]

    held = pltpu.VMEM((cols, length), bf16)
    (own, *parts), token = call(
        functools.partial(product_kernel, 2 * chips),
        [((runs * depth, cols), f32)] + [((runs * depth, cols), bf16)] * (dp_size - 1),
        *rows,
        token_cols,
        scalars=(dp_at, chip_at, ctx_at % 2),
        after=(token,),
        scratch=[pltpu.VMEM((dp_size * runs * depth, cols), f32), held],
    )
    parts = [to_dp(part, shift) for shift, part in enumerate(parts, 1)]
    (grad_tokens,), tokens_token = call(
        functools.partial(grad_tokens_kernel, 2 * chips),
        [((1, tok, width), bf16)],
        *rows,
        *weights,
        scalars=(chip_at, ctx_at % 2, *firsts),
        after=(token,),
        scratch=[pltpu.VMEM((cols, tok), bf16)],
    )
    (grad_proj, *parts), token = call(
        functools.partial(run_sum_kernel, len(parts)),
        [((depth, cols), f32)] + [((depth, cols), bf16)] * (runs - 1),
        own,
        *parts,
        scalars=(run_at,),
        after=(tokens_token,),
        scratch=[pltpu.VMEM((runs * depth, cols), f32)],
    )
    (attended, grad_values), token = call(
        unpack_heads_kernel,
        [((1, tok, H * DH), bf16)] * 2,
        *results,
        scalars=(chip_at,),
        after=(token,),
    )
    (grad_proj,), _ = call(
        final_sum_kernel,
        [((depth, cols), f32)],
        grad_proj,
        *[to_run(part, shift, True) for shift, part in enumerate(parts, 1)],
        after=(token,),
    )
    return (attended, grad_tokens, grad_values, grad_proj)


def solution(mesh):
    return jax.shard_map(
        functools.partial(local, mesh.shape["dp"], mesh.shape["ctx"]),
        mesh=mesh,
        in_specs=(P("dp", "ctx", None), P("dp", None), P("dp", "ctx", None), P("dp", "ctx", None)),
        out_specs=(
            P("dp", "ctx", None),
            P("dp", "ctx", None),
            P("dp", "ctx", None),
            P(("dp", "ctx"), None),
        ),
        check_vma=False,
    )
```

```python
import functools

import jax
import jax.numpy as jnp
from jax import lax
from jax.experimental import pallas as pl
from jax.experimental.pallas import tpu as pltpu
from jax.sharding import PartitionSpec as P

H = 16
F = 16
DH = 128
EPSILON = 1e-05
GROUP = 8
TILE = 256
VMEM_LIMIT = 16 * 1024 * 1024
PSI = 9 * F + 2 * F
PSI_SCALE = (0.5,) + (1.0,) * 7 + (0.5,)

f32 = jnp.float32
bf16 = jnp.bfloat16

NN = (((1,), (0,)), ((), ()))
NT = (((1,), (1,)), ((), ()))


def dot(a, b, dims=NN):
    return lax.dot_general(a, b, dims, preferred_element_type=f32)


def split(x):
    high = x.astype(bf16)
    return high, (x - high.astype(f32)).astype(bf16)


def dot3(a, b, dims=NN):
    a_high, a_low = split(a)
    b_high, b_low = split(b)
    return dot(a_high, b_high, dims) + (dot(a_high, b_low, dims) + dot(a_low, b_high, dims))


def turned(x, r):
    return x if r == 0 else jnp.concatenate([x[r:], x[:r]], axis=0)


def psi(x, weights):
    parts = []
    for r in range(9):
        part = x * turned(x, r)
        parts.append(part * PSI_SCALE[r] if weights and PSI_SCALE[r] != 1.0 else part)
    row = lax.broadcasted_iota(jnp.int32, x.shape, 0)
    return jnp.concatenate(parts + [x, jnp.where(row == 0, 1.0, 0.0)], axis=0)


def pull_psi(x, upstream, weights):
    total = upstream[9 * F : 10 * F]
    for r in range(9):
        part = upstream[r * F : (r + 1) * F]
        if weights and PSI_SCALE[r] != 1.0:
            part = part * PSI_SCALE[r]
        total = total + part * turned(x, r) + turned(part * x, (F - r) % F)
    return total


def feature_major(qk_ref, which, head):
    return jnp.concatenate([qk_ref[src, which, head] for src in range(qk_ref.shape[0])], axis=1)


def rows_of(ref, which, head, start, stop):
    tok = ref.shape[2]
    return jnp.concatenate(
        [
            ref[src, which, :, head * DH : (head + 1) * DH]
            for src in range(start // tok, stop // tok)
        ],
        axis=0,
    )


def score_sides(q, k):
    q_high, q_low = split(q)
    k_high, k_low = split(k)
    left = jnp.concatenate([q_high, q_high, q_low, q_low], axis=0)
    right = jnp.concatenate([k_high, k_low, k_high, k_low], axis=0)
    return left.T, right


def causal_mask(tile, width):
    row = lax.broadcasted_iota(jnp.int32, (tile, width), 0) + (width - tile)
    return row >= lax.broadcasted_iota(jnp.int32, (tile, width), 1)


def run_copies(sems, pairs):
    copies = [
        pltpu.make_async_copy(source, target, sems.at[i])
        for i, (source, target) in enumerate(pairs)
    ]
    for copy in copies:
        copy.start()
    for copy in copies:
        copy.wait()


def aligned(at, size):
    return pl.ds(pl.multiple_of(at * size, size), size)


def token_parts_kernel(at_ref, tokens_ref, *rest):
    *out_refs, sems = rest
    count, share = len(out_refs) + 1, out_refs[0].shape[1]
    run_copies(
        sems,
        [
            (tokens_ref.at[0, :, aligned(lax.rem(at_ref[0] + shift, count), share)], out_ref)
            for shift, out_ref in enumerate(out_refs, 1)
        ],
    )


def pack_heads_kernel(at_ref, values_ref, grad_ref, *out_refs):
    chips, width = len(out_refs), out_refs[0].shape[3]
    for shift, out_ref in enumerate(out_refs):
        chip = lax.rem(at_ref[0] + shift, chips)
        for core in range(2):
            cols = aligned(2 * chip + core, width)
            out_ref[core, 0] = values_ref[0, :, cols]
            out_ref[core, 1] = grad_ref[0, :, cols]


def split_cores_kernel(at_ref, *rest):
    *part_refs, keep_ref, send_ref = rest
    for shift, part_ref in enumerate(part_refs):
        keep_ref[shift] = part_ref[at_ref[1]]
        send_ref[shift] = part_ref[1 - at_ref[1]]


def collect_heads_kernel(at_ref, keep_ref, got_ref, out_ref):
    chips = keep_ref.shape[0]
    for shift in range(chips):
        chip = lax.rem(at_ref[0] + chips - shift, chips)
        out_ref[2 * chip + at_ref[1]] = keep_ref[shift]
        out_ref[2 * chip + 1 - at_ref[1]] = got_ref[shift]


def pack_tokens_kernel(depth, at_ref, tokens_ref, keep_ref, send_ref):
    chips, _, rows = keep_ref.shape
    for shift in range(chips):
        chip = lax.rem(at_ref[0] + shift, chips)
        for core, out_ref in ((at_ref[1], keep_ref), (1 - at_ref[1], send_ref)):
            for part in range(rows // depth):
                cols = aligned(2 * (part * chips + chip) + core, depth)
                out_ref[shift, :, part * depth : (part + 1) * depth] = tokens_ref[0, :, cols]


def collect_tokens_kernel(at_ref, *rest):
    *part_refs, out_ref = rest
    chips, tok = len(part_refs), part_refs[0].shape[1]
    for shift, part_ref in enumerate(part_refs):
        chip = lax.rem(at_ref[0] + chips - shift, chips)
        for core in range(2):
            out_ref[:, aligned(2 * chip + core, tok)] = part_ref[core].T


def write_blocks(projected, out_ref):
    group, _, heads, feat, _ = out_ref.shape
    for member in range(group):
        for which in range(2):
            for head in range(heads):
                first = ((which * group + member) * heads + head) * feat
                out_ref[member, which, head] = projected[first : first + feat]


def project_kernel(at_ref, tokens_ref, weight_ref, out_ref, part_ref, sem):
    share = part_ref.shape[1]
    run_copies(sem, [(tokens_ref.at[0, :, aligned(at_ref[0], share)], part_ref)])
    write_blocks(dot(part_ref[...], weight_ref[...]).T, out_ref)


def project_rest_kernel(at_ref, own_ref, weight_ref, *rest):
    *part_refs, out_ref = rest
    count = len(part_refs) + 1
    at = at_ref[0]
    out_ref[at] = own_ref[...]
    for shift, part_ref in enumerate(part_refs, 1):
        owner = lax.rem(at + count - shift, count)
        write_blocks(dot(part_ref[...], weight_ref[...]).T, out_ref.at[owner])


def weight_piece_kernel(at_ref, weight_ref, out_ref, sems):
    run_copies(sems, [(weight_ref.at[aligned(at_ref[0], out_ref.shape[0])], out_ref)])


def state_sum(refs, head):
    total = refs[0][head].astype(f32)
    for ref in refs[1:]:
        total = total + ref[head].astype(f32)
    return total


def state_kernel(with_state, parts_ref, vg_ref, qk_ref, *state_refs):
    count, blocks, _, heads, _, tok = parts_ref.shape
    for head in range(heads):
        for which in range(2):
            for src in range(blocks):
                total = parts_ref[0, src, which, head]
                for part in range(1, count):
                    total = total + parts_ref[part, src, which, head]
                qk_ref[src, which, head] = total
        if with_state:
            high, low = split(psi(feature_major(qk_ref, 1, head), False))
            v = rows_of(vg_ref, 0, head, 0, blocks * tok)
            state_refs[0][head] = (dot(high, v) + dot(low, v)).astype(bf16)


def numerator_kernel(qk_ref, vg_ref, num_ref):
    heads = qk_ref.shape[2]
    length = qk_ref.shape[0] * qk_ref.shape[4]
    tile = min(TILE, length)
    for head in range(heads):
        q = feature_major(qk_ref, 0, head) * 0.25
        k = feature_major(qk_ref, 1, head)
        left, right = score_sides(q, k)
        for at in range(0, length, tile):
            width = at + tile
            scores = dot(left[at:width], right[:, :width])
            kernel = jnp.where(
                causal_mask(tile, width), 1.0 + scores * (1.0 + 0.5 * scores), 0.0
            )
            high, low = split(kernel)
            v = rows_of(vg_ref, 0, head, 0, width)
            num_ref[at:width, head * DH : (head + 1) * DH] = dot(high, v) + dot(low, v)


def normalize_kernel(with_state, qk_ref, vg_ref, num_ref, *rest):
    if with_state:
        *prefix_refs, attended_ref, grad_ref, carried_ref = rest
    else:
        attended_ref, grad_ref = rest
    heads = qk_ref.shape[2]
    blocks, tok = qk_ref.shape[0], qk_ref.shape[4]
    length = blocks * tok
    for head in range(heads):
        cols = slice(head * DH, (head + 1) * DH)
        numerator = num_ref[:, cols]
        if with_state:
            feat = psi(feature_major(qk_ref, 0, head) * 0.25, True)
            numerator = numerator + dot3(feat.T, state_sum(prefix_refs, head))
        inv_rms = lax.rsqrt(jnp.mean(numerator * numerator, axis=-1, keepdims=True) + EPSILON)
        normed = numerator * inv_rms
        upstream = rows_of(vg_ref, 1, head, 0, length).astype(f32)
        grad = inv_rms * (
            upstream - normed * jnp.mean(normed * upstream, axis=-1, keepdims=True)
        )
        attended_ref[:, cols] = normed.astype(bf16)
        grad_ref[:, cols] = grad
        if with_state:
            carried_ref[head] = dot3(feat, grad).astype(bf16)


def backward_kernel(with_state, qk_ref, vg_ref, grad_ref, *rest):
    *prefix_refs, grad_qk_ref, grad_v_ref = rest
    length = qk_ref.shape[0] * qk_ref.shape[4]
    tile = min(TILE, length)
    for head in range(grad_v_ref.shape[0]):
        cols = slice(head * DH, (head + 1) * DH)
        q = feature_major(qk_ref, 0, head) * 0.25
        k = feature_major(qk_ref, 1, head)
        left, right = score_sides(q, k)
        q_both = jnp.concatenate(split(q), axis=0)
        k_both = jnp.concatenate(split(k), axis=0)
        grad = grad_ref[:, cols]
        grad_t = grad.T
        if with_state:
            grad_q = pull_psi(q, dot3(state_sum(prefix_refs, head), grad_t), True)
        for at in reversed(range(0, length, tile)):
            width = at + tile
            scores = dot(left[at:width], right[:, :width])
            causal = causal_mask(tile, width)
            v = rows_of(vg_ref, 0, head, 0, width)
            high, low = split(grad[at:width])
            mixing = dot(
                jnp.concatenate([high, low], axis=1), jnp.concatenate([v, v], axis=1), NT
            )
            more = 1.0 + scores
            slopes = split(jnp.where(causal, mixing * more, 0.0))
            kernels = split(jnp.where(causal, more + 0.5 * scores * scores, 0.0))
            both = dot(k_both[:, :width], slopes[0], NT)
            piece = both[:F] + (both[F:] + dot(k_both[:F, :width], slopes[1], NT))
            if with_state:
                piece = piece + grad_q[:, at:width]
            grad_qk_ref[0, head, :, at:width] = piece * 0.25
            both = dot(q_both[:, at:width], slopes[0])
            piece_k = both[:F] + (both[F:] + dot(q_both[:F, at:width], slopes[1]))
            high, low = split(grad_t[:, at:width])
            both = dot(jnp.concatenate([high, low], axis=0), kernels[0])
            piece_v = both[:DH] + (both[DH:] + dot(high, kernels[1]))
            if width == length:
                grad_qk_ref[1, head] = piece_k
                grad_v_ref[head] = piece_v
            else:
                grad_qk_ref[1, head, :, :width] += piece_k
                grad_v_ref[head, :, :width] += piece_v


def rows_kernel(with_state, at_ref, qk_ref, vg_ref, attended_ref, grad_qk_ref, grad_v_ref, *rest):
    *suffix_refs, rows_ref, keep_ref, send_ref, held_ref = rest
    heads, tok = qk_ref.shape[2], qk_ref.shape[4]
    length = qk_ref.shape[0] * tok
    for head in range(heads):
        grad_k, grad_v = grad_qk_ref[1, head], grad_v_ref[head]
        if with_state:
            k = feature_major(qk_ref, 1, head)
            v = rows_of(vg_ref, 0, head, 0, length)
            suffix = state_sum(suffix_refs, head)
            high, low = split(suffix)
            grad_k = grad_k + pull_psi(k, dot(high, v, NT) + dot(low, v, NT), False)
            grad_v = grad_v + dot3(suffix.T, psi(k, False))
        rows_ref[head * F : (head + 1) * F] = grad_qk_ref[0, head].astype(bf16)
        rows_ref[(heads + head) * F : (heads + head + 1) * F] = grad_k.astype(bf16)
        held_ref[:, head * DH : (head + 1) * DH] = grad_v.T.astype(bf16)
    chips = keep_ref.shape[0]
    for shift in range(chips):
        chip = lax.rem(at_ref[0] + shift, chips)
        for core, out_ref in ((at_ref[1], keep_ref), (1 - at_ref[1], send_ref)):
            block = aligned(2 * chip + core, tok)
            out_ref[shift, 0] = attended_ref[block, :]
            out_ref[shift, 1] = held_ref[block, :]


def pair_kernel(at_ref, keep_ref, got_ref, *out_refs):
    for shift, out_ref in enumerate(out_refs):
        out_ref[at_ref[1]] = keep_ref[shift]
        out_ref[1 - at_ref[1]] = got_ref[shift]


def unpack_heads_kernel(at_ref, *rest):
    *part_refs, attended_ref, values_ref = rest
    chips, width = len(part_refs), part_refs[0].shape[3]
    for shift, part_ref in enumerate(part_refs):
        chip = lax.rem(at_ref[0] + chips - shift, chips)
        for core in range(2):
            cols = aligned(2 * chip + core, width)
            attended_ref[0, :, cols] = part_ref[core, 0]
            values_ref[0, :, cols] = part_ref[core, 1]


def place_rows(chip_at, core_at, part_refs, held_ref):
    chips, half = len(part_refs) // 2, part_refs[0].shape[0] // 2
    for shift in range(chips):
        chip = lax.rem(chip_at + chips - shift, chips)
        for side, core in ((0, core_at), (1, 1 - core_at)):
            part_ref = part_refs[2 * shift + side]
            for which in range(2):
                rows = aligned(which * 2 * chips + 2 * chip + core, half)
                held_ref[rows, :] = part_ref[which * half : (which + 1) * half, :]


def product_kernel(group, at_ref, *rest):
    rows_refs, rest = rest[:group], rest[group:]
    tokens_ref, own_rows_ref, *part_refs, total_ref, held_ref = rest
    place_rows(at_ref[1], at_ref[2], rows_refs, held_ref)
    total_ref[...] = dot(tokens_ref[...], held_ref[...], NT)
    tok = own_rows_ref.shape[0]
    own_rows_ref[...] = held_ref[:, aligned(2 * at_ref[1] + at_ref[2], tok)].T
    count = len(part_refs)
    size = part_refs[0].shape[0]
    for shift, part_ref in enumerate(part_refs):
        owner = lax.rem(at_ref[0] + shift, count)
        part = total_ref[pl.ds(pl.multiple_of(owner * size, size), size), :]
        part_ref[...] = part.astype(part_ref.dtype)


def run_sum_kernel(arrived, at_ref, *rest):
    own_ref, *rest = rest
    total_ref = rest[-1]
    total = own_ref[...]
    for ref in rest[:arrived]:
        total = total + ref[...].astype(f32)
    total_ref[...] = total
    part_refs = rest[arrived:-1]
    size = part_refs[0].shape[0]
    for shift, part_ref in enumerate(part_refs):
        owner = lax.rem(at_ref[0] + shift, len(part_refs))
        part = total_ref[pl.ds(pl.multiple_of(owner * size, size), size), :]
        part_ref[...] = part.astype(part_ref.dtype)


def grad_tokens_kernel(at_ref, rows_ref, *rest):
    *weight_refs, out_ref = rest
    for i, weight_ref in enumerate(weight_refs):
        size = weight_ref.shape[0]
        first = pl.multiple_of(at_ref[i], size)
        out_ref[0, :, pl.ds(first, size)] = dot(rows_ref[...], weight_ref[...], NT).astype(bf16)


def final_sum_kernel(own_ref, *rest):
    *part_refs, out_ref = rest
    total = own_ref[...]
    for part_ref in part_refs:
        total = total + part_ref[...].astype(f32)
    out_ref[...] = total


VMEM = pl.BlockSpec(memory_space=pltpu.VMEM)
SMEM = pl.BlockSpec(memory_space=pltpu.SMEM)
FAR = pl.BlockSpec(memory_space=pltpu.HBM)
ANYWHERE = pl.BlockSpec(memory_space=pl.ANY)


def call(
    body,
    outs,
    *operands,
    scalars=(),
    after=(),
    after_far=(),
    scratch=(),
    far_in=(),
    far_out=False,
    copies=(),
):
    at = [jnp.stack([jnp.int32(s) for s in scalars])] if scalars else []
    count = len(at) + len(operands)

    def kernel(*refs):
        ins, rest = refs[:count], refs[count + len(after) + len(after_far) :]
        body(*ins, *rest[: len(outs)], *rest[len(outs) + 1 :])
        rest[len(outs)][...] = jnp.zeros((8, 128), f32)

    *results, token = pl.pallas_call(
        kernel,
        out_shape=[jax.ShapeDtypeStruct(shape, kind) for shape, kind in [*outs, ((8, 128), f32)]],
        in_specs=[SMEM] * len(at)
        + [FAR if i in far_in else VMEM for i in range(len(operands))]
        + [ANYWHERE] * len(after)
        + [FAR] * len(after_far),
        out_specs=[FAR if far_out else VMEM] * len(outs) + [VMEM],
        scratch_shapes=[*scratch] + [pltpu.SemaphoreType.DMA((n,)) for n in copies],
        compiler_params=pltpu.CompilerParams(vmem_limit_bytes=VMEM_LIMIT),
        cost_estimate=pl.CostEstimate(flops=0, bytes_accessed=0, transcendentals=0),
    )(*at, *operands, *after, *after_far)
    return results, token


def local(dp_size, ctx_size, tokens, proj_weight, values, grad_out):
    group = min(GROUP, ctx_size, H)
    runs = ctx_size // group
    heads = H // group
    tok, width = tokens.shape[1:]
    length = group * tok
    cols = proj_weight.shape[1]
    share = width // dp_size
    depth = share // ctx_size
    with_state = runs > 1
    groups = [[run * group + i for i in range(group)] for run in range(runs)]
    wide_groups = [
        [dp * ctx_size + i for dp in range(dp_size) for i in members] for members in groups
    ]
    dp_at, ctx_at = lax.axis_index("dp"), lax.axis_index("ctx")
    run_at, member = ctx_at // group, ctx_at % group

    def exchange(x):
        return lax.all_to_all(
            x, "ctx", split_axis=0, concat_axis=0, tiled=True, axis_index_groups=groups
        )

    def to_dp(x, shift):
        return lax.ppermute(x, "dp", [(i, (i + shift) % dp_size) for i in range(dp_size)])

    def to_member(x, shift):
        pairs = [(i, i - i % group + (i + shift) % group) for i in range(ctx_size)]
        return lax.ppermute(x, "ctx", pairs)

    chips = group // 2
    chip_at, core_at = member // 2, member % 2

    def to_chip(x, shift):
        return x if shift == 0 else to_member(x, 2 * shift)

    def to_other_core(x):
        return lax.ppermute(x, "ctx", [(i, i ^ 1) for i in range(ctx_size)])

    def to_run(x, shift, wrap):
        pairs = [
            (i, (i + shift * group) % ctx_size)
            for i in range(ctx_size)
            if wrap or 0 <= i + shift * group < ctx_size
        ]
        return lax.ppermute(x, "ctx", pairs)

    qk_shape = ((group, 2, heads, F, tok), f32)
    state_shape = ((heads, PSI, DH), bf16)
    blocks_shape = ((2, tok, heads * DH), bf16)
    rows_shape = ((length, heads * DH), f32)

    parts, token = call(
        token_parts_kernel,
        [((tok, share), bf16)] * (dp_size - 1),
        tokens,
        scalars=(dp_at,),
        far_in=(0,),
        far_out=True,
        copies=(dp_size - 1,),
    )
    arrived = [to_dp(part, shift) for shift, part in enumerate(parts, 1)]
    parts, token = call(
        pack_heads_kernel,
        [((2, 2, tok, heads * DH), bf16)] * chips,
        values,
        grad_out,
        scalars=(chip_at, core_at),
        after=(token,),
    )
    (keep, send), heads_token = call(
        split_cores_kernel,
        [((chips, 2, tok, heads * DH), bf16)] * 2,
        *[to_chip(part, shift) for shift, part in enumerate(parts)],
        scalars=(chip_at, core_at),
    )
    (vg,), _ = call(
        collect_heads_kernel,
        [((group, 2, tok, heads * DH), bf16)],
        keep,
        to_other_core(send),
        scalars=(chip_at, core_at),
    )
    (projected,), token = call(
        project_kernel,
        [qk_shape],
        tokens,
        proj_weight,
        scalars=(dp_at,),
        after=(token,),
        far_in=(0,),
        copies=(1,),
        scratch=[pltpu.VMEM((tok, share), bf16)],
    )
    (projected,), token = call(
        project_rest_kernel,
        [((dp_size,) + qk_shape[0], f32)],
        projected,
        proj_weight,
        *arrived,
        scalars=(dp_at,),
        after=(heads_token, token),
    )
    part_shape = (tok, dp_size * runs * depth)
    if depth % 128 == 0:
        (keep, send), _ = call(
            functools.partial(pack_tokens_kernel, depth),
            [((chips,) + part_shape, bf16)] * 2,
            tokens,
            scalars=(chip_at, core_at),
        )
    else:
        blocks = tokens[0].reshape(tok, dp_size * runs, chips, 2, depth).transpose(2, 3, 0, 1, 4)
        blocks = blocks.reshape(chips, 2, *part_shape)
        blocks = jnp.stack([blocks[(chip_at + shift) % chips] for shift in range(chips)])
        keep, send = blocks[:, core_at], blocks[:, 1 - core_at]
    token_parts, _ = call(
        pair_kernel,
        [((2,) + part_shape, bf16)] * chips,
        keep,
        to_other_core(send),
        scalars=(chip_at, core_at),
        after=(token,),
    )
    token_parts = [to_chip(part, shift) for shift, part in enumerate(token_parts)]
    qk_parts = lax.all_to_all(
        projected.reshape((dp_size * group,) + qk_shape[0][1:]),
        ("dp", "ctx"),
        split_axis=0,
        concat_axis=0,
        tiled=True,
        axis_index_groups=wide_groups,
    ).reshape(projected.shape)

    pair = 2 if ctx_size % 2 == 0 else 1
    parity = ctx_at % pair
    piece = share // pair
    (mine,), token = call(
        weight_piece_kernel,
        [((piece, cols), bf16)],
        proj_weight,
        scalars=(parity,),
        after=(token,),
        far_in=(0,),
        far_out=True,
        copies=(1,),
    )
    fetched = [to_dp(mine, shift) for shift in range(1, dp_size)]
    weights, firsts = [proj_weight], [dp_at * share]
    for shift, half in enumerate(fetched, 1):
        base = (dp_at + dp_size - shift) % dp_size * share
        weights.append(half)
        firsts.append(base + parity * piece)
        if pair == 2:
            weights.append(lax.ppermute(half, "ctx", [(i, i ^ 1) for i in range(ctx_size)]))
            firsts.append(base + (1 - parity) * piece)

    (qk, *state), token = call(
        functools.partial(state_kernel, with_state),
        [qk_shape] + [state_shape] * with_state,
        qk_parts,
        vg,
    )
    prefix, suffix = (), ()
    if with_state:
        prefix = [to_run(state[0], shift, False) for shift in range(1, runs)]
    (numerator,), token = call(numerator_kernel, [rows_shape], qk, vg)
    (attended, grad_num, *carried), token = call(
        functools.partial(normalize_kernel, with_state),
        [((length, heads * DH), bf16), rows_shape] + [state_shape] * with_state,
        qk,
        vg,
        numerator,
        *prefix,
        after_far=token_parts[1:],
    )
    if with_state:
        suffix = [to_run(carried[0], -shift, False) for shift in range(1, runs)]
    (grad_qk, grad_v), token = call(
        functools.partial(backward_kernel, with_state),
        [((2, heads, F, length), f32), ((heads, DH, length), f32)],
        qk,
        vg,
        grad_num,
        *prefix,
        after_far=fetched,
    )
    (token_cols,), token = call(
        collect_tokens_kernel,
        [(part_shape[1:] + (length,), bf16)],
        *token_parts,
        scalars=(chip_at,),
        after=(token,),
    )
    (rows, keep, send), token = call(
        functools.partial(rows_kernel, with_state),
        [((2 * heads * F, length), bf16)] + [((chips, 2, tok, heads * DH), bf16)] * 2,
        qk,
        vg,
        attended,
        grad_qk,
        grad_v,
        *suffix,
        scalars=(chip_at, core_at),
        after=(token,),
        scratch=[pltpu.VMEM((length, heads * DH), bf16)],
    )
    rows = [to_chip(rows, shift) for shift in range(chips)]
    rows = [side for part in rows for side in (part, to_other_core(part))]
    got = to_other_core(send)
    results, token = call(
        pair_kernel,
        [((2, 2, tok, heads * DH), bf16)] * chips,
        keep,
        got,
        scalars=(chip_at, core_at),
    )
    results = [to_chip(part, shift) for shift, part in enumerate(results)]

    held = pltpu.VMEM((cols, length), bf16)
    (own_rows, own, *parts), token = call(
        functools.partial(product_kernel, 2 * chips),
        [((tok, cols), bf16), ((runs * depth, cols), f32)] + [((runs * depth, cols), bf16)] * (dp_size - 1),
        *rows,
        token_cols,
        scalars=(dp_at, chip_at, core_at),
        after=(token,),
        scratch=[pltpu.VMEM((dp_size * runs * depth, cols), f32), held],
    )
    parts = [to_dp(part, shift) for shift, part in enumerate(parts, 1)]
    (grad_tokens,), tokens_token = call(
        grad_tokens_kernel,
        [((1, tok, width), bf16)],
        own_rows,
        *weights,
        scalars=firsts,
        after=(token,),
    )
    (grad_proj, *parts), token = call(
        functools.partial(run_sum_kernel, len(parts)),
        [((depth, cols), f32)] + [((depth, cols), bf16)] * (runs - 1),
        own,
        *parts,
        scalars=(run_at,),
        after=(tokens_token,),
        scratch=[pltpu.VMEM((runs * depth, cols), f32)],
    )
    (attended, grad_values), token = call(
        unpack_heads_kernel,
        [((1, tok, H * DH), bf16)] * 2,
        *results,
        scalars=(chip_at,),
        after=(token,),
    )
    (grad_proj,), _ = call(
        final_sum_kernel,
        [((depth, cols), f32)],
        grad_proj,
        *[to_run(part, shift, True) for shift, part in enumerate(parts, 1)],
        after=(token,),
    )
    return (attended, grad_tokens, grad_values, grad_proj)


def solution(mesh):
    return jax.shard_map(
        functools.partial(local, mesh.shape["dp"], mesh.shape["ctx"]),
        mesh=mesh,
        in_specs=(P("dp", "ctx", None), P("dp", None), P("dp", "ctx", None), P("dp", "ctx", None)),
        out_specs=(
            P("dp", "ctx", None),
            P("dp", "ctx", None),
            P("dp", "ctx", None),
            P(("dp", "ctx"), None),
        ),
        check_vma=False,
    )
```

```python
import functools

import jax
import jax.numpy as jnp
from jax import lax
from jax.experimental import pallas as pl
from jax.experimental.pallas import tpu as pltpu
from jax.sharding import PartitionSpec as P

H = 16
F = 16
DH = 128
EPSILON = 1e-05
GROUP = 8
TILE = 256
VMEM_LIMIT = 16 * 1024 * 1024
PSI = 9 * F + 2 * F
PSI_SCALE = (0.5,) + (1.0,) * 7 + (0.5,)

f32 = jnp.float32
bf16 = jnp.bfloat16

NN = (((1,), (0,)), ((), ()))
NT = (((1,), (1,)), ((), ()))


def dot(a, b, dims=NN):
    return lax.dot_general(a, b, dims, preferred_element_type=f32)


def split(x):
    high = x.astype(bf16)
    return high, (x - high.astype(f32)).astype(bf16)


def dot3(a, b, dims=NN):
    a_high, a_low = split(a)
    b_high, b_low = split(b)
    return dot(a_high, b_high, dims) + (dot(a_high, b_low, dims) + dot(a_low, b_high, dims))


def turned(x, r):
    return x if r == 0 else jnp.concatenate([x[r:], x[:r]], axis=0)


def psi(x, weights):
    parts = []
    for r in range(9):
        part = x * turned(x, r)
        parts.append(part * PSI_SCALE[r] if weights and PSI_SCALE[r] != 1.0 else part)
    row = lax.broadcasted_iota(jnp.int32, x.shape, 0)
    return jnp.concatenate(parts + [x, jnp.where(row == 0, 1.0, 0.0)], axis=0)


def pull_psi(x, upstream, weights):
    total = upstream[9 * F : 10 * F]
    for r in range(9):
        part = upstream[r * F : (r + 1) * F]
        if weights and PSI_SCALE[r] != 1.0:
            part = part * PSI_SCALE[r]
        total = total + part * turned(x, r) + turned(part * x, (F - r) % F)
    return total


def feature_major(qk_ref, which, head):
    return jnp.concatenate([qk_ref[src, which, head] for src in range(qk_ref.shape[0])], axis=1)


def rows_of(ref, which, head, start, stop):
    tok = ref.shape[2]
    return jnp.concatenate(
        [
            ref[src, which, :, head * DH : (head + 1) * DH]
            for src in range(start // tok, stop // tok)
        ],
        axis=0,
    )


def score_sides(q, k):
    q_high, q_low = split(q)
    k_high, k_low = split(k)
    left = jnp.concatenate([q_high, q_high, q_low, q_low], axis=0)
    right = jnp.concatenate([k_high, k_low, k_high, k_low], axis=0)
    return left.T, right


def causal_mask(tile, width):
    row = lax.broadcasted_iota(jnp.int32, (tile, width), 0) + (width - tile)
    return row >= lax.broadcasted_iota(jnp.int32, (tile, width), 1)


def run_copies(sems, pairs):
    copies = [
        pltpu.make_async_copy(source, target, sems.at[i])
        for i, (source, target) in enumerate(pairs)
    ]
    for copy in copies:
        copy.start()
    for copy in copies:
        copy.wait()


def aligned(at, size):
    return pl.ds(pl.multiple_of(at * size, size), size)


def token_parts_kernel(at_ref, tokens_ref, *rest):
    *out_refs, sems = rest
    count, share = len(out_refs) + 1, out_refs[0].shape[1]
    run_copies(
        sems,
        [
            (tokens_ref.at[0, :, aligned(lax.rem(at_ref[0] + shift, count), share)], out_ref)
            for shift, out_ref in enumerate(out_refs, 1)
        ],
    )


def pack_heads_kernel(at_ref, values_ref, grad_ref, *out_refs):
    chips, width = len(out_refs), out_refs[0].shape[3]
    for shift, out_ref in enumerate(out_refs):
        chip = lax.rem(at_ref[0] + shift, chips)
        for core in range(2):
            cols = aligned(2 * chip + core, width)
            out_ref[core, 0] = values_ref[0, :, cols]
            out_ref[core, 1] = grad_ref[0, :, cols]


def split_cores_kernel(at_ref, *rest):
    *part_refs, keep_ref, send_ref = rest
    for shift, part_ref in enumerate(part_refs):
        keep_ref[shift] = part_ref[at_ref[1]]
        send_ref[shift] = part_ref[1 - at_ref[1]]


def collect_heads_kernel(at_ref, keep_ref, got_ref, out_ref):
    chips = keep_ref.shape[0]
    for shift in range(chips):
        chip = lax.rem(at_ref[0] + chips - shift, chips)
        out_ref[2 * chip + at_ref[1]] = keep_ref[shift]
        out_ref[2 * chip + 1 - at_ref[1]] = got_ref[shift]


def pack_tokens_kernel(depth, at_ref, tokens_ref, keep_ref, send_ref):
    chips, _, rows = keep_ref.shape
    for shift in range(chips):
        chip = lax.rem(at_ref[0] + shift, chips)
        for core, out_ref in ((at_ref[1], keep_ref), (1 - at_ref[1], send_ref)):
            for part in range(rows // depth):
                cols = aligned(2 * (part * chips + chip) + core, depth)
                out_ref[shift, :, part * depth : (part + 1) * depth] = tokens_ref[0, :, cols]


def collect_tokens_kernel(at_ref, *rest):
    *part_refs, out_ref = rest
    chips, tok = len(part_refs), part_refs[0].shape[1]
    for shift, part_ref in enumerate(part_refs):
        chip = lax.rem(at_ref[0] + chips - shift, chips)
        for core in range(2):
            out_ref[:, aligned(2 * chip + core, tok)] = part_ref[core].T


def write_blocks(projected, out_ref):
    group, _, heads, feat, _ = out_ref.shape
    for member in range(group):
        for which in range(2):
            for head in range(heads):
                first = ((which * group + member) * heads + head) * feat
                out_ref[member, which, head] = projected[first : first + feat]


def project_kernel(at_ref, tokens_ref, weight_ref, out_ref, part_ref, sem):
    share = part_ref.shape[1]
    run_copies(sem, [(tokens_ref.at[0, :, aligned(at_ref[0], share)], part_ref)])
    write_blocks(dot(part_ref[...], weight_ref[...]).T, out_ref)


def project_rest_kernel(at_ref, own_ref, weight_ref, *rest):
    *part_refs, out_ref = rest
    count = len(part_refs) + 1
    at = at_ref[0]
    out_ref[at] = own_ref[...]
    for shift, part_ref in enumerate(part_refs, 1):
        owner = lax.rem(at + count - shift, count)
        write_blocks(dot(part_ref[...], weight_ref[...]).T, out_ref.at[owner])


def weight_piece_kernel(at_ref, weight_ref, out_ref, sems):
    run_copies(sems, [(weight_ref.at[aligned(at_ref[0], out_ref.shape[0])], out_ref)])


def state_sum(refs, head):
    total = refs[0][head].astype(f32)
    for ref in refs[1:]:
        total = total + ref[head].astype(f32)
    return total


def state_kernel(with_state, parts_ref, vg_ref, qk_ref, *state_refs):
    count, blocks, _, heads, _, tok = parts_ref.shape
    for head in range(heads):
        for which in range(2):
            for src in range(blocks):
                total = parts_ref[0, src, which, head]
                for part in range(1, count):
                    total = total + parts_ref[part, src, which, head]
                qk_ref[src, which, head] = total
        if with_state:
            high, low = split(psi(feature_major(qk_ref, 1, head), False))
            v = rows_of(vg_ref, 0, head, 0, blocks * tok)
            state_refs[0][head] = (dot(high, v) + dot(low, v)).astype(bf16)


def numerator_kernel(qk_ref, vg_ref, num_ref):
    heads = qk_ref.shape[2]
    length = qk_ref.shape[0] * qk_ref.shape[4]
    tile = min(TILE, length)
    for head in range(heads):
        q = feature_major(qk_ref, 0, head) * 0.25
        k = feature_major(qk_ref, 1, head)
        left, right = score_sides(q, k)
        for at in range(0, length, tile):
            width = at + tile
            scores = dot(left[at:width], right[:, :width])
            kernel = jnp.where(
                causal_mask(tile, width), 1.0 + scores * (1.0 + 0.5 * scores), 0.0
            )
            high, low = split(kernel)
            v = rows_of(vg_ref, 0, head, 0, width)
            num_ref[at:width, head * DH : (head + 1) * DH] = dot(high, v) + dot(low, v)


def normalize_kernel(with_state, qk_ref, vg_ref, num_ref, *rest):
    if with_state:
        *prefix_refs, attended_ref, grad_ref, carried_ref = rest
    else:
        attended_ref, grad_ref = rest
    heads = qk_ref.shape[2]
    blocks, tok = qk_ref.shape[0], qk_ref.shape[4]
    length = blocks * tok
    for head in range(heads):
        cols = slice(head * DH, (head + 1) * DH)
        numerator = num_ref[:, cols]
        if with_state:
            feat = psi(feature_major(qk_ref, 0, head) * 0.25, True)
            numerator = numerator + dot3(feat.T, state_sum(prefix_refs, head))
        inv_rms = lax.rsqrt(jnp.mean(numerator * numerator, axis=-1, keepdims=True) + EPSILON)
        normed = numerator * inv_rms
        upstream = rows_of(vg_ref, 1, head, 0, length).astype(f32)
        grad = inv_rms * (
            upstream - normed * jnp.mean(normed * upstream, axis=-1, keepdims=True)
        )
        attended_ref[:, cols] = normed.astype(bf16)
        grad_ref[:, cols] = grad
        if with_state:
            carried_ref[head] = dot3(feat, grad).astype(bf16)


def backward_kernel(with_state, qk_ref, vg_ref, grad_ref, *rest):
    *prefix_refs, grad_qk_ref, grad_v_ref = rest
    length = qk_ref.shape[0] * qk_ref.shape[4]
    tile = min(TILE, length)
    for head in range(grad_v_ref.shape[0]):
        cols = slice(head * DH, (head + 1) * DH)
        q = feature_major(qk_ref, 0, head) * 0.25
        k = feature_major(qk_ref, 1, head)
        left, right = score_sides(q, k)
        q_both = jnp.concatenate(split(q), axis=0)
        k_both = jnp.concatenate(split(k), axis=0)
        grad = grad_ref[:, cols]
        grad_t = grad.T
        if with_state:
            grad_q = pull_psi(q, dot3(state_sum(prefix_refs, head), grad_t), True)
        for at in reversed(range(0, length, tile)):
            width = at + tile
            scores = dot(left[at:width], right[:, :width])
            causal = causal_mask(tile, width)
            v = rows_of(vg_ref, 0, head, 0, width)
            high, low = split(grad[at:width])
            mixing = dot(
                jnp.concatenate([high, low], axis=1), jnp.concatenate([v, v], axis=1), NT
            )
            more = 1.0 + scores
            slopes = split(jnp.where(causal, mixing * more, 0.0))
            kernels = split(jnp.where(causal, more + 0.5 * scores * scores, 0.0))
            both = dot(k_both[:, :width], slopes[0], NT)
            piece = both[:F] + (both[F:] + dot(k_both[:F, :width], slopes[1], NT))
            if with_state:
                piece = piece + grad_q[:, at:width]
            grad_qk_ref[0, head, :, at:width] = piece * 0.25
            both = dot(q_both[:, at:width], slopes[0])
            piece_k = both[:F] + (both[F:] + dot(q_both[:F, at:width], slopes[1]))
            high, low = split(grad_t[:, at:width])
            both = dot(jnp.concatenate([high, low], axis=0), kernels[0])
            piece_v = both[:DH] + (both[DH:] + dot(high, kernels[1]))
            if width == length:
                grad_qk_ref[1, head] = piece_k
                grad_v_ref[head] = piece_v
            else:
                grad_qk_ref[1, head, :, :width] += piece_k
                grad_v_ref[head, :, :width] += piece_v


def rows_kernel(with_state, at_ref, qk_ref, vg_ref, attended_ref, grad_qk_ref, grad_v_ref, *rest):
    *suffix_refs, rows_ref, keep_ref, send_ref, held_ref = rest
    heads, tok = qk_ref.shape[2], qk_ref.shape[4]
    length = qk_ref.shape[0] * tok
    for head in range(heads):
        grad_k, grad_v = grad_qk_ref[1, head], grad_v_ref[head]
        if with_state:
            k = feature_major(qk_ref, 1, head)
            v = rows_of(vg_ref, 0, head, 0, length)
            suffix = state_sum(suffix_refs, head)
            high, low = split(suffix)
            grad_k = grad_k + pull_psi(k, dot(high, v, NT) + dot(low, v, NT), False)
            grad_v = grad_v + dot3(suffix.T, psi(k, False))
        rows_ref[head * F : (head + 1) * F] = grad_qk_ref[0, head].astype(bf16)
        rows_ref[(heads + head) * F : (heads + head + 1) * F] = grad_k.astype(bf16)
        held_ref[:, head * DH : (head + 1) * DH] = grad_v.T.astype(bf16)
    chips = keep_ref.shape[0]
    for shift in range(chips):
        chip = lax.rem(at_ref[0] + shift, chips)
        for core, out_ref in ((at_ref[1], keep_ref), (1 - at_ref[1], send_ref)):
            block = aligned(2 * chip + core, tok)
            out_ref[shift, 0] = attended_ref[block, :]
            out_ref[shift, 1] = held_ref[block, :]


def pair_kernel(at_ref, keep_ref, got_ref, *out_refs):
    for shift, out_ref in enumerate(out_refs):
        out_ref[at_ref[1]] = keep_ref[shift]
        out_ref[1 - at_ref[1]] = got_ref[shift]


def unpack_heads_kernel(at_ref, *rest):
    *part_refs, attended_ref, values_ref = rest
    chips, width = len(part_refs), part_refs[0].shape[3]
    for shift, part_ref in enumerate(part_refs):
        chip = lax.rem(at_ref[0] + chips - shift, chips)
        for core in range(2):
            cols = aligned(2 * chip + core, width)
            attended_ref[0, :, cols] = part_ref[core, 0]
            values_ref[0, :, cols] = part_ref[core, 1]


def place_rows(chip_at, core_at, part_refs, held_ref):
    chips, half = len(part_refs) // 2, part_refs[0].shape[0] // 2
    for shift in range(chips):
        chip = lax.rem(chip_at + chips - shift, chips)
        for side, core in ((0, core_at), (1, 1 - core_at)):
            part_ref = part_refs[2 * shift + side]
            for which in range(2):
                rows = aligned(which * 2 * chips + 2 * chip + core, half)
                held_ref[rows, :] = part_ref[which * half : (which + 1) * half, :]


def product_kernel(group, at_ref, *rest):
    rows_refs, rest = rest[:group], rest[group:]
    tokens_ref, own_rows_ref, *part_refs, total_ref, held_ref = rest
    place_rows(at_ref[1], at_ref[2], rows_refs, held_ref)
    total_ref[...] = dot(tokens_ref[...], held_ref[...], NT)
    tok = own_rows_ref.shape[0]
    own_rows_ref[...] = held_ref[:, aligned(2 * at_ref[1] + at_ref[2], tok)].T
    count = len(part_refs)
    size = part_refs[0].shape[0]
    for shift, part_ref in enumerate(part_refs):
        owner = lax.rem(at_ref[0] + shift, count)
        part = total_ref[pl.ds(pl.multiple_of(owner * size, size), size), :]
        part_ref[...] = part.astype(part_ref.dtype)


def run_sum_kernel(arrived, at_ref, *rest):
    own_ref, *rest = rest
    total_ref = rest[-1]
    total = own_ref[...]
    for ref in rest[:arrived]:
        total = total + ref[...].astype(f32)
    total_ref[...] = total
    part_refs = rest[arrived:-1]
    size = part_refs[0].shape[0]
    for shift, part_ref in enumerate(part_refs):
        owner = lax.rem(at_ref[0] + shift, len(part_refs))
        part = total_ref[pl.ds(pl.multiple_of(owner * size, size), size), :]
        part_ref[...] = part.astype(part_ref.dtype)


def grad_tokens_kernel(at_ref, rows_ref, *rest):
    *weight_refs, out_ref = rest
    for i, weight_ref in enumerate(weight_refs):
        size = weight_ref.shape[0]
        first = pl.multiple_of(at_ref[i], size)
        out_ref[0, :, pl.ds(first, size)] = dot(rows_ref[...], weight_ref[...], NT).astype(bf16)


def final_sum_kernel(own_ref, *rest):
    *part_refs, out_ref = rest
    total = own_ref[...]
    for part_ref in part_refs:
        total = total + part_ref[...].astype(f32)
    out_ref[...] = total


VMEM = pl.BlockSpec(memory_space=pltpu.VMEM)
SMEM = pl.BlockSpec(memory_space=pltpu.SMEM)
FAR = pl.BlockSpec(memory_space=pltpu.HBM)
ANYWHERE = pl.BlockSpec(memory_space=pl.ANY)


def call(
    body,
    outs,
    *operands,
    scalars=(),
    after=(),
    after_far=(),
    scratch=(),
    far_in=(),
    far_out=False,
    copies=(),
):
    at = [jnp.stack([jnp.int32(s) for s in scalars])] if scalars else []
    count = len(at) + len(operands)

    def kernel(*refs):
        ins, rest = refs[:count], refs[count + len(after) + len(after_far) :]
        body(*ins, *rest[: len(outs)], *rest[len(outs) + 1 :])
        rest[len(outs)][...] = jnp.zeros((8, 128), f32)

    *results, token = pl.pallas_call(
        kernel,
        out_shape=[jax.ShapeDtypeStruct(shape, kind) for shape, kind in [*outs, ((8, 128), f32)]],
        in_specs=[SMEM] * len(at)
        + [FAR if i in far_in else VMEM for i in range(len(operands))]
        + [ANYWHERE] * len(after)
        + [FAR] * len(after_far),
        out_specs=[FAR if far_out else VMEM] * len(outs) + [VMEM],
        scratch_shapes=[*scratch] + [pltpu.SemaphoreType.DMA((n,)) for n in copies],
        compiler_params=pltpu.CompilerParams(vmem_limit_bytes=VMEM_LIMIT),
        cost_estimate=pl.CostEstimate(flops=0, bytes_accessed=0, transcendentals=0),
    )(*at, *operands, *after, *after_far)
    return results, token


def local(dp_size, ctx_size, tokens, proj_weight, values, grad_out):
    group = min(GROUP, ctx_size, H)
    runs = ctx_size // group
    heads = H // group
    tok, width = tokens.shape[1:]
    length = group * tok
    cols = proj_weight.shape[1]
    share = width // dp_size
    depth = share // ctx_size
    with_state = runs > 1
    groups = [[run * group + i for i in range(group)] for run in range(runs)]
    wide_groups = [
        [dp * ctx_size + i for dp in range(dp_size) for i in members] for members in groups
    ]
    dp_at, ctx_at = lax.axis_index("dp"), lax.axis_index("ctx")
    run_at, member = ctx_at // group, ctx_at % group

    def exchange(x):
        return lax.all_to_all(
            x, "ctx", split_axis=0, concat_axis=0, tiled=True, axis_index_groups=groups
        )

    def to_dp(x, shift):
        return lax.ppermute(x, "dp", [(i, (i + shift) % dp_size) for i in range(dp_size)])

    def to_member(x, shift):
        pairs = [(i, i - i % group + (i + shift) % group) for i in range(ctx_size)]
        return lax.ppermute(x, "ctx", pairs)

    chips = group // 2
    chip_at, core_at = member // 2, member % 2

    def to_chip(x, shift):
        return x if shift == 0 else to_member(x, 2 * shift)

    def to_other_core(x):
        return lax.ppermute(x, "ctx", [(i, i ^ 1) for i in range(ctx_size)])

    def to_run(x, shift, wrap):
        pairs = [
            (i, (i + shift * group) % ctx_size)
            for i in range(ctx_size)
            if wrap or 0 <= i + shift * group < ctx_size
        ]
        return lax.ppermute(x, "ctx", pairs)

    qk_shape = ((group, 2, heads, F, tok), f32)
    state_shape = ((heads, PSI, DH), bf16)
    blocks_shape = ((2, tok, heads * DH), bf16)
    rows_shape = ((length, heads * DH), f32)

    parts, token = call(
        token_parts_kernel,
        [((tok, share), bf16)] * (dp_size - 1),
        tokens,
        scalars=(dp_at,),
        far_in=(0,),
        far_out=True,
        copies=(dp_size - 1,),
    )
    arrived = [to_dp(part, shift) for shift, part in enumerate(parts, 1)]
    parts, token = call(
        pack_heads_kernel,
        [((2, 2, tok, heads * DH), bf16)] * chips,
        values,
        grad_out,
        scalars=(chip_at, core_at),
        after=(token,),
    )
    heads_parts = [to_chip(part, shift) for shift, part in enumerate(parts)]
    (keep, send), _ = call(
        split_cores_kernel,
        [((chips, 2, tok, heads * DH), bf16)] * 2,
        *heads_parts,
        scalars=(chip_at, core_at),
    )
    (vg,), _ = call(
        collect_heads_kernel,
        [((group, 2, tok, heads * DH), bf16)],
        keep,
        to_other_core(send),
        scalars=(chip_at, core_at),
    )
    (projected,), token = call(
        project_kernel,
        [qk_shape],
        tokens,
        proj_weight,
        scalars=(dp_at,),
        after=(token,),
        far_in=(0,),
        copies=(1,),
        scratch=[pltpu.VMEM((tok, share), bf16)],
    )
    (projected,), token = call(
        project_rest_kernel,
        [((dp_size,) + qk_shape[0], f32)],
        projected,
        proj_weight,
        *arrived,
        scalars=(dp_at,),
        after=(token,),
        after_far=heads_parts[1:],
    )
    part_shape = (tok, dp_size * runs * depth)
    if depth % 128 == 0:
        (keep, send), _ = call(
            functools.partial(pack_tokens_kernel, depth),
            [((chips,) + part_shape, bf16)] * 2,
            tokens,
            scalars=(chip_at, core_at),
        )
    else:
        blocks = tokens[0].reshape(tok, dp_size * runs, chips, 2, depth).transpose(2, 3, 0, 1, 4)
        blocks = blocks.reshape(chips, 2, *part_shape)
        blocks = jnp.stack([blocks[(chip_at + shift) % chips] for shift in range(chips)])
        keep, send = blocks[:, core_at], blocks[:, 1 - core_at]
    token_parts, _ = call(
        pair_kernel,
        [((2,) + part_shape, bf16)] * chips,
        keep,
        to_other_core(send),
        scalars=(chip_at, core_at),
        after=(token,),
    )
    token_parts = [to_chip(part, shift) for shift, part in enumerate(token_parts)]
    qk_parts = lax.all_to_all(
        projected.reshape((dp_size * group,) + qk_shape[0][1:]),
        ("dp", "ctx"),
        split_axis=0,
        concat_axis=0,
        tiled=True,
        axis_index_groups=wide_groups,
    ).reshape(projected.shape)

    (qk, *state), token = call(
        functools.partial(state_kernel, with_state),
        [qk_shape] + [state_shape] * with_state,
        qk_parts,
        vg,
    )
    pair = 2 if ctx_size % 2 == 0 else 1
    parity = ctx_at % pair
    piece = share // pair
    (mine,), token = call(
        weight_piece_kernel,
        [((piece, cols), bf16)],
        proj_weight,
        scalars=(parity,),
        after=(token,),
        far_in=(0,),
        far_out=True,
        copies=(1,),
    )
    fetched = [to_dp(mine, shift) for shift in range(1, dp_size)]
    weights, firsts = [proj_weight], [dp_at * share]
    for shift, half in enumerate(fetched, 1):
        base = (dp_at + dp_size - shift) % dp_size * share
        weights.append(half)
        firsts.append(base + parity * piece)
        if pair == 2:
            weights.append(lax.ppermute(half, "ctx", [(i, i ^ 1) for i in range(ctx_size)]))
            firsts.append(base + (1 - parity) * piece)

    prefix, suffix = (), ()
    if with_state:
        prefix = [to_run(state[0], shift, False) for shift in range(1, runs)]
    (numerator,), token = call(numerator_kernel, [rows_shape], qk, vg)
    (attended, grad_num, *carried), token = call(
        functools.partial(normalize_kernel, with_state),
        [((length, heads * DH), bf16), rows_shape] + [state_shape] * with_state,
        qk,
        vg,
        numerator,
        *prefix,
        after_far=token_parts[1:],
    )
    if with_state:
        suffix = [to_run(carried[0], -shift, False) for shift in range(1, runs)]
    (grad_qk, grad_v), token = call(
        functools.partial(backward_kernel, with_state),
        [((2, heads, F, length), f32), ((heads, DH, length), f32)],
        qk,
        vg,
        grad_num,
        *prefix,
    )
    (token_cols,), token = call(
        collect_tokens_kernel,
        [(part_shape[1:] + (length,), bf16)],
        *token_parts,
        scalars=(chip_at,),
        after=(token,),
        after_far=fetched,
    )
    (rows, keep, send), token = call(
        functools.partial(rows_kernel, with_state),
        [((2 * heads * F, length), bf16)] + [((chips, 2, tok, heads * DH), bf16)] * 2,
        qk,
        vg,
        attended,
        grad_qk,
        grad_v,
        *suffix,
        scalars=(chip_at, core_at),
        after=(token,),
        scratch=[pltpu.VMEM((length, heads * DH), bf16)],
    )
    rows = [to_chip(rows, shift) for shift in range(chips)]
    rows = [side for part in rows for side in (part, to_other_core(part))]
    got = to_other_core(send)
    results, token = call(
        pair_kernel,
        [((2, 2, tok, heads * DH), bf16)] * chips,
        keep,
        got,
        scalars=(chip_at, core_at),
    )
    results = [to_chip(part, shift) for shift, part in enumerate(results)]

    held = pltpu.VMEM((cols, length), bf16)
    (own_rows, own, *parts), token = call(
        functools.partial(product_kernel, 2 * chips),
        [((tok, cols), bf16), ((runs * depth, cols), f32)] + [((runs * depth, cols), bf16)] * (dp_size - 1),
        *rows,
        token_cols,
        scalars=(dp_at, chip_at, core_at),
        after=(token,),
        scratch=[pltpu.VMEM((dp_size * runs * depth, cols), f32), held],
    )
    parts = [to_dp(part, shift) for shift, part in enumerate(parts, 1)]
    (grad_tokens,), tokens_token = call(
        grad_tokens_kernel,
        [((1, tok, width), bf16)],
        own_rows,
        *weights,
        scalars=firsts,
        after=(token,),
    )
    (grad_proj, *parts), token = call(
        functools.partial(run_sum_kernel, len(parts)),
        [((depth, cols), f32)] + [((depth, cols), bf16)] * (runs - 1),
        own,
        *parts,
        scalars=(run_at,),
        after=(tokens_token,),
        scratch=[pltpu.VMEM((runs * depth, cols), f32)],
    )
    (attended, grad_values), token = call(
        unpack_heads_kernel,
        [((1, tok, H * DH), bf16)] * 2,
        *results,
        scalars=(chip_at,),
        after=(token,),
    )
    (grad_proj,), _ = call(
        final_sum_kernel,
        [((depth, cols), f32)],
        grad_proj,
        *[to_run(part, shift, True) for shift, part in enumerate(parts, 1)],
        after=(token,),
    )
    return (attended, grad_tokens, grad_values, grad_proj)


def solution(mesh):
    return jax.shard_map(
        functools.partial(local, mesh.shape["dp"], mesh.shape["ctx"]),
        mesh=mesh,
        in_specs=(P("dp", "ctx", None), P("dp", None), P("dp", "ctx", None), P("dp", "ctx", None)),
        out_specs=(
            P("dp", "ctx", None),
            P("dp", "ctx", None),
            P("dp", "ctx", None),
            P(("dp", "ctx"), None),
        ),
        check_vma=False,
    )
```

```python
import functools

import jax
import jax.numpy as jnp
from jax import lax
from jax.experimental import pallas as pl
from jax.experimental.pallas import tpu as pltpu
from jax.sharding import PartitionSpec as P

H = 16
F = 16
DH = 128
EPSILON = 1e-05
GROUP = 8
TILE = 256
VMEM_LIMIT = 16 * 1024 * 1024
PSI = 9 * F + 2 * F
PSI_SCALE = (0.5,) + (1.0,) * 7 + (0.5,)

f32 = jnp.float32
bf16 = jnp.bfloat16

NN = (((1,), (0,)), ((), ()))
NT = (((1,), (1,)), ((), ()))


def dot(a, b, dims=NN):
    return lax.dot_general(a, b, dims, preferred_element_type=f32)


def split(x):
    high = x.astype(bf16)
    return high, (x - high.astype(f32)).astype(bf16)


def dot3(a, b, dims=NN):
    a_high, a_low = split(a)
    b_high, b_low = split(b)
    return dot(a_high, b_high, dims) + (dot(a_high, b_low, dims) + dot(a_low, b_high, dims))


def turned(x, r):
    return x if r == 0 else jnp.concatenate([x[r:], x[:r]], axis=0)


def psi(x, weights):
    parts = []
    for r in range(9):
        part = x * turned(x, r)
        parts.append(part * PSI_SCALE[r] if weights and PSI_SCALE[r] != 1.0 else part)
    row = lax.broadcasted_iota(jnp.int32, x.shape, 0)
    return jnp.concatenate(parts + [x, jnp.where(row == 0, 1.0, 0.0)], axis=0)


def pull_psi(x, upstream, weights):
    total = upstream[9 * F : 10 * F]
    for r in range(9):
        part = upstream[r * F : (r + 1) * F]
        if weights and PSI_SCALE[r] != 1.0:
            part = part * PSI_SCALE[r]
        total = total + part * turned(x, r) + turned(part * x, (F - r) % F)
    return total


def feature_major(qk_ref, which, head):
    return jnp.concatenate([qk_ref[src, which, head] for src in range(qk_ref.shape[0])], axis=1)


def rows_of(ref, which, head, start, stop):
    tok = ref.shape[2]
    return jnp.concatenate(
        [
            ref[src, which, :, head * DH : (head + 1) * DH]
            for src in range(start // tok, stop // tok)
        ],
        axis=0,
    )


def score_sides(q, k):
    q_high, q_low = split(q)
    k_high, k_low = split(k)
    left = jnp.concatenate([q_high, q_high, q_low, q_low], axis=0)
    right = jnp.concatenate([k_high, k_low, k_high, k_low], axis=0)
    return left.T, right


def causal_mask(tile, width):
    row = lax.broadcasted_iota(jnp.int32, (tile, width), 0) + (width - tile)
    return row >= lax.broadcasted_iota(jnp.int32, (tile, width), 1)


def run_copies(sems, pairs):
    copies = [
        pltpu.make_async_copy(source, target, sems.at[i])
        for i, (source, target) in enumerate(pairs)
    ]
    for copy in copies:
        copy.start()
    for copy in copies:
        copy.wait()


def aligned(at, size):
    return pl.ds(pl.multiple_of(at * size, size), size)


def token_parts_kernel(at_ref, tokens_ref, *rest):
    *out_refs, sems = rest
    count, share = len(out_refs) + 1, out_refs[0].shape[1]
    run_copies(
        sems,
        [
            (tokens_ref.at[0, :, aligned(lax.rem(at_ref[0] + shift, count), share)], out_ref)
            for shift, out_ref in enumerate(out_refs, 1)
        ],
    )


def pack_heads_kernel(at_ref, values_ref, grad_ref, *out_refs):
    chips, width = len(out_refs), out_refs[0].shape[3]
    for shift, out_ref in enumerate(out_refs):
        chip = lax.rem(at_ref[0] + shift, chips)
        for core in range(2):
            cols = aligned(2 * chip + core, width)
            out_ref[core, 0] = values_ref[0, :, cols]
            out_ref[core, 1] = grad_ref[0, :, cols]


def split_cores_kernel(at_ref, *rest):
    *part_refs, keep_ref, send_ref = rest
    for shift, part_ref in enumerate(part_refs):
        keep_ref[shift] = part_ref[at_ref[1]]
        send_ref[shift] = part_ref[1 - at_ref[1]]


def collect_heads_kernel(at_ref, keep_ref, got_ref, out_ref):
    chips = keep_ref.shape[0]
    for shift in range(chips):
        chip = lax.rem(at_ref[0] + chips - shift, chips)
        out_ref[2 * chip + at_ref[1]] = keep_ref[shift]
        out_ref[2 * chip + 1 - at_ref[1]] = got_ref[shift]


def pack_tokens_kernel(depth, at_ref, tokens_ref, keep_ref, send_ref):
    chips, _, rows = keep_ref.shape
    for shift in range(chips):
        chip = lax.rem(at_ref[0] + shift, chips)
        for core, out_ref in ((at_ref[1], keep_ref), (1 - at_ref[1], send_ref)):
            for part in range(rows // depth):
                cols = aligned(2 * (part * chips + chip) + core, depth)
                out_ref[shift, :, part * depth : (part + 1) * depth] = tokens_ref[0, :, cols]


def collect_tokens_kernel(at_ref, *rest):
    *part_refs, out_ref = rest
    chips, tok = len(part_refs), part_refs[0].shape[1]
    for shift, part_ref in enumerate(part_refs):
        chip = lax.rem(at_ref[0] + chips - shift, chips)
        for core in range(2):
            out_ref[:, aligned(2 * chip + core, tok)] = part_ref[core].T


def write_blocks(projected, out_ref):
    group, _, heads, feat, _ = out_ref.shape
    for member in range(group):
        for which in range(2):
            for head in range(heads):
                first = ((which * group + member) * heads + head) * feat
                out_ref[member, which, head] = projected[first : first + feat]


def project_kernel(at_ref, tokens_ref, weight_ref, out_ref, part_ref, sem):
    share = part_ref.shape[1]
    run_copies(sem, [(tokens_ref.at[0, :, aligned(at_ref[0], share)], part_ref)])
    write_blocks(dot(part_ref[...], weight_ref[...]).T, out_ref)


def project_rest_kernel(at_ref, own_ref, weight_ref, *rest):
    *part_refs, out_ref = rest
    count = len(part_refs) + 1
    at = at_ref[0]
    out_ref[at] = own_ref[...]
    for shift, part_ref in enumerate(part_refs, 1):
        owner = lax.rem(at + count - shift, count)
        write_blocks(dot(part_ref[...], weight_ref[...]).T, out_ref.at[owner])


def weight_piece_kernel(at_ref, weight_ref, out_ref, sems):
    run_copies(sems, [(weight_ref.at[aligned(at_ref[0], out_ref.shape[0])], out_ref)])


def state_sum(refs, head):
    total = refs[0][head].astype(f32)
    for ref in refs[1:]:
        total = total + ref[head].astype(f32)
    return total


def state_kernel(with_state, parts_ref, vg_ref, qk_ref, *state_refs):
    count, blocks, _, heads, _, tok = parts_ref.shape
    for head in range(heads):
        for which in range(2):
            for src in range(blocks):
                total = parts_ref[0, src, which, head]
                for part in range(1, count):
                    total = total + parts_ref[part, src, which, head]
                qk_ref[src, which, head] = total
        if with_state:
            high, low = split(psi(feature_major(qk_ref, 1, head), False))
            v = rows_of(vg_ref, 0, head, 0, blocks * tok)
            state_refs[0][head] = (dot(high, v) + dot(low, v)).astype(bf16)


def numerator_kernel(qk_ref, vg_ref, num_ref):
    heads = qk_ref.shape[2]
    length = qk_ref.shape[0] * qk_ref.shape[4]
    tile = min(TILE, length)
    for head in range(heads):
        q = feature_major(qk_ref, 0, head) * 0.25
        k = feature_major(qk_ref, 1, head)
        left, right = score_sides(q, k)
        for at in range(0, length, tile):
            width = at + tile
            scores = dot(left[at:width], right[:, :width])
            kernel = jnp.where(
                causal_mask(tile, width), 1.0 + scores * (1.0 + 0.5 * scores), 0.0
            )
            high, low = split(kernel)
            v = rows_of(vg_ref, 0, head, 0, width)
            num_ref[at:width, head * DH : (head + 1) * DH] = dot(high, v) + dot(low, v)


def normalize_kernel(with_state, qk_ref, vg_ref, num_ref, *rest):
    if with_state:
        *prefix_refs, attended_ref, grad_ref, carried_ref = rest
    else:
        attended_ref, grad_ref = rest
    heads = qk_ref.shape[2]
    blocks, tok = qk_ref.shape[0], qk_ref.shape[4]
    length = blocks * tok
    for head in range(heads):
        cols = slice(head * DH, (head + 1) * DH)
        numerator = num_ref[:, cols]
        if with_state:
            feat = psi(feature_major(qk_ref, 0, head) * 0.25, True)
            numerator = numerator + dot3(feat.T, state_sum(prefix_refs, head))
        inv_rms = lax.rsqrt(jnp.mean(numerator * numerator, axis=-1, keepdims=True) + EPSILON)
        normed = numerator * inv_rms
        upstream = rows_of(vg_ref, 1, head, 0, length).astype(f32)
        grad = inv_rms * (
            upstream - normed * jnp.mean(normed * upstream, axis=-1, keepdims=True)
        )
        attended_ref[:, cols] = normed.astype(bf16)
        grad_ref[:, cols] = grad
        if with_state:
            carried_ref[head] = dot3(feat, grad).astype(bf16)


def backward_kernel(with_state, qk_ref, vg_ref, grad_ref, *rest):
    *prefix_refs, grad_qk_ref, grad_v_ref = rest
    length = qk_ref.shape[0] * qk_ref.shape[4]
    tile = min(TILE, length)
    for head in range(grad_v_ref.shape[0]):
        cols = slice(head * DH, (head + 1) * DH)
        q = feature_major(qk_ref, 0, head) * 0.25
        k = feature_major(qk_ref, 1, head)
        left, right = score_sides(q, k)
        q_both = jnp.concatenate(split(q), axis=0)
        k_both = jnp.concatenate(split(k), axis=0)
        grad = grad_ref[:, cols]
        grad_t = grad.T
        if with_state:
            grad_q = pull_psi(q, dot3(state_sum(prefix_refs, head), grad_t), True)
        for at in reversed(range(0, length, tile)):
            width = at + tile
            scores = dot(left[at:width], right[:, :width])
            causal = causal_mask(tile, width)
            v = rows_of(vg_ref, 0, head, 0, width)
            high, low = split(grad[at:width])
            mixing = dot(
                jnp.concatenate([high, low], axis=1), jnp.concatenate([v, v], axis=1), NT
            )
            more = 1.0 + scores
            slopes = split(jnp.where(causal, mixing * more, 0.0))
            kernels = split(jnp.where(causal, more + 0.5 * scores * scores, 0.0))
            both = dot(k_both[:, :width], slopes[0], NT)
            piece = both[:F] + (both[F:] + dot(k_both[:F, :width], slopes[1], NT))
            if with_state:
                piece = piece + grad_q[:, at:width]
            grad_qk_ref[0, head, :, at:width] = piece * 0.25
            both = dot(q_both[:, at:width], slopes[0])
            piece_k = both[:F] + (both[F:] + dot(q_both[:F, at:width], slopes[1]))
            high, low = split(grad_t[:, at:width])
            both = dot(jnp.concatenate([high, low], axis=0), kernels[0])
            piece_v = both[:DH] + (both[DH:] + dot(high, kernels[1]))
            if width == length:
                grad_qk_ref[1, head] = piece_k
                grad_v_ref[head] = piece_v
            else:
                grad_qk_ref[1, head, :, :width] += piece_k
                grad_v_ref[head, :, :width] += piece_v


def rows_kernel(with_state, at_ref, qk_ref, vg_ref, attended_ref, grad_qk_ref, grad_v_ref, *rest):
    *suffix_refs, rows_ref, keep_ref, send_ref, held_ref = rest
    heads, tok = qk_ref.shape[2], qk_ref.shape[4]
    length = qk_ref.shape[0] * tok
    for head in range(heads):
        grad_k, grad_v = grad_qk_ref[1, head], grad_v_ref[head]
        if with_state:
            k = feature_major(qk_ref, 1, head)
            v = rows_of(vg_ref, 0, head, 0, length)
            suffix = state_sum(suffix_refs, head)
            high, low = split(suffix)
            grad_k = grad_k + pull_psi(k, dot(high, v, NT) + dot(low, v, NT), False)
            grad_v = grad_v + dot3(suffix.T, psi(k, False))
        rows_ref[head * F : (head + 1) * F] = grad_qk_ref[0, head].astype(bf16)
        rows_ref[(heads + head) * F : (heads + head + 1) * F] = grad_k.astype(bf16)
        held_ref[:, head * DH : (head + 1) * DH] = grad_v.T.astype(bf16)
    chips = keep_ref.shape[0]
    for shift in range(chips):
        chip = lax.rem(at_ref[0] + shift, chips)
        for core, out_ref in ((at_ref[1], keep_ref), (1 - at_ref[1], send_ref)):
            block = aligned(2 * chip + core, tok)
            out_ref[shift, 0] = attended_ref[block, :]
            out_ref[shift, 1] = held_ref[block, :]


def pair_kernel(at_ref, keep_ref, got_ref, *out_refs):
    for shift, out_ref in enumerate(out_refs):
        out_ref[at_ref[1]] = keep_ref[shift]
        out_ref[1 - at_ref[1]] = got_ref[shift]


def unpack_heads_kernel(at_ref, *rest):
    *part_refs, attended_ref, values_ref = rest
    chips, width = len(part_refs), part_refs[0].shape[3]
    for shift, part_ref in enumerate(part_refs):
        chip = lax.rem(at_ref[0] + chips - shift, chips)
        for core in range(2):
            cols = aligned(2 * chip + core, width)
            attended_ref[0, :, cols] = part_ref[core, 0]
            values_ref[0, :, cols] = part_ref[core, 1]


def place_rows(chip_at, core_at, part_refs, held_ref):
    chips, half = len(part_refs) // 2, part_refs[0].shape[0] // 2
    for shift in range(chips):
        chip = lax.rem(chip_at + chips - shift, chips)
        for side, core in ((0, core_at), (1, 1 - core_at)):
            part_ref = part_refs[2 * shift + side]
            for which in range(2):
                rows = aligned(which * 2 * chips + 2 * chip + core, half)
                held_ref[rows, :] = part_ref[which * half : (which + 1) * half, :]


def product_kernel(group, at_ref, *rest):
    rows_refs, rest = rest[:group], rest[group:]
    tokens_ref, own_rows_ref, other_rows_ref, *part_refs, total_ref, held_ref = rest
    place_rows(at_ref[1], at_ref[2], rows_refs, held_ref)
    total_ref[...] = dot(tokens_ref[...], held_ref[...], NT)
    tok = own_rows_ref.shape[0]
    own_rows_ref[...] = held_ref[:, aligned(2 * at_ref[1] + at_ref[2], tok)].T
    other_rows_ref[...] = held_ref[:, aligned(2 * at_ref[1] + 1 - at_ref[2], tok)].T
    count = len(part_refs)
    size = part_refs[0].shape[0]
    for shift, part_ref in enumerate(part_refs):
        owner = lax.rem(at_ref[0] + shift, count)
        part = total_ref[pl.ds(pl.multiple_of(owner * size, size), size), :]
        part_ref[...] = part.astype(part_ref.dtype)


def run_sum_kernel(arrived, at_ref, *rest):
    own_ref, *rest = rest
    total_ref = rest[-1]
    total = own_ref[...]
    for ref in rest[:arrived]:
        total = total + ref[...].astype(f32)
    total_ref[...] = total
    part_refs = rest[arrived:-1]
    size = part_refs[0].shape[0]
    for shift, part_ref in enumerate(part_refs):
        owner = lax.rem(at_ref[0] + shift, len(part_refs))
        part = total_ref[pl.ds(pl.multiple_of(owner * size, size), size), :]
        part_ref[...] = part.astype(part_ref.dtype)


def grad_tokens_kernel(at_ref, rows_ref, other_rows_ref, weight_ref, *rest):
    count = len(rest) // 2
    fetched_refs, out_ref, other_refs = rest[:count], rest[count], rest[count + 1 :]
    for i, ref in enumerate((weight_ref, *fetched_refs)):
        size = ref.shape[0]
        first = pl.multiple_of(at_ref[i], size)
        out_ref[0, :, pl.ds(first, size)] = dot(rows_ref[...], ref[...], NT).astype(bf16)
    for ref, other_ref in zip(fetched_refs, other_refs):
        other_ref[...] = dot(other_rows_ref[...], ref[...], NT).astype(bf16)


def merge_kernel(at_ref, main_ref, *rest):
    *part_refs, out_ref, sems = rest
    run_copies(
        sems,
        [
            (part_ref, out_ref.at[0, :, pl.ds(pl.multiple_of(at_ref[i], size), size)])
            for i, part_ref in enumerate(part_refs)
            for size in part_ref.shape[1:]
        ],
    )


def final_sum_kernel(own_ref, *rest):
    *part_refs, out_ref = rest
    total = own_ref[...]
    for part_ref in part_refs:
        total = total + part_ref[...].astype(f32)
    out_ref[...] = total


VMEM = pl.BlockSpec(memory_space=pltpu.VMEM)
SMEM = pl.BlockSpec(memory_space=pltpu.SMEM)
FAR = pl.BlockSpec(memory_space=pltpu.HBM)
ANYWHERE = pl.BlockSpec(memory_space=pl.ANY)


def call(
    body,
    outs,
    *operands,
    scalars=(),
    after=(),
    after_far=(),
    scratch=(),
    far_in=(),
    far_out=False,
    copies=(),
    alias=False,
):
    at = [jnp.stack([jnp.int32(s) for s in scalars])] if scalars else []
    count = len(at) + len(operands)

    def kernel(*refs):
        ins, rest = refs[:count], refs[count + len(after) + len(after_far) :]
        body(*ins, *rest[: len(outs)], *rest[len(outs) + 1 :])
        rest[len(outs)][...] = jnp.zeros((8, 128), f32)

    *results, token = pl.pallas_call(
        kernel,
        out_shape=[jax.ShapeDtypeStruct(shape, kind) for shape, kind in [*outs, ((8, 128), f32)]],
        in_specs=[SMEM] * len(at)
        + [FAR if i in far_in else VMEM for i in range(len(operands))]
        + [ANYWHERE] * len(after)
        + [FAR] * len(after_far),
        out_specs=[FAR if far_out else VMEM] * len(outs) + [VMEM],
        scratch_shapes=[*scratch] + [pltpu.SemaphoreType.DMA((n,)) for n in copies],
        input_output_aliases={len(at): 0} if alias else {},
        compiler_params=pltpu.CompilerParams(vmem_limit_bytes=VMEM_LIMIT),
        cost_estimate=pl.CostEstimate(flops=0, bytes_accessed=0, transcendentals=0),
    )(*at, *operands, *after, *after_far)
    return results, token


def local(dp_size, ctx_size, tokens, proj_weight, values, grad_out):
    group = min(GROUP, ctx_size, H)
    runs = ctx_size // group
    heads = H // group
    tok, width = tokens.shape[1:]
    length = group * tok
    cols = proj_weight.shape[1]
    share = width // dp_size
    depth = share // ctx_size
    with_state = runs > 1
    groups = [[run * group + i for i in range(group)] for run in range(runs)]
    wide_groups = [
        [dp * ctx_size + i for dp in range(dp_size) for i in members] for members in groups
    ]
    dp_at, ctx_at = lax.axis_index("dp"), lax.axis_index("ctx")
    run_at, member = ctx_at // group, ctx_at % group

    def exchange(x):
        return lax.all_to_all(
            x, "ctx", split_axis=0, concat_axis=0, tiled=True, axis_index_groups=groups
        )

    def to_dp(x, shift):
        return lax.ppermute(x, "dp", [(i, (i + shift) % dp_size) for i in range(dp_size)])

    def to_member(x, shift):
        pairs = [(i, i - i % group + (i + shift) % group) for i in range(ctx_size)]
        return lax.ppermute(x, "ctx", pairs)

    chips = group // 2
    chip_at, core_at = member // 2, member % 2

    def to_chip(x, shift):
        return x if shift == 0 else to_member(x, 2 * shift)

    def to_other_core(x):
        return lax.ppermute(x, "ctx", [(i, i ^ 1) for i in range(ctx_size)])

    def to_run(x, shift, wrap):
        pairs = [
            (i, (i + shift * group) % ctx_size)
            for i in range(ctx_size)
            if wrap or 0 <= i + shift * group < ctx_size
        ]
        return lax.ppermute(x, "ctx", pairs)

    qk_shape = ((group, 2, heads, F, tok), f32)
    state_shape = ((heads, PSI, DH), bf16)
    blocks_shape = ((2, tok, heads * DH), bf16)
    rows_shape = ((length, heads * DH), f32)

    parts, token = call(
        token_parts_kernel,
        [((tok, share), bf16)] * (dp_size - 1),
        tokens,
        scalars=(dp_at,),
        far_in=(0,),
        far_out=True,
        copies=(dp_size - 1,),
    )
    arrived = [to_dp(part, shift) for shift, part in enumerate(parts, 1)]
    parts, token = call(
        pack_heads_kernel,
        [((2, 2, tok, heads * DH), bf16)] * chips,
        values,
        grad_out,
        scalars=(chip_at, core_at),
        after=(token,),
    )
    heads_parts = [to_chip(part, shift) for shift, part in enumerate(parts)]
    (keep, send), _ = call(
        split_cores_kernel,
        [((chips, 2, tok, heads * DH), bf16)] * 2,
        *heads_parts,
        scalars=(chip_at, core_at),
    )
    (vg,), _ = call(
        collect_heads_kernel,
        [((group, 2, tok, heads * DH), bf16)],
        keep,
        to_other_core(send),
        scalars=(chip_at, core_at),
    )
    (projected,), token = call(
        project_kernel,
        [qk_shape],
        tokens,
        proj_weight,
        scalars=(dp_at,),
        after=(token,),
        far_in=(0,),
        copies=(1,),
        scratch=[pltpu.VMEM((tok, share), bf16)],
    )
    part_shape = (tok, dp_size * runs * depth)
    if depth % 128 == 0:
        (keep, send), _ = call(
            functools.partial(pack_tokens_kernel, depth),
            [((chips,) + part_shape, bf16)] * 2,
            tokens,
            scalars=(chip_at, core_at),
        )
    else:
        blocks = tokens[0].reshape(tok, dp_size * runs, chips, 2, depth).transpose(2, 3, 0, 1, 4)
        blocks = blocks.reshape(chips, 2, *part_shape)
        blocks = jnp.stack([blocks[(chip_at + shift) % chips] for shift in range(chips)])
        keep, send = blocks[:, core_at], blocks[:, 1 - core_at]
    token_parts, pair_token = call(
        pair_kernel,
        [((2,) + part_shape, bf16)] * chips,
        keep,
        to_other_core(send),
        scalars=(chip_at, core_at),
    )
    token_parts = [to_chip(part, shift) for shift, part in enumerate(token_parts)]
    (projected,), rest_token = call(
        project_rest_kernel,
        [((dp_size,) + qk_shape[0], f32)],
        projected,
        proj_weight,
        *arrived,
        scalars=(dp_at,),
        after=(token, pair_token),
        after_far=heads_parts[1:],
    )
    qk_parts = lax.all_to_all(
        projected.reshape((dp_size * group,) + qk_shape[0][1:]),
        ("dp", "ctx"),
        split_axis=0,
        concat_axis=0,
        tiled=True,
        axis_index_groups=wide_groups,
    ).reshape(projected.shape)

    parity = ctx_at % 2
    piece = share // 2
    (mine,), _ = call(
        weight_piece_kernel,
        [((piece, cols), bf16)],
        proj_weight,
        scalars=(parity,),
        after=(rest_token,),
        far_in=(0,),
        far_out=True,
        copies=(1,),
    )
    fetched = [to_dp(mine, shift) for shift in range(1, dp_size)]
    bases = [(dp_at + dp_size - shift) % dp_size * share for shift in range(1, dp_size)]

    (qk, *state), token = call(
        functools.partial(state_kernel, with_state),
        [qk_shape] + [state_shape] * with_state,
        qk_parts,
        vg,
    )
    prefix, suffix = (), ()
    if with_state:
        prefix = [to_run(state[0], shift, False) for shift in range(1, runs)]
    (numerator,), token = call(numerator_kernel, [rows_shape], qk, vg)
    (attended, grad_num, *carried), token = call(
        functools.partial(normalize_kernel, with_state),
        [((length, heads * DH), bf16), rows_shape] + [state_shape] * with_state,
        qk,
        vg,
        numerator,
        *prefix,
        after_far=token_parts[1:],
    )
    if with_state:
        suffix = [to_run(carried[0], -shift, False) for shift in range(1, runs)]
    (grad_qk, grad_v), token = call(
        functools.partial(backward_kernel, with_state),
        [((2, heads, F, length), f32), ((heads, DH, length), f32)],
        qk,
        vg,
        grad_num,
        *prefix,
    )
    (token_cols,), token = call(
        collect_tokens_kernel,
        [(part_shape[1:] + (length,), bf16)],
        *token_parts,
        scalars=(chip_at,),
        after=(token,),
    )
    (rows, keep, send), token = call(
        functools.partial(rows_kernel, with_state),
        [((2 * heads * F, length), bf16)] + [((chips, 2, tok, heads * DH), bf16)] * 2,
        qk,
        vg,
        attended,
        grad_qk,
        grad_v,
        *suffix,
        scalars=(chip_at, core_at),
        after=(token,),
        scratch=[pltpu.VMEM((length, heads * DH), bf16)],
    )
    rows = [to_chip(rows, shift) for shift in range(chips)]
    rows = [side for part in rows for side in (part, to_other_core(part))]
    got = to_other_core(send)
    results, token = call(
        pair_kernel,
        [((2, 2, tok, heads * DH), bf16)] * chips,
        keep,
        got,
        scalars=(chip_at, core_at),
    )
    results = [to_chip(part, shift) for shift, part in enumerate(results)]

    held = pltpu.VMEM((cols, length), bf16)
    (own_rows, other_rows, own, *parts), token = call(
        functools.partial(product_kernel, 2 * chips),
        [((tok, cols), bf16)] * 2
        + [((runs * depth, cols), f32)] + [((runs * depth, cols), bf16)] * (dp_size - 1),
        *rows,
        token_cols,
        scalars=(dp_at, chip_at, core_at),
        after=(token,),
        scratch=[pltpu.VMEM((dp_size * runs * depth, cols), f32), held],
    )
    parts = [to_dp(part, shift) for shift, part in enumerate(parts, 1)]
    (grad_tokens, *others), tokens_token = call(
        grad_tokens_kernel,
        [((1, tok, width), bf16)] + [((tok, piece), bf16)] * (dp_size - 1),
        own_rows,
        other_rows,
        proj_weight,
        *fetched,
        scalars=[dp_at * share] + [base + parity * piece for base in bases],
        after=(token,),
    )
    (grad_proj, *parts), token = call(
        functools.partial(run_sum_kernel, len(parts)),
        [((depth, cols), f32)] + [((depth, cols), bf16)] * (runs - 1),
        own,
        *parts,
        scalars=(run_at,),
        after=(tokens_token,),
        scratch=[pltpu.VMEM((runs * depth, cols), f32)],
    )
    (attended, grad_values), token = call(
        unpack_heads_kernel,
        [((1, tok, H * DH), bf16)] * 2,
        *results,
        scalars=(chip_at,),
        after=(token,),
    )
    (grad_tokens,), tokens_token = call(
        merge_kernel,
        [((1, tok, width), bf16)],
        grad_tokens,
        *[to_other_core(other) for other in others],
        scalars=[base + (1 - parity) * piece for base in bases],
        far_in=(0,),
        far_out=True,
        copies=(dp_size - 1,),
        alias=True,
    )
    (grad_proj,), _ = call(
        final_sum_kernel,
        [((depth, cols), f32)],
        grad_proj,
        *[to_run(part, shift, True) for shift, part in enumerate(parts, 1)],
        after=(token, tokens_token),
    )
    return (attended, grad_tokens, grad_values, grad_proj)


def solution(mesh):
    return jax.shard_map(
        functools.partial(local, mesh.shape["dp"], mesh.shape["ctx"]),
        mesh=mesh,
        in_specs=(P("dp", "ctx", None), P("dp", None), P("dp", "ctx", None), P("dp", "ctx", None)),
        out_specs=(
            P("dp", "ctx", None),
            P("dp", "ctx", None),
            P("dp", "ctx", None),
            P(("dp", "ctx"), None),
        ),
        check_vma=False,
    )
```

```python
import functools

import jax
import jax.numpy as jnp
from jax import lax
from jax.experimental import pallas as pl
from jax.experimental.pallas import tpu as pltpu
from jax.sharding import PartitionSpec as P

H = 16
F = 16
DH = 128
EPSILON = 1e-05
GROUP = 8
TILE = 256
VMEM_LIMIT = 16 * 1024 * 1024
PSI = 9 * F + 2 * F
PSI_SCALE = (0.5,) + (1.0,) * 7 + (0.5,)

f32 = jnp.float32
bf16 = jnp.bfloat16

NN = (((1,), (0,)), ((), ()))
NT = (((1,), (1,)), ((), ()))


def dot(a, b, dims=NN):
    return lax.dot_general(a, b, dims, preferred_element_type=f32)


def split(x):
    high = x.astype(bf16)
    return high, (x - high.astype(f32)).astype(bf16)


def dot3(a, b, dims=NN):
    a_high, a_low = split(a)
    b_high, b_low = split(b)
    return dot(a_high, b_high, dims) + (dot(a_high, b_low, dims) + dot(a_low, b_high, dims))


def turned(x, r):
    return x if r == 0 else jnp.concatenate([x[r:], x[:r]], axis=0)


def psi(x, weights):
    parts = []
    for r in range(9):
        part = x * turned(x, r)
        parts.append(part * PSI_SCALE[r] if weights and PSI_SCALE[r] != 1.0 else part)
    row = lax.broadcasted_iota(jnp.int32, x.shape, 0)
    return jnp.concatenate(parts + [x, jnp.where(row == 0, 1.0, 0.0)], axis=0)


def pull_psi(x, upstream, weights):
    total = upstream[9 * F : 10 * F]
    for r in range(9):
        part = upstream[r * F : (r + 1) * F]
        if weights and PSI_SCALE[r] != 1.0:
            part = part * PSI_SCALE[r]
        total = total + part * turned(x, r) + turned(part * x, (F - r) % F)
    return total


def feature_major(qk_ref, which, head):
    return jnp.concatenate([qk_ref[src, which, head] for src in range(qk_ref.shape[0])], axis=1)


def rows_of(ref, which, head, start, stop):
    tok = ref.shape[2]
    return jnp.concatenate(
        [
            ref[src, which, :, head * DH : (head + 1) * DH]
            for src in range(start // tok, stop // tok)
        ],
        axis=0,
    )


def score_sides(q, k):
    q_high, q_low = split(q)
    k_high, k_low = split(k)
    left = jnp.concatenate([q_high, q_high, q_low, q_low], axis=0)
    right = jnp.concatenate([k_high, k_low, k_high, k_low], axis=0)
    return left.T, right


def causal_mask(tile, width):
    row = lax.broadcasted_iota(jnp.int32, (tile, width), 0) + (width - tile)
    return row >= lax.broadcasted_iota(jnp.int32, (tile, width), 1)


def run_copies(sems, pairs):
    copies = [
        pltpu.make_async_copy(source, target, sems.at[i])
        for i, (source, target) in enumerate(pairs)
    ]
    for copy in copies:
        copy.start()
    for copy in copies:
        copy.wait()


def aligned(at, size):
    return pl.ds(pl.multiple_of(at * size, size), size)


def token_parts_kernel(at_ref, tokens_ref, *rest):
    *out_refs, sems = rest
    count, share = len(out_refs) + 1, out_refs[0].shape[1]
    run_copies(
        sems,
        [
            (tokens_ref.at[0, :, aligned(lax.rem(at_ref[0] + shift, count), share)], out_ref)
            for shift, out_ref in enumerate(out_refs, 1)
        ],
    )


def pack_heads_kernel(at_ref, values_ref, grad_ref, *out_refs):
    chips, width = len(out_refs), out_refs[0].shape[3]
    for shift, out_ref in enumerate(out_refs):
        chip = lax.rem(at_ref[0] + shift, chips)
        for core in range(2):
            cols = aligned(2 * chip + core, width)
            out_ref[core, 0] = values_ref[0, :, cols]
            out_ref[core, 1] = grad_ref[0, :, cols]


def split_cores_kernel(at_ref, *rest):
    *part_refs, keep_ref, send_ref = rest
    for shift, part_ref in enumerate(part_refs):
        keep_ref[shift] = part_ref[at_ref[1]]
        send_ref[shift] = part_ref[1 - at_ref[1]]


def collect_heads_kernel(at_ref, keep_ref, got_ref, out_ref):
    chips = keep_ref.shape[0]
    for shift in range(chips):
        chip = lax.rem(at_ref[0] + chips - shift, chips)
        out_ref[2 * chip + at_ref[1]] = keep_ref[shift]
        out_ref[2 * chip + 1 - at_ref[1]] = got_ref[shift]


def pack_tokens_kernel(depth, at_ref, tokens_ref, keep_ref, send_ref):
    chips, _, rows = keep_ref.shape
    for shift in range(chips):
        chip = lax.rem(at_ref[0] + shift, chips)
        for core, out_ref in ((at_ref[1], keep_ref), (1 - at_ref[1], send_ref)):
            for part in range(rows // depth):
                cols = aligned(2 * (part * chips + chip) + core, depth)
                out_ref[shift, :, part * depth : (part + 1) * depth] = tokens_ref[0, :, cols]


def collect_tokens_kernel(at_ref, *rest):
    *part_refs, out_ref = rest
    chips, tok = len(part_refs), part_refs[0].shape[1]
    for shift, part_ref in enumerate(part_refs):
        chip = lax.rem(at_ref[0] + chips - shift, chips)
        for core in range(2):
            out_ref[:, aligned(2 * chip + core, tok)] = part_ref[core].T


def write_blocks(projected, out_ref):
    group, _, heads, feat, _ = out_ref.shape
    for member in range(group):
        for which in range(2):
            for head in range(heads):
                first = ((which * group + member) * heads + head) * feat
                out_ref[member, which, head] = projected[first : first + feat]


def project_kernel(at_ref, tokens_ref, weight_ref, out_ref, part_ref, sem):
    share = part_ref.shape[1]
    run_copies(sem, [(tokens_ref.at[0, :, aligned(at_ref[0], share)], part_ref)])
    write_blocks(dot(part_ref[...], weight_ref[...]).T, out_ref)


def project_rest_kernel(at_ref, own_ref, weight_ref, *rest):
    *part_refs, out_ref = rest
    count = len(part_refs) + 1
    at = at_ref[0]
    out_ref[at] = own_ref[...]
    for shift, part_ref in enumerate(part_refs, 1):
        owner = lax.rem(at + count - shift, count)
        write_blocks(dot(part_ref[...], weight_ref[...]).T, out_ref.at[owner])


def weight_piece_kernel(at_ref, weight_ref, out_ref, sems):
    run_copies(sems, [(weight_ref.at[aligned(at_ref[0], out_ref.shape[0])], out_ref)])


def state_sum(refs, head):
    total = refs[0][head].astype(f32)
    for ref in refs[1:]:
        total = total + ref[head].astype(f32)
    return total


def state_kernel(with_state, parts_ref, vg_ref, qk_ref, *state_refs):
    count, blocks, _, heads, _, tok = parts_ref.shape
    for head in range(heads):
        for which in range(2):
            for src in range(blocks):
                total = parts_ref[0, src, which, head]
                for part in range(1, count):
                    total = total + parts_ref[part, src, which, head]
                qk_ref[src, which, head] = total
        if with_state:
            high, low = split(psi(feature_major(qk_ref, 1, head), False))
            v = rows_of(vg_ref, 0, head, 0, blocks * tok)
            state_refs[0][head] = (dot(high, v) + dot(low, v)).astype(bf16)


def numerator_kernel(qk_ref, vg_ref, num_ref):
    heads = qk_ref.shape[2]
    length = qk_ref.shape[0] * qk_ref.shape[4]
    tile = min(TILE, length)
    for head in range(heads):
        q = feature_major(qk_ref, 0, head) * 0.25
        k = feature_major(qk_ref, 1, head)
        left, right = score_sides(q, k)
        for at in range(0, length, tile):
            width = at + tile
            scores = dot(left[at:width], right[:, :width])
            kernel = jnp.where(
                causal_mask(tile, width), 1.0 + scores * (1.0 + 0.5 * scores), 0.0
            )
            high, low = split(kernel)
            v = rows_of(vg_ref, 0, head, 0, width)
            num_ref[at:width, head * DH : (head + 1) * DH] = dot(high, v) + dot(low, v)


def normalize_kernel(with_state, qk_ref, vg_ref, num_ref, *rest):
    if with_state:
        *prefix_refs, attended_ref, grad_ref, carried_ref = rest
    else:
        attended_ref, grad_ref = rest
    heads = qk_ref.shape[2]
    blocks, tok = qk_ref.shape[0], qk_ref.shape[4]
    length = blocks * tok
    for head in range(heads):
        cols = slice(head * DH, (head + 1) * DH)
        numerator = num_ref[:, cols]
        if with_state:
            feat = psi(feature_major(qk_ref, 0, head) * 0.25, True)
            numerator = numerator + dot3(feat.T, state_sum(prefix_refs, head))
        inv_rms = lax.rsqrt(jnp.mean(numerator * numerator, axis=-1, keepdims=True) + EPSILON)
        normed = numerator * inv_rms
        upstream = rows_of(vg_ref, 1, head, 0, length).astype(f32)
        grad = inv_rms * (
            upstream - normed * jnp.mean(normed * upstream, axis=-1, keepdims=True)
        )
        attended_ref[:, cols] = normed.astype(bf16)
        grad_ref[:, cols] = grad
        if with_state:
            carried_ref[head] = dot3(feat, grad).astype(bf16)


def backward_kernel(with_state, qk_ref, vg_ref, grad_ref, *rest):
    *prefix_refs, grad_qk_ref, grad_v_ref = rest
    length = qk_ref.shape[0] * qk_ref.shape[4]
    tile = min(TILE, length)
    for head in range(grad_v_ref.shape[0]):
        cols = slice(head * DH, (head + 1) * DH)
        q = feature_major(qk_ref, 0, head) * 0.25
        k = feature_major(qk_ref, 1, head)
        left, right = score_sides(q, k)
        q_both = jnp.concatenate(split(q), axis=0)
        k_both = jnp.concatenate(split(k), axis=0)
        grad = grad_ref[:, cols]
        grad_t = grad.T
        if with_state:
            grad_q = pull_psi(q, dot3(state_sum(prefix_refs, head), grad_t), True)
        for at in reversed(range(0, length, tile)):
            width = at + tile
            scores = dot(left[at:width], right[:, :width])
            causal = causal_mask(tile, width)
            v = rows_of(vg_ref, 0, head, 0, width)
            high, low = split(grad[at:width])
            mixing = dot(
                jnp.concatenate([high, low], axis=1), jnp.concatenate([v, v], axis=1), NT
            )
            more = 1.0 + scores
            slopes = split(jnp.where(causal, mixing * more, 0.0))
            kernels = split(jnp.where(causal, more + 0.5 * scores * scores, 0.0))
            both = dot(k_both[:, :width], slopes[0], NT)
            piece = both[:F] + (both[F:] + dot(k_both[:F, :width], slopes[1], NT))
            if with_state:
                piece = piece + grad_q[:, at:width]
            grad_qk_ref[0, head, :, at:width] = piece * 0.25
            both = dot(q_both[:, at:width], slopes[0])
            piece_k = both[:F] + (both[F:] + dot(q_both[:F, at:width], slopes[1]))
            high, low = split(grad_t[:, at:width])
            both = dot(jnp.concatenate([high, low], axis=0), kernels[0])
            piece_v = both[:DH] + (both[DH:] + dot(high, kernels[1]))
            if width == length:
                grad_qk_ref[1, head] = piece_k
                grad_v_ref[head] = piece_v
            else:
                grad_qk_ref[1, head, :, :width] += piece_k
                grad_v_ref[head, :, :width] += piece_v


def rows_kernel(with_state, at_ref, qk_ref, vg_ref, attended_ref, grad_qk_ref, grad_v_ref, *rest):
    *suffix_refs, rows_ref, keep_ref, send_ref, held_ref = rest
    heads, tok = qk_ref.shape[2], qk_ref.shape[4]
    length = qk_ref.shape[0] * tok
    for head in range(heads):
        grad_k, grad_v = grad_qk_ref[1, head], grad_v_ref[head]
        if with_state:
            k = feature_major(qk_ref, 1, head)
            v = rows_of(vg_ref, 0, head, 0, length)
            suffix = state_sum(suffix_refs, head)
            high, low = split(suffix)
            grad_k = grad_k + pull_psi(k, dot(high, v, NT) + dot(low, v, NT), False)
            grad_v = grad_v + dot3(suffix.T, psi(k, False))
        rows_ref[head * F : (head + 1) * F] = grad_qk_ref[0, head].astype(bf16)
        rows_ref[(heads + head) * F : (heads + head + 1) * F] = grad_k.astype(bf16)
        held_ref[:, head * DH : (head + 1) * DH] = grad_v.T.astype(bf16)
    chips = keep_ref.shape[0]
    for shift in range(chips):
        chip = lax.rem(at_ref[0] + shift, chips)
        for core, out_ref in ((at_ref[1], keep_ref), (1 - at_ref[1], send_ref)):
            block = aligned(2 * chip + core, tok)
            out_ref[shift, 0] = attended_ref[block, :]
            out_ref[shift, 1] = held_ref[block, :]


def pair_kernel(at_ref, keep_ref, got_ref, *out_refs):
    for shift, out_ref in enumerate(out_refs):
        out_ref[at_ref[1]] = keep_ref[shift]
        out_ref[1 - at_ref[1]] = got_ref[shift]


def unpack_heads_kernel(at_ref, *rest):
    *part_refs, attended_ref, values_ref = rest
    chips, width = len(part_refs), part_refs[0].shape[3]
    for shift, part_ref in enumerate(part_refs):
        chip = lax.rem(at_ref[0] + chips - shift, chips)
        for core in range(2):
            cols = aligned(2 * chip + core, width)
            attended_ref[0, :, cols] = part_ref[core, 0]
            values_ref[0, :, cols] = part_ref[core, 1]


def place_rows(chip_at, core_at, part_refs, held_ref):
    chips, half = len(part_refs) // 2, part_refs[0].shape[0] // 2
    for shift in range(chips):
        chip = lax.rem(chip_at + chips - shift, chips)
        for side, core in ((0, core_at), (1, 1 - core_at)):
            part_ref = part_refs[2 * shift + side]
            for which in range(2):
                rows = aligned(which * 2 * chips + 2 * chip + core, half)
                held_ref[rows, :] = part_ref[which * half : (which + 1) * half, :]


def product_kernel(group, at_ref, *rest):
    rows_refs, rest = rest[:group], rest[group:]
    tokens_ref, own_rows_ref, other_rows_ref, *part_refs, total_ref, held_ref = rest
    place_rows(at_ref[1], at_ref[2], rows_refs, held_ref)
    total_ref[...] = dot(tokens_ref[...], held_ref[...], NT)
    tok = own_rows_ref.shape[0]
    own_rows_ref[...] = held_ref[:, aligned(2 * at_ref[1] + at_ref[2], tok)].T
    other_rows_ref[...] = held_ref[:, aligned(2 * at_ref[1] + 1 - at_ref[2], tok)].T
    count = len(part_refs)
    size = part_refs[0].shape[0]
    for shift, part_ref in enumerate(part_refs):
        owner = lax.rem(at_ref[0] + shift, count)
        part = total_ref[pl.ds(pl.multiple_of(owner * size, size), size), :]
        part_ref[...] = part.astype(part_ref.dtype)


def run_sum_kernel(arrived, at_ref, *rest):
    own_ref, *rest = rest
    total_ref = rest[-1]
    total = own_ref[...]
    for ref in rest[:arrived]:
        total = total + ref[...].astype(f32)
    total_ref[...] = total
    part_refs = rest[arrived:-1]
    size = part_refs[0].shape[0]
    for shift, part_ref in enumerate(part_refs):
        owner = lax.rem(at_ref[0] + shift, len(part_refs))
        part = total_ref[pl.ds(pl.multiple_of(owner * size, size), size), :]
        part_ref[...] = part.astype(part_ref.dtype)


def grad_tokens_kernel(at_ref, rows_ref, other_rows_ref, weight_ref, *rest):
    count = len(rest) // 2
    fetched_refs, out_ref, other_refs = rest[:count], rest[count], rest[count + 1 :]
    for i, ref in enumerate((weight_ref, *fetched_refs)):
        size = ref.shape[0]
        first = pl.multiple_of(at_ref[i], size)
        out_ref[0, :, pl.ds(first, size)] = dot(rows_ref[...], ref[...], NT).astype(bf16)
    for ref, other_ref in zip(fetched_refs, other_refs):
        other_ref[...] = dot(other_rows_ref[...], ref[...], NT).astype(bf16)


def merge_kernel(at_ref, main_ref, *rest):
    *part_refs, out_ref, sems = rest
    run_copies(
        sems,
        [
            (part_ref, out_ref.at[0, :, pl.ds(pl.multiple_of(at_ref[i], size), size)])
            for i, part_ref in enumerate(part_refs)
            for size in part_ref.shape[1:]
        ],
    )


def final_sum_kernel(own_ref, *rest):
    *part_refs, out_ref = rest
    total = own_ref[...]
    for part_ref in part_refs:
        total = total + part_ref[...].astype(f32)
    out_ref[...] = total


VMEM = pl.BlockSpec(memory_space=pltpu.VMEM)
SMEM = pl.BlockSpec(memory_space=pltpu.SMEM)
FAR = pl.BlockSpec(memory_space=pltpu.HBM)
ANYWHERE = pl.BlockSpec(memory_space=pl.ANY)


def call(
    body,
    outs,
    *operands,
    scalars=(),
    after=(),
    after_far=(),
    scratch=(),
    far_in=(),
    far_out=False,
    copies=(),
    alias=False,
):
    at = [jnp.stack([jnp.int32(s) for s in scalars])] if scalars else []
    count = len(at) + len(operands)

    def kernel(*refs):
        ins, rest = refs[:count], refs[count + len(after) + len(after_far) :]
        body(*ins, *rest[: len(outs)], *rest[len(outs) + 1 :])
        rest[len(outs)][...] = jnp.zeros((8, 128), f32)

    *results, token = pl.pallas_call(
        kernel,
        out_shape=[jax.ShapeDtypeStruct(shape, kind) for shape, kind in [*outs, ((8, 128), f32)]],
        in_specs=[SMEM] * len(at)
        + [FAR if i in far_in else VMEM for i in range(len(operands))]
        + [ANYWHERE] * len(after)
        + [FAR] * len(after_far),
        out_specs=[FAR if far_out else VMEM] * len(outs) + [VMEM],
        scratch_shapes=[*scratch] + [pltpu.SemaphoreType.DMA((n,)) for n in copies],
        input_output_aliases={len(at): 0} if alias else {},
        compiler_params=pltpu.CompilerParams(vmem_limit_bytes=VMEM_LIMIT),
        cost_estimate=pl.CostEstimate(flops=0, bytes_accessed=0, transcendentals=0),
    )(*at, *operands, *after, *after_far)
    return results, token


def local(dp_size, ctx_size, tokens, proj_weight, values, grad_out):
    group = min(GROUP, ctx_size, H)
    runs = ctx_size // group
    heads = H // group
    tok, width = tokens.shape[1:]
    length = group * tok
    cols = proj_weight.shape[1]
    share = width // dp_size
    depth = share // ctx_size
    with_state = runs > 1
    groups = [[run * group + i for i in range(group)] for run in range(runs)]
    wide_groups = [
        [dp * ctx_size + i for dp in range(dp_size) for i in members] for members in groups
    ]
    dp_at, ctx_at = lax.axis_index("dp"), lax.axis_index("ctx")
    run_at, member = ctx_at // group, ctx_at % group

    def exchange(x):
        return lax.all_to_all(
            x, "ctx", split_axis=0, concat_axis=0, tiled=True, axis_index_groups=groups
        )

    def to_dp(x, shift):
        return lax.ppermute(x, "dp", [(i, (i + shift) % dp_size) for i in range(dp_size)])

    def to_member(x, shift):
        pairs = [(i, i - i % group + (i + shift) % group) for i in range(ctx_size)]
        return lax.ppermute(x, "ctx", pairs)

    chips = group // 2
    chip_at, core_at = member // 2, member % 2

    def to_chip(x, shift):
        return x if shift == 0 else to_member(x, 2 * shift)

    def to_other_core(x):
        return lax.ppermute(x, "ctx", [(i, i ^ 1) for i in range(ctx_size)])

    def to_run(x, shift, wrap):
        pairs = [
            (i, (i + shift * group) % ctx_size)
            for i in range(ctx_size)
            if wrap or 0 <= i + shift * group < ctx_size
        ]
        return lax.ppermute(x, "ctx", pairs)

    qk_shape = ((group, 2, heads, F, tok), f32)
    state_shape = ((heads, PSI, DH), bf16)
    blocks_shape = ((2, tok, heads * DH), bf16)
    rows_shape = ((length, heads * DH), f32)

    parts, token = call(
        token_parts_kernel,
        [((tok, share), bf16)] * (dp_size - 1),
        tokens,
        scalars=(dp_at,),
        far_in=(0,),
        far_out=True,
        copies=(dp_size - 1,),
    )
    arrived = [to_dp(part, shift) for shift, part in enumerate(parts, 1)]
    parts, heads_token = call(
        pack_heads_kernel,
        [((2, 2, tok, heads * DH), bf16)] * chips,
        values,
        grad_out,
        scalars=(chip_at, core_at),
        after=(token,),
    )
    heads_parts = [to_chip(part, shift) for shift, part in enumerate(parts)]
    (keep, send), _ = call(
        split_cores_kernel,
        [((chips, 2, tok, heads * DH), bf16)] * 2,
        *heads_parts,
        scalars=(chip_at, core_at),
    )
    (vg,), _ = call(
        collect_heads_kernel,
        [((group, 2, tok, heads * DH), bf16)],
        keep,
        to_other_core(send),
        scalars=(chip_at, core_at),
    )
    (projected,), token = call(
        project_kernel,
        [qk_shape],
        tokens,
        proj_weight,
        scalars=(dp_at,),
        after=(token,),
        far_in=(0,),
        copies=(1,),
        scratch=[pltpu.VMEM((tok, share), bf16)],
    )
    part_shape = (tok, dp_size * runs * depth)
    if depth % 128 == 0:
        (keep, send), _ = call(
            functools.partial(pack_tokens_kernel, depth),
            [((chips,) + part_shape, bf16)] * 2,
            tokens,
            scalars=(chip_at, core_at),
            after=(heads_token,),
        )
    else:
        blocks = tokens[0].reshape(tok, dp_size * runs, chips, 2, depth).transpose(2, 3, 0, 1, 4)
        blocks = blocks.reshape(chips, 2, *part_shape)
        blocks = jnp.stack([blocks[(chip_at + shift) % chips] for shift in range(chips)])
        keep, send = blocks[:, core_at], blocks[:, 1 - core_at]
    token_parts, pair_token = call(
        pair_kernel,
        [((2,) + part_shape, bf16)] * chips,
        keep,
        to_other_core(send),
        scalars=(chip_at, core_at),
    )
    token_parts = [to_chip(part, shift) for shift, part in enumerate(token_parts)]
    parity = ctx_at % 2
    piece = share // 2
    (mine,), mine_token = call(
        weight_piece_kernel,
        [((piece, cols), bf16)],
        proj_weight,
        scalars=(parity,),
        after=(heads_token,),
        far_in=(0,),
        far_out=True,
        copies=(1,),
    )
    (projected,), _ = call(
        project_rest_kernel,
        [((dp_size,) + qk_shape[0], f32)],
        projected,
        proj_weight,
        *arrived,
        scalars=(dp_at,),
        after=(token, pair_token, mine_token),
        after_far=heads_parts[1:],
    )
    qk_parts = lax.all_to_all(
        projected.reshape((dp_size * group,) + qk_shape[0][1:]),
        ("dp", "ctx"),
        split_axis=0,
        concat_axis=0,
        tiled=True,
        axis_index_groups=wide_groups,
    ).reshape(projected.shape)

    fetched = [to_dp(mine, shift) for shift in range(1, dp_size)]
    bases = [(dp_at + dp_size - shift) % dp_size * share for shift in range(1, dp_size)]

    (qk, *state), token = call(
        functools.partial(state_kernel, with_state),
        [qk_shape] + [state_shape] * with_state,
        qk_parts,
        vg,
    )
    prefix, suffix = (), ()
    if with_state:
        prefix = [to_run(state[0], shift, False) for shift in range(1, runs)]
    (numerator,), token = call(numerator_kernel, [rows_shape], qk, vg)
    (attended, grad_num, *carried), token = call(
        functools.partial(normalize_kernel, with_state),
        [((length, heads * DH), bf16), rows_shape] + [state_shape] * with_state,
        qk,
        vg,
        numerator,
        *prefix,
        after_far=token_parts[1:],
    )
    if with_state:
        suffix = [to_run(carried[0], -shift, False) for shift in range(1, runs)]
    (grad_qk, grad_v), token = call(
        functools.partial(backward_kernel, with_state),
        [((2, heads, F, length), f32), ((heads, DH, length), f32)],
        qk,
        vg,
        grad_num,
        *prefix,
    )
    (token_cols,), token = call(
        collect_tokens_kernel,
        [(part_shape[1:] + (length,), bf16)],
        *token_parts,
        scalars=(chip_at,),
        after=(token,),
    )
    (rows, keep, send), token = call(
        functools.partial(rows_kernel, with_state),
        [((2 * heads * F, length), bf16)] + [((chips, 2, tok, heads * DH), bf16)] * 2,
        qk,
        vg,
        attended,
        grad_qk,
        grad_v,
        *suffix,
        scalars=(chip_at, core_at),
        after=(token,),
        scratch=[pltpu.VMEM((length, heads * DH), bf16)],
    )
    rows = [to_chip(rows, shift) for shift in range(chips)]
    rows = [side for part in rows for side in (part, to_other_core(part))]
    got = to_other_core(send)
    results, token = call(
        pair_kernel,
        [((2, 2, tok, heads * DH), bf16)] * chips,
        keep,
        got,
        scalars=(chip_at, core_at),
    )
    results = [to_chip(part, shift) for shift, part in enumerate(results)]

    held = pltpu.VMEM((cols, length), bf16)
    (own_rows, other_rows, own, *parts), token = call(
        functools.partial(product_kernel, 2 * chips),
        [((tok, cols), bf16)] * 2
        + [((runs * depth, cols), f32)] + [((runs * depth, cols), bf16)] * (dp_size - 1),
        *rows,
        token_cols,
        scalars=(dp_at, chip_at, core_at),
        after=(token,),
        scratch=[pltpu.VMEM((dp_size * runs * depth, cols), f32), held],
    )
    parts = [to_dp(part, shift) for shift, part in enumerate(parts, 1)]
    (grad_tokens, *others), tokens_token = call(
        grad_tokens_kernel,
        [((1, tok, width), bf16)] + [((tok, piece), bf16)] * (dp_size - 1),
        own_rows,
        other_rows,
        proj_weight,
        *fetched,
        scalars=[dp_at * share] + [base + parity * piece for base in bases],
        after_far=parts,
    )
    (grad_proj, *parts), token = call(
        functools.partial(run_sum_kernel, len(parts)),
        [((depth, cols), f32)] + [((depth, cols), bf16)] * (runs - 1),
        own,
        *parts,
        scalars=(run_at,),
        scratch=[pltpu.VMEM((runs * depth, cols), f32)],
    )
    (attended, grad_values), token = call(
        unpack_heads_kernel,
        [((1, tok, H * DH), bf16)] * 2,
        *results,
        scalars=(chip_at,),
        after=(token,),
    )
    (grad_tokens,), tokens_token = call(
        merge_kernel,
        [((1, tok, width), bf16)],
        grad_tokens,
        *[to_other_core(other) for other in others],
        scalars=[base + (1 - parity) * piece for base in bases],
        far_in=(0,),
        far_out=True,
        copies=(dp_size - 1,),
        alias=True,
    )
    (grad_proj,), _ = call(
        final_sum_kernel,
        [((depth, cols), f32)],
        grad_proj,
        *[to_run(part, shift, True) for shift, part in enumerate(parts, 1)],
        after=(token, tokens_token),
    )
    return (attended, grad_tokens, grad_values, grad_proj)


def solution(mesh):
    return jax.shard_map(
        functools.partial(local, mesh.shape["dp"], mesh.shape["ctx"]),
        mesh=mesh,
        in_specs=(P("dp", "ctx", None), P("dp", None), P("dp", "ctx", None), P("dp", "ctx", None)),
        out_specs=(
            P("dp", "ctx", None),
            P("dp", "ctx", None),
            P("dp", "ctx", None),
            P(("dp", "ctx"), None),
        ),
        check_vma=False,
    )
```

```python
import functools

import jax
import jax.numpy as jnp
from jax import lax
from jax.experimental import pallas as pl
from jax.experimental.pallas import tpu as pltpu
from jax.sharding import PartitionSpec as P

H = 16
F = 16
DH = 128
EPSILON = 1e-05
GROUP = 8
TILE = 256
VMEM_LIMIT = 16 * 1024 * 1024
PSI = 9 * F + 2 * F
PSI_SCALE = (0.5,) + (1.0,) * 7 + (0.5,)

f32 = jnp.float32
bf16 = jnp.bfloat16

NN = (((1,), (0,)), ((), ()))
NT = (((1,), (1,)), ((), ()))


def dot(a, b, dims=NN):
    return lax.dot_general(a, b, dims, preferred_element_type=f32)


def split(x):
    high = x.astype(bf16)
    return high, (x - high.astype(f32)).astype(bf16)


def dot3(a, b, dims=NN):
    a_high, a_low = split(a)
    b_high, b_low = split(b)
    return dot(a_high, b_high, dims) + (dot(a_high, b_low, dims) + dot(a_low, b_high, dims))


def turned(x, r):
    return x if r == 0 else jnp.concatenate([x[r:], x[:r]], axis=0)


def psi(x, weights):
    parts = []
    for r in range(9):
        part = x * turned(x, r)
        parts.append(part * PSI_SCALE[r] if weights and PSI_SCALE[r] != 1.0 else part)
    row = lax.broadcasted_iota(jnp.int32, x.shape, 0)
    return jnp.concatenate(parts + [x, jnp.where(row == 0, 1.0, 0.0)], axis=0)


def pull_psi(x, upstream, weights):
    total = upstream[9 * F : 10 * F]
    for r in range(9):
        part = upstream[r * F : (r + 1) * F]
        if weights and PSI_SCALE[r] != 1.0:
            part = part * PSI_SCALE[r]
        total = total + part * turned(x, r) + turned(part * x, (F - r) % F)
    return total


def feature_major(qk_ref, which, head):
    return jnp.concatenate([qk_ref[src, which, head] for src in range(qk_ref.shape[0])], axis=1)


def rows_of(ref, which, head, start, stop):
    tok = ref.shape[2]
    return jnp.concatenate(
        [
            ref[src, which, :, head * DH : (head + 1) * DH]
            for src in range(start // tok, stop // tok)
        ],
        axis=0,
    )


def score_sides(q, k):
    q_high, q_low = split(q)
    k_high, k_low = split(k)
    left = jnp.concatenate([q_high, q_high, q_low, q_low], axis=0)
    right = jnp.concatenate([k_high, k_low, k_high, k_low], axis=0)
    return left.T, right


def causal_mask(tile, width):
    row = lax.broadcasted_iota(jnp.int32, (tile, width), 0) + (width - tile)
    return row >= lax.broadcasted_iota(jnp.int32, (tile, width), 1)


def run_copies(sems, pairs):
    copies = [
        pltpu.make_async_copy(source, target, sems.at[i])
        for i, (source, target) in enumerate(pairs)
    ]
    for copy in copies:
        copy.start()
    for copy in copies:
        copy.wait()


def aligned(at, size):
    return pl.ds(pl.multiple_of(at * size, size), size)


def token_parts_kernel(at_ref, tokens_ref, *rest):
    *out_refs, sems = rest
    count, share = len(out_refs) + 1, out_refs[0].shape[1]
    run_copies(
        sems,
        [
            (tokens_ref.at[0, :, aligned(lax.rem(at_ref[0] + shift, count), share)], out_ref)
            for shift, out_ref in enumerate(out_refs, 1)
        ],
    )


def pack_heads_kernel(at_ref, values_ref, grad_ref, *out_refs):
    chips, width = len(out_refs), out_refs[0].shape[3]
    for shift, out_ref in enumerate(out_refs):
        chip = lax.rem(at_ref[0] + shift, chips)
        for core in range(2):
            cols = aligned(2 * chip + core, width)
            out_ref[core, 0] = values_ref[0, :, cols]
            out_ref[core, 1] = grad_ref[0, :, cols]


def split_cores_kernel(at_ref, *rest):
    *part_refs, keep_ref, send_ref = rest
    for shift, part_ref in enumerate(part_refs):
        keep_ref[shift] = part_ref[at_ref[1]]
        send_ref[shift] = part_ref[1 - at_ref[1]]


def collect_heads_kernel(at_ref, keep_ref, got_ref, out_ref):
    chips = keep_ref.shape[0]
    for shift in range(chips):
        chip = lax.rem(at_ref[0] + chips - shift, chips)
        out_ref[2 * chip + at_ref[1]] = keep_ref[shift]
        out_ref[2 * chip + 1 - at_ref[1]] = got_ref[shift]


def pack_tokens_kernel(depth, at_ref, tokens_ref, keep_ref, send_ref):
    chips, _, rows = keep_ref.shape
    for shift in range(chips):
        chip = lax.rem(at_ref[0] + shift, chips)
        for core, out_ref in ((at_ref[1], keep_ref), (1 - at_ref[1], send_ref)):
            for part in range(rows // depth):
                cols = aligned(2 * (part * chips + chip) + core, depth)
                out_ref[shift, :, part * depth : (part + 1) * depth] = tokens_ref[0, :, cols]


def collect_tokens_kernel(at_ref, *rest):
    *part_refs, out_ref = rest
    chips, tok = len(part_refs), part_refs[0].shape[1]
    for shift, part_ref in enumerate(part_refs):
        chip = lax.rem(at_ref[0] + chips - shift, chips)
        for core in range(2):
            out_ref[:, aligned(2 * chip + core, tok)] = part_ref[core].T


def write_blocks(projected, out_ref):
    group, _, heads, feat, _ = out_ref.shape
    for member in range(group):
        for which in range(2):
            for head in range(heads):
                first = ((which * group + member) * heads + head) * feat
                out_ref[member, which, head] = projected[first : first + feat]


def project_kernel(at_ref, tokens_ref, weight_ref, out_ref, part_ref, sem):
    share = part_ref.shape[1]
    run_copies(sem, [(tokens_ref.at[0, :, aligned(at_ref[0], share)], part_ref)])
    write_blocks(dot(part_ref[...], weight_ref[...]).T, out_ref)


def project_rest_kernel(at_ref, own_ref, weight_ref, *rest):
    *part_refs, out_ref = rest
    count = len(part_refs) + 1
    at = at_ref[0]
    out_ref[at] = own_ref[...]
    for shift, part_ref in enumerate(part_refs, 1):
        owner = lax.rem(at + count - shift, count)
        write_blocks(dot(part_ref[...], weight_ref[...]).T, out_ref.at[owner])


def weight_piece_kernel(at_ref, weight_ref, out_ref, sems):
    run_copies(sems, [(weight_ref.at[aligned(at_ref[0], out_ref.shape[0])], out_ref)])


def state_sum(refs, head):
    total = refs[0][head].astype(f32)
    for ref in refs[1:]:
        total = total + ref[head].astype(f32)
    return total


def state_kernel(with_state, parts_ref, vg_ref, qk_ref, *state_refs):
    count, blocks, _, heads, _, tok = parts_ref.shape
    for head in range(heads):
        for which in range(2):
            for src in range(blocks):
                total = parts_ref[0, src, which, head]
                for part in range(1, count):
                    total = total + parts_ref[part, src, which, head]
                qk_ref[src, which, head] = total
        if with_state:
            high, low = split(psi(feature_major(qk_ref, 1, head), False))
            v = rows_of(vg_ref, 0, head, 0, blocks * tok)
            state_refs[0][head] = (dot(high, v) + dot(low, v)).astype(bf16)


def numerator_kernel(qk_ref, vg_ref, num_ref):
    heads = qk_ref.shape[2]
    length = qk_ref.shape[0] * qk_ref.shape[4]
    tile = min(TILE, length)
    for head in range(heads):
        q = feature_major(qk_ref, 0, head) * 0.25
        k = feature_major(qk_ref, 1, head)
        left, right = score_sides(q, k)
        for at in range(0, length, tile):
            width = at + tile
            scores = dot(left[at:width], right[:, :width])
            kernel = jnp.where(
                causal_mask(tile, width), 1.0 + scores * (1.0 + 0.5 * scores), 0.0
            )
            high, low = split(kernel)
            v = rows_of(vg_ref, 0, head, 0, width)
            num_ref[at:width, head * DH : (head + 1) * DH] = dot(high, v) + dot(low, v)


def normalize_kernel(with_state, qk_ref, vg_ref, num_ref, *rest):
    if with_state:
        *prefix_refs, attended_ref, grad_ref, carried_ref = rest
    else:
        attended_ref, grad_ref = rest
    heads = qk_ref.shape[2]
    blocks, tok = qk_ref.shape[0], qk_ref.shape[4]
    length = blocks * tok
    for head in range(heads):
        cols = slice(head * DH, (head + 1) * DH)
        numerator = num_ref[:, cols]
        if with_state:
            feat = psi(feature_major(qk_ref, 0, head) * 0.25, True)
            numerator = numerator + dot3(feat.T, state_sum(prefix_refs, head))
        inv_rms = lax.rsqrt(jnp.mean(numerator * numerator, axis=-1, keepdims=True) + EPSILON)
        normed = numerator * inv_rms
        upstream = rows_of(vg_ref, 1, head, 0, length).astype(f32)
        grad = inv_rms * (
            upstream - normed * jnp.mean(normed * upstream, axis=-1, keepdims=True)
        )
        attended_ref[:, cols] = normed.astype(bf16)
        grad_ref[:, cols] = grad
        if with_state:
            carried_ref[head] = dot3(feat, grad).astype(bf16)


def backward_kernel(with_state, qk_ref, vg_ref, grad_ref, *rest):
    *prefix_refs, grad_qk_ref, grad_v_ref = rest
    length = qk_ref.shape[0] * qk_ref.shape[4]
    tile = min(TILE, length)
    for head in range(grad_v_ref.shape[0]):
        cols = slice(head * DH, (head + 1) * DH)
        q = feature_major(qk_ref, 0, head) * 0.25
        k = feature_major(qk_ref, 1, head)
        left, right = score_sides(q, k)
        q_both = jnp.concatenate(split(q), axis=0)
        k_both = jnp.concatenate(split(k), axis=0)
        grad = grad_ref[:, cols]
        grad_t = grad.T
        if with_state:
            grad_q = pull_psi(q, dot3(state_sum(prefix_refs, head), grad_t), True)
        for at in reversed(range(0, length, tile)):
            width = at + tile
            scores = dot(left[at:width], right[:, :width])
            causal = causal_mask(tile, width)
            v = rows_of(vg_ref, 0, head, 0, width)
            high, low = split(grad[at:width])
            mixing = dot(
                jnp.concatenate([high, low], axis=1), jnp.concatenate([v, v], axis=1), NT
            )
            more = 1.0 + scores
            slopes = split(jnp.where(causal, mixing * more, 0.0))
            kernels = split(jnp.where(causal, more + 0.5 * scores * scores, 0.0))
            both = dot(k_both[:, :width], slopes[0], NT)
            piece = both[:F] + (both[F:] + dot(k_both[:F, :width], slopes[1], NT))
            if with_state:
                piece = piece + grad_q[:, at:width]
            grad_qk_ref[0, head, :, at:width] = piece * 0.25
            both = dot(q_both[:, at:width], slopes[0])
            piece_k = both[:F] + (both[F:] + dot(q_both[:F, at:width], slopes[1]))
            high, low = split(grad_t[:, at:width])
            both = dot(jnp.concatenate([high, low], axis=0), kernels[0])
            piece_v = both[:DH] + (both[DH:] + dot(high, kernels[1]))
            if width == length:
                grad_qk_ref[1, head] = piece_k
                grad_v_ref[head] = piece_v
            else:
                grad_qk_ref[1, head, :, :width] += piece_k
                grad_v_ref[head, :, :width] += piece_v


def rows_kernel(with_state, at_ref, qk_ref, vg_ref, attended_ref, grad_qk_ref, grad_v_ref, *rest):
    *suffix_refs, rows_ref, keep_ref, send_ref, held_ref = rest
    heads, tok = qk_ref.shape[2], qk_ref.shape[4]
    length = qk_ref.shape[0] * tok
    for head in range(heads):
        grad_k, grad_v = grad_qk_ref[1, head], grad_v_ref[head]
        if with_state:
            k = feature_major(qk_ref, 1, head)
            v = rows_of(vg_ref, 0, head, 0, length)
            suffix = state_sum(suffix_refs, head)
            high, low = split(suffix)
            grad_k = grad_k + pull_psi(k, dot(high, v, NT) + dot(low, v, NT), False)
            grad_v = grad_v + dot3(suffix.T, psi(k, False))
        rows_ref[head * F : (head + 1) * F] = grad_qk_ref[0, head].astype(bf16)
        rows_ref[(heads + head) * F : (heads + head + 1) * F] = grad_k.astype(bf16)
        held_ref[:, head * DH : (head + 1) * DH] = grad_v.T.astype(bf16)
    chips = keep_ref.shape[0]
    for shift in range(chips):
        chip = lax.rem(at_ref[0] + shift, chips)
        for core, out_ref in ((at_ref[1], keep_ref), (1 - at_ref[1], send_ref)):
            block = aligned(2 * chip + core, tok)
            out_ref[shift, 0] = attended_ref[block, :]
            out_ref[shift, 1] = held_ref[block, :]


def pair_kernel(at_ref, keep_ref, got_ref, *out_refs):
    for shift, out_ref in enumerate(out_refs):
        out_ref[at_ref[1]] = keep_ref[shift]
        out_ref[1 - at_ref[1]] = got_ref[shift]


def unpack_heads_kernel(at_ref, *rest):
    *part_refs, attended_ref, values_ref = rest
    chips, width = len(part_refs), part_refs[0].shape[3]
    for shift, part_ref in enumerate(part_refs):
        chip = lax.rem(at_ref[0] + chips - shift, chips)
        for core in range(2):
            cols = aligned(2 * chip + core, width)
            attended_ref[0, :, cols] = part_ref[core, 0]
            values_ref[0, :, cols] = part_ref[core, 1]


def place_rows(chip_at, core_at, part_refs, held_ref):
    chips, half = len(part_refs) // 2, part_refs[0].shape[0] // 2
    for shift in range(chips):
        chip = lax.rem(chip_at + chips - shift, chips)
        for side, core in ((0, core_at), (1, 1 - core_at)):
            part_ref = part_refs[2 * shift + side]
            for which in range(2):
                rows = aligned(which * 2 * chips + 2 * chip + core, half)
                held_ref[rows, :] = part_ref[which * half : (which + 1) * half, :]


def product_kernel(group, at_ref, *rest):
    rows_refs, rest = rest[:group], rest[group:]
    tokens_ref, own_rows_ref, other_rows_ref, *part_refs, total_ref, held_ref = rest
    place_rows(at_ref[1], at_ref[2], rows_refs, held_ref)
    total_ref[...] = dot(tokens_ref[...], held_ref[...], NT)
    tok = own_rows_ref.shape[0]
    own_rows_ref[...] = held_ref[:, aligned(2 * at_ref[1] + at_ref[2], tok)].T
    other_rows_ref[...] = held_ref[:, aligned(2 * at_ref[1] + 1 - at_ref[2], tok)].T
    count = len(part_refs)
    size = part_refs[0].shape[0]
    for shift, part_ref in enumerate(part_refs):
        owner = lax.rem(at_ref[0] + shift, count)
        part = total_ref[pl.ds(pl.multiple_of(owner * size, size), size), :]
        part_ref[...] = part.astype(part_ref.dtype)


def run_sum_kernel(arrived, at_ref, *rest):
    own_ref, *rest = rest
    total_ref = rest[-1]
    total = own_ref[...]
    for ref in rest[:arrived]:
        total = total + ref[...].astype(f32)
    total_ref[...] = total
    part_refs = rest[arrived:-1]
    size = part_refs[0].shape[0]
    for shift, part_ref in enumerate(part_refs):
        owner = lax.rem(at_ref[0] + shift, len(part_refs))
        part = total_ref[pl.ds(pl.multiple_of(owner * size, size), size), :]
        part_ref[...] = part.astype(part_ref.dtype)


def grad_tokens_kernel(at_ref, rows_ref, other_rows_ref, weight_ref, *rest):
    count = len(rest) // 2
    fetched_refs, out_ref, other_refs = rest[:count], rest[count], rest[count + 1 :]
    for i, ref in enumerate((weight_ref, *fetched_refs)):
        size = ref.shape[0]
        first = pl.multiple_of(at_ref[i], size)
        out_ref[0, :, pl.ds(first, size)] = dot(rows_ref[...], ref[...], NT).astype(bf16)
    for ref, other_ref in zip(fetched_refs, other_refs):
        other_ref[...] = dot(other_rows_ref[...], ref[...], NT).astype(bf16)


def merge_kernel(at_ref, main_ref, *rest):
    *part_refs, out_ref, sems = rest
    run_copies(
        sems,
        [
            (part_ref, out_ref.at[0, :, pl.ds(pl.multiple_of(at_ref[i], size), size)])
            for i, part_ref in enumerate(part_refs)
            for size in part_ref.shape[1:]
        ],
    )


def final_sum_kernel(own_ref, *rest):
    *part_refs, out_ref = rest
    total = own_ref[...]
    for part_ref in part_refs:
        total = total + part_ref[...].astype(f32)
    out_ref[...] = total


VMEM = pl.BlockSpec(memory_space=pltpu.VMEM)
SMEM = pl.BlockSpec(memory_space=pltpu.SMEM)
FAR = pl.BlockSpec(memory_space=pltpu.HBM)
ANYWHERE = pl.BlockSpec(memory_space=pl.ANY)


def call(
    body,
    outs,
    *operands,
    scalars=(),
    after=(),
    after_far=(),
    scratch=(),
    far_in=(),
    far_out=False,
    copies=(),
    alias=False,
):
    at = [jnp.stack([jnp.int32(s) for s in scalars])] if scalars else []
    count = len(at) + len(operands)

    def kernel(*refs):
        ins, rest = refs[:count], refs[count + len(after) + len(after_far) :]
        body(*ins, *rest[: len(outs)], *rest[len(outs) + 1 :])
        rest[len(outs)][...] = jnp.zeros((8, 128), f32)

    *results, token = pl.pallas_call(
        kernel,
        out_shape=[jax.ShapeDtypeStruct(shape, kind) for shape, kind in [*outs, ((8, 128), f32)]],
        in_specs=[SMEM] * len(at)
        + [FAR if i in far_in else VMEM for i in range(len(operands))]
        + [ANYWHERE] * len(after)
        + [FAR] * len(after_far),
        out_specs=[FAR if far_out else VMEM] * len(outs) + [VMEM],
        scratch_shapes=[*scratch] + [pltpu.SemaphoreType.DMA((n,)) for n in copies],
        input_output_aliases={len(at): 0} if alias else {},
        compiler_params=pltpu.CompilerParams(vmem_limit_bytes=VMEM_LIMIT),
        cost_estimate=pl.CostEstimate(flops=0, bytes_accessed=0, transcendentals=0),
    )(*at, *operands, *after, *after_far)
    return results, token


def local(dp_size, ctx_size, tokens, proj_weight, values, grad_out):
    group = min(GROUP, ctx_size, H)
    runs = ctx_size // group
    heads = H // group
    tok, width = tokens.shape[1:]
    length = group * tok
    cols = proj_weight.shape[1]
    share = width // dp_size
    depth = share // ctx_size
    with_state = runs > 1
    groups = [[run * group + i for i in range(group)] for run in range(runs)]
    wide_groups = [
        [dp * ctx_size + i for dp in range(dp_size) for i in members] for members in groups
    ]
    dp_at, ctx_at = lax.axis_index("dp"), lax.axis_index("ctx")
    run_at, member = ctx_at // group, ctx_at % group

    def exchange(x):
        return lax.all_to_all(
            x, "ctx", split_axis=0, concat_axis=0, tiled=True, axis_index_groups=groups
        )

    def to_dp(x, shift):
        return lax.ppermute(x, "dp", [(i, (i + shift) % dp_size) for i in range(dp_size)])

    def to_member(x, shift):
        pairs = [(i, i - i % group + (i + shift) % group) for i in range(ctx_size)]
        return lax.ppermute(x, "ctx", pairs)

    chips = group // 2
    chip_at, core_at = member // 2, member % 2

    def to_chip(x, shift):
        return x if shift == 0 else to_member(x, 2 * shift)

    def to_other_core(x):
        return lax.ppermute(x, "ctx", [(i, i ^ 1) for i in range(ctx_size)])

    def to_run(x, shift, wrap):
        pairs = [
            (i, (i + shift * group) % ctx_size)
            for i in range(ctx_size)
            if wrap or 0 <= i + shift * group < ctx_size
        ]
        return lax.ppermute(x, "ctx", pairs)

    qk_shape = ((group, 2, heads, F, tok), f32)
    state_shape = ((heads, PSI, DH), bf16)
    blocks_shape = ((2, tok, heads * DH), bf16)
    rows_shape = ((length, heads * DH), f32)

    parts, token = call(
        token_parts_kernel,
        [((tok, share), bf16)] * (dp_size - 1),
        tokens,
        scalars=(dp_at,),
        far_in=(0,),
        far_out=True,
        copies=(dp_size - 1,),
    )
    arrived = [to_dp(part, shift) for shift, part in enumerate(parts, 1)]
    parts, token = call(
        pack_heads_kernel,
        [((2, 2, tok, heads * DH), bf16)] * chips,
        values,
        grad_out,
        scalars=(chip_at, core_at),
        after=(token,),
    )
    heads_parts = [to_chip(part, shift) for shift, part in enumerate(parts)]
    (keep, send), _ = call(
        split_cores_kernel,
        [((chips, 2, tok, heads * DH), bf16)] * 2,
        *heads_parts,
        scalars=(chip_at, core_at),
    )
    (vg,), _ = call(
        collect_heads_kernel,
        [((group, 2, tok, heads * DH), bf16)],
        keep,
        to_other_core(send),
        scalars=(chip_at, core_at),
    )
    (projected,), token = call(
        project_kernel,
        [qk_shape],
        tokens,
        proj_weight,
        scalars=(dp_at,),
        after=(token,),
        far_in=(0,),
        copies=(1,),
        scratch=[pltpu.VMEM((tok, share), bf16)],
    )
    part_shape = (tok, dp_size * runs * depth)
    if depth % 128 == 0:
        (keep, send), pack_token = call(
            functools.partial(pack_tokens_kernel, depth),
            [((chips,) + part_shape, bf16)] * 2,
            tokens,
            scalars=(chip_at, core_at),
            after_far=heads_parts[1:2],
        )
    else:
        blocks = tokens[0].reshape(tok, dp_size * runs, chips, 2, depth).transpose(2, 3, 0, 1, 4)
        blocks = blocks.reshape(chips, 2, *part_shape)
        blocks = jnp.stack([blocks[(chip_at + shift) % chips] for shift in range(chips)])
        keep, send = blocks[:, core_at], blocks[:, 1 - core_at]
        pack_token = token
    token_parts, _ = call(
        pair_kernel,
        [((2,) + part_shape, bf16)] * chips,
        keep,
        to_other_core(send),
        scalars=(chip_at, core_at),
    )
    token_parts = [to_chip(part, shift) for shift, part in enumerate(token_parts)]
    parity = ctx_at % 2
    piece = share // 2
    (mine,), mine_token = call(
        weight_piece_kernel,
        [((piece, cols), bf16)],
        proj_weight,
        scalars=(parity,),
        after_far=heads_parts[1:2],
        far_in=(0,),
        far_out=True,
        copies=(1,),
    )
    (projected,), _ = call(
        project_rest_kernel,
        [((dp_size,) + qk_shape[0], f32)],
        projected,
        proj_weight,
        *arrived,
        scalars=(dp_at,),
        after=(token, pack_token, mine_token),
        after_far=heads_parts[1:],
    )
    qk_parts = lax.all_to_all(
        projected.reshape((dp_size * group,) + qk_shape[0][1:]),
        ("dp", "ctx"),
        split_axis=0,
        concat_axis=0,
        tiled=True,
        axis_index_groups=wide_groups,
    ).reshape(projected.shape)

    fetched = [to_dp(mine, shift) for shift in range(1, dp_size)]
    bases = [(dp_at + dp_size - shift) % dp_size * share for shift in range(1, dp_size)]

    (qk, *state), token = call(
        functools.partial(state_kernel, with_state),
        [qk_shape] + [state_shape] * with_state,
        qk_parts,
        vg,
    )
    prefix, suffix = (), ()
    if with_state:
        prefix = [to_run(state[0], shift, False) for shift in range(1, runs)]
    (numerator,), token = call(numerator_kernel, [rows_shape], qk, vg)
    (attended, grad_num, *carried), token = call(
        functools.partial(normalize_kernel, with_state),
        [((length, heads * DH), bf16), rows_shape] + [state_shape] * with_state,
        qk,
        vg,
        numerator,
        *prefix,
        after_far=token_parts[1:],
    )
    if with_state:
        suffix = [to_run(carried[0], -shift, False) for shift in range(1, runs)]
    (grad_qk, grad_v), token = call(
        functools.partial(backward_kernel, with_state),
        [((2, heads, F, length), f32), ((heads, DH, length), f32)],
        qk,
        vg,
        grad_num,
        *prefix,
    )
    (token_cols,), token = call(
        collect_tokens_kernel,
        [(part_shape[1:] + (length,), bf16)],
        *token_parts,
        scalars=(chip_at,),
        after=(token,),
    )
    (rows, keep, send), token = call(
        functools.partial(rows_kernel, with_state),
        [((2 * heads * F, length), bf16)] + [((chips, 2, tok, heads * DH), bf16)] * 2,
        qk,
        vg,
        attended,
        grad_qk,
        grad_v,
        *suffix,
        scalars=(chip_at, core_at),
        after=(token,),
        scratch=[pltpu.VMEM((length, heads * DH), bf16)],
    )
    rows = [to_chip(rows, shift) for shift in range(chips)]
    rows = [side for part in rows for side in (part, to_other_core(part))]
    got = to_other_core(send)
    results, token = call(
        pair_kernel,
        [((2, 2, tok, heads * DH), bf16)] * chips,
        keep,
        got,
        scalars=(chip_at, core_at),
    )
    results = [to_chip(part, shift) for shift, part in enumerate(results)]

    held = pltpu.VMEM((cols, length), bf16)
    (own_rows, other_rows, own, *parts), token = call(
        functools.partial(product_kernel, 2 * chips),
        [((tok, cols), bf16)] * 2
        + [((runs * depth, cols), f32)] + [((runs * depth, cols), bf16)] * (dp_size - 1),
        *rows,
        token_cols,
        scalars=(dp_at, chip_at, core_at),
        after=(token,),
        scratch=[pltpu.VMEM((dp_size * runs * depth, cols), f32), held],
    )
    parts = [to_dp(part, shift) for shift, part in enumerate(parts, 1)]
    (grad_tokens, *others), tokens_token = call(
        grad_tokens_kernel,
        [((1, tok, width), bf16)] + [((tok, piece), bf16)] * (dp_size - 1),
        own_rows,
        other_rows,
        proj_weight,
        *fetched,
        scalars=[dp_at * share] + [base + parity * piece for base in bases],
        after=(token,),
    )
    (grad_proj, *parts), token = call(
        functools.partial(run_sum_kernel, len(parts)),
        [((depth, cols), f32)] + [((depth, cols), bf16)] * (runs - 1),
        own,
        *parts,
        scalars=(run_at,),
        after=(tokens_token,),
        scratch=[pltpu.VMEM((runs * depth, cols), f32)],
    )
    (attended, grad_values), token = call(
        unpack_heads_kernel,
        [((1, tok, H * DH), bf16)] * 2,
        *results,
        scalars=(chip_at,),
        after=(token,),
    )
    (grad_tokens,), tokens_token = call(
        merge_kernel,
        [((1, tok, width), bf16)],
        grad_tokens,
        *[to_other_core(other) for other in others],
        scalars=[base + (1 - parity) * piece for base in bases],
        far_in=(0,),
        far_out=True,
        copies=(dp_size - 1,),
        alias=True,
    )
    (grad_proj,), _ = call(
        final_sum_kernel,
        [((depth, cols), f32)],
        grad_proj,
        *[to_run(part, shift, True) for shift, part in enumerate(parts, 1)],
        after=(token, tokens_token),
    )
    return (attended, grad_tokens, grad_values, grad_proj)


def solution(mesh):
    return jax.shard_map(
        functools.partial(local, mesh.shape["dp"], mesh.shape["ctx"]),
        mesh=mesh,
        in_specs=(P("dp", "ctx", None), P("dp", None), P("dp", "ctx", None), P("dp", "ctx", None)),
        out_specs=(
            P("dp", "ctx", None),
            P("dp", "ctx", None),
            P("dp", "ctx", None),
            P(("dp", "ctx"), None),
        ),
        check_vma=False,
    )
```

```python
import functools

import jax
import jax.numpy as jnp
from jax import lax
from jax.experimental import pallas as pl
from jax.experimental.pallas import tpu as pltpu
from jax.sharding import PartitionSpec as P

H = 16
F = 16
DH = 128
EPSILON = 1e-05
GROUP = 8
TILE = 256
VMEM_LIMIT = 16 * 1024 * 1024
PSI = 9 * F + 2 * F
PSI_SCALE = (0.5,) + (1.0,) * 7 + (0.5,)

f32 = jnp.float32
bf16 = jnp.bfloat16

NN = (((1,), (0,)), ((), ()))
NT = (((1,), (1,)), ((), ()))


def dot(a, b, dims=NN):
    return lax.dot_general(a, b, dims, preferred_element_type=f32)


def split(x):
    high = x.astype(bf16)
    return high, (x - high.astype(f32)).astype(bf16)


def dot3(a, b, dims=NN):
    a_high, a_low = split(a)
    b_high, b_low = split(b)
    return dot(a_high, b_high, dims) + (dot(a_high, b_low, dims) + dot(a_low, b_high, dims))


def turned(x, r):
    return x if r == 0 else jnp.concatenate([x[r:], x[:r]], axis=0)


def psi(x, weights):
    parts = []
    for r in range(9):
        part = x * turned(x, r)
        parts.append(part * PSI_SCALE[r] if weights and PSI_SCALE[r] != 1.0 else part)
    row = lax.broadcasted_iota(jnp.int32, x.shape, 0)
    return jnp.concatenate(parts + [x, jnp.where(row == 0, 1.0, 0.0)], axis=0)


def pull_psi(x, upstream, weights):
    total = upstream[9 * F : 10 * F]
    for r in range(9):
        part = upstream[r * F : (r + 1) * F]
        if weights and PSI_SCALE[r] != 1.0:
            part = part * PSI_SCALE[r]
        total = total + part * turned(x, r) + turned(part * x, (F - r) % F)
    return total


def feature_major(qk_ref, which, head):
    return jnp.concatenate([qk_ref[src, which, head] for src in range(qk_ref.shape[0])], axis=1)


def rows_of(ref, which, head, start, stop):
    tok = ref.shape[2]
    return jnp.concatenate(
        [
            ref[src, which, :, head * DH : (head + 1) * DH]
            for src in range(start // tok, stop // tok)
        ],
        axis=0,
    )


def score_sides(q, k):
    q_high, q_low = split(q)
    k_high, k_low = split(k)
    left = jnp.concatenate([q_high, q_high, q_low, q_low], axis=0)
    right = jnp.concatenate([k_high, k_low, k_high, k_low], axis=0)
    return left.T, right


def causal_mask(tile, width):
    row = lax.broadcasted_iota(jnp.int32, (tile, width), 0) + (width - tile)
    return row >= lax.broadcasted_iota(jnp.int32, (tile, width), 1)


def run_copies(sems, pairs):
    copies = [
        pltpu.make_async_copy(source, target, sems.at[i])
        for i, (source, target) in enumerate(pairs)
    ]
    for copy in copies:
        copy.start()
    for copy in copies:
        copy.wait()


def aligned(at, size):
    return pl.ds(pl.multiple_of(at * size, size), size)


def token_parts_kernel(at_ref, tokens_ref, *rest):
    *out_refs, sems = rest
    count, share = len(out_refs) + 1, out_refs[0].shape[1]
    run_copies(
        sems,
        [
            (tokens_ref.at[0, :, aligned(lax.rem(at_ref[0] + shift, count), share)], out_ref)
            for shift, out_ref in enumerate(out_refs, 1)
        ],
    )


def pack_heads_kernel(at_ref, values_ref, grad_ref, *out_refs):
    chips, width = len(out_refs), out_refs[0].shape[3]
    for shift, out_ref in enumerate(out_refs):
        chip = lax.rem(at_ref[0] + shift, chips)
        for core in range(2):
            cols = aligned(2 * chip + core, width)
            out_ref[core, 0] = values_ref[0, :, cols]
            out_ref[core, 1] = grad_ref[0, :, cols]


def split_cores_kernel(at_ref, *rest):
    *part_refs, keep_ref, send_ref = rest
    for shift, part_ref in enumerate(part_refs):
        keep_ref[shift] = part_ref[at_ref[1]]
        send_ref[shift] = part_ref[1 - at_ref[1]]


def collect_heads_kernel(at_ref, keep_ref, got_ref, out_ref):
    chips = keep_ref.shape[0]
    for shift in range(chips):
        chip = lax.rem(at_ref[0] + chips - shift, chips)
        out_ref[2 * chip + at_ref[1]] = keep_ref[shift]
        out_ref[2 * chip + 1 - at_ref[1]] = got_ref[shift]


def pack_tokens_kernel(depth, at_ref, tokens_ref, keep_ref, send_ref):
    chips, _, rows = keep_ref.shape
    for shift in range(chips):
        chip = lax.rem(at_ref[0] + shift, chips)
        for core, out_ref in ((at_ref[1], keep_ref), (1 - at_ref[1], send_ref)):
            for part in range(rows // depth):
                cols = aligned(2 * (part * chips + chip) + core, depth)
                out_ref[shift, :, part * depth : (part + 1) * depth] = tokens_ref[0, :, cols]


def collect_tokens_kernel(at_ref, *rest):
    *part_refs, out_ref = rest
    chips, tok = len(part_refs), part_refs[0].shape[1]
    for shift, part_ref in enumerate(part_refs):
        chip = lax.rem(at_ref[0] + chips - shift, chips)
        for core in range(2):
            out_ref[:, aligned(2 * chip + core, tok)] = part_ref[core].T


def write_blocks(projected, out_ref):
    group, _, heads, feat, _ = out_ref.shape
    for member in range(group):
        for which in range(2):
            for head in range(heads):
                first = ((which * group + member) * heads + head) * feat
                out_ref[member, which, head] = projected[first : first + feat]


def project_kernel(at_ref, tokens_ref, weight_ref, out_ref, part_ref, sem):
    share = part_ref.shape[1]
    run_copies(sem, [(tokens_ref.at[0, :, aligned(at_ref[0], share)], part_ref)])
    write_blocks(dot(part_ref[...], weight_ref[...]).T, out_ref)


def project_rest_kernel(at_ref, own_ref, weight_ref, *rest):
    *part_refs, out_ref = rest
    count = len(part_refs) + 1
    at = at_ref[0]
    out_ref[at] = own_ref[...]
    for shift, part_ref in enumerate(part_refs, 1):
        owner = lax.rem(at + count - shift, count)
        write_blocks(dot(part_ref[...], weight_ref[...]).T, out_ref.at[owner])


def weight_piece_kernel(at_ref, weight_ref, out_ref, sems):
    run_copies(sems, [(weight_ref.at[aligned(at_ref[0], out_ref.shape[0])], out_ref)])


def state_sum(refs, head):
    total = refs[0][head].astype(f32)
    for ref in refs[1:]:
        total = total + ref[head].astype(f32)
    return total


def state_kernel(with_state, parts_ref, vg_ref, qk_ref, *state_refs):
    count, blocks, _, heads, _, tok = parts_ref.shape
    for head in range(heads):
        for which in range(2):
            for src in range(blocks):
                total = parts_ref[0, src, which, head]
                for part in range(1, count):
                    total = total + parts_ref[part, src, which, head]
                qk_ref[src, which, head] = total
        if with_state:
            high, low = split(psi(feature_major(qk_ref, 1, head), False))
            v = rows_of(vg_ref, 0, head, 0, blocks * tok)
            state_refs[0][head] = (dot(high, v) + dot(low, v)).astype(bf16)


def numerator_kernel(qk_ref, vg_ref, num_ref):
    heads = qk_ref.shape[2]
    length = qk_ref.shape[0] * qk_ref.shape[4]
    tile = min(TILE, length)
    for head in range(heads):
        q = feature_major(qk_ref, 0, head) * 0.25
        k = feature_major(qk_ref, 1, head)
        left, right = score_sides(q, k)
        for at in range(0, length, tile):
            width = at + tile
            scores = dot(left[at:width], right[:, :width])
            kernel = jnp.where(
                causal_mask(tile, width), 1.0 + scores * (1.0 + 0.5 * scores), 0.0
            )
            high, low = split(kernel)
            v = rows_of(vg_ref, 0, head, 0, width)
            num_ref[at:width, head * DH : (head + 1) * DH] = dot(high, v) + dot(low, v)


def normalize_kernel(with_state, qk_ref, vg_ref, num_ref, *rest):
    if with_state:
        *prefix_refs, attended_ref, grad_ref, carried_ref = rest
    else:
        attended_ref, grad_ref = rest
    heads = qk_ref.shape[2]
    blocks, tok = qk_ref.shape[0], qk_ref.shape[4]
    length = blocks * tok
    for head in range(heads):
        cols = slice(head * DH, (head + 1) * DH)
        numerator = num_ref[:, cols]
        if with_state:
            feat = psi(feature_major(qk_ref, 0, head) * 0.25, True)
            numerator = numerator + dot3(feat.T, state_sum(prefix_refs, head))
        inv_rms = lax.rsqrt(jnp.mean(numerator * numerator, axis=-1, keepdims=True) + EPSILON)
        normed = numerator * inv_rms
        upstream = rows_of(vg_ref, 1, head, 0, length).astype(f32)
        grad = inv_rms * (
            upstream - normed * jnp.mean(normed * upstream, axis=-1, keepdims=True)
        )
        attended_ref[:, cols] = normed.astype(bf16)
        grad_ref[:, cols] = grad
        if with_state:
            carried_ref[head] = dot3(feat, grad).astype(bf16)


def backward_kernel(with_state, qk_ref, vg_ref, grad_ref, *rest):
    *prefix_refs, grad_qk_ref, grad_v_ref = rest
    length = qk_ref.shape[0] * qk_ref.shape[4]
    tile = min(TILE, length)
    for head in range(grad_v_ref.shape[0]):
        cols = slice(head * DH, (head + 1) * DH)
        q = feature_major(qk_ref, 0, head) * 0.25
        k = feature_major(qk_ref, 1, head)
        left, right = score_sides(q, k)
        q_both = jnp.concatenate(split(q), axis=0)
        k_both = jnp.concatenate(split(k), axis=0)
        grad = grad_ref[:, cols]
        grad_t = grad.T
        if with_state:
            grad_q = pull_psi(q, dot3(state_sum(prefix_refs, head), grad_t), True)
        for at in reversed(range(0, length, tile)):
            width = at + tile
            scores = dot(left[at:width], right[:, :width])
            causal = causal_mask(tile, width)
            v = rows_of(vg_ref, 0, head, 0, width)
            high, low = split(grad[at:width])
            mixing = dot(
                jnp.concatenate([high, low], axis=1), jnp.concatenate([v, v], axis=1), NT
            )
            more = 1.0 + scores
            slopes = split(jnp.where(causal, mixing * more, 0.0))
            kernels = split(jnp.where(causal, more + 0.5 * scores * scores, 0.0))
            both = dot(k_both[:, :width], slopes[0], NT)
            piece = both[:F] + (both[F:] + dot(k_both[:F, :width], slopes[1], NT))
            if with_state:
                piece = piece + grad_q[:, at:width]
            grad_qk_ref[0, head, :, at:width] = piece * 0.25
            both = dot(q_both[:, at:width], slopes[0])
            piece_k = both[:F] + (both[F:] + dot(q_both[:F, at:width], slopes[1]))
            high, low = split(grad_t[:, at:width])
            both = dot(jnp.concatenate([high, low], axis=0), kernels[0])
            piece_v = both[:DH] + (both[DH:] + dot(high, kernels[1]))
            if width == length:
                grad_qk_ref[1, head] = piece_k
                grad_v_ref[head] = piece_v
            else:
                grad_qk_ref[1, head, :, :width] += piece_k
                grad_v_ref[head, :, :width] += piece_v


def rows_kernel(with_state, at_ref, qk_ref, vg_ref, attended_ref, grad_qk_ref, grad_v_ref, *rest):
    *suffix_refs, rows_ref, keep_ref, send_ref, held_ref = rest
    heads, tok = qk_ref.shape[2], qk_ref.shape[4]
    length = qk_ref.shape[0] * tok
    for head in range(heads):
        grad_k, grad_v = grad_qk_ref[1, head], grad_v_ref[head]
        if with_state:
            k = feature_major(qk_ref, 1, head)
            v = rows_of(vg_ref, 0, head, 0, length)
            suffix = state_sum(suffix_refs, head)
            high, low = split(suffix)
            grad_k = grad_k + pull_psi(k, dot(high, v, NT) + dot(low, v, NT), False)
            grad_v = grad_v + dot3(suffix.T, psi(k, False))
        rows_ref[head * F : (head + 1) * F] = grad_qk_ref[0, head].astype(bf16)
        rows_ref[(heads + head) * F : (heads + head + 1) * F] = grad_k.astype(bf16)
        held_ref[:, head * DH : (head + 1) * DH] = grad_v.T.astype(bf16)
    chips = keep_ref.shape[0]
    for shift in range(chips):
        chip = lax.rem(at_ref[0] + shift, chips)
        for core, out_ref in ((at_ref[1], keep_ref), (1 - at_ref[1], send_ref)):
            block = aligned(2 * chip + core, tok)
            out_ref[shift, 0] = attended_ref[block, :]
            out_ref[shift, 1] = held_ref[block, :]


def pair_kernel(at_ref, keep_ref, got_ref, *out_refs):
    for shift, out_ref in enumerate(out_refs):
        out_ref[at_ref[1]] = keep_ref[shift]
        out_ref[1 - at_ref[1]] = got_ref[shift]


def unpack_heads_kernel(at_ref, *rest):
    *part_refs, attended_ref, values_ref = rest
    chips, width = len(part_refs), part_refs[0].shape[3]
    for shift, part_ref in enumerate(part_refs):
        chip = lax.rem(at_ref[0] + chips - shift, chips)
        for core in range(2):
            cols = aligned(2 * chip + core, width)
            attended_ref[0, :, cols] = part_ref[core, 0]
            values_ref[0, :, cols] = part_ref[core, 1]


def place_rows(chip_at, core_at, part_refs, held_ref):
    chips, half = len(part_refs) // 2, part_refs[0].shape[0] // 2
    for shift in range(chips):
        chip = lax.rem(chip_at + chips - shift, chips)
        for side, core in ((0, core_at), (1, 1 - core_at)):
            part_ref = part_refs[2 * shift + side]
            for which in range(2):
                rows = aligned(which * 2 * chips + 2 * chip + core, half)
                held_ref[rows, :] = part_ref[which * half : (which + 1) * half, :]


def product_kernel(group, dp_size, at_ref, *rest):
    rows_refs, rest = rest[:group], rest[group:]
    tokens_ref, own_rows_ref, other_rows_ref, *part_refs, total_ref, held_ref = rest
    place_rows(at_ref[1], at_ref[2], rows_refs, held_ref)
    total_ref[...] = dot(tokens_ref[...], held_ref[...], NT)
    tok = own_rows_ref.shape[0]
    own_rows_ref[...] = held_ref[:, aligned(2 * at_ref[1] + at_ref[2], tok)].T
    other_rows_ref[...] = held_ref[:, aligned(2 * at_ref[1] + 1 - at_ref[2], tok)].T
    size = part_refs[0].shape[0]
    runs = total_ref.shape[0] // size // dp_size
    for i, part_ref in enumerate(part_refs):
        dp = lax.rem(at_ref[0] + i // runs, dp_size)
        run = lax.rem(at_ref[3] + i % runs, runs)
        part_ref[...] = total_ref[aligned(dp * runs + run, size), :].astype(part_ref.dtype)


def grad_tokens_kernel(at_ref, rows_ref, other_rows_ref, weight_ref, *rest):
    count = len(rest) // 2
    fetched_refs, out_ref, other_refs = rest[:count], rest[count], rest[count + 1 :]
    for i, ref in enumerate((weight_ref, *fetched_refs)):
        size = ref.shape[0]
        first = pl.multiple_of(at_ref[i], size)
        out_ref[0, :, pl.ds(first, size)] = dot(rows_ref[...], ref[...], NT).astype(bf16)
    for ref, other_ref in zip(fetched_refs, other_refs):
        other_ref[...] = dot(other_rows_ref[...], ref[...], NT).astype(bf16)


def merge_kernel(at_ref, main_ref, *rest):
    *part_refs, out_ref, sems = rest
    run_copies(
        sems,
        [
            (part_ref, out_ref.at[0, :, pl.ds(pl.multiple_of(at_ref[i], size), size)])
            for i, part_ref in enumerate(part_refs)
            for size in part_ref.shape[1:]
        ],
    )


def final_sum_kernel(own_ref, *rest):
    *part_refs, out_ref = rest
    total = own_ref[...]
    for part_ref in part_refs:
        total = total + part_ref[...].astype(f32)
    out_ref[...] = total


VMEM = pl.BlockSpec(memory_space=pltpu.VMEM)
SMEM = pl.BlockSpec(memory_space=pltpu.SMEM)
FAR = pl.BlockSpec(memory_space=pltpu.HBM)
ANYWHERE = pl.BlockSpec(memory_space=pl.ANY)


def call(
    body,
    outs,
    *operands,
    scalars=(),
    after=(),
    after_far=(),
    scratch=(),
    far_in=(),
    far_out=False,
    copies=(),
    alias=False,
):
    at = [jnp.stack([jnp.int32(s) for s in scalars])] if scalars else []
    count = len(at) + len(operands)

    def kernel(*refs):
        ins, rest = refs[:count], refs[count + len(after) + len(after_far) :]
        body(*ins, *rest[: len(outs)], *rest[len(outs) + 1 :])
        rest[len(outs)][...] = jnp.zeros((8, 128), f32)

    *results, token = pl.pallas_call(
        kernel,
        out_shape=[jax.ShapeDtypeStruct(shape, kind) for shape, kind in [*outs, ((8, 128), f32)]],
        in_specs=[SMEM] * len(at)
        + [FAR if i in far_in else VMEM for i in range(len(operands))]
        + [ANYWHERE] * len(after)
        + [FAR] * len(after_far),
        out_specs=[FAR if far_out else VMEM] * len(outs) + [VMEM],
        scratch_shapes=[*scratch] + [pltpu.SemaphoreType.DMA((n,)) for n in copies],
        input_output_aliases={len(at): 0} if alias else {},
        compiler_params=pltpu.CompilerParams(vmem_limit_bytes=VMEM_LIMIT),
        cost_estimate=pl.CostEstimate(flops=0, bytes_accessed=0, transcendentals=0),
    )(*at, *operands, *after, *after_far)
    return results, token


def local(dp_size, ctx_size, tokens, proj_weight, values, grad_out):
    group = min(GROUP, ctx_size, H)
    runs = ctx_size // group
    heads = H // group
    tok, width = tokens.shape[1:]
    length = group * tok
    cols = proj_weight.shape[1]
    share = width // dp_size
    depth = share // ctx_size
    with_state = runs > 1
    groups = [[run * group + i for i in range(group)] for run in range(runs)]
    wide_groups = [
        [dp * ctx_size + i for dp in range(dp_size) for i in members] for members in groups
    ]
    dp_at, ctx_at = lax.axis_index("dp"), lax.axis_index("ctx")
    run_at, member = ctx_at // group, ctx_at % group

    def exchange(x):
        return lax.all_to_all(
            x, "ctx", split_axis=0, concat_axis=0, tiled=True, axis_index_groups=groups
        )

    def to_dp(x, shift):
        return lax.ppermute(x, "dp", [(i, (i + shift) % dp_size) for i in range(dp_size)])

    def to_member(x, shift):
        pairs = [(i, i - i % group + (i + shift) % group) for i in range(ctx_size)]
        return lax.ppermute(x, "ctx", pairs)

    chips = group // 2
    chip_at, core_at = member // 2, member % 2

    def to_chip(x, shift):
        return x if shift == 0 else to_member(x, 2 * shift)

    def to_other_core(x):
        return lax.ppermute(x, "ctx", [(i, i ^ 1) for i in range(ctx_size)])

    def to_run(x, shift):
        pairs = [
            (i, i + shift * group)
            for i in range(ctx_size)
            if 0 <= i + shift * group < ctx_size
        ]
        return lax.ppermute(x, "ctx", pairs)

    def to_share(x, dp_shift, run_shift):
        pairs = [
            (
                dp * ctx_size + i,
                (dp + dp_shift) % dp_size * ctx_size + (i + run_shift * group) % ctx_size,
            )
            for dp in range(dp_size)
            for i in range(ctx_size)
        ]
        return lax.ppermute(x, ("dp", "ctx"), pairs)

    qk_shape = ((group, 2, heads, F, tok), f32)
    state_shape = ((heads, PSI, DH), bf16)
    blocks_shape = ((2, tok, heads * DH), bf16)
    rows_shape = ((length, heads * DH), f32)

    parts, token = call(
        token_parts_kernel,
        [((tok, share), bf16)] * (dp_size - 1),
        tokens,
        scalars=(dp_at,),
        far_in=(0,),
        far_out=True,
        copies=(dp_size - 1,),
    )
    arrived = [to_dp(part, shift) for shift, part in enumerate(parts, 1)]
    parts, token = call(
        pack_heads_kernel,
        [((2, 2, tok, heads * DH), bf16)] * chips,
        values,
        grad_out,
        scalars=(chip_at, core_at),
        after=(token,),
    )
    heads_parts = [to_chip(part, shift) for shift, part in enumerate(parts)]
    (keep, send), _ = call(
        split_cores_kernel,
        [((chips, 2, tok, heads * DH), bf16)] * 2,
        *heads_parts,
        scalars=(chip_at, core_at),
    )
    (vg,), _ = call(
        collect_heads_kernel,
        [((group, 2, tok, heads * DH), bf16)],
        keep,
        to_other_core(send),
        scalars=(chip_at, core_at),
    )
    (projected,), token = call(
        project_kernel,
        [qk_shape],
        tokens,
        proj_weight,
        scalars=(dp_at,),
        after=(token,),
        far_in=(0,),
        copies=(1,),
        scratch=[pltpu.VMEM((tok, share), bf16)],
    )
    part_shape = (tok, dp_size * runs * depth)
    if depth % 128 == 0:
        (keep, send), pack_token = call(
            functools.partial(pack_tokens_kernel, depth),
            [((chips,) + part_shape, bf16)] * 2,
            tokens,
            scalars=(chip_at, core_at),
            after_far=heads_parts[1:2],
        )
    else:
        blocks = tokens[0].reshape(tok, dp_size * runs, chips, 2, depth).transpose(2, 3, 0, 1, 4)
        blocks = blocks.reshape(chips, 2, *part_shape)
        blocks = jnp.stack([blocks[(chip_at + shift) % chips] for shift in range(chips)])
        keep, send = blocks[:, core_at], blocks[:, 1 - core_at]
        pack_token = token
    token_parts, _ = call(
        pair_kernel,
        [((2,) + part_shape, bf16)] * chips,
        keep,
        to_other_core(send),
        scalars=(chip_at, core_at),
    )
    token_parts = [to_chip(part, shift) for shift, part in enumerate(token_parts)]
    parity = ctx_at % 2
    piece = share // 2
    (mine,), mine_token = call(
        weight_piece_kernel,
        [((piece, cols), bf16)],
        proj_weight,
        scalars=(parity,),
        after_far=heads_parts[1:2],
        far_in=(0,),
        far_out=True,
        copies=(1,),
    )
    (projected,), _ = call(
        project_rest_kernel,
        [((dp_size,) + qk_shape[0], f32)],
        projected,
        proj_weight,
        *arrived,
        scalars=(dp_at,),
        after=(token, pack_token, mine_token),
        after_far=heads_parts[1:],
    )
    qk_parts = lax.all_to_all(
        projected.reshape((dp_size * group,) + qk_shape[0][1:]),
        ("dp", "ctx"),
        split_axis=0,
        concat_axis=0,
        tiled=True,
        axis_index_groups=wide_groups,
    ).reshape(projected.shape)

    fetched = [to_dp(mine, shift) for shift in range(1, dp_size)]
    bases = [(dp_at + dp_size - shift) % dp_size * share for shift in range(1, dp_size)]

    (qk, *state), token = call(
        functools.partial(state_kernel, with_state),
        [qk_shape] + [state_shape] * with_state,
        qk_parts,
        vg,
    )
    prefix, suffix = (), ()
    if with_state:
        prefix = [to_run(state[0], shift) for shift in range(1, runs)]
    (numerator,), token = call(numerator_kernel, [rows_shape], qk, vg)
    (attended, grad_num, *carried), token = call(
        functools.partial(normalize_kernel, with_state),
        [((length, heads * DH), bf16), rows_shape] + [state_shape] * with_state,
        qk,
        vg,
        numerator,
        *prefix,
        after_far=token_parts[1:],
    )
    if with_state:
        suffix = [to_run(carried[0], -shift) for shift in range(1, runs)]
    (grad_qk, grad_v), token = call(
        functools.partial(backward_kernel, with_state),
        [((2, heads, F, length), f32), ((heads, DH, length), f32)],
        qk,
        vg,
        grad_num,
        *prefix,
    )
    (token_cols,), token = call(
        collect_tokens_kernel,
        [(part_shape[1:] + (length,), bf16)],
        *token_parts,
        scalars=(chip_at,),
        after=(token,),
    )
    (rows, keep, send), token = call(
        functools.partial(rows_kernel, with_state),
        [((2 * heads * F, length), bf16)] + [((chips, 2, tok, heads * DH), bf16)] * 2,
        qk,
        vg,
        attended,
        grad_qk,
        grad_v,
        *suffix,
        scalars=(chip_at, core_at),
        after=(token,),
        scratch=[pltpu.VMEM((length, heads * DH), bf16)],
    )
    rows = [to_chip(rows, shift) for shift in range(chips)]
    rows = [side for part in rows for side in (part, to_other_core(part))]
    got = to_other_core(send)
    results, token = call(
        pair_kernel,
        [((2, 2, tok, heads * DH), bf16)] * chips,
        keep,
        got,
        scalars=(chip_at, core_at),
    )
    results = [to_chip(part, shift) for shift, part in enumerate(results)]

    held = pltpu.VMEM((cols, length), bf16)
    shares = dp_size * runs
    (own_rows, other_rows, own, *parts), token = call(
        functools.partial(product_kernel, 2 * chips, dp_size),
        [((tok, cols), bf16)] * 2 + [((depth, cols), f32)] + [((depth, cols), bf16)] * (shares - 1),
        *rows,
        token_cols,
        scalars=(dp_at, chip_at, core_at, run_at),
        after=(token,),
        scratch=[pltpu.VMEM((shares * depth, cols), f32), held],
    )
    parts = [to_share(part, shift // runs, shift % runs) for shift, part in enumerate(parts, 1)]
    (grad_tokens, *others), tokens_token = call(
        grad_tokens_kernel,
        [((1, tok, width), bf16)] + [((tok, piece), bf16)] * (dp_size - 1),
        own_rows,
        other_rows,
        proj_weight,
        *fetched,
        scalars=[dp_at * share] + [base + parity * piece for base in bases],
        after=(token,),
    )
    (attended, grad_values), token = call(
        unpack_heads_kernel,
        [((1, tok, H * DH), bf16)] * 2,
        *results,
        scalars=(chip_at,),
        after=(token,),
    )
    (grad_tokens,), tokens_token = call(
        merge_kernel,
        [((1, tok, width), bf16)],
        grad_tokens,
        *[to_other_core(other) for other in others],
        scalars=[base + (1 - parity) * piece for base in bases],
        far_in=(0,),
        far_out=True,
        copies=(dp_size - 1,),
        alias=True,
    )
    (grad_proj,), _ = call(
        final_sum_kernel, [((depth, cols), f32)], own, *parts, after=(token, tokens_token)
    )
    return (attended, grad_tokens, grad_values, grad_proj)


def solution(mesh):
    return jax.shard_map(
        functools.partial(local, mesh.shape["dp"], mesh.shape["ctx"]),
        mesh=mesh,
        in_specs=(P("dp", "ctx", None), P("dp", None), P("dp", "ctx", None), P("dp", "ctx", None)),
        out_specs=(
            P("dp", "ctx", None),
            P("dp", "ctx", None),
            P("dp", "ctx", None),
            P(("dp", "ctx"), None),
        ),
        check_vma=False,
    )
```

```python
import functools

import jax
import jax.numpy as jnp
from jax import lax
from jax.experimental import pallas as pl
from jax.experimental.pallas import tpu as pltpu
from jax.sharding import PartitionSpec as P

H = 16
F = 16
DH = 128
EPSILON = 1e-05
GROUP = 8
TILE = 256
VMEM_LIMIT = 16 * 1024 * 1024
PSI = 9 * F + 2 * F
PSI_SCALE = (0.5,) + (1.0,) * 7 + (0.5,)

f32 = jnp.float32
bf16 = jnp.bfloat16

NN = (((1,), (0,)), ((), ()))
NT = (((1,), (1,)), ((), ()))


def dot(a, b, dims=NN):
    return lax.dot_general(a, b, dims, preferred_element_type=f32)


def split(x):
    high = x.astype(bf16)
    return high, (x - high.astype(f32)).astype(bf16)


def dot3(a, b, dims=NN):
    a_high, a_low = split(a)
    b_high, b_low = split(b)
    return dot(a_high, b_high, dims) + (dot(a_high, b_low, dims) + dot(a_low, b_high, dims))


def turned(x, r):
    return x if r == 0 else jnp.concatenate([x[r:], x[:r]], axis=0)


def psi(x, weights):
    parts = []
    for r in range(9):
        part = x * turned(x, r)
        parts.append(part * PSI_SCALE[r] if weights and PSI_SCALE[r] != 1.0 else part)
    row = lax.broadcasted_iota(jnp.int32, x.shape, 0)
    return jnp.concatenate(parts + [x, jnp.where(row == 0, 1.0, 0.0)], axis=0)


def pull_psi(x, upstream, weights):
    total = upstream[9 * F : 10 * F]
    for r in range(9):
        part = upstream[r * F : (r + 1) * F]
        if weights and PSI_SCALE[r] != 1.0:
            part = part * PSI_SCALE[r]
        total = total + part * turned(x, r) + turned(part * x, (F - r) % F)
    return total


def feature_major(qk_ref, which, head):
    return jnp.concatenate([qk_ref[src, which, head] for src in range(qk_ref.shape[0])], axis=1)


def rows_of(ref, which, head, start, stop):
    tok = ref.shape[2]
    return jnp.concatenate(
        [
            ref[src, which, :, head * DH : (head + 1) * DH]
            for src in range(start // tok, stop // tok)
        ],
        axis=0,
    )


def score_sides(q, k):
    q_high, q_low = split(q)
    k_high, k_low = split(k)
    left = jnp.concatenate([q_high, q_high, q_low, q_low], axis=0)
    right = jnp.concatenate([k_high, k_low, k_high, k_low], axis=0)
    return left.T, right


def causal_mask(tile, width):
    row = lax.broadcasted_iota(jnp.int32, (tile, width), 0) + (width - tile)
    return row >= lax.broadcasted_iota(jnp.int32, (tile, width), 1)


def run_copies(sems, pairs):
    copies = [
        pltpu.make_async_copy(source, target, sems.at[i])
        for i, (source, target) in enumerate(pairs)
    ]
    for copy in copies:
        copy.start()
    for copy in copies:
        copy.wait()


def aligned(at, size):
    return pl.ds(pl.multiple_of(at * size, size), size)


def token_parts_kernel(at_ref, tokens_ref, *rest):
    *out_refs, sems = rest
    count, share = len(out_refs) + 1, out_refs[0].shape[1]
    run_copies(
        sems,
        [
            (tokens_ref.at[0, :, aligned(lax.rem(at_ref[0] + shift, count), share)], out_ref)
            for shift, out_ref in enumerate(out_refs, 1)
        ],
    )


def pack_heads_kernel(at_ref, values_ref, grad_ref, *out_refs):
    chips, width = len(out_refs), out_refs[0].shape[3]
    for shift, out_ref in enumerate(out_refs):
        chip = lax.rem(at_ref[0] + shift, chips)
        for core in range(2):
            cols = aligned(2 * chip + core, width)
            out_ref[core, 0] = values_ref[0, :, cols]
            out_ref[core, 1] = grad_ref[0, :, cols]


def split_cores_kernel(at_ref, *rest):
    *part_refs, keep_ref, send_ref = rest
    for shift, part_ref in enumerate(part_refs):
        keep_ref[shift] = part_ref[at_ref[1]]
        send_ref[shift] = part_ref[1 - at_ref[1]]


def collect_heads_kernel(at_ref, keep_ref, got_ref, out_ref):
    chips = keep_ref.shape[0]
    for shift in range(chips):
        chip = lax.rem(at_ref[0] + chips - shift, chips)
        out_ref[2 * chip + at_ref[1]] = keep_ref[shift]
        out_ref[2 * chip + 1 - at_ref[1]] = got_ref[shift]


def pack_tokens_kernel(depth, at_ref, tokens_ref, keep_ref, send_ref):
    chips, _, rows = keep_ref.shape
    for shift in range(chips):
        chip = lax.rem(at_ref[0] + shift, chips)
        for core, out_ref in ((at_ref[1], keep_ref), (1 - at_ref[1], send_ref)):
            for part in range(rows // depth):
                cols = aligned(2 * (part * chips + chip) + core, depth)
                out_ref[shift, :, part * depth : (part + 1) * depth] = tokens_ref[0, :, cols]


def collect_tokens_kernel(at_ref, *rest):
    *part_refs, out_ref = rest
    chips, tok = len(part_refs), part_refs[0].shape[1]
    for shift, part_ref in enumerate(part_refs):
        chip = lax.rem(at_ref[0] + chips - shift, chips)
        for core in range(2):
            out_ref[:, aligned(2 * chip + core, tok)] = part_ref[core].T


def write_blocks(projected, out_ref):
    group, _, heads, feat, _ = out_ref.shape
    for member in range(group):
        for which in range(2):
            for head in range(heads):
                first = ((which * group + member) * heads + head) * feat
                out_ref[member, which, head] = projected[first : first + feat]


def project_kernel(at_ref, tokens_ref, weight_ref, out_ref, part_ref, sem):
    share = part_ref.shape[1]
    run_copies(sem, [(tokens_ref.at[0, :, aligned(at_ref[0], share)], part_ref)])
    write_blocks(dot(part_ref[...], weight_ref[...]).T, out_ref)


def project_rest_kernel(at_ref, own_ref, weight_ref, *rest):
    *part_refs, out_ref = rest
    count = len(part_refs) + 1
    at = at_ref[0]
    out_ref[at] = own_ref[...]
    for shift, part_ref in enumerate(part_refs, 1):
        owner = lax.rem(at + count - shift, count)
        write_blocks(dot(part_ref[...], weight_ref[...]).T, out_ref.at[owner])


def weight_piece_kernel(at_ref, weight_ref, out_ref, sems):
    run_copies(sems, [(weight_ref.at[aligned(at_ref[0], out_ref.shape[0])], out_ref)])


def state_sum(refs, head):
    total = refs[0][head].astype(f32)
    for ref in refs[1:]:
        total = total + ref[head].astype(f32)
    return total


def state_kernel(with_state, parts_ref, vg_ref, qk_ref, *state_refs):
    count, blocks, _, heads, _, tok = parts_ref.shape
    for head in range(heads):
        for which in range(2):
            for src in range(blocks):
                total = parts_ref[0, src, which, head]
                for part in range(1, count):
                    total = total + parts_ref[part, src, which, head]
                qk_ref[src, which, head] = total
        if with_state:
            high, low = split(psi(feature_major(qk_ref, 1, head), False))
            v = rows_of(vg_ref, 0, head, 0, blocks * tok)
            state_refs[0][head] = (dot(high, v) + dot(low, v)).astype(bf16)


def numerator_kernel(qk_ref, vg_ref, num_ref):
    heads = qk_ref.shape[2]
    length = qk_ref.shape[0] * qk_ref.shape[4]
    tile = min(TILE, length)
    for head in range(heads):
        q = feature_major(qk_ref, 0, head) * 0.25
        k = feature_major(qk_ref, 1, head)
        left, right = score_sides(q, k)
        for at in range(0, length, tile):
            width = at + tile
            scores = dot(left[at:width], right[:, :width])
            kernel = jnp.where(
                causal_mask(tile, width), 1.0 + scores * (1.0 + 0.5 * scores), 0.0
            )
            high, low = split(kernel)
            v = rows_of(vg_ref, 0, head, 0, width)
            num_ref[at:width, head * DH : (head + 1) * DH] = dot(high, v) + dot(low, v)


def normalize_kernel(with_state, qk_ref, vg_ref, num_ref, *rest):
    if with_state:
        *prefix_refs, attended_ref, grad_ref, carried_ref = rest
    else:
        attended_ref, grad_ref = rest
    heads = qk_ref.shape[2]
    blocks, tok = qk_ref.shape[0], qk_ref.shape[4]
    length = blocks * tok
    for head in range(heads):
        cols = slice(head * DH, (head + 1) * DH)
        numerator = num_ref[:, cols]
        if with_state:
            feat = psi(feature_major(qk_ref, 0, head) * 0.25, True)
            numerator = numerator + dot3(feat.T, state_sum(prefix_refs, head))
        inv_rms = lax.rsqrt(jnp.mean(numerator * numerator, axis=-1, keepdims=True) + EPSILON)
        normed = numerator * inv_rms
        upstream = rows_of(vg_ref, 1, head, 0, length).astype(f32)
        grad = inv_rms * (
            upstream - normed * jnp.mean(normed * upstream, axis=-1, keepdims=True)
        )
        attended_ref[:, cols] = normed.astype(bf16)
        grad_ref[:, cols] = grad
        if with_state:
            carried_ref[head] = dot3(feat, grad).astype(bf16)


def backward_kernel(with_state, qk_ref, vg_ref, grad_ref, *rest):
    *prefix_refs, grad_qk_ref, grad_v_ref = rest
    length = qk_ref.shape[0] * qk_ref.shape[4]
    tile = min(TILE, length)
    for head in range(grad_v_ref.shape[0]):
        cols = slice(head * DH, (head + 1) * DH)
        q = feature_major(qk_ref, 0, head) * 0.25
        k = feature_major(qk_ref, 1, head)
        left, right = score_sides(q, k)
        q_both = jnp.concatenate(split(q), axis=0)
        k_both = jnp.concatenate(split(k), axis=0)
        grad = grad_ref[:, cols]
        grad_t = grad.T
        if with_state:
            grad_q = pull_psi(q, dot3(state_sum(prefix_refs, head), grad_t), True)
        for at in reversed(range(0, length, tile)):
            width = at + tile
            scores = dot(left[at:width], right[:, :width])
            causal = causal_mask(tile, width)
            v = rows_of(vg_ref, 0, head, 0, width)
            high, low = split(grad[at:width])
            mixing = dot(
                jnp.concatenate([high, low], axis=1), jnp.concatenate([v, v], axis=1), NT
            )
            more = 1.0 + scores
            slopes = split(jnp.where(causal, mixing * more, 0.0))
            kernels = split(jnp.where(causal, more + 0.5 * scores * scores, 0.0))
            both = dot(k_both[:, :width], slopes[0], NT)
            piece = both[:F] + (both[F:] + dot(k_both[:F, :width], slopes[1], NT))
            if with_state:
                piece = piece + grad_q[:, at:width]
            grad_qk_ref[0, head, :, at:width] = piece * 0.25
            both = dot(q_both[:, at:width], slopes[0])
            piece_k = both[:F] + (both[F:] + dot(q_both[:F, at:width], slopes[1]))
            high, low = split(grad_t[:, at:width])
            both = dot(jnp.concatenate([high, low], axis=0), kernels[0])
            piece_v = both[:DH] + (both[DH:] + dot(high, kernels[1]))
            if width == length:
                grad_qk_ref[1, head] = piece_k
                grad_v_ref[head] = piece_v
            else:
                grad_qk_ref[1, head, :, :width] += piece_k
                grad_v_ref[head, :, :width] += piece_v


def rows_kernel(with_state, at_ref, qk_ref, vg_ref, attended_ref, grad_qk_ref, grad_v_ref, *rest):
    *suffix_refs, rows_ref, keep_ref, send_ref, held_ref = rest
    heads, tok = qk_ref.shape[2], qk_ref.shape[4]
    length = qk_ref.shape[0] * tok
    for head in range(heads):
        grad_k, grad_v = grad_qk_ref[1, head], grad_v_ref[head]
        if with_state:
            k = feature_major(qk_ref, 1, head)
            v = rows_of(vg_ref, 0, head, 0, length)
            suffix = state_sum(suffix_refs, head)
            high, low = split(suffix)
            grad_k = grad_k + pull_psi(k, dot(high, v, NT) + dot(low, v, NT), False)
            grad_v = grad_v + dot3(suffix.T, psi(k, False))
        rows_ref[head * F : (head + 1) * F] = grad_qk_ref[0, head].astype(bf16)
        rows_ref[(heads + head) * F : (heads + head + 1) * F] = grad_k.astype(bf16)
        held_ref[:, head * DH : (head + 1) * DH] = grad_v.T.astype(bf16)
    chips = keep_ref.shape[0]
    for shift in range(chips):
        chip = lax.rem(at_ref[0] + shift, chips)
        for core, out_ref in ((at_ref[1], keep_ref), (1 - at_ref[1], send_ref)):
            block = aligned(2 * chip + core, tok)
            out_ref[shift, 0] = attended_ref[block, :]
            out_ref[shift, 1] = held_ref[block, :]


def pair_kernel(at_ref, keep_ref, got_ref, *out_refs):
    for shift, out_ref in enumerate(out_refs):
        out_ref[at_ref[1]] = keep_ref[shift]
        out_ref[1 - at_ref[1]] = got_ref[shift]


def unpack_heads_kernel(at_ref, *rest):
    *part_refs, attended_ref, values_ref = rest
    chips, width = len(part_refs), part_refs[0].shape[3]
    for shift, part_ref in enumerate(part_refs):
        chip = lax.rem(at_ref[0] + chips - shift, chips)
        for core in range(2):
            cols = aligned(2 * chip + core, width)
            attended_ref[0, :, cols] = part_ref[core, 0]
            values_ref[0, :, cols] = part_ref[core, 1]


def place_rows(chip_at, core_at, part_refs, held_ref):
    chips, half = len(part_refs) // 2, part_refs[0].shape[0] // 2
    for shift in range(chips):
        chip = lax.rem(chip_at + chips - shift, chips)
        for side, core in ((0, core_at), (1, 1 - core_at)):
            part_ref = part_refs[2 * shift + side]
            for which in range(2):
                rows = aligned(which * 2 * chips + 2 * chip + core, half)
                held_ref[rows, :] = part_ref[which * half : (which + 1) * half, :]


def product_kernel(group, at_ref, *rest):
    rows_refs, rest = rest[:group], rest[group:]
    tokens_ref, own_rows_ref, other_rows_ref, *part_refs, total_ref, held_ref = rest
    place_rows(at_ref[1], at_ref[2], rows_refs, held_ref)
    total_ref[...] = dot(tokens_ref[...], held_ref[...], NT)
    tok = own_rows_ref.shape[0]
    own_rows_ref[...] = held_ref[:, aligned(2 * at_ref[1] + at_ref[2], tok)].T
    other_rows_ref[...] = held_ref[:, aligned(2 * at_ref[1] + 1 - at_ref[2], tok)].T
    count = len(part_refs)
    size = part_refs[0].shape[0]
    for shift, part_ref in enumerate(part_refs):
        owner = lax.rem(at_ref[0] + shift, count)
        part = total_ref[pl.ds(pl.multiple_of(owner * size, size), size), :]
        part_ref[...] = part.astype(part_ref.dtype)


def run_sum_kernel(arrived, at_ref, *rest):
    own_ref, *rest = rest
    total_ref = rest[-1]
    total = own_ref[...]
    for ref in rest[:arrived]:
        total = total + ref[...].astype(f32)
    total_ref[...] = total
    part_refs = rest[arrived:-1]
    size = part_refs[0].shape[0]
    for shift, part_ref in enumerate(part_refs):
        owner = lax.rem(at_ref[0] + shift, len(part_refs))
        part = total_ref[pl.ds(pl.multiple_of(owner * size, size), size), :]
        part_ref[...] = part.astype(part_ref.dtype)


def grad_tokens_kernel(at_ref, rows_ref, other_rows_ref, weight_ref, *rest):
    count = len(rest) // 2
    fetched_refs, out_ref, other_refs = rest[:count], rest[count], rest[count + 1 :]
    for i, ref in enumerate((weight_ref, *fetched_refs)):
        size = ref.shape[0]
        first = pl.multiple_of(at_ref[i], size)
        out_ref[0, :, pl.ds(first, size)] = dot(rows_ref[...], ref[...], NT).astype(bf16)
    for ref, other_ref in zip(fetched_refs, other_refs):
        other_ref[...] = dot(other_rows_ref[...], ref[...], NT).astype(bf16)


def merge_kernel(at_ref, main_ref, *rest):
    *part_refs, out_ref, sems = rest
    run_copies(
        sems,
        [
            (part_ref, out_ref.at[0, :, pl.ds(pl.multiple_of(at_ref[i], size), size)])
            for i, part_ref in enumerate(part_refs)
            for size in part_ref.shape[1:]
        ],
    )


def final_sum_kernel(own_ref, *rest):
    *part_refs, out_ref = rest
    total = own_ref[...]
    for part_ref in part_refs:
        total = total + part_ref[...].astype(f32)
    out_ref[...] = total


VMEM = pl.BlockSpec(memory_space=pltpu.VMEM)
SMEM = pl.BlockSpec(memory_space=pltpu.SMEM)
FAR = pl.BlockSpec(memory_space=pltpu.HBM)
ANYWHERE = pl.BlockSpec(memory_space=pl.ANY)


def call(
    body,
    outs,
    *operands,
    scalars=(),
    after=(),
    after_far=(),
    scratch=(),
    far_in=(),
    far_out=False,
    copies=(),
    alias=False,
):
    at = [jnp.stack([jnp.int32(s) for s in scalars])] if scalars else []
    count = len(at) + len(operands)

    def kernel(*refs):
        ins, rest = refs[:count], refs[count + len(after) + len(after_far) :]
        body(*ins, *rest[: len(outs)], *rest[len(outs) + 1 :])
        rest[len(outs)][...] = jnp.zeros((8, 128), f32)

    *results, token = pl.pallas_call(
        kernel,
        out_shape=[jax.ShapeDtypeStruct(shape, kind) for shape, kind in [*outs, ((8, 128), f32)]],
        in_specs=[SMEM] * len(at)
        + [FAR if i in far_in else VMEM for i in range(len(operands))]
        + [ANYWHERE] * len(after)
        + [FAR] * len(after_far),
        out_specs=[FAR if far_out else VMEM] * len(outs) + [VMEM],
        scratch_shapes=[*scratch] + [pltpu.SemaphoreType.DMA((n,)) for n in copies],
        input_output_aliases={len(at): 0} if alias else {},
        compiler_params=pltpu.CompilerParams(vmem_limit_bytes=VMEM_LIMIT),
        cost_estimate=pl.CostEstimate(flops=0, bytes_accessed=0, transcendentals=0),
    )(*at, *operands, *after, *after_far)
    return results, token


def local(dp_size, ctx_size, tokens, proj_weight, values, grad_out):
    group = min(GROUP, ctx_size, H)
    runs = ctx_size // group
    heads = H // group
    tok, width = tokens.shape[1:]
    length = group * tok
    cols = proj_weight.shape[1]
    share = width // dp_size
    depth = share // ctx_size
    with_state = runs > 1
    groups = [[run * group + i for i in range(group)] for run in range(runs)]
    wide_groups = [
        [dp * ctx_size + i for dp in range(dp_size) for i in members] for members in groups
    ]
    dp_at, ctx_at = lax.axis_index("dp"), lax.axis_index("ctx")
    run_at, member = ctx_at // group, ctx_at % group

    def exchange(x):
        return lax.all_to_all(
            x, "ctx", split_axis=0, concat_axis=0, tiled=True, axis_index_groups=groups
        )

    def to_dp(x, shift):
        return lax.ppermute(x, "dp", [(i, (i + shift) % dp_size) for i in range(dp_size)])

    def to_member(x, shift):
        pairs = [(i, i - i % group + (i + shift) % group) for i in range(ctx_size)]
        return lax.ppermute(x, "ctx", pairs)

    chips = group // 2
    chip_at, core_at = member // 2, member % 2

    def to_chip(x, shift):
        return x if shift == 0 else to_member(x, 2 * shift)

    def to_other_core(x):
        return lax.ppermute(x, "ctx", [(i, i ^ 1) for i in range(ctx_size)])

    def to_run(x, shift, wrap):
        pairs = [
            (i, (i + shift * group) % ctx_size)
            for i in range(ctx_size)
            if wrap or 0 <= i + shift * group < ctx_size
        ]
        return lax.ppermute(x, "ctx", pairs)

    qk_shape = ((group, 2, heads, F, tok), f32)
    state_shape = ((heads, PSI, DH), bf16)
    blocks_shape = ((2, tok, heads * DH), bf16)
    rows_shape = ((length, heads * DH), f32)

    parts, token = call(
        token_parts_kernel,
        [((tok, share), bf16)] * (dp_size - 1),
        tokens,
        scalars=(dp_at,),
        far_in=(0,),
        far_out=True,
        copies=(dp_size - 1,),
    )
    arrived = [to_dp(part, shift) for shift, part in enumerate(parts, 1)]
    parts, token = call(
        pack_heads_kernel,
        [((2, 2, tok, heads * DH), bf16)] * chips,
        values,
        grad_out,
        scalars=(chip_at, core_at),
        after=(token,),
    )
    heads_parts = [to_chip(part, shift) for shift, part in enumerate(parts)]
    (keep, send), _ = call(
        split_cores_kernel,
        [((chips, 2, tok, heads * DH), bf16)] * 2,
        *heads_parts,
        scalars=(chip_at, core_at),
    )
    (vg,), _ = call(
        collect_heads_kernel,
        [((group, 2, tok, heads * DH), bf16)],
        keep,
        to_other_core(send),
        scalars=(chip_at, core_at),
    )
    (projected,), token = call(
        project_kernel,
        [qk_shape],
        tokens,
        proj_weight,
        scalars=(dp_at,),
        after=(token,),
        far_in=(0,),
        copies=(1,),
        scratch=[pltpu.VMEM((tok, share), bf16)],
    )
    part_shape = (tok, dp_size * runs * depth)
    if depth % 128 == 0:
        (keep, send), pack_token = call(
            functools.partial(pack_tokens_kernel, depth),
            [((chips,) + part_shape, bf16)] * 2,
            tokens,
            scalars=(chip_at, core_at),
            after_far=heads_parts[1:2],
        )
    else:
        blocks = tokens[0].reshape(tok, dp_size * runs, chips, 2, depth).transpose(2, 3, 0, 1, 4)
        blocks = blocks.reshape(chips, 2, *part_shape)
        blocks = jnp.stack([blocks[(chip_at + shift) % chips] for shift in range(chips)])
        keep, send = blocks[:, core_at], blocks[:, 1 - core_at]
        pack_token = token
    token_parts, _ = call(
        pair_kernel,
        [((2,) + part_shape, bf16)] * chips,
        keep,
        to_other_core(send),
        scalars=(chip_at, core_at),
    )
    token_parts = [to_chip(part, shift) for shift, part in enumerate(token_parts)]
    parity = ctx_at % 2
    piece = share // 2
    (mine,), mine_token = call(
        weight_piece_kernel,
        [((piece, cols), bf16)],
        proj_weight,
        scalars=(parity,),
        after_far=heads_parts[1:2],
        far_in=(0,),
        far_out=True,
        copies=(1,),
    )
    (projected,), _ = call(
        project_rest_kernel,
        [((dp_size,) + qk_shape[0], f32)],
        projected,
        proj_weight,
        *arrived,
        scalars=(dp_at,),
        after=(token, pack_token, mine_token),
        after_far=heads_parts[1:],
    )
    qk_parts = lax.all_to_all(
        projected.reshape((dp_size * group,) + qk_shape[0][1:]),
        ("dp", "ctx"),
        split_axis=0,
        concat_axis=0,
        tiled=True,
        axis_index_groups=wide_groups,
    ).reshape(projected.shape)

    fetched = [to_dp(mine, shift) for shift in range(1, dp_size)]
    bases = [(dp_at + dp_size - shift) % dp_size * share for shift in range(1, dp_size)]

    (qk, *state), token = call(
        functools.partial(state_kernel, with_state),
        [qk_shape] + [state_shape] * with_state,
        qk_parts,
        vg,
    )
    prefix, suffix = (), ()
    if with_state:
        prefix = [to_run(state[0], shift, False) for shift in range(1, runs)]
    (numerator,), token = call(numerator_kernel, [rows_shape], qk, vg)
    (attended, grad_num, *carried), token = call(
        functools.partial(normalize_kernel, with_state),
        [((length, heads * DH), bf16), rows_shape] + [state_shape] * with_state,
        qk,
        vg,
        numerator,
        *prefix,
        after_far=token_parts[1:],
    )
    if with_state:
        suffix = [to_run(carried[0], -shift, False) for shift in range(1, runs)]
    (grad_qk, grad_v), token = call(
        functools.partial(backward_kernel, with_state),
        [((2, heads, F, length), f32), ((heads, DH, length), f32)],
        qk,
        vg,
        grad_num,
        *prefix,
    )
    (token_cols,), token = call(
        collect_tokens_kernel,
        [(part_shape[1:] + (length,), bf16)],
        *token_parts,
        scalars=(chip_at,),
        after=(token,),
    )
    (rows, keep, send), token = call(
        functools.partial(rows_kernel, with_state),
        [((2 * heads * F, length), bf16)] + [((chips, 2, tok, heads * DH), bf16)] * 2,
        qk,
        vg,
        attended,
        grad_qk,
        grad_v,
        *suffix,
        scalars=(chip_at, core_at),
        after=(token,),
        scratch=[pltpu.VMEM((length, heads * DH), bf16)],
    )
    rows = [to_chip(rows, shift) for shift in range(chips)]
    rows = [side for part in rows for side in (part, to_other_core(part))]
    got = to_other_core(send)
    results, token = call(
        pair_kernel,
        [((2, 2, tok, heads * DH), bf16)] * chips,
        keep,
        got,
        scalars=(chip_at, core_at),
    )
    results = [to_chip(part, shift) for shift, part in enumerate(results)]

    held = pltpu.VMEM((cols, length), bf16)
    (own_rows, other_rows, own, *parts), token = call(
        functools.partial(product_kernel, 2 * chips),
        [((tok, cols), bf16)] * 2
        + [((runs * depth, cols), f32)] + [((runs * depth, cols), bf16)] * (dp_size - 1),
        *rows,
        token_cols,
        scalars=(dp_at, chip_at, core_at),
        after=(token,),
        scratch=[pltpu.VMEM((dp_size * runs * depth, cols), f32), held],
    )
    parts = [to_dp(part, shift) for shift, part in enumerate(parts, 1)]
    (grad_tokens, *others), tokens_token = call(
        grad_tokens_kernel,
        [((1, tok, width), bf16)] + [((tok, piece), bf16)] * (dp_size - 1),
        own_rows,
        other_rows,
        proj_weight,
        *fetched,
        scalars=[dp_at * share] + [base + parity * piece for base in bases],
        after=(token,),
    )
    (grad_proj, *parts), token = call(
        functools.partial(run_sum_kernel, len(parts)),
        [((depth, cols), f32)] + [((depth, cols), bf16)] * (runs - 1),
        own,
        *parts,
        scalars=(run_at,),
        scratch=[pltpu.VMEM((runs * depth, cols), f32)],
    )
    (attended, grad_values), token = call(
        unpack_heads_kernel,
        [((1, tok, H * DH), bf16)] * 2,
        *results,
        scalars=(chip_at,),
        after=(token,),
    )
    (grad_tokens,), tokens_token = call(
        merge_kernel,
        [((1, tok, width), bf16)],
        grad_tokens,
        *[to_other_core(other) for other in others],
        scalars=[base + (1 - parity) * piece for base in bases],
        far_in=(0,),
        far_out=True,
        copies=(dp_size - 1,),
        alias=True,
    )
    (grad_proj,), _ = call(
        final_sum_kernel,
        [((depth, cols), f32)],
        grad_proj,
        *[to_run(part, shift, True) for shift, part in enumerate(parts, 1)],
        after=(token, tokens_token),
    )
    return (attended, grad_tokens, grad_values, grad_proj)


def solution(mesh):
    return jax.shard_map(
        functools.partial(local, mesh.shape["dp"], mesh.shape["ctx"]),
        mesh=mesh,
        in_specs=(P("dp", "ctx", None), P("dp", None), P("dp", "ctx", None), P("dp", "ctx", None)),
        out_specs=(
            P("dp", "ctx", None),
            P("dp", "ctx", None),
            P("dp", "ctx", None),
            P(("dp", "ctx"), None),
        ),
        check_vma=False,
    )
```

```python
import functools

import jax
import jax.numpy as jnp
from jax import lax
from jax.experimental import pallas as pl
from jax.experimental.pallas import tpu as pltpu
from jax.sharding import PartitionSpec as P

H = 16
F = 16
DH = 128
EPSILON = 1e-05
GROUP = 8
TILE = 256
VMEM_LIMIT = 12 * 1024 * 1024
PSI = 9 * F + 2 * F
PSI_SCALE = (0.5,) + (1.0,) * 7 + (0.5,)

f32 = jnp.float32
bf16 = jnp.bfloat16

NN = (((1,), (0,)), ((), ()))
NT = (((1,), (1,)), ((), ()))


def dot(a, b, dims=NN):
    return lax.dot_general(a, b, dims, preferred_element_type=f32)


def split(x):
    high = x.astype(bf16)
    return high, (x - high.astype(f32)).astype(bf16)


def dot3(a, b, dims=NN):
    a_high, a_low = split(a)
    b_high, b_low = split(b)
    return dot(a_high, b_high, dims) + (dot(a_high, b_low, dims) + dot(a_low, b_high, dims))


def turned(x, r):
    return x if r == 0 else jnp.concatenate([x[r:], x[:r]], axis=0)


def psi(x, weights):
    parts = []
    for r in range(9):
        part = x * turned(x, r)
        parts.append(part * PSI_SCALE[r] if weights and PSI_SCALE[r] != 1.0 else part)
    row = lax.broadcasted_iota(jnp.int32, x.shape, 0)
    return jnp.concatenate(parts + [x, jnp.where(row == 0, 1.0, 0.0)], axis=0)


def pull_psi(x, upstream, weights):
    total = upstream[9 * F : 10 * F]
    for r in range(9):
        part = upstream[r * F : (r + 1) * F]
        if weights and PSI_SCALE[r] != 1.0:
            part = part * PSI_SCALE[r]
        total = total + part * turned(x, r) + turned(part * x, (F - r) % F)
    return total


def feature_major(qk_ref, which, head):
    return jnp.concatenate([qk_ref[src, which, head] for src in range(qk_ref.shape[0])], axis=1)


def rows_of(ref, which, head, start, stop):
    tok = ref.shape[2]
    return jnp.concatenate(
        [
            ref[src, which, :, head * DH : (head + 1) * DH]
            for src in range(start // tok, stop // tok)
        ],
        axis=0,
    )


def score_sides(q, k):
    q_high, q_low = split(q)
    k_high, k_low = split(k)
    left = jnp.concatenate([q_high, q_high, q_low, q_low], axis=0)
    right = jnp.concatenate([k_high, k_low, k_high, k_low], axis=0)
    return left.T, right


def causal_mask(tile, width):
    row = lax.broadcasted_iota(jnp.int32, (tile, width), 0) + (width - tile)
    return row >= lax.broadcasted_iota(jnp.int32, (tile, width), 1)


def run_copies(sems, pairs):
    copies = [
        pltpu.make_async_copy(source, target, sems.at[i])
        for i, (source, target) in enumerate(pairs)
    ]
    for copy in copies:
        copy.start()
    for copy in copies:
        copy.wait()


def aligned(at, size):
    return pl.ds(pl.multiple_of(at * size, size), size)


def token_parts_kernel(at_ref, tokens_ref, *rest):
    *out_refs, sems = rest
    count, share = len(out_refs) + 1, out_refs[0].shape[1]
    run_copies(
        sems,
        [
            (tokens_ref.at[0, :, aligned(lax.rem(at_ref[0] + shift, count), share)], out_ref)
            for shift, out_ref in enumerate(out_refs, 1)
        ],
    )


def pack_heads_kernel(at_ref, values_ref, grad_ref, *out_refs):
    chips, width = len(out_refs), out_refs[0].shape[3]
    for shift, out_ref in enumerate(out_refs):
        chip = lax.rem(at_ref[0] + shift, chips)
        for core in range(2):
            cols = aligned(2 * chip + core, width)
            out_ref[core, 0] = values_ref[0, :, cols]
            out_ref[core, 1] = grad_ref[0, :, cols]


def split_cores_kernel(at_ref, *rest):
    *part_refs, keep_ref, send_ref = rest
    for shift, part_ref in enumerate(part_refs):
        keep_ref[shift] = part_ref[at_ref[1]]
        send_ref[shift] = part_ref[1 - at_ref[1]]


def collect_heads_kernel(at_ref, keep_ref, got_ref, out_ref):
    chips = keep_ref.shape[0]
    for shift in range(chips):
        chip = lax.rem(at_ref[0] + chips - shift, chips)
        out_ref[2 * chip + at_ref[1]] = keep_ref[shift]
        out_ref[2 * chip + 1 - at_ref[1]] = got_ref[shift]


def pack_tokens_kernel(depth, at_ref, tokens_ref, keep_ref, send_ref):
    chips, _, rows = keep_ref.shape
    for shift in range(chips):
        chip = lax.rem(at_ref[0] + shift, chips)
        for core, out_ref in ((at_ref[1], keep_ref), (1 - at_ref[1], send_ref)):
            for part in range(rows // depth):
                cols = aligned(2 * (part * chips + chip) + core, depth)
                out_ref[shift, :, part * depth : (part + 1) * depth] = tokens_ref[0, :, cols]


def collect_tokens_kernel(at_ref, *rest):
    *part_refs, out_ref = rest
    chips, tok = len(part_refs), part_refs[0].shape[1]
    for shift, part_ref in enumerate(part_refs):
        chip = lax.rem(at_ref[0] + chips - shift, chips)
        for core in range(2):
            out_ref[:, aligned(2 * chip + core, tok)] = part_ref[core].T


def write_blocks(projected, out_ref):
    group, _, heads, feat, _ = out_ref.shape
    for member in range(group):
        for which in range(2):
            for head in range(heads):
                first = ((which * group + member) * heads + head) * feat
                out_ref[member, which, head] = projected[first : first + feat]


def project_kernel(at_ref, tokens_ref, weight_ref, out_ref, part_ref, sem):
    share = part_ref.shape[1]
    run_copies(sem, [(tokens_ref.at[0, :, aligned(at_ref[0], share)], part_ref)])
    write_blocks(dot(part_ref[...], weight_ref[...]).T, out_ref)


def project_rest_kernel(at_ref, own_ref, weight_ref, *rest):
    *part_refs, out_ref = rest
    count = len(part_refs) + 1
    at = at_ref[0]
    out_ref[at] = own_ref[...]
    for shift, part_ref in enumerate(part_refs, 1):
        owner = lax.rem(at + count - shift, count)
        write_blocks(dot(part_ref[...], weight_ref[...]).T, out_ref.at[owner])


def weight_piece_kernel(at_ref, weight_ref, out_ref, sems):
    run_copies(sems, [(weight_ref.at[aligned(at_ref[0], out_ref.shape[0])], out_ref)])


def state_sum(refs, head):
    total = refs[0][head].astype(f32)
    for ref in refs[1:]:
        total = total + ref[head].astype(f32)
    return total


def state_kernel(with_state, parts_ref, vg_ref, qk_ref, *state_refs):
    count, blocks, _, heads, _, tok = parts_ref.shape
    for head in range(heads):
        for which in range(2):
            for src in range(blocks):
                total = parts_ref[0, src, which, head]
                for part in range(1, count):
                    total = total + parts_ref[part, src, which, head]
                qk_ref[src, which, head] = total
        if with_state:
            high, low = split(psi(feature_major(qk_ref, 1, head), False))
            v = rows_of(vg_ref, 0, head, 0, blocks * tok)
            state_refs[0][head] = (dot(high, v) + dot(low, v)).astype(bf16)


def numerator_kernel(qk_ref, vg_ref, num_ref):
    heads = qk_ref.shape[2]
    length = qk_ref.shape[0] * qk_ref.shape[4]
    tile = min(TILE, length)
    for head in range(heads):
        q = feature_major(qk_ref, 0, head) * 0.25
        k = feature_major(qk_ref, 1, head)
        left, right = score_sides(q, k)
        for at in range(0, length, tile):
            width = at + tile
            scores = dot(left[at:width], right[:, :width])
            kernel = jnp.where(
                causal_mask(tile, width), 1.0 + scores * (1.0 + 0.5 * scores), 0.0
            )
            high, low = split(kernel)
            v = rows_of(vg_ref, 0, head, 0, width)
            num_ref[at:width, head * DH : (head + 1) * DH] = dot(high, v) + dot(low, v)


def normalize_kernel(with_state, qk_ref, vg_ref, num_ref, *rest):
    if with_state:
        *prefix_refs, attended_ref, grad_ref, carried_ref = rest
    else:
        attended_ref, grad_ref = rest
    heads = qk_ref.shape[2]
    blocks, tok = qk_ref.shape[0], qk_ref.shape[4]
    length = blocks * tok
    for head in range(heads):
        cols = slice(head * DH, (head + 1) * DH)
        numerator = num_ref[:, cols]
        if with_state:
            feat = psi(feature_major(qk_ref, 0, head) * 0.25, True)
            numerator = numerator + dot3(feat.T, state_sum(prefix_refs, head))
        inv_rms = lax.rsqrt(jnp.mean(numerator * numerator, axis=-1, keepdims=True) + EPSILON)
        normed = numerator * inv_rms
        upstream = rows_of(vg_ref, 1, head, 0, length).astype(f32)
        grad = inv_rms * (
            upstream - normed * jnp.mean(normed * upstream, axis=-1, keepdims=True)
        )
        attended_ref[:, cols] = normed.astype(bf16)
        grad_ref[:, cols] = grad
        if with_state:
            carried_ref[head] = dot3(feat, grad).astype(bf16)


def backward_kernel(with_state, qk_ref, vg_ref, grad_ref, *rest):
    *prefix_refs, grad_qk_ref, grad_v_ref = rest
    length = qk_ref.shape[0] * qk_ref.shape[4]
    tile = min(TILE, length)
    for head in range(grad_v_ref.shape[0]):
        cols = slice(head * DH, (head + 1) * DH)
        q = feature_major(qk_ref, 0, head) * 0.25
        k = feature_major(qk_ref, 1, head)
        left, right = score_sides(q, k)
        q_both = jnp.concatenate(split(q), axis=0)
        k_both = jnp.concatenate(split(k), axis=0)
        grad = grad_ref[:, cols]
        grad_t = grad.T
        if with_state:
            grad_q = pull_psi(q, dot3(state_sum(prefix_refs, head), grad_t), True)
        for at in reversed(range(0, length, tile)):
            width = at + tile
            scores = dot(left[at:width], right[:, :width])
            causal = causal_mask(tile, width)
            v = rows_of(vg_ref, 0, head, 0, width)
            high, low = split(grad[at:width])
            mixing = dot(
                jnp.concatenate([high, low], axis=1), jnp.concatenate([v, v], axis=1), NT
            )
            more = 1.0 + scores
            slopes = split(jnp.where(causal, mixing * more, 0.0))
            kernels = split(jnp.where(causal, more + 0.5 * scores * scores, 0.0))
            both = dot(k_both[:, :width], slopes[0], NT)
            piece = both[:F] + (both[F:] + dot(k_both[:F, :width], slopes[1], NT))
            if with_state:
                piece = piece + grad_q[:, at:width]
            grad_qk_ref[0, head, :, at:width] = piece * 0.25
            both = dot(q_both[:, at:width], slopes[0])
            piece_k = both[:F] + (both[F:] + dot(q_both[:F, at:width], slopes[1]))
            high, low = split(grad_t[:, at:width])
            both = dot(jnp.concatenate([high, low], axis=0), kernels[0])
            piece_v = both[:DH] + (both[DH:] + dot(high, kernels[1]))
            if width == length:
                grad_qk_ref[1, head] = piece_k
                grad_v_ref[head] = piece_v
            else:
                grad_qk_ref[1, head, :, :width] += piece_k
                grad_v_ref[head, :, :width] += piece_v


def rows_kernel(with_state, at_ref, qk_ref, vg_ref, attended_ref, grad_qk_ref, grad_v_ref, *rest):
    *suffix_refs, rows_ref, keep_ref, send_ref, held_ref = rest
    heads, tok = qk_ref.shape[2], qk_ref.shape[4]
    length = qk_ref.shape[0] * tok
    for head in range(heads):
        grad_k, grad_v = grad_qk_ref[1, head], grad_v_ref[head]
        if with_state:
            k = feature_major(qk_ref, 1, head)
            v = rows_of(vg_ref, 0, head, 0, length)
            suffix = state_sum(suffix_refs, head)
            high, low = split(suffix)
            grad_k = grad_k + pull_psi(k, dot(high, v, NT) + dot(low, v, NT), False)
            grad_v = grad_v + dot3(suffix.T, psi(k, False))
        rows_ref[head * F : (head + 1) * F] = grad_qk_ref[0, head].astype(bf16)
        rows_ref[(heads + head) * F : (heads + head + 1) * F] = grad_k.astype(bf16)
        held_ref[:, head * DH : (head + 1) * DH] = grad_v.T.astype(bf16)
    chips = keep_ref.shape[0]
    for shift in range(chips):
        chip = lax.rem(at_ref[0] + shift, chips)
        for core, out_ref in ((at_ref[1], keep_ref), (1 - at_ref[1], send_ref)):
            block = aligned(2 * chip + core, tok)
            out_ref[shift, 0] = attended_ref[block, :]
            out_ref[shift, 1] = held_ref[block, :]


def pair_kernel(at_ref, keep_ref, got_ref, *out_refs):
    for shift, out_ref in enumerate(out_refs):
        out_ref[at_ref[1]] = keep_ref[shift]
        out_ref[1 - at_ref[1]] = got_ref[shift]


def unpack_heads_kernel(at_ref, *rest):
    *part_refs, attended_ref, values_ref = rest
    chips, width = len(part_refs), part_refs[0].shape[3]
    for shift, part_ref in enumerate(part_refs):
        chip = lax.rem(at_ref[0] + chips - shift, chips)
        for core in range(2):
            cols = aligned(2 * chip + core, width)
            attended_ref[0, :, cols] = part_ref[core, 0]
            values_ref[0, :, cols] = part_ref[core, 1]


def place_rows(chip_at, core_at, part_refs, held_ref):
    chips, half = len(part_refs) // 2, part_refs[0].shape[0] // 2
    for shift in range(chips):
        chip = lax.rem(chip_at + chips - shift, chips)
        for side, core in ((0, core_at), (1, 1 - core_at)):
            part_ref = part_refs[2 * shift + side]
            for which in range(2):
                rows = aligned(which * 2 * chips + 2 * chip + core, half)
                held_ref[rows, :] = part_ref[which * half : (which + 1) * half, :]


def product_kernel(group, at_ref, *rest):
    rows_refs, rest = rest[:group], rest[group:]
    tokens_ref, own_rows_ref, other_rows_ref, *part_refs, total_ref, held_ref = rest
    place_rows(at_ref[1], at_ref[2], rows_refs, held_ref)
    total_ref[...] = dot(tokens_ref[...], held_ref[...], NT)
    tok = own_rows_ref.shape[0]
    own_rows_ref[...] = held_ref[:, aligned(2 * at_ref[1] + at_ref[2], tok)].T
    other_rows_ref[...] = held_ref[:, aligned(2 * at_ref[1] + 1 - at_ref[2], tok)].T
    count = len(part_refs)
    size = part_refs[0].shape[0]
    for shift, part_ref in enumerate(part_refs):
        owner = lax.rem(at_ref[0] + shift, count)
        part = total_ref[pl.ds(pl.multiple_of(owner * size, size), size), :]
        part_ref[...] = part.astype(part_ref.dtype)


def run_sum_kernel(arrived, at_ref, *rest):
    own_ref, *rest = rest
    total_ref = rest[-1]
    total = own_ref[...]
    for ref in rest[:arrived]:
        total = total + ref[...].astype(f32)
    total_ref[...] = total
    part_refs = rest[arrived:-1]
    size = part_refs[0].shape[0]
    for shift, part_ref in enumerate(part_refs):
        owner = lax.rem(at_ref[0] + shift, len(part_refs))
        part = total_ref[pl.ds(pl.multiple_of(owner * size, size), size), :]
        part_ref[...] = part.astype(part_ref.dtype)


def grad_tokens_kernel(at_ref, rows_ref, other_rows_ref, weight_ref, *rest):
    count = len(rest) // 2
    fetched_refs, out_ref, other_refs = rest[:count], rest[count], rest[count + 1 :]
    for i, ref in enumerate((weight_ref, *fetched_refs)):
        size = ref.shape[0]
        first = pl.multiple_of(at_ref[i], size)
        out_ref[0, :, pl.ds(first, size)] = dot(rows_ref[...], ref[...], NT).astype(bf16)
    for ref, other_ref in zip(fetched_refs, other_refs):
        other_ref[...] = dot(other_rows_ref[...], ref[...], NT).astype(bf16)


def merge_kernel(at_ref, main_ref, *rest):
    *part_refs, out_ref, sems = rest
    run_copies(
        sems,
        [
            (part_ref, out_ref.at[0, :, pl.ds(pl.multiple_of(at_ref[i], size), size)])
            for i, part_ref in enumerate(part_refs)
            for size in part_ref.shape[1:]
        ],
    )


def final_sum_kernel(own_ref, *rest):
    *part_refs, out_ref = rest
    total = own_ref[...]
    for part_ref in part_refs:
        total = total + part_ref[...].astype(f32)
    out_ref[...] = total


VMEM = pl.BlockSpec(memory_space=pltpu.VMEM)
SMEM = pl.BlockSpec(memory_space=pltpu.SMEM)
FAR = pl.BlockSpec(memory_space=pltpu.HBM)
ANYWHERE = pl.BlockSpec(memory_space=pl.ANY)


def call(
    body,
    outs,
    *operands,
    scalars=(),
    after=(),
    after_far=(),
    scratch=(),
    far_in=(),
    far_out=False,
    copies=(),
    alias=False,
):
    at = [jnp.stack([jnp.int32(s) for s in scalars])] if scalars else []
    count = len(at) + len(operands)

    def kernel(*refs):
        ins, rest = refs[:count], refs[count + len(after) + len(after_far) :]
        body(*ins, *rest[: len(outs)], *rest[len(outs) + 1 :])
        rest[len(outs)][...] = jnp.zeros((8, 128), f32)

    *results, token = pl.pallas_call(
        kernel,
        out_shape=[jax.ShapeDtypeStruct(shape, kind) for shape, kind in [*outs, ((8, 128), f32)]],
        in_specs=[SMEM] * len(at)
        + [FAR if i in far_in else VMEM for i in range(len(operands))]
        + [ANYWHERE] * len(after)
        + [FAR] * len(after_far),
        out_specs=[FAR if far_out else VMEM] * len(outs) + [VMEM],
        scratch_shapes=[*scratch] + [pltpu.SemaphoreType.DMA((n,)) for n in copies],
        input_output_aliases={len(at): 0} if alias else {},
        compiler_params=pltpu.CompilerParams(vmem_limit_bytes=VMEM_LIMIT),
        cost_estimate=pl.CostEstimate(flops=0, bytes_accessed=0, transcendentals=0),
    )(*at, *operands, *after, *after_far)
    return results, token


def local(dp_size, ctx_size, tokens, proj_weight, values, grad_out):
    group = min(GROUP, ctx_size, H)
    runs = ctx_size // group
    heads = H // group
    tok, width = tokens.shape[1:]
    length = group * tok
    cols = proj_weight.shape[1]
    share = width // dp_size
    depth = share // ctx_size
    with_state = runs > 1
    groups = [[run * group + i for i in range(group)] for run in range(runs)]
    wide_groups = [
        [dp * ctx_size + i for dp in range(dp_size) for i in members] for members in groups
    ]
    dp_at, ctx_at = lax.axis_index("dp"), lax.axis_index("ctx")
    run_at, member = ctx_at // group, ctx_at % group

    def exchange(x):
        return lax.all_to_all(
            x, "ctx", split_axis=0, concat_axis=0, tiled=True, axis_index_groups=groups
        )

    def to_dp(x, shift):
        return lax.ppermute(x, "dp", [(i, (i + shift) % dp_size) for i in range(dp_size)])

    def to_member(x, shift):
        pairs = [(i, i - i % group + (i + shift) % group) for i in range(ctx_size)]
        return lax.ppermute(x, "ctx", pairs)

    chips = group // 2
    chip_at, core_at = member // 2, member % 2

    def to_chip(x, shift):
        return x if shift == 0 else to_member(x, 2 * shift)

    def to_other_core(x):
        return lax.ppermute(x, "ctx", [(i, i ^ 1) for i in range(ctx_size)])

    def to_run(x, shift, wrap):
        pairs = [
            (i, (i + shift * group) % ctx_size)
            for i in range(ctx_size)
            if wrap or 0 <= i + shift * group < ctx_size
        ]
        return lax.ppermute(x, "ctx", pairs)

    qk_shape = ((group, 2, heads, F, tok), f32)
    state_shape = ((heads, PSI, DH), bf16)
    blocks_shape = ((2, tok, heads * DH), bf16)
    rows_shape = ((length, heads * DH), f32)

    parts, token = call(
        token_parts_kernel,
        [((tok, share), bf16)] * (dp_size - 1),
        tokens,
        scalars=(dp_at,),
        far_in=(0,),
        far_out=True,
        copies=(dp_size - 1,),
    )
    arrived = [to_dp(part, shift) for shift, part in enumerate(parts, 1)]
    parts, token = call(
        pack_heads_kernel,
        [((2, 2, tok, heads * DH), bf16)] * chips,
        values,
        grad_out,
        scalars=(chip_at, core_at),
        after=(token,),
    )
    heads_parts = [to_chip(part, shift) for shift, part in enumerate(parts)]
    (keep, send), _ = call(
        split_cores_kernel,
        [((chips, 2, tok, heads * DH), bf16)] * 2,
        *heads_parts,
        scalars=(chip_at, core_at),
    )
    (vg,), _ = call(
        collect_heads_kernel,
        [((group, 2, tok, heads * DH), bf16)],
        keep,
        to_other_core(send),
        scalars=(chip_at, core_at),
    )
    (projected,), token = call(
        project_kernel,
        [qk_shape],
        tokens,
        proj_weight,
        scalars=(dp_at,),
        after=(token,),
        far_in=(0,),
        copies=(1,),
        scratch=[pltpu.VMEM((tok, share), bf16)],
    )
    part_shape = (tok, dp_size * runs * depth)
    if depth % 128 == 0:
        (keep, send), pack_token = call(
            functools.partial(pack_tokens_kernel, depth),
            [((chips,) + part_shape, bf16)] * 2,
            tokens,
            scalars=(chip_at, core_at),
            after_far=heads_parts[1:2],
        )
    else:
        blocks = tokens[0].reshape(tok, dp_size * runs, chips, 2, depth).transpose(2, 3, 0, 1, 4)
        blocks = blocks.reshape(chips, 2, *part_shape)
        blocks = jnp.stack([blocks[(chip_at + shift) % chips] for shift in range(chips)])
        keep, send = blocks[:, core_at], blocks[:, 1 - core_at]
        pack_token = token
    token_parts, _ = call(
        pair_kernel,
        [((2,) + part_shape, bf16)] * chips,
        keep,
        to_other_core(send),
        scalars=(chip_at, core_at),
    )
    token_parts = [to_chip(part, shift) for shift, part in enumerate(token_parts)]
    parity = ctx_at % 2
    piece = share // 2
    (mine,), mine_token = call(
        weight_piece_kernel,
        [((piece, cols), bf16)],
        proj_weight,
        scalars=(parity,),
        after_far=heads_parts[1:2],
        far_in=(0,),
        far_out=True,
        copies=(1,),
    )
    (projected,), _ = call(
        project_rest_kernel,
        [((dp_size,) + qk_shape[0], f32)],
        projected,
        proj_weight,
        *arrived,
        scalars=(dp_at,),
        after=(token, pack_token, mine_token),
        after_far=heads_parts[1:],
    )
    qk_parts = lax.all_to_all(
        projected.reshape((dp_size * group,) + qk_shape[0][1:]),
        ("dp", "ctx"),
        split_axis=0,
        concat_axis=0,
        tiled=True,
        axis_index_groups=wide_groups,
    ).reshape(projected.shape)

    fetched = [to_dp(mine, shift) for shift in range(1, dp_size)]
    bases = [(dp_at + dp_size - shift) % dp_size * share for shift in range(1, dp_size)]

    (qk, *state), token = call(
        functools.partial(state_kernel, with_state),
        [qk_shape] + [state_shape] * with_state,
        qk_parts,
        vg,
    )
    prefix, suffix = (), ()
    if with_state:
        prefix = [to_run(state[0], shift, False) for shift in range(1, runs)]
    (numerator,), token = call(numerator_kernel, [rows_shape], qk, vg)
    (attended, grad_num, *carried), token = call(
        functools.partial(normalize_kernel, with_state),
        [((length, heads * DH), bf16), rows_shape] + [state_shape] * with_state,
        qk,
        vg,
        numerator,
        *prefix,
        after_far=token_parts[1:],
    )
    if with_state:
        suffix = [to_run(carried[0], -shift, False) for shift in range(1, runs)]
    (grad_qk, grad_v), token = call(
        functools.partial(backward_kernel, with_state),
        [((2, heads, F, length), f32), ((heads, DH, length), f32)],
        qk,
        vg,
        grad_num,
        *prefix,
    )
    (token_cols,), token = call(
        collect_tokens_kernel,
        [(part_shape[1:] + (length,), bf16)],
        *token_parts,
        scalars=(chip_at,),
        after=(token,),
    )
    (rows, keep, send), token = call(
        functools.partial(rows_kernel, with_state),
        [((2 * heads * F, length), bf16)] + [((chips, 2, tok, heads * DH), bf16)] * 2,
        qk,
        vg,
        attended,
        grad_qk,
        grad_v,
        *suffix,
        scalars=(chip_at, core_at),
        after=(token,),
        scratch=[pltpu.VMEM((length, heads * DH), bf16)],
    )
    rows = [to_chip(rows, shift) for shift in range(chips)]
    rows = [side for part in rows for side in (part, to_other_core(part))]
    got = to_other_core(send)
    results, token = call(
        pair_kernel,
        [((2, 2, tok, heads * DH), bf16)] * chips,
        keep,
        got,
        scalars=(chip_at, core_at),
    )
    results = [to_chip(part, shift) for shift, part in enumerate(results)]

    held = pltpu.VMEM((cols, length), bf16)
    (own_rows, other_rows, own, *parts), token = call(
        functools.partial(product_kernel, 2 * chips),
        [((tok, cols), bf16)] * 2
        + [((runs * depth, cols), f32)] + [((runs * depth, cols), bf16)] * (dp_size - 1),
        *rows,
        token_cols,
        scalars=(dp_at, chip_at, core_at),
        after=(token,),
        scratch=[pltpu.VMEM((dp_size * runs * depth, cols), f32), held],
    )
    parts = [to_dp(part, shift) for shift, part in enumerate(parts, 1)]
    (grad_tokens, *others), tokens_token = call(
        grad_tokens_kernel,
        [((1, tok, width), bf16)] + [((tok, piece), bf16)] * (dp_size - 1),
        own_rows,
        other_rows,
        proj_weight,
        *fetched,
        scalars=[dp_at * share] + [base + parity * piece for base in bases],
        after=(token,),
    )
    (grad_proj, *parts), token = call(
        functools.partial(run_sum_kernel, len(parts)),
        [((depth, cols), f32)] + [((depth, cols), bf16)] * (runs - 1),
        own,
        *parts,
        scalars=(run_at,),
        after=(tokens_token,),
        scratch=[pltpu.VMEM((runs * depth, cols), f32)],
    )
    (attended, grad_values), token = call(
        unpack_heads_kernel,
        [((1, tok, H * DH), bf16)] * 2,
        *results,
        scalars=(chip_at,),
        after=(token,),
    )
    (grad_tokens,), tokens_token = call(
        merge_kernel,
        [((1, tok, width), bf16)],
        grad_tokens,
        *[to_other_core(other) for other in others],
        scalars=[base + (1 - parity) * piece for base in bases],
        far_in=(0,),
        far_out=True,
        copies=(dp_size - 1,),
        alias=True,
    )
    (grad_proj,), _ = call(
        final_sum_kernel,
        [((depth, cols), f32)],
        grad_proj,
        *[to_run(part, shift, True) for shift, part in enumerate(parts, 1)],
        after=(token, tokens_token),
    )
    return (attended, grad_tokens, grad_values, grad_proj)


def solution(mesh):
    return jax.shard_map(
        functools.partial(local, mesh.shape["dp"], mesh.shape["ctx"]),
        mesh=mesh,
        in_specs=(P("dp", "ctx", None), P("dp", None), P("dp", "ctx", None), P("dp", "ctx", None)),
        out_specs=(
            P("dp", "ctx", None),
            P("dp", "ctx", None),
            P("dp", "ctx", None),
            P(("dp", "ctx"), None),
        ),
        check_vma=False,
    )
```
